32 devices in a mesh: dp: 8 (over z, y), tensor: 4 (over x, core).
Axes of the slice: x: 2, y: 2, z: 4, core: 2. Of those that a mesh axis runs over, the one named last changes fastest.
Arguments:
- tokens: bfloat16 [8192, 1024], P('dp'), may hold values from -6 to 6
- lengths: int32 [8], P('dp'), may hold values from 256 to 1024, as said below
- chosen: int32 [8192, 8], P('dp'), may hold values from 0 to 15, all different within a row
- gate_values: float32 [8192, 8], P('dp'), may hold values from 0.05 to 0.25
- cotangent: bfloat16 [8192, 1024], P('dp'), may hold values from -6 to 6
- norm_attn: float32 [1024], replicated, may hold values from 0.5 to 1.5
- w_query: bfloat16 [1024, 1024], P(None, 'tensor'), may hold values from -0.1875 to 0.1875
- w_key: bfloat16 [1024, 512], P(None, 'tensor'), may hold values from -0.1875 to 0.1875
- w_value: bfloat16 [1024, 512], P(None, 'tensor'), may hold values from -0.1875 to 0.1875
- w_out: bfloat16 [1024, 1024], P('tensor'), may hold values from -3 to 3
- norm_moe: float32 [1024], replicated, may hold values from 0.5 to 1.5
- w_gate: bfloat16 [16, 1024, 512], P(None, None, 'tensor'), may hold values from -0.1875 to 0.1875
- w_up: bfloat16 [16, 1024, 512], P(None, None, 'tensor'), may hold values from -0.1875 to 0.1875
- w_down: bfloat16 [16, 512, 1024], P(None, 'tensor'), may hold values from -1 to 1
Outputs:
- result: bfloat16 [8192, 1024], P('dp')
- grad_tokens: bfloat16 [8192, 1024], P('dp')
- grad_gates: float32 [8192, 8], P('dp')
- grad_norm_attn: float32 [1024], replicated
- grad_query: float32 [1024, 1024], P(None, 'tensor')
- grad_key: float32 [1024, 512], P(None, 'tensor')
- grad_value: float32 [1024, 512], P(None, 'tensor')
- grad_out: float32 [1024, 1024], P('tensor')
- grad_norm_moe: float32 [1024], replicated
- grad_gate: float32 [16, 1024, 512], P(None, None, 'tensor')
- grad_up: float32 [16, 1024, 512], P(None, None, 'tensor')
- grad_down: float32 [16, 512, 1024], P(None, 'tensor')
The draws below stay inside these ranges and needn't reach their ends.
Inputs may be any that keep to these rules, and one draw needn't show every extreme that they name: `lengths`: valid length of each sequence, at least 256; some sequence fills all 1024 slots.
All inputs are finite; a program needn't handle non-finite values.
Results may differ from the reference program's by a relative error of at most 0.015.
Values sent between devices are 32-bit elements; how exact they have to be, the bound alone decides.
A program may use at most 320 MiB of HBM per device.

```python
import math
import jax
import jax.numpy as jnp
from jax import lax

WIDTH = 1024
HEADS = 16
KV_HEADS = 8
HEAD_DIM = 64
HIDDEN_SIZE = 512
TOP_K = 8
EXPERTS = 16
SEQ_LEN = 1024
SEQS_DEV = 1
SEQS = 8
TOKENS = 8192
MIN_LEN = 256
CAPACITY = 640
N_DP = 8


def draw_lengths(key, part):
    key = jax.random.fold_in(key, 7)
    key_len, key_pick = jax.random.split(key)
    drawn_len = jax.random.randint(key_len, (SEQS,), MIN_LEN, SEQ_LEN + 1)
    chosen_seq = jax.random.randint(key_pick, (), 0, SEQS)
    return jnp.where(jnp.arange(SEQS) == chosen_seq, SEQ_LEN, drawn_len).astype(jnp.int32)


def level_of(own_key, shape, cuts, low, top_value):
    def one(dim, shards_of):
        heights = jax.random.uniform(jax.random.fold_in(jax.random.fold_in(own_key, 6), dim), (shards_of,), jnp.float32, low / len(cuts), top_value / len(cuts))
        return jnp.repeat(jnp.exp(heights), shape[dim] // shards_of).reshape((-1,) + (1,) * (len(shape) - dim - 1))

    level = one(*cuts[0])
    for cut in cuts[1:]:
        level = level * one(*cut)
    return level


def distinct(rng, rows, amount, top, lift):
    order = jax.random.permutation(jax.random.fold_in(rng, 1), amount)
    favour = order
    for power in range(3):
        favour = favour * favour // amount
    favour = favour * lift // amount
    tickets = jax.random.randint(jax.random.fold_in(rng, 2), (rows, amount), 0, 4096) + favour
    sure = jax.random.permutation(jax.random.fold_in(rng, 3), rows)[jnp.arange(amount) % rows]
    tickets = jnp.where(jnp.arange(rows)[:, None] == sure[None, :], 1 << 14, tickets)
    merit = tickets * amount + jnp.arange(amount)
    return lax.top_k(merit.astype(jnp.int32), top)[1].astype(jnp.int32)


def gaussian(own_key, shape, spread, most, cuts=(), held_as=jnp.bfloat16):
    factor_of = level_of(own_key, shape, cuts, -0.22, 0.18) if cuts else 1.0
    drawn = jax.random.normal(own_key, shape, jnp.float32) * spread * factor_of
    return jnp.minimum(jnp.maximum(drawn, -most), most).astype(held_as)


def setup_inputs(seed: int = 0) -> dict:
    seeds = jax.random.split(jax.random.key(seed), 15)
    return {
        "tokens": gaussian(seeds[0], (TOKENS, WIDTH), 1.0, 6.0, ((0, 8),)),
        "lengths": draw_lengths(jax.random.fold_in(seeds[14], 71), 0),
        "chosen": distinct(seeds[2], TOKENS, EXPERTS, TOP_K, 4096),
        "gate_values": jnp.clip(jnp.exp(math.log(0.25) - 1.609438 * jax.random.uniform(seeds[3], (TOKENS, TOP_K), jnp.float32) ** level_of(seeds[3], (TOKENS, TOP_K), ((0, 8),), -0.2, 0.2)), 0.05, 0.25),
        "cotangent": gaussian(seeds[4], (TOKENS, WIDTH), 1.0, 6.0, ((0, 8),)),
        "norm_attn": jnp.clip(1.0 + 0.1 * jax.random.normal(seeds[5], (WIDTH,), jnp.float32), 0.5, 1.5),
        "w_query": gaussian(seeds[6], (WIDTH, HEADS * HEAD_DIM), WIDTH ** -0.5, 0.1875, ((1, 4),)),
        "w_key": gaussian(seeds[7], (WIDTH, KV_HEADS * HEAD_DIM), WIDTH ** -0.5, 0.1875, ((1, 4),)),
        "w_value": gaussian(seeds[8], (WIDTH, KV_HEADS * HEAD_DIM), WIDTH ** -0.5, 0.1875, ((1, 4),)),
        "w_out": gaussian(seeds[9], (HEADS * HEAD_DIM, WIDTH), (max(4, HEADS * HEAD_DIM // 256)) ** -0.5, 3.0, ((0, 4),)),
        "norm_moe": jnp.clip(1.0 + 0.1 * jax.random.normal(seeds[10], (WIDTH,), jnp.float32), 0.5, 1.5),
        "w_gate": gaussian(seeds[11], (EXPERTS, WIDTH, HIDDEN_SIZE), WIDTH ** -0.5, 0.1875, ((2, 4),)),
        "w_up": gaussian(seeds[12], (EXPERTS, WIDTH, HIDDEN_SIZE), WIDTH ** -0.5, 0.1875, ((2, 4),)),
        "w_down": gaussian(seeds[13], (EXPERTS, HIDDEN_SIZE, WIDTH), (HIDDEN_SIZE // 16) ** -0.5, 1.0, ((1, 4),)),
    }


@jax.custom_vjp
def low(v):
    return lax.optimization_barrier(v.astype(jnp.bfloat16)).astype(jnp.float32)

@jax.custom_vjp
def low_back(v):
    return v

def low_keep(v):
    return (low(v), None)

def low_pass(kept, grad):
    return (grad,)

def back_keep(v):
    return (v, None)

def back_low(kept, grad):
    return (low(grad),)
low.defvjp(low_keep, low_pass)
low_back.defvjp(back_keep, back_low)
EPSILON = 1e-05
THETA = 10000.0
NEGATIVE = -1e+30

def matmul_hi(left, right):
    return jnp.dot(left, right, precision=lax.Precision.HIGHEST, preferred_element_type=jnp.float32)

def rms_norm(values, gain):
    return values * lax.rsqrt(lax.optimization_barrier(jnp.mean(values * values, axis=-1, keepdims=True)) + EPSILON) * gain

def rope_tables(positions, width):
    half_w = width // 2
    freqs = THETA ** (-jnp.arange(half_w, dtype=jnp.float32) * 2.0 / width)
    angles = jnp.arange(positions, dtype=jnp.float32)[:, None] * freqs[None, :]
    cosine = jnp.concatenate([jnp.cos(angles), jnp.cos(angles)], axis=1)
    sine = jnp.concatenate([jnp.sin(angles), jnp.sin(angles)], axis=1)
    return (cosine, sine)

def rotate(values, cosine, sine):
    half_w = values.shape[-1] // 2
    turned = jnp.concatenate([-values[..., half_w:], values[..., :half_w]], axis=-1)
    return values * cosine[:, None, :] + turned * sine[:, None, :]

def route_pairs(valid, chosen):
    tok_rows = chosen.shape[0]
    live_int = valid.astype(jnp.int32)
    expert_ids = jnp.arange(EXPERTS, dtype=jnp.int32)
    hits = lax.optimization_barrier(jnp.sum((chosen[:, :, None] == expert_ids[None, None, :]).astype(jnp.int32), axis=1)) * live_int[:, None]
    before = jnp.cumsum(hits, axis=0) - hits
    places = jnp.take_along_axis(before, chosen, axis=1)
    pairs = jnp.sum(live_int) * TOP_K
    limit = (5 * pairs + 4 * EXPERTS - 1) // (4 * EXPERTS)
    kept = (places < limit) & (live_int[:, None] > 0)
    dump_at = EXPERTS * CAPACITY
    target = jnp.where(kept, chosen * CAPACITY + places, dump_at).astype(jnp.int32)
    row_ids = jnp.broadcast_to(jnp.arange(tok_rows, dtype=jnp.int32)[:, None], chosen.shape)
    slot_token = jnp.zeros((dump_at + 1,), jnp.int32).at[target.reshape(-1)].set(row_ids.reshape(-1))[:dump_at]
    slot_live = jnp.zeros((dump_at + 1,), jnp.int32).at[target.reshape(-1)].set(1)[:dump_at]
    return (slot_token, slot_live, target, kept)

def attend_block(q_block, start, keys, values, length):
    rows_q = q_block.shape[0]
    grouped = q_block.reshape(rows_q, KV_HEADS, HEADS // KV_HEADS, HEAD_DIM)
    scores = jnp.einsum('qkgd,skd->kgqs', grouped, keys, precision=lax.Precision.HIGHEST) * (1.0 / math.sqrt(HEAD_DIM))
    q_pos = start + jnp.arange(rows_q, dtype=jnp.int32)
    k_pos = jnp.arange(keys.shape[0], dtype=jnp.int32)
    allowed = (k_pos[None, :] <= q_pos[:, None]) & (k_pos[None, :] < length)
    scores = low_back(jnp.where(allowed, scores, NEGATIVE))
    top_s = lax.optimization_barrier(jnp.max(scores, axis=-1, keepdims=True))
    expo = jnp.exp(scores - top_s)
    probs = low(expo / lax.optimization_barrier(jnp.sum(expo, axis=-1, keepdims=True)))
    out_b = jnp.einsum('kgqs,skd->qkgd', probs, values, precision=lax.Precision.HIGHEST)
    return out_b.reshape(rows_q, HEADS * HEAD_DIM)

def attend_sequence(q_seq, k_seq, v_seq, length):
    q_rows = min(512, SEQ_LEN)
    n_blocks = SEQ_LEN // q_rows
    blocks = q_seq.reshape(n_blocks, q_rows, HEADS, HEAD_DIM)
    starts = jnp.arange(n_blocks, dtype=jnp.int32) * q_rows
    step_fn = jax.checkpoint(lambda item: attend_block(item[0], item[1], k_seq, v_seq, length))
    return lax.map(step_fn, (blocks, starts)).reshape(SEQ_LEN, HEADS * HEAD_DIM)

def group_forward(lengths, chosen, tokens, gate_values, norm_attn, w_query, w_key, w_value, w_out, norm_moe, w_gate, w_up, w_down):
    tok_rows = tokens.shape[0]
    valid = (jnp.arange(SEQ_LEN, dtype=jnp.int32)[None, :] < lengths[:, None]).reshape(-1)
    valid_f = jnp.where(valid, 1.0, 0.0).astype(tokens.dtype)[:, None]
    cosine, sine = rope_tables(SEQ_LEN, HEAD_DIM)
    h_attn = low(rms_norm(tokens, norm_attn))
    shape_q = (SEQS_DEV, SEQ_LEN, HEADS, HEAD_DIM)
    shape_k = (SEQS_DEV, SEQ_LEN, KV_HEADS, HEAD_DIM)
    q_rot = low(rotate(low_back(matmul_hi(h_attn, w_query)).reshape(shape_q), cosine, sine))
    k_rot = low(rotate(low_back(matmul_hi(h_attn, w_key)).reshape(shape_k), cosine, sine))
    v_att = low(low_back(matmul_hi(h_attn, w_value))).reshape(shape_k)
    attended = lax.map(lambda item: attend_sequence(item[0], item[1], item[2], item[3]), (q_rot, k_rot, v_att, lengths))
    attn_cat = low(low_back(attended.reshape(tok_rows, HEADS * HEAD_DIM)))
    resid = tokens + low_back(matmul_hi(attn_cat, w_out))
    h_moe = low(rms_norm(resid, norm_moe))
    slot_token, slot_live, target, kept = route_pairs(valid, chosen)
    slot_index = jnp.minimum(target, EXPERTS * CAPACITY - 1)
    dispatched = (h_moe[slot_token] * slot_live.astype(h_moe.dtype)[:, None]).reshape(EXPERTS, CAPACITY, WIDTH)
    gate_act = low_back(jnp.einsum('ecd,edf->ecf', dispatched, w_gate, precision=lax.Precision.HIGHEST))
    up_act = low_back(jnp.einsum('ecd,edf->ecf', dispatched, w_up, precision=lax.Precision.HIGHEST))
    hidden = low(jax.nn.silu(gate_act) * up_act)
    produced = low_back(jnp.einsum('ecf,efd->ecd', hidden, w_down, precision=lax.Precision.HIGHEST))
    picked = produced.reshape(EXPERTS * CAPACITY, WIDTH)[slot_index]
    weights = jnp.where(kept, gate_values, 0.0)
    moe = jnp.einsum('tk,tkd->td', weights, picked, precision=lax.Precision.HIGHEST)
    return (resid + moe) * valid_f

def reference(tokens, lengths, chosen, gate_values, cotangent, norm_attn, w_query, w_key, w_value, w_out, norm_moe, w_gate, w_up, w_down):
    group_rows = SEQS_DEV * SEQ_LEN
    params = tuple((w.astype(jnp.float32) for w in (norm_attn, w_query, w_key, w_value, w_out, norm_moe, w_gate, w_up, w_down)))
    x_groups = tokens.astype(jnp.float32).reshape(N_DP, group_rows, WIDTH)
    d_groups = cotangent.astype(jnp.float32).reshape(N_DP, group_rows, WIDTH)
    g_groups = gate_values.astype(jnp.float32).reshape(N_DP, group_rows, TOP_K)
    c_groups = chosen.reshape(N_DP, group_rows, TOP_K)
    l_groups = lengths.reshape(N_DP, SEQS_DEV)

    def one_group(carry, item):
        x_one, l_one, c_one, g_one, d_one = item

        def forward(x_val, g_val, *weights_in):
            return group_forward(l_one, c_one, x_val, g_val, *weights_in)
        out_one, pull = jax.vjp(forward, x_one, g_one, *params)
        grads = pull(d_one)
        carry = tuple((c_val + g_val for c_val, g_val in zip(carry, grads[2:])))
        return (carry, (out_one, grads[0], grads[1]))
    zeros_in = tuple((jnp.zeros_like(p_val) for p_val in params))
    totals, (outs, d_toks, d_gates) = lax.scan(one_group, zeros_in, (x_groups, l_groups, c_groups, g_groups, d_groups))
    result = outs.reshape(-1, WIDTH).astype(jnp.bfloat16)
    grad_tokens = d_toks.reshape(-1, WIDTH).astype(jnp.bfloat16)
    grad_gates = d_gates.reshape(-1, TOP_K)
    return (result, grad_tokens, grad_gates, totals[0], totals[1], totals[2], totals[3], totals[4], totals[5], totals[6], totals[7], totals[8])
```

```python
import math

import jax
import jax.numpy as jnp
from jax import lax
from jax.sharding import PartitionSpec as P

HEAD_DIM = 64
TOP_K = 8
EXPERTS = 16


EPSILON = 1e-05
THETA = 10000.0
NEGATIVE = -1e30


def dot_f(left, right):
    return jnp.dot(left, right, preferred_element_type=jnp.float32)


def rms_norm(values, gain):
    return values * lax.rsqrt(jnp.mean(values * values, axis=-1, keepdims=True) + EPSILON) * gain


def rope_tables(positions, width):
    half_w = width // 2
    freqs = THETA ** (-jnp.arange(half_w, dtype=jnp.float32) * 2.0 / width)
    angles = jnp.arange(positions, dtype=jnp.float32)[:, None] * freqs[None, :]
    cosine = jnp.concatenate([jnp.cos(angles), jnp.cos(angles)], axis=1)
    sine = jnp.concatenate([jnp.sin(angles), jnp.sin(angles)], axis=1)
    return (cosine, sine)


def rotate(values, cosine, sine):
    half_w = values.shape[-1] // 2
    turned = jnp.concatenate([-values[..., half_w:], values[..., :half_w]], axis=-1)
    return values * cosine[:, None, :] + turned * sine[:, None, :]


def route_weights(valid, chosen, gate_values):
    tok_rows = chosen.shape[0]
    live_int = valid.astype(jnp.int32)
    onehot = chosen[:, :, None] == jnp.arange(EXPERTS, dtype=jnp.int32)[None, None, :]
    onehot_f = onehot.astype(jnp.float32)
    hits = jnp.sum(onehot_f, axis=1) * valid.astype(jnp.float32)[:, None]
    earlier = (
        jnp.arange(tok_rows, dtype=jnp.int32)[None, :] < jnp.arange(tok_rows, dtype=jnp.int32)[:, None]
    ).astype(jnp.bfloat16)
    places = dot_f(earlier, hits.astype(jnp.bfloat16))
    pairs = jnp.sum(live_int) * TOP_K
    limit = ((5 * pairs + 4 * EXPERTS - 1) // (4 * EXPERTS)).astype(jnp.float32)
    kept = jnp.where((places < limit) & (hits > 0), 1.0, 0.0)
    weights = jnp.sum(onehot_f * gate_values[:, :, None], axis=1) * kept
    return (weights, kept, onehot_f)


def block_scores(q_block, start, k_seq, length, scaling):
    rows_q = q_block.shape[0]
    kv_here = k_seq.shape[1]
    grouped = q_block.reshape(rows_q, kv_here, q_block.shape[1] // kv_here, q_block.shape[2])
    scores = (
        jnp.einsum("qkgd,skd->kgqs", grouped, k_seq, preferred_element_type=jnp.float32) * scaling
    )
    q_pos = start + jnp.arange(rows_q, dtype=jnp.int32)
    k_pos = jnp.arange(k_seq.shape[0], dtype=jnp.int32)
    allowed = (k_pos[None, :] <= q_pos[:, None]) & (k_pos[None, :] < length)
    return (jnp.where(allowed, scores, NEGATIVE), grouped)


def forward_block(q_block, start, k_seq, v_seq, length, scaling):
    scores, grouped = block_scores(q_block, start, k_seq, length, scaling)
    top_s = jnp.max(scores, axis=-1, keepdims=True)
    expo = jnp.exp(scores - top_s)
    total = jnp.sum(expo, axis=-1, keepdims=True)
    probs = (expo / total).astype(jnp.bfloat16)
    lse_part = (top_s + jnp.log(total))[..., 0]
    out_b = jnp.einsum("kgqs,skd->qkgd", probs, v_seq, preferred_element_type=jnp.float32)
    return (out_b.reshape(q_block.shape[0], -1), lse_part)


def backward_block(q_block, d_block, start, lse_block, k_seq, v_seq, length, scaling):
    scores, grouped = block_scores(q_block, start, k_seq, length, scaling)
    exact = jnp.exp(scores - lse_block[..., None])
    probs = exact.astype(jnp.bfloat16)
    d_grouped = d_block.reshape(grouped.shape)
    d_probs = jnp.einsum("qkgd,skd->kgqs", d_grouped, v_seq, preferred_element_type=jnp.float32)
    inner = jnp.sum(exact * d_probs, axis=-1, keepdims=True)
    d_scores = (exact * (d_probs - inner)).astype(jnp.bfloat16)
    d_query = (
        jnp.einsum("kgqs,skd->qkgd", d_scores, k_seq, preferred_element_type=jnp.float32) * scaling
    )
    d_key = (
        jnp.einsum("kgqs,qkgd->skd", d_scores, grouped, preferred_element_type=jnp.float32)
        * scaling
    )
    d_value = jnp.einsum("kgqs,qkgd->skd", probs, d_grouped, preferred_element_type=jnp.float32)
    return (d_query.reshape(q_block.shape), d_key, d_value)


def attend_forward(q_all, k_all, v_all, lengths, scaling):
    seq_len = q_all.shape[1]
    q_rows = min(512, seq_len)
    n_blocks = seq_len // q_rows

    def one_sequence(item):
        q_seq, k_seq, v_seq, length = item
        outs = []
        lses = []
        for block in range(n_blocks):
            start = block * q_rows
            finish = start + q_rows
            out_b, lse_b = forward_block(
                q_seq[start:finish], start, k_seq[:finish], v_seq[:finish], length, scaling
            )
            outs.append(out_b)
            lses.append(lse_b)
        return (jnp.concatenate(outs, axis=0), jnp.stack(lses, axis=0))

    return lax.map(one_sequence, (q_all, k_all, v_all, lengths))


def attend_backward(q_all, k_all, v_all, d_all, lse_all, lengths, scaling):
    seq_len = q_all.shape[1]
    q_rows = min(512, seq_len)
    n_blocks = seq_len // q_rows

    def one_sequence(item):
        q_seq, k_seq, v_seq, d_seq, lse_seq, length = item
        sum_key = jnp.zeros(k_seq.shape, jnp.float32)
        sum_value = jnp.zeros(k_seq.shape, jnp.float32)
        d_queries = []
        for block in range(n_blocks):
            start = block * q_rows
            finish = start + q_rows
            d_query, d_key, d_value = backward_block(
                q_seq[start:finish],
                d_seq[start:finish],
                start,
                lse_seq[block],
                k_seq[:finish],
                v_seq[:finish],
                length,
                scaling,
            )
            padding = ((0, seq_len - finish), (0, 0), (0, 0))
            sum_key = sum_key + jnp.pad(d_key, padding)
            sum_value = sum_value + jnp.pad(d_value, padding)
            d_queries.append(d_query)
        return (jnp.concatenate(d_queries, axis=0), sum_key, sum_value)

    return lax.map(one_sequence, (q_all, k_all, v_all, d_all, lse_all, lengths))


def per_device(
    tokens,
    lengths,
    chosen,
    gate_values,
    cotangent,
    norm_attn,
    w_query,
    w_key,
    w_value,
    w_out,
    norm_moe,
    w_gate,
    w_up,
    w_down,
):
    seq_count = lengths.shape[0]
    tok_rows = tokens.shape[0]
    seq_len = tok_rows // seq_count
    width = tokens.shape[1]
    heads_here = w_query.shape[1] // HEAD_DIM
    kv_here = w_key.shape[1] // HEAD_DIM
    scaling = 1.0 / math.sqrt(HEAD_DIM)
    valid = (jnp.arange(seq_len, dtype=jnp.int32)[None, :] < lengths[:, None]).reshape(-1)
    valid_f = valid.astype(jnp.float32)[:, None]
    cosine, sine = rope_tables(seq_len, HEAD_DIM)
    x_in = tokens.astype(jnp.float32)
    h_attn = rms_norm(x_in, norm_attn).astype(jnp.bfloat16)
    q_lin = dot_f(h_attn, w_query).reshape(seq_count, seq_len, heads_here, HEAD_DIM)
    k_lin = dot_f(h_attn, w_key).reshape(seq_count, seq_len, kv_here, HEAD_DIM)
    v_att = (
        dot_f(h_attn, w_value).astype(jnp.bfloat16).reshape(seq_count, seq_len, kv_here, HEAD_DIM)
    )
    q_rot = rotate(q_lin, cosine, sine).astype(jnp.bfloat16)
    k_rot = rotate(k_lin, cosine, sine).astype(jnp.bfloat16)
    attended, lse_all = attend_forward(q_rot, k_rot, v_att, lengths, scaling)
    attn_cat = attended.reshape(tok_rows, heads_here * HEAD_DIM).astype(jnp.bfloat16)
    attn_sum = lax.psum(dot_f(attn_cat, w_out), "tensor")
    resid = x_in + attn_sum
    h_moe = rms_norm(resid, norm_moe).astype(jnp.bfloat16)
    weights, kept, onehot_f = route_weights(valid, chosen, gate_values)
    d_out = cotangent.astype(jnp.float32) * valid_f
    gate_act = jnp.einsum("td,edf->tef", h_moe, w_gate, preferred_element_type=jnp.float32)
    up_act = jnp.einsum("td,edf->tef", h_moe, w_up, preferred_element_type=jnp.float32)
    d_raw = jnp.einsum("td,efd->tef", cotangent, w_down, preferred_element_type=jnp.float32)
    sigma = jax.nn.sigmoid(gate_act)
    silu_g = gate_act * sigma
    hidden = silu_g * up_act
    hidden_w = (hidden * weights[:, :, None]).astype(jnp.bfloat16)
    gate_dot = jnp.sum(hidden * d_raw, axis=-1) * kept
    d_gate_part = jnp.sum(onehot_f * gate_dot[:, None, :], axis=-1)
    d_hidden = d_raw * weights[:, :, None]
    d_gate_b = (d_hidden * up_act * sigma * (1.0 + gate_act * (1.0 - sigma))).astype(jnp.bfloat16)
    d_up_b = (d_hidden * silu_g).astype(jnp.bfloat16)
    moe_part = jnp.einsum("tef,efd->td", hidden_w, w_down, preferred_element_type=jnp.float32)
    moe_sum = lax.psum(moe_part, "tensor")
    result = ((resid + moe_sum) * valid_f).astype(jnp.bfloat16)
    grad_down = jnp.einsum("tef,td->efd", hidden_w, cotangent, preferred_element_type=jnp.float32)
    grad_gate = jnp.einsum("td,tef->edf", h_moe, d_gate_b, preferred_element_type=jnp.float32)
    grad_up = jnp.einsum("td,tef->edf", h_moe, d_up_b, preferred_element_type=jnp.float32)
    d_h_part = jnp.einsum("tef,edf->td", d_gate_b, w_gate, preferred_element_type=jnp.float32)
    d_h_part = d_h_part + jnp.einsum(
        "tef,edf->td", d_up_b, w_up, preferred_element_type=jnp.float32
    )
    d_h_moe, d_gates = lax.psum((d_h_part, d_gate_part), "tensor")
    unused_m, pull_moe = jax.vjp(rms_norm, resid, norm_moe)
    d_resid_n, grad_norm_moe = pull_moe(d_h_moe)
    d_resid = d_out + d_resid_n
    d_resid_b = d_resid.astype(jnp.bfloat16)
    grad_out = jnp.einsum("tf,td->fd", attn_cat, d_resid_b, preferred_element_type=jnp.float32)
    d_attn = jnp.einsum("td,fd->tf", d_resid_b, w_out, preferred_element_type=jnp.float32).astype(
        jnp.bfloat16
    )
    d_attn = d_attn.reshape(seq_count, seq_len, heads_here, HEAD_DIM)
    d_q_rot, d_k_rot, d_v_all = attend_backward(
        q_rot, k_rot, v_att, d_attn, lse_all, lengths, scaling
    )
    unused_q, pull_query = jax.vjp(lambda values: rotate(values, cosine, sine), q_lin)
    unused_k, pull_key = jax.vjp(lambda values: rotate(values, cosine, sine), k_lin)
    d_query = pull_query(d_q_rot)[0].astype(jnp.bfloat16).reshape(tok_rows, -1)
    d_key = pull_key(d_k_rot)[0].astype(jnp.bfloat16).reshape(tok_rows, -1)
    d_value = d_v_all.astype(jnp.bfloat16).reshape(tok_rows, -1)
    grad_query = jnp.einsum("td,tf->df", h_attn, d_query, preferred_element_type=jnp.float32)
    grad_key = jnp.einsum("td,tf->df", h_attn, d_key, preferred_element_type=jnp.float32)
    grad_value = jnp.einsum("td,tf->df", h_attn, d_value, preferred_element_type=jnp.float32)
    d_h_part_a = jnp.einsum("tf,df->td", d_query, w_query, preferred_element_type=jnp.float32)
    d_h_part_a = d_h_part_a + jnp.einsum(
        "tf,df->td", d_key, w_key, preferred_element_type=jnp.float32
    )
    d_h_part_a = d_h_part_a + jnp.einsum(
        "tf,df->td", d_value, w_value, preferred_element_type=jnp.float32
    )
    d_h_attn = lax.psum(d_h_part_a, "tensor")
    unused_a, pull_attn = jax.vjp(rms_norm, x_in, norm_attn)
    d_x_n, grad_norm_attn = pull_attn(d_h_attn)
    grad_tokens = (d_resid + d_x_n).astype(jnp.bfloat16)
    summed = (
        lax.psum_scatter(grad_norm_attn, "dp", scatter_dimension=0, tiled=True),
        lax.psum_scatter(grad_query, "dp", scatter_dimension=0, tiled=True),
        lax.psum_scatter(grad_key, "dp", scatter_dimension=0, tiled=True),
        lax.psum_scatter(grad_value, "dp", scatter_dimension=0, tiled=True),
        lax.psum_scatter(grad_out, "dp", scatter_dimension=1, tiled=True),
        lax.psum_scatter(grad_norm_moe, "dp", scatter_dimension=0, tiled=True),
        lax.psum_scatter(grad_gate, "dp", scatter_dimension=1, tiled=True),
        lax.psum_scatter(grad_up, "dp", scatter_dimension=1, tiled=True),
        lax.psum_scatter(grad_down, "dp", scatter_dimension=2, tiled=True),
    )
    full = (
        lax.all_gather(summed[0], "dp", axis=0, tiled=True),
        lax.all_gather(summed[1], "dp", axis=0, tiled=True),
        lax.all_gather(summed[2], "dp", axis=0, tiled=True),
        lax.all_gather(summed[3], "dp", axis=0, tiled=True),
        lax.all_gather(summed[4], "dp", axis=1, tiled=True),
        lax.all_gather(summed[5], "dp", axis=0, tiled=True),
        lax.all_gather(summed[6], "dp", axis=1, tiled=True),
        lax.all_gather(summed[7], "dp", axis=1, tiled=True),
        lax.all_gather(summed[8], "dp", axis=2, tiled=True),
    )
    return (
        result,
        grad_tokens,
        d_gates,
        full[0],
        full[1],
        full[2],
        full[3],
        full[4],
        full[5],
        full[6],
        full[7],
        full[8],
    )


def solution(mesh):
    placed = (
        P("dp", None),
        P("dp"),
        P("dp", None),
        P("dp", None),
        P("dp", None),
        P(),
        P(None, "tensor"),
        P(None, "tensor"),
        P(None, "tensor"),
        P("tensor", None),
        P(),
        P(None, None, "tensor"),
        P(None, None, "tensor"),
        P(None, "tensor", None),
    )
    return jax.shard_map(
        per_device,
        mesh=mesh,
        in_specs=placed,
        out_specs=(
            P("dp", None),
            P("dp", None),
            P("dp", None),
            P(),
            P(None, "tensor"),
            P(None, "tensor"),
            P(None, "tensor"),
            P("tensor", None),
            P(),
            P(None, None, "tensor"),
            P(None, None, "tensor"),
            P(None, "tensor", None),
        ),
        check_vma=False,
    )
```

```python
import functools
import math

import jax
import jax.numpy as jnp
from jax import lax
from jax.experimental import pallas as pl
from jax.experimental.pallas import tpu as pltpu
from jax.sharding import PartitionSpec as P

HEAD_DIM = 64
TOP_K = 8
EXPERTS = 16


EPSILON = 1e-05
THETA = 10000.0
NEGATIVE = -1e30


def dot_f(left, right):
    return jnp.dot(left, right, preferred_element_type=jnp.float32)


def rms_norm(values, gain):
    return values * lax.rsqrt(jnp.mean(values * values, axis=-1, keepdims=True) + EPSILON) * gain


def rope_tables(positions, width):
    half_w = width // 2
    freqs = THETA ** (-jnp.arange(half_w, dtype=jnp.float32) * 2.0 / width)
    angles = jnp.arange(positions, dtype=jnp.float32)[:, None] * freqs[None, :]
    cosine = jnp.concatenate([jnp.cos(angles), jnp.cos(angles)], axis=1)
    sine = jnp.concatenate([jnp.sin(angles), jnp.sin(angles)], axis=1)
    return (cosine, sine)


def rotate(values, cosine, sine):
    half_w = values.shape[-1] // 2
    turned = jnp.concatenate([-values[..., half_w:], values[..., :half_w]], axis=-1)
    return values * cosine[:, None, :] + turned * sine[:, None, :]


def route_weights(valid, chosen, gate_values):
    tok_rows = chosen.shape[0]
    live_int = valid.astype(jnp.int32)
    onehot = chosen[:, :, None] == jnp.arange(EXPERTS, dtype=jnp.int32)[None, None, :]
    onehot_f = onehot.astype(jnp.float32)
    hits = jnp.sum(onehot_f, axis=1) * valid.astype(jnp.float32)[:, None]
    earlier = (
        jnp.arange(tok_rows, dtype=jnp.int32)[None, :] < jnp.arange(tok_rows, dtype=jnp.int32)[:, None]
    ).astype(jnp.bfloat16)
    places = dot_f(earlier, hits.astype(jnp.bfloat16))
    pairs = jnp.sum(live_int) * TOP_K
    limit = ((5 * pairs + 4 * EXPERTS - 1) // (4 * EXPERTS)).astype(jnp.float32)
    kept = jnp.where((places < limit) & (hits > 0), 1.0, 0.0)
    weights = jnp.sum(onehot_f * gate_values[:, :, None], axis=1) * kept
    return (weights, kept, onehot_f)


def block_scores(q_block, start, k_seq, length, scaling):
    rows_q = q_block.shape[0]
    kv_here = k_seq.shape[1]
    grouped = q_block.reshape(rows_q, kv_here, q_block.shape[1] // kv_here, q_block.shape[2])
    scores = (
        jnp.einsum("qkgd,skd->kgqs", grouped, k_seq, preferred_element_type=jnp.float32) * scaling
    )
    q_pos = start + jnp.arange(rows_q, dtype=jnp.int32)
    k_pos = jnp.arange(k_seq.shape[0], dtype=jnp.int32)
    allowed = (k_pos[None, :] <= q_pos[:, None]) & (k_pos[None, :] < length)
    return (jnp.where(allowed, scores, NEGATIVE), grouped)


def forward_block(q_block, start, k_seq, v_seq, length, scaling):
    scores, grouped = block_scores(q_block, start, k_seq, length, scaling)
    top_s = jnp.max(scores, axis=-1, keepdims=True)
    expo = jnp.exp(scores - top_s)
    total = jnp.sum(expo, axis=-1, keepdims=True)
    probs = (expo / total).astype(jnp.bfloat16)
    lse_part = (top_s + jnp.log(total))[..., 0]
    out_b = jnp.einsum("kgqs,skd->qkgd", probs, v_seq, preferred_element_type=jnp.float32)
    return (out_b.reshape(q_block.shape[0], -1), lse_part)


def backward_block(q_block, d_block, start, lse_block, k_seq, v_seq, length, scaling):
    scores, grouped = block_scores(q_block, start, k_seq, length, scaling)
    exact = jnp.exp(scores - lse_block[..., None])
    probs = exact.astype(jnp.bfloat16)
    d_grouped = d_block.reshape(grouped.shape)
    d_probs = jnp.einsum("qkgd,skd->kgqs", d_grouped, v_seq, preferred_element_type=jnp.float32)
    inner = jnp.sum(exact * d_probs, axis=-1, keepdims=True)
    d_scores = (exact * (d_probs - inner)).astype(jnp.bfloat16)
    d_query = (
        jnp.einsum("kgqs,skd->qkgd", d_scores, k_seq, preferred_element_type=jnp.float32) * scaling
    )
    d_key = (
        jnp.einsum("kgqs,qkgd->skd", d_scores, grouped, preferred_element_type=jnp.float32)
        * scaling
    )
    d_value = jnp.einsum("kgqs,qkgd->skd", probs, d_grouped, preferred_element_type=jnp.float32)
    return (d_query.reshape(q_block.shape), d_key, d_value)


def attend_forward(q_all, k_all, v_all, lengths, scaling):
    seq_len = q_all.shape[1]
    q_rows = min(512, seq_len)
    n_blocks = seq_len // q_rows

    def one_sequence(item):
        q_seq, k_seq, v_seq, length = item
        outs = []
        lses = []
        for block in range(n_blocks):
            start = block * q_rows
            finish = start + q_rows
            out_b, lse_b = forward_block(
                q_seq[start:finish], start, k_seq[:finish], v_seq[:finish], length, scaling
            )
            outs.append(out_b)
            lses.append(lse_b)
        return (jnp.concatenate(outs, axis=0), jnp.stack(lses, axis=0))

    return lax.map(one_sequence, (q_all, k_all, v_all, lengths))


def attend_backward(q_all, k_all, v_all, d_all, lse_all, lengths, scaling):
    seq_len = q_all.shape[1]
    q_rows = min(512, seq_len)
    n_blocks = seq_len // q_rows

    def one_sequence(item):
        q_seq, k_seq, v_seq, d_seq, lse_seq, length = item
        sum_key = jnp.zeros(k_seq.shape, jnp.float32)
        sum_value = jnp.zeros(k_seq.shape, jnp.float32)
        d_queries = []
        for block in range(n_blocks):
            start = block * q_rows
            finish = start + q_rows
            d_query, d_key, d_value = backward_block(
                q_seq[start:finish],
                d_seq[start:finish],
                start,
                lse_seq[block],
                k_seq[:finish],
                v_seq[:finish],
                length,
                scaling,
            )
            padding = ((0, seq_len - finish), (0, 0), (0, 0))
            sum_key = sum_key + jnp.pad(d_key, padding)
            sum_value = sum_value + jnp.pad(d_value, padding)
            d_queries.append(d_query)
        return (jnp.concatenate(d_queries, axis=0), sum_key, sum_value)

    return lax.map(one_sequence, (q_all, k_all, v_all, d_all, lse_all, lengths))


MESH=pl.DeviceIdType.MESH
N_CLASS = 108
HOP = 2

def dp_kernel(nz, hop, ring, WhT, dout, hT, dgu, haT, dq, dkv, acT, drb,
              o_gate, o_up, o_down, o_q, o_k, o_v, o_out,
              lhs, rhs, pbuf, zbuf, ybuf, ld_sem,
              ys, yr, zs, zr, fs, fr, gs, gr, os0, os1):
    dp = lax.axis_index("dp")
    base = dp - dp % (2 * nz)
    z, y = (dp % (2 * nz)) // 2, dp % 2
    last = nz - 1
    mate = base + z * 2 + (1 - y)
    up_id = base + jnp.minimum(z + 1, last) * 2 + y
    dn_id = base + jnp.maximum(z - 1, 0) * 2 + y

    loads = [pltpu.make_async_copy(WhT.at[pl.ds(128 * b, 128)], lhs.at[b], ld_sem.at[b]) for b in range(16)]
    loads += [pltpu.make_async_copy(hT.at[pl.ds(128 * b, 128)], lhs.at[16 + b], ld_sem.at[16 + b]) for b in range(8)]
    loads += [pltpu.make_async_copy(haT.at[pl.ds(128 * b, 128)], lhs.at[24 + b], ld_sem.at[24 + b]) for b in range(8)]
    loads += [pltpu.make_async_copy(acT.at[pl.ds(128 * b, 128)], lhs.at[32 + b], ld_sem.at[32 + b]) for b in range(2)]
    loads += [pltpu.make_async_copy(dout.at[:, pl.ds(256 * b, 256)], rhs.at[b], ld_sem.at[34 + b]) for b in range(4)]
    loads += [pltpu.make_async_copy(dgu.at[b], rhs.at[4 + b], ld_sem.at[38 + b]) for b in range(16)]
    loads += [pltpu.make_async_copy(dq, rhs.at[20], ld_sem.at[54]), pltpu.make_async_copy(dkv, rhs.at[21], ld_sem.at[55])]
    loads += [pltpu.make_async_copy(drb.at[:, pl.ds(256 * b, 256)], rhs.at[22 + b], ld_sem.at[56 + b]) for b in range(4)]
    for ld in loads:
        ld.start()

    bar = pltpu.get_barrier_semaphore()
    pl.semaphore_signal(bar, inc=1, device_id={"dp": mate}, device_id_type=MESH)

    @pl.when(z < last)
    def _():
        pl.semaphore_signal(bar, inc=1, device_id={"dp": up_id}, device_id_type=MESH)

    @pl.when(z > 0)
    def _():
        pl.semaphore_signal(bar, inc=1, device_id={"dp": dn_id}, device_id_type=MESH)

    pl.semaphore_wait(bar, 1 + (z < last).astype(jnp.int32) + (z > 0).astype(jnp.int32))

    for ld in loads:
        ld.wait()

    def remote(src, dst, ssem, rsem, dev):
        return pltpu.make_async_remote_copy(src_ref=src, dst_ref=dst, send_sem=ssem, recv_sem=rsem,
                                            device_id={"dp": dev}, device_id_type=MESH)

    own = pl.ds(pl.multiple_of(y * 64, 64), 64)
    oth = pl.ds(pl.multiple_of((1 - y) * 64, 64), 64)
    half = pl.ds(0, 64)

    def stage(c, t):
        p = z if c == 0 else last - z
        nxt, prv = (up_id, dn_id) if c == 0 else (dn_id, up_id)

        def at(delay, body):
            i = t - delay

            @pl.when((i >= 0) & (i < N_CLASS))
            def _():
                body(i, i % ring, i % 2 == 0)

        def ycopy_a(s):
            return remote(pbuf.at[c, s, oth], ybuf.at[c, s, half], ys.at[c, s], yr.at[c, s], mate)

        def ycopy_b(s):
            return remote(zbuf.at[c, s], ybuf.at[c, s], ys.at[c, s], yr.at[c, s], mate)

        def zcopy_a(s):
            return remote(zbuf.at[c, s, half], zbuf.at[c, s, half], zs.at[c, s], zr.at[c, s], nxt)

        def zcopy_b(s):
            return remote(zbuf.at[c, s], zbuf.at[c, s], zs.at[c, s], zr.at[c, s], nxt)

        def fcopy_a(s):
            return remote(pbuf.at[c, s, own], pbuf.at[c, s, own], fs.at[c, s], fr.at[c, s], prv)

        def fcopy_b(s):
            return remote(pbuf.at[c, s], pbuf.at[c, s], fs.at[c, s], fr.at[c, s], prv)

        def gcopy(s):
            return remote(pbuf.at[c, s, own], ybuf.at[c, s, pl.ds(64, 64)], gs.at[c, s], gr.at[c, s], mate)

        def first(i, s, is_a):
            g = 2 * i + c
            expert, part = g // 12, g % 12
            a = g - 192
            in_moe = g < 192
            l_moe = jnp.where(part < 4, expert, 12 + part)
            r_moe = jnp.where(part < 4, part, 4 + expert)
            l_att = jnp.where(a < 16, 24 + a % 8, 32 + (a - 16) // 4)
            r_att = jnp.where(a < 16, 20 + a // 8, 22 + (a - 16) % 4)
            li = jnp.where(in_moe, l_moe, l_att)
            ri = jnp.where(in_moe, r_moe, r_att)
            pbuf[c, s] = jnp.dot(lhs[li], rhs[ri], preferred_element_type=jnp.float32)

            @pl.when(is_a)
            def _():
                ycopy_a(s).start()

        def second(i, s, is_a):
            @pl.when(is_a)
            def _():
                ycopy_a(s).wait_recv()

                @pl.when(p > 0)
                def _():
                    zcopy_a(s).wait_recv()
                    zbuf[c, s, half] = zbuf[c, s, half] + (pbuf[c, s, own] + ybuf[c, s, half])

                @pl.when(p == 0)
                def _():
                    zbuf[c, s, half] = pbuf[c, s, own] + ybuf[c, s, half]

                @pl.when(p < last)
                def _():
                    zcopy_a(s).start()

                @pl.when(p == last)
                def _():
                    pbuf[c, s, own] = zbuf[c, s, half]
                    fcopy_a(s).start()
                    gcopy(s).start()

            @pl.when(jnp.logical_not(is_a))
            def _():
                @pl.when(p > 0)
                def _():
                    zcopy_b(s).wait_recv()
                    zbuf[c, s] = zbuf[c, s] + pbuf[c, s]

                @pl.when(p == 0)
                def _():
                    zbuf[c, s] = pbuf[c, s]

                @pl.when(p < last)
                def _():
                    zcopy_b(s).start()

                @pl.when(p == last)
                def _():
                    ycopy_b(s).start()

        def third(i, s, is_a):
            @pl.when(jnp.logical_not(is_a) & (p == last))
            def _():
                ycopy_b(s).wait_recv()
                pbuf[c, s] = zbuf[c, s] + ybuf[c, s]
                fcopy_b(s).start()

        def fourth(i, s, is_a):
            @pl.when(p < last)
            def _():
                @pl.when(is_a)
                def _():
                    fcopy_a(s).wait_recv()

                    @pl.when(p > 0)
                    def _():
                        fcopy_a(s).start()

                    gcopy(s).start()

                @pl.when(jnp.logical_not(is_a))
                def _():
                    fcopy_b(s).wait_recv()

                    @pl.when(p > 0)
                    def _():
                        fcopy_b(s).start()

        def store(s, dst0, dst1):
            pltpu.make_async_copy(pbuf.at[c, s, :, pl.ds(0, 128)], dst0, os0.at[c, s]).start()
            pltpu.make_async_copy(pbuf.at[c, s, :, pl.ds(128, 128)], dst1, os1.at[c, s]).start()

        def fifth(i, s, is_a):
            @pl.when(is_a)
            def _():
                gcopy(s).wait_recv()
                ycopy_a(s).wait_send()
                pbuf[c, s, oth] = ybuf[c, s, pl.ds(64, 64)]

            g = 2 * i + c
            expert, part = g // 12, g % 12
            a = g - 192

            @pl.when((g < 192) & (part < 4))
            def _():
                col = pl.multiple_of(part * 256, 128)
                col1 = pl.multiple_of(part * 256 + 128, 128)
                store(s, o_down.at[expert, :, pl.ds(col, 128)], o_down.at[expert, :, pl.ds(col1, 128)])

            @pl.when((g < 192) & (part >= 4))
            def _():
                rows = pl.ds(pl.multiple_of((part - 4) * 128, 128), 128)
                store(s, o_gate.at[expert, rows], o_up.at[expert, rows])

            @pl.when((g >= 192) & (a < 8))
            def _():
                rows = pl.ds(pl.multiple_of(a * 128, 128), 128)
                store(s, o_q.at[rows, pl.ds(0, 128)], o_q.at[rows, pl.ds(128, 128)])

            @pl.when((a >= 8) & (a < 16))
            def _():
                rows = pl.ds(pl.multiple_of((a - 8) * 128, 128), 128)
                store(s, o_k.at[rows], o_v.at[rows])

            @pl.when(a >= 16)
            def _():
                b = a - 16
                rows = pl.ds(pl.multiple_of((b // 4) * 128, 128), 128)
                col = pl.multiple_of((b % 4) * 256, 128)
                col1 = pl.multiple_of((b % 4) * 256 + 128, 128)
                store(s, o_out.at[rows, pl.ds(col, 128)], o_out.at[rows, pl.ds(col1, 128)])

        def sixth(i, s, is_a):
            pltpu.make_async_copy(pbuf.at[c, s, :, pl.ds(0, 128)], o_k.at[pl.ds(0, 128)], os0.at[c, s]).wait()
            pltpu.make_async_copy(pbuf.at[c, s, :, pl.ds(0, 128)], o_k.at[pl.ds(0, 128)], os1.at[c, s]).wait()

            @pl.when(is_a)
            def _():
                gcopy(s).wait_send()

                @pl.when(p < last)
                def _():
                    zcopy_a(s).wait_send()

                @pl.when(p > 0)
                def _():
                    fcopy_a(s).wait_send()

            @pl.when(jnp.logical_not(is_a))
            def _():
                @pl.when(p < last)
                def _():
                    zcopy_b(s).wait_send()

                @pl.when(p == last)
                def _():
                    ycopy_b(s).wait_send()

                @pl.when(p > 0)
                def _():
                    fcopy_b(s).wait_send()

        t2 = hop * (1 + p)
        t3 = hop * (2 + last)
        t4 = t3 + hop * (last - p)
        t5 = t4 + hop
        t6 = t5 + hop
        return [(0, first, at), (t2, second, at), (t3, third, at), (t4, fourth, at), (t5, fifth, at), (t6, sixth, at)]

    def body(t, carry):
        both = [stage(0, t), stage(1, t)]
        for k in (1, 2, 3, 4, 5, 0):
            for st in both:
                delay, fn, at = st[k]
                at(delay, fn)
        return carry

    total = N_CLASS + hop * (2 * last + 4) + 1
    lax.fori_loop(0, total, body, 0)


def dp_reduce(mesh, WhT, dout, hT, dgu, haT, dq, dkv, acT, drb, hop=HOP):
    groups = mesh.shape["dp"]
    nz = 4 if groups % 8 == 0 else groups // 2
    last = nz - 1
    ring = hop * (2 * last + 4) + 2
    ring += ring % 2
    sh = jax.ShapeDtypeStruct
    f32 = jnp.float32
    outs = [sh((16, 1024, 128), f32)] * 2 + [sh((16, 128, 1024), f32), sh((1024, 256), f32), sh((1024, 128), f32), sh((1024, 128), f32), sh((256, 1024), f32)]
    anyspec = pl.BlockSpec(memory_space=pl.ANY)
    sem = pltpu.SemaphoreType.DMA
    sums = pl.pallas_call(
        functools.partial(dp_kernel, nz, hop, ring),
        out_shape=outs, in_specs=[anyspec] * 9, out_specs=[anyspec] * 7,
        scratch_shapes=[pltpu.VMEM((34, 128, 1024), jnp.bfloat16), pltpu.VMEM((26, 1024, 256), jnp.bfloat16),
                        pltpu.VMEM((2, ring, 128, 256), f32), pltpu.VMEM((2, ring, 128, 256), f32), pltpu.VMEM((2, ring, 128, 256), f32),
                        sem((60,))] + [sem((2, ring))] * 10,
        compiler_params=pltpu.CompilerParams(collective_id=0, has_side_effects=True, vmem_limit_bytes=58 * 2**20),
    )(WhT, dout, hT, dgu, haT, dq, dkv, acT, drb)
    if groups > 2 * nz:
        same = [[2 * nz * block + place for block in range(groups // (2 * nz))] for place in range(2 * nz)]
        sums = lax.psum(tuple(sums), "dp", axis_index_groups=same)
    return sums


def per_device(
    mesh,
    tokens,
    lengths,
    chosen,
    gate_values,
    cotangent,
    norm_attn,
    w_query,
    w_key,
    w_value,
    w_out,
    norm_moe,
    w_gate,
    w_up,
    w_down,
):
    seq_count = lengths.shape[0]
    tok_rows = tokens.shape[0]
    seq_len = tok_rows // seq_count
    width = tokens.shape[1]
    heads_here = w_query.shape[1] // HEAD_DIM
    kv_here = w_key.shape[1] // HEAD_DIM
    scaling = 1.0 / math.sqrt(HEAD_DIM)
    valid = (jnp.arange(seq_len, dtype=jnp.int32)[None, :] < lengths[:, None]).reshape(-1)
    valid_f = valid.astype(jnp.float32)[:, None]
    cosine, sine = rope_tables(seq_len, HEAD_DIM)
    x_in = tokens.astype(jnp.float32)
    h_attn = rms_norm(x_in, norm_attn).astype(jnp.bfloat16)
    q_lin = dot_f(h_attn, w_query).reshape(seq_count, seq_len, heads_here, HEAD_DIM)
    k_lin = dot_f(h_attn, w_key).reshape(seq_count, seq_len, kv_here, HEAD_DIM)
    v_att = (
        dot_f(h_attn, w_value).astype(jnp.bfloat16).reshape(seq_count, seq_len, kv_here, HEAD_DIM)
    )
    q_rot = rotate(q_lin, cosine, sine).astype(jnp.bfloat16)
    k_rot = rotate(k_lin, cosine, sine).astype(jnp.bfloat16)
    attended, lse_all = attend_forward(q_rot, k_rot, v_att, lengths, scaling)
    attn_cat = attended.reshape(tok_rows, heads_here * HEAD_DIM).astype(jnp.bfloat16)
    attn_sum = lax.psum(dot_f(attn_cat, w_out), "tensor")
    resid = x_in + attn_sum
    h_moe = rms_norm(resid, norm_moe).astype(jnp.bfloat16)
    weights, kept, onehot_f = route_weights(valid, chosen, gate_values)
    d_out = cotangent.astype(jnp.float32) * valid_f
    gate_act = jnp.einsum("td,edf->tef", h_moe, w_gate, preferred_element_type=jnp.float32)
    up_act = jnp.einsum("td,edf->tef", h_moe, w_up, preferred_element_type=jnp.float32)
    d_raw = jnp.einsum("td,efd->tef", cotangent, w_down, preferred_element_type=jnp.float32)
    sigma = jax.nn.sigmoid(gate_act)
    silu_g = gate_act * sigma
    hidden = silu_g * up_act
    hidden_w = (hidden * weights[:, :, None]).astype(jnp.bfloat16)
    gate_dot = jnp.sum(hidden * d_raw, axis=-1) * kept
    d_gate_part = jnp.sum(onehot_f * gate_dot[:, None, :], axis=-1)
    d_hidden = d_raw * weights[:, :, None]
    d_gate_b = (d_hidden * up_act * sigma * (1.0 + gate_act * (1.0 - sigma))).astype(jnp.bfloat16)
    d_up_b = (d_hidden * silu_g).astype(jnp.bfloat16)
    moe_part = jnp.einsum("tef,efd->td", hidden_w, w_down, preferred_element_type=jnp.float32)
    moe_sum = lax.psum(moe_part, "tensor")
    result = ((resid + moe_sum) * valid_f).astype(jnp.bfloat16)
    d_h_part = jnp.einsum("tef,edf->td", d_gate_b, w_gate, preferred_element_type=jnp.float32)
    d_h_part = d_h_part + jnp.einsum(
        "tef,edf->td", d_up_b, w_up, preferred_element_type=jnp.float32
    )
    d_h_moe, d_gates = lax.psum((d_h_part, d_gate_part), "tensor")
    unused_m, pull_moe = jax.vjp(rms_norm, resid, norm_moe)
    d_resid_n, grad_norm_moe = pull_moe(d_h_moe)
    d_resid = d_out + d_resid_n
    d_resid_b = d_resid.astype(jnp.bfloat16)
    d_attn = jnp.einsum("td,fd->tf", d_resid_b, w_out, preferred_element_type=jnp.float32).astype(
        jnp.bfloat16
    )
    d_attn = d_attn.reshape(seq_count, seq_len, heads_here, HEAD_DIM)
    d_q_rot, d_k_rot, d_v_all = attend_backward(
        q_rot, k_rot, v_att, d_attn, lse_all, lengths, scaling
    )
    unused_q, pull_query = jax.vjp(lambda values: rotate(values, cosine, sine), q_lin)
    unused_k, pull_key = jax.vjp(lambda values: rotate(values, cosine, sine), k_lin)
    d_query = pull_query(d_q_rot)[0].astype(jnp.bfloat16).reshape(tok_rows, -1)
    d_key = pull_key(d_k_rot)[0].astype(jnp.bfloat16).reshape(tok_rows, -1)
    d_value = d_v_all.astype(jnp.bfloat16).reshape(tok_rows, -1)
    d_h_part_a = jnp.einsum("tf,df->td", d_query, w_query, preferred_element_type=jnp.float32)
    d_h_part_a = d_h_part_a + jnp.einsum(
        "tf,df->td", d_key, w_key, preferred_element_type=jnp.float32
    )
    d_h_part_a = d_h_part_a + jnp.einsum(
        "tf,df->td", d_value, w_value, preferred_element_type=jnp.float32
    )
    d_h_attn = lax.psum(d_h_part_a, "tensor")
    unused_a, pull_attn = jax.vjp(rms_norm, x_in, norm_attn)
    d_x_n, grad_norm_attn = pull_attn(d_h_attn)
    grad_tokens = (d_resid + d_x_n).astype(jnp.bfloat16)
    grad_norm_attn, grad_norm_moe = lax.psum((grad_norm_attn, grad_norm_moe), "dp")
    hidden_t = hidden_w.reshape(tok_rows, -1).T
    d_gate_up = jnp.concatenate([d_gate_b, d_up_b], axis=2).transpose(1, 0, 2)
    grad_gate, grad_up, grad_down, grad_query, grad_key, grad_value, grad_out = dp_reduce(
        mesh,
        hidden_t,
        cotangent,
        h_moe.T,
        d_gate_up,
        h_attn.T,
        d_query,
        jnp.concatenate([d_key, d_value], axis=1),
        attn_cat.T,
        d_resid_b,
    )
    return (
        result,
        grad_tokens,
        d_gates,
        grad_norm_attn,
        grad_query,
        grad_key,
        grad_value,
        grad_out,
        grad_norm_moe,
        grad_gate,
        grad_up,
        grad_down,
    )


def solution(mesh):
    placed = (
        P("dp", None),
        P("dp"),
        P("dp", None),
        P("dp", None),
        P("dp", None),
        P(),
        P(None, "tensor"),
        P(None, "tensor"),
        P(None, "tensor"),
        P("tensor", None),
        P(),
        P(None, None, "tensor"),
        P(None, None, "tensor"),
        P(None, "tensor", None),
    )
    return jax.shard_map(
        functools.partial(per_device, mesh),
        mesh=mesh,
        in_specs=placed,
        out_specs=(
            P("dp", None),
            P("dp", None),
            P("dp", None),
            P(),
            P(None, "tensor"),
            P(None, "tensor"),
            P(None, "tensor"),
            P("tensor", None),
            P(),
            P(None, None, "tensor"),
            P(None, None, "tensor"),
            P(None, "tensor", None),
        ),
        check_vma=False,
    )
```

```python
import functools
import math

import jax
import jax.numpy as jnp
from jax import lax
from jax.experimental import pallas as pl
from jax.experimental.pallas import tpu as pltpu
from jax.sharding import PartitionSpec as P

MESH = pl.DeviceIdType.MESH

HEAD_DIM = 64
TOP_K = 8
EXPERTS = 16


EPSILON = 1e-05
THETA = 10000.0
NEGATIVE = -1e30


def dot_f(left, right):
    return jnp.dot(left, right, preferred_element_type=jnp.float32)


def rms_norm(values, gain):
    return values * lax.rsqrt(jnp.mean(values * values, axis=-1, keepdims=True) + EPSILON) * gain


def rope_tables(positions, width):
    half_w = width // 2
    freqs = THETA ** (-jnp.arange(half_w, dtype=jnp.float32) * 2.0 / width)
    angles = jnp.arange(positions, dtype=jnp.float32)[:, None] * freqs[None, :]
    cosine = jnp.concatenate([jnp.cos(angles), jnp.cos(angles)], axis=1)
    sine = jnp.concatenate([jnp.sin(angles), jnp.sin(angles)], axis=1)
    return (cosine, sine)


def rotate(values, cosine, sine):
    half_w = values.shape[-1] // 2
    turned = jnp.concatenate([-values[..., half_w:], values[..., :half_w]], axis=-1)
    return values * cosine[:, None, :] + turned * sine[:, None, :]


def route_weights(valid, chosen, gate_values):
    tok_rows = chosen.shape[0]
    live_int = valid.astype(jnp.int32)
    onehot = chosen[:, :, None] == jnp.arange(EXPERTS, dtype=jnp.int32)[None, None, :]
    onehot_f = onehot.astype(jnp.float32)
    hits = jnp.sum(onehot_f, axis=1) * valid.astype(jnp.float32)[:, None]
    earlier = (
        jnp.arange(tok_rows, dtype=jnp.int32)[None, :] < jnp.arange(tok_rows, dtype=jnp.int32)[:, None]
    ).astype(jnp.bfloat16)
    places = dot_f(earlier, hits.astype(jnp.bfloat16))
    pairs = jnp.sum(live_int) * TOP_K
    limit = ((5 * pairs + 4 * EXPERTS - 1) // (4 * EXPERTS)).astype(jnp.float32)
    kept = jnp.where((places < limit) & (hits > 0), 1.0, 0.0)
    weights = jnp.sum(onehot_f * gate_values[:, :, None], axis=1) * kept
    return (weights, onehot_f)


def block_scores(q_block, start, k_seq, length, scaling):
    rows_q = q_block.shape[0]
    kv_here = k_seq.shape[1]
    grouped = q_block.reshape(rows_q, kv_here, q_block.shape[1] // kv_here, q_block.shape[2])
    scores = (
        jnp.einsum("qkgd,skd->kgqs", grouped, k_seq, preferred_element_type=jnp.float32) * scaling
    )
    q_pos = start + jnp.arange(rows_q, dtype=jnp.int32)
    k_pos = jnp.arange(k_seq.shape[0], dtype=jnp.int32)
    allowed = (k_pos[None, :] <= q_pos[:, None]) & (k_pos[None, :] < length)
    return (jnp.where(allowed, scores, NEGATIVE), grouped)


def forward_block(q_block, start, k_seq, v_seq, length, scaling):
    scores, grouped = block_scores(q_block, start, k_seq, length, scaling)
    top_s = jnp.max(scores, axis=-1, keepdims=True)
    expo = jnp.exp(scores - top_s)
    total = jnp.sum(expo, axis=-1, keepdims=True)
    probs = (expo / total).astype(jnp.bfloat16)
    lse_part = (top_s + jnp.log(total))[..., 0]
    out_b = jnp.einsum("kgqs,skd->qkgd", probs, v_seq, preferred_element_type=jnp.float32)
    return (out_b.reshape(q_block.shape[0], -1), lse_part)


def attend_forward(q_all, k_all, v_all, lengths, scaling):
    seq_len = q_all.shape[1]
    q_rows = min(512, seq_len)
    n_blocks = seq_len // q_rows

    def one_sequence(item):
        q_seq, k_seq, v_seq, length = item
        outs = []
        lses = []
        for block in range(n_blocks):
            start = block * q_rows
            finish = start + q_rows
            out_b, lse_b = forward_block(
                q_seq[start:finish], start, k_seq[:finish], v_seq[:finish], length, scaling
            )
            outs.append(out_b)
            lses.append(lse_b)
        return (jnp.concatenate(outs, axis=0), jnp.stack(lses, axis=0))

    return lax.map(one_sequence, (q_all, k_all, v_all, lengths))


LANES = 128
ROWS = 256
N_CLASS = 109
HOP = 2
T_HEAD = 19
T_SUM1 = 16
T_MID1 = 33
T_ATT = 37
T_TURN = 53
T_PROJ = 57
T_SUM2 = 61
T_TOK = 78
T_MOE = 82
T_SUM3 = 90
T_RES = 107


def dot_nt(left, right):
    return lax.dot_general(
        left, right, (((1,), (1,)), ((), ())), preferred_element_type=jnp.float32
    )


def dot_tn(left, right):
    return lax.dot_general(
        left, right, (((0,), (0,)), ((), ())), preferred_element_type=jnp.float32
    )


def layer_kernel(
    nz, hop, ring,
    length, cat_in, w_full, x_in, d_out, w_slot, gains, w_gate, w_up, w_down,
    q_in, k_in, v_in, kt_in, lse_in, cos_in, sin_in, wo_in, wq_in, wkv_in,
    o_gate, o_up, o_down, o_q, o_k, o_v, o_out, o_norm, o_result, o_tokens, o_dots, s_resid, s_dres,
    lhs, rhs, pbuf, zbuf, ybuf, acc, buf1, buf2, hbuf, wgu, wdb, q2, k2, v2, kt2, lse, cos_t, sin_t,
    da2, dk_acc, dv_acc, slot_w, gain, norms,
    ld, wsem, iosem, ys, yr, zs, zr, fs, fr, gs, gr, os0, os1,
    cs_c, cr_c, cs_x, cr_x, cs_f, cr_f, s1s, s1r, s2s, s2r, s3s, s3r, ready1, ready2, ready3,
):
    f32, bf16 = jnp.float32, jnp.bfloat16
    dp = lax.axis_index("dp")
    tensor = lax.axis_index("tensor")
    base = dp - dp % (2 * nz)
    z, y = (dp % (2 * nz)) // 2, dp % 2
    last = nz - 1
    mate = base + z * 2 + (1 - y)
    up_id = base + jnp.minimum(z + 1, last) * 2 + y
    dn_id = base + jnp.maximum(z - 1, 0) * 2 + y
    core = tensor % 2
    core_mate = tensor - core + (1 - core)
    x_mate = (tensor + 2) % 4

    def local(src, dst, sem):
        return pltpu.make_async_copy(src, dst, sem)

    def remote(src, dst, ssem, rsem, dev, axis="dp"):
        return pltpu.make_async_remote_copy(
            src_ref=src, dst_ref=dst, send_sem=ssem, recv_sem=rsem,
            device_id={axis: dev}, device_id_type=MESH,
        )

    def block(b, size=ROWS):
        return pl.ds(pl.multiple_of(b * size, size), size)

    bar = pltpu.get_barrier_semaphore()
    for axis, dev in (("dp", mate), ("tensor", core_mate), ("tensor", x_mate)):
        pl.semaphore_signal(bar, inc=1, device_id={axis: dev}, device_id_type=MESH)

    @pl.when(z < last)
    def _():
        pl.semaphore_signal(bar, inc=1, device_id={"dp": up_id}, device_id_type=MESH)

    @pl.when(z > 0)
    def _():
        pl.semaphore_signal(bar, inc=1, device_id={"dp": dn_id}, device_id_type=MESH)

    wide = pl.ds(0, 1024)
    loads = [
        local(w_full.at[pl.ds(0, 512)], buf1.at[:, wide], ld.at[0]),
        local(w_full.at[pl.ds(512, 512)], buf2.at[:, wide], ld.at[1]),
        local(x_in, hbuf, ld.at[2]),
        local(gains, gain, ld.at[3]),
        local(w_slot, slot_w, ld.at[4]),
        local(d_out.at[:, pl.ds(0, 256)], rhs.at[0], ld.at[5]),
        local(d_out.at[:, pl.ds(256, 256)], rhs.at[1], ld.at[6]),
        local(d_out.at[:, pl.ds(512, 256)], rhs.at[2], ld.at[7]),
        local(d_out.at[:, pl.ds(768, 256)], rhs.at[3], ld.at[8]),
        local(cat_in, acc.at[:, block(tensor)], ld.at[9]),
        local(q_in, q2, ld.at[10]),
        local(k_in, k2, ld.at[11]),
        local(v_in, v2, ld.at[12]),
        local(kt_in, kt2, ld.at[13]),
        local(lse_in, lse, ld.at[14]),
        local(cos_in, cos_t, ld.at[15]),
        local(sin_in, sin_t, ld.at[16]),
    ]

    def expert_load(e, s):
        return [
            local(w_gate.at[e], wgu.at[s, :, pl.ds(0, LANES)], wsem.at[s, 0]),
            local(w_up.at[e], wgu.at[s, :, pl.ds(LANES, LANES)], wsem.at[s, 1]),
            local(w_down.at[e], wdb.at[s], wsem.at[s, 2]),
        ]

    for copy in loads:
        copy.start()
    for copy in expert_load(0, 0):
        copy.start()
    pl.semaphore_wait(bar, 3 + (z < last).astype(jnp.int32) + (z > 0).astype(jnp.int32))

    def gather_x(b):
        return remote(
            cat_in.at[block(b)], acc.at[block(b), block(tensor)], cs_x.at[b], cr_x.at[b], x_mate, "tensor"
        )

    def gather_c(b):
        return remote(
            cat_in.at[block(b)], acc.at[block(b), block(tensor)], cs_c.at[b], cr_c.at[b], core_mate, "tensor"
        )

    def gather_f(b):
        part = acc.at[block(b), block(x_mate)]
        return remote(part, part, cs_f.at[b], cr_f.at[b], core_mate, "tensor")

    for b in range(4):
        gather_x(b).start()
    for b in range(4):
        gather_c(b).start()
    for copy in loads:
        copy.wait()

    def cast_out(b, carry):
        for col in range(4):
            rhs[22 + col, block(b, 64), :] = buf1[block(b, 64), 256 * col : 256 * col + 256].astype(bf16)
            rhs[22 + col, pl.ds(pl.multiple_of(512 + b * 64, 64), 64), :] = buf2[
                block(b, 64), 256 * col : 256 * col + 256
            ].astype(bf16)
        return carry

    lax.fori_loop(0, 8, cast_out, 0)

    def forward_rows(b, carry):
        rows = block(b)
        for k in range(4):
            part = acc[rows, 256 * k : 256 * k + 256].astype(bf16)
            if k == 0:
                sums = [
                    hbuf[rows, 256 * col : 256 * col + 256].astype(f32) + dot_f(part, rhs[22 + col, 0:256, :])
                    for col in range(4)
                ]
            else:
                sums = [
                    sums[col] + dot_f(part, rhs[22 + col, 256 * k : 256 * k + 256, :]) for col in range(4)
                ]
        for half_c in range(2):
            own_c = pl.ds(pl.multiple_of(tensor * 256 + half_c * 128, 128), 128)
            lhs[32 + half_c, :, rows] = acc[rows, own_c].T.astype(bf16)
        square = sum(jnp.sum(v * v, axis=1, keepdims=True) for v in sums)
        scale_r = lax.rsqrt(square * (1.0 / 1024.0) + EPSILON)
        for col in range(4):
            acc[rows, 256 * col : 256 * col + 256] = sums[col]
            normed = sums[col] * scale_r * gain[0:1, 256 * col : 256 * col + 256]
            hbuf[rows, 256 * col : 256 * col + 256] = normed.astype(bf16)
            for half_c in range(2):
                lhs[16 + 2 * col + half_c, :, rows] = normed[:, 128 * half_c : 128 * half_c + 128].T.astype(bf16)
        return carry

    for b in range(4):
        gather_x(b).wait_recv()
        gather_f(b).start()
    for b in range(4):
        gather_c(b).wait_recv()
        gather_f(b).wait_recv()
        gather_f(b).wait_send()
        forward_rows(b, 0)
    for b in range(4):
        gather_x(b).wait_send()
        gather_c(b).wait_send()
    keep = local(acc.at[:, wide], s_resid, iosem.at[0])
    keep.start()
    keep.wait()

    def clear(b, carry):
        acc[block(b, 64), :] = jnp.zeros((64, 1152), f32)
        return carry

    lax.fori_loop(0, 16, clear, 0)
    dk_acc[...] = jnp.zeros_like(dk_acc)
    dv_acc[...] = jnp.zeros_like(dv_acc)
    norms[...] = jnp.zeros_like(norms)

    def expert(e):
        s = e % 2
        for copy in expert_load(e, s):
            copy.wait()

        @pl.when(e + 1 < EXPERTS)
        def _():
            for copy in expert_load(e + 1, 1 - s):
                copy.start()

        def rows_of(b, carry):
            rows = block(b)
            both = dot_f(hbuf[rows, :], wgu[s])
            gate, up = both[:, :LANES], both[:, LANES:]
            d_raw = dot_nt(rhs[0, rows, :], wdb[s, :, 0:256])
            for col in range(1, 4):
                d_raw = d_raw + dot_nt(rhs[col, rows, :], wdb[s, :, 256 * col : 256 * col + 256])
            lane = lax.broadcasted_iota(jnp.int32, (ROWS, LANES), 1)
            weight = jnp.sum(jnp.where(lane == e, slot_w[rows, :], 0.0), axis=1, keepdims=True)
            sigma = 1.0 / (1.0 + jnp.exp(-gate))
            silu = gate * sigma
            hidden = silu * up
            lhs[e, :, rows] = (hidden * weight).T.astype(bf16)
            inner = jnp.sum(hidden * d_raw, axis=1, keepdims=True)
            inner = jnp.where(weight > 0.0, inner, 0.0)
            acc[rows, 1024:1152] = jnp.where(lane == e, inner, acc[rows, 1024:1152])
            d_hidden = d_raw * weight
            d_gate = (d_hidden * up * sigma * (1.0 + gate * (1.0 - sigma))).astype(bf16)
            d_up = (d_hidden * silu).astype(bf16)
            rhs[4 + e, rows, 0:LANES] = d_gate
            rhs[4 + e, rows, LANES:] = d_up
            acc[rows, 0:1024] += dot_nt(rhs[4 + e, rows, :], wgu[s])
            return carry

        lax.fori_loop(0, 4, rows_of, 0)

    mine = pl.ds(pl.multiple_of(core * 512, 512), 512)
    other = pl.ds(pl.multiple_of((1 - core) * 512, 512), 512)

    def span(k):
        return pl.ds(0, 1152 if k == 0 else 1024)

    def sum_a(k):
        return remote(acc.at[other, span(k)], buf1.at[:, span(k)], s1s.at[k], s1r.at[k], core_mate, "tensor")

    def sum_b(k):
        return remote(acc.at[mine, span(k)], buf2.at[:, span(k)], s2s.at[k], s2r.at[k], x_mate, "tensor")

    def sum_c(k):
        part = acc.at[mine, span(k)]
        return remote(part, part, s3s.at[k], s3r.at[k], core_mate, "tensor")

    def add_in(k, buf):
        def step(b, carry):
            rows = pl.ds(pl.multiple_of(core * 512 + b * 64, 64), 64)
            acc[rows, span(k)] += buf[block(b, 64), span(k)]
            return carry

        lax.fori_loop(0, 8, step, 0)

    def sum_first(k):
        pl.semaphore_signal(ready1.at[k], inc=1, device_id={"tensor": core_mate}, device_id_type=MESH)
        pl.semaphore_signal(ready2.at[k], inc=1, device_id={"tensor": x_mate}, device_id_type=MESH)
        pl.semaphore_wait(ready1.at[k], 1)
        sum_a(k).start()

    def sum_second(k):
        sum_a(k).wait_recv()
        add_in(k, buf1)
        sum_a(k).wait_send()
        pl.semaphore_signal(ready3.at[k], inc=1, device_id={"tensor": core_mate}, device_id_type=MESH)
        pl.semaphore_wait(ready2.at[k], 1)
        sum_b(k).start()

    def sum_third(k):
        sum_b(k).wait_recv()
        sum_b(k).wait_send()
        add_in(k, buf2)
        pl.semaphore_wait(ready3.at[k], 1)
        sum_c(k).start()

    def sum_last(k):
        sum_c(k).wait_recv()
        sum_c(k).wait_send()

    def head_rows(b):
        rows = block(b)
        vals = [hbuf[rows, 256 * col : 256 * col + 256].astype(f32) for col in range(4)]
        square = sum(jnp.sum(v * v, axis=1, keepdims=True) for v in vals)
        scale_r = lax.rsqrt(square * (1.0 / 1024.0) + EPSILON)
        for col in range(4):
            normed = vals[col] * scale_r * gain[1:2, 256 * col : 256 * col + 256]
            for half_c in range(2):
                lhs[24 + 2 * col + half_c, :, rows] = normed[:, 128 * half_c : 128 * half_c + 128].T.astype(bf16)

    def in_halves(b, body):
        @pl.when(b < 2)
        def _():
            body(buf1, block(b))

        @pl.when(b >= 2)
        def _():
            body(buf2, block(b - 2))

    def norm_back(values, scale_r, grads, which):
        inner = sum(
            jnp.sum(v * scale_r * (g * gain[which : which + 1, 256 * c : 256 * c + 256]), axis=1, keepdims=True)
            for c, (v, g) in enumerate(zip(values, grads))
        ) * (1.0 / 1024.0)
        outs = []
        for c, (v, g) in enumerate(zip(values, grads)):
            normed = v * scale_r
            row = 4 * which + c
            norms[row : row + 1, :] += jnp.sum(g * normed, axis=0, keepdims=True)
            outs.append(scale_r * (g * gain[which : which + 1, 256 * c : 256 * c + 256] - normed * inner))
        return outs

    def middle_rows(b):
        rows = block(b)

        def body(buf, part):
            values = [buf[part, 256 * c : 256 * c + 256] for c in range(4)]
            grads = [acc[rows, 256 * c : 256 * c + 256] for c in range(4)]
            square = sum(jnp.sum(v * v, axis=1, keepdims=True) for v in values)
            scale_r = lax.rsqrt(square * (1.0 / 1024.0) + EPSILON)
            back = norm_back(values, scale_r, grads, 0)
            for c in range(4):
                total = rhs[c, rows, :].astype(f32) + back[c]
                acc[rows, 256 * c : 256 * c + 256] = total
                rhs[22 + c, rows, :] = total.astype(bf16)
            for h in range(4):
                d_head = dot_nt(rhs[22, rows, :], wdb[h, :, 0:256])
                for c in range(1, 4):
                    d_head = d_head + dot_nt(rhs[22 + c, rows, :], wdb[h, :, 256 * c : 256 * c + 256])
                da2[h, rows, :] = d_head.astype(bf16)

        in_halves(b, body)

    scaling = 1.0 / math.sqrt(HEAD_DIM)

    def turn_back(grad, cols):
        sine = grad * sin_t[:, cols]
        return grad * cos_t[:, cols] + jnp.concatenate([sine[32:], -sine[:32]], axis=0)

    def attend_back(h, qb):
        keys = ROWS * (qb + 1)
        rows = pl.ds(ROWS * qb, ROWS)
        q_rows = q2[h, rows, :]
        d_rows = da2[h, rows, :]
        scores = dot_nt(k2[0:keys, :], q_rows) * scaling
        k_pos = lax.broadcasted_iota(jnp.int32, (keys, ROWS), 0)
        q_pos = lax.broadcasted_iota(jnp.int32, (keys, ROWS), 1) + ROWS * qb
        allowed = (k_pos <= q_pos) & (k_pos < length[0])
        exact = jnp.exp(jnp.where(allowed, scores, NEGATIVE) - lse[pl.ds(h, 1), rows])
        d_probs = dot_nt(v2[0:keys, :], d_rows)
        inner = jnp.sum(exact * d_probs, axis=0, keepdims=True)
        d_scores = (exact * (d_probs - inner)).astype(bf16)
        dk_acc[0:keys, :] += dot_f(d_scores, q_rows)
        dv_acc[0:keys, :] += dot_f(exact.astype(bf16), d_rows)
        k_head = kt2[pl.ds(pl.multiple_of((h // 2) * 64, 64), 64), 0:keys]
        d_q = dot_f(k_head, d_scores) * scaling
        buf2[pl.ds(pl.multiple_of(h * 64, 64), 64), rows] = turn_back(d_q, rows)

    def turn_rows(b):
        rows = block(b)
        rhs[20, rows, :] = buf2[0:256, rows].T.astype(bf16)
        d_k = (dk_acc[rows, :] * scaling).T
        d_k = jnp.concatenate([turn_back(d_k[:64], rows), turn_back(d_k[64:], rows)], axis=0)
        rhs[21, rows, 0:LANES] = d_k.T.astype(bf16)
        rhs[21, rows, LANES:] = dv_acc[rows, :].astype(bf16)

    def project_rows(b):
        rows = block(b)
        acc[rows, 0:1024] = dot_nt(rhs[20, rows, :], wgu[0]) + dot_nt(rhs[21, rows, :], wgu[1])

    def token_rows(b):
        rows = block(b)

        def body(buf, part):
            values = [hbuf[rows, 256 * c : 256 * c + 256].astype(f32) for c in range(4)]
            grads = [acc[rows, 256 * c : 256 * c + 256] for c in range(4)]
            square = sum(jnp.sum(v * v, axis=1, keepdims=True) for v in values)
            scale_r = lax.rsqrt(square * (1.0 / 1024.0) + EPSILON)
            back = norm_back(values, scale_r, grads, 1)
            for c in range(4):
                cols = slice(256 * c, 256 * c + 256)
                hbuf[rows, cols] = (buf[part, cols] + back[c]).astype(bf16)

        in_halves(b, body)

    def pair_load(pair, s):
        return local(w_down.at[pl.ds(2 * pair, 2)], wdb.at[pl.ds(2 * s, 2)], wsem.at[s, 2])

    def moe_pair(pair):
        s = pair % 2
        pair_load(pair, s).wait()

        @pl.when(pair + 1 < EXPERTS // 2)
        def _():
            pair_load(pair + 1, 1 - s).start()

        def rows_of(b, carry):
            rows = block(b)
            hidden = lhs[pl.ds(2 * pair, 2), :, rows].reshape(256, ROWS)
            down = wdb[pl.ds(2 * s, 2)].reshape(256, 1024)
            part = dot_tn(hidden, down)

            @pl.when(pair == 0)
            def _():
                acc[rows, 0:1024] = part

            @pl.when(pair > 0)
            def _():
                acc[rows, 0:1024] += part

            return carry

        lax.fori_loop(0, 4, rows_of, 0)

    def result_rows(b):
        rows = block(b)

        def body(buf, part):
            pos = lax.broadcasted_iota(jnp.int32, (ROWS, 1024), 0) + b * ROWS
            total = buf[part, wide] + acc[rows, 0:1024]
            hbuf[rows, :] = jnp.where(pos < length[0], total, 0.0).astype(bf16)

        in_halves(b, body)

    def halves_in(src):
        return [
            local(src.at[pl.ds(0, 512)], buf1.at[:, wide], iosem.at[1]),
            local(src.at[pl.ds(512, 512)], buf2.at[:, wide], iosem.at[2]),
        ]

    def start(copies):
        for copy in copies:
            copy.start()

    def wait(copies):
        for copy in copies:
            copy.wait()

    tokens_in = [local(x_in, hbuf, iosem.at[3])]
    wo_load = [local(wo_in, wdb, iosem.at[4])]
    proj_load = [local(wq_in, wgu.at[0], iosem.at[5]), local(wkv_in, wgu.at[1], iosem.at[6])]
    dots_out = [local(acc.at[:, pl.ds(1024, LANES)], o_dots, iosem.at[7])]
    dres_out = [local(acc.at[:, wide], s_dres, iosem.at[8])]
    tokens_out = [local(hbuf, o_tokens, iosem.at[9])]
    result_out = [local(hbuf, o_result, iosem.at[10])]

    def do_all(*steps):
        for step in steps:
            step()

    once = {
        T_SUM1: lambda: do_all(lambda: sum_first(0), lambda: start(tokens_in + wo_load + proj_load)),
        T_SUM1 + 2: lambda: do_all(lambda: sum_second(0), lambda: wait(tokens_in)),
        T_MID1 - 3: lambda: sum_third(0),
        T_MID1 - 1: lambda: do_all(
            lambda: sum_last(0), lambda: start(halves_in(s_resid) + dots_out), lambda: wait(wo_load)
        ),
        T_ATT: lambda: do_all(lambda: wait(dots_out), lambda: start(dres_out)),
        T_PROJ - 1: lambda: do_all(lambda: wait(dres_out), lambda: wait(proj_load)),
        T_SUM2: lambda: sum_first(1),
        T_SUM2 + 2: lambda: sum_second(1),
        T_TOK - 3: lambda: sum_third(1),
        T_TOK - 1: lambda: do_all(
            lambda: sum_last(1), lambda: start(halves_in(s_dres)), lambda: start([pair_load(0, 0)])
        ),
        T_MOE: lambda: start(tokens_out),
        T_SUM3: lambda: do_all(lambda: wait(tokens_out), lambda: sum_first(2)),
        T_SUM3 + 2: lambda: sum_second(2),
        T_RES - 3: lambda: sum_third(2),
        T_RES - 1: lambda: do_all(lambda: sum_last(2), lambda: start(halves_in(s_resid))),
        T_RES + 4: lambda: start(result_out),
        T_RES + 8: lambda: wait(result_out),
    }
    halves_wait = {T_MID1: s_resid, T_TOK: s_dres, T_RES: s_resid}

    def work(t):
        for when_t, fn in sorted(once.items()):
            pl.when(t == when_t)(fn)
        for when_t, src in halves_wait.items():
            pl.when(t == when_t)(lambda src=src: wait(halves_in(src)))
        for begin, count, fn in (
            (0, EXPERTS, expert),
            (T_HEAD, 4, head_rows),
            (T_MID1, 4, middle_rows),
            (T_TURN, 4, turn_rows),
            (T_PROJ, 4, project_rows),
            (T_TOK, 4, token_rows),
            (T_MOE, EXPERTS // 2, moe_pair),
            (T_RES, 4, result_rows),
        ):
            pl.when((t >= begin) & (t < begin + count))(lambda fn=fn, begin=begin: fn(t - begin))
        for qb in range(4):
            u = t - T_ATT
            pl.when((u >= 0) & (u < 16) & (u % 4 == qb))(lambda qb=qb, u=u: attend_back(u // 4, qb))

    own = pl.ds(pl.multiple_of(y * 64, 64), 64)
    oth = pl.ds(pl.multiple_of((1 - y) * 64, 64), 64)
    half = pl.ds(0, 64)

    def stage(c, t):
        p = z if c == 0 else last - z
        nxt, prv = (up_id, dn_id) if c == 0 else (dn_id, up_id)
        def at(delay, body):
            i = t - delay

            @pl.when((i >= 0) & (i < N_CLASS))
            def _():
                body(i, i % ring, i % 2 == 0)

        def ycopy_a(s):
            return remote(pbuf.at[c, s, oth], ybuf.at[c, s, half], ys.at[c, s], yr.at[c, s], mate)

        def ycopy_b(s):
            return remote(zbuf.at[c, s], ybuf.at[c, s], ys.at[c, s], yr.at[c, s], mate)

        def zcopy_a(s):
            return remote(zbuf.at[c, s, half], zbuf.at[c, s, half], zs.at[c, s], zr.at[c, s], nxt)

        def zcopy_b(s):
            return remote(zbuf.at[c, s], zbuf.at[c, s], zs.at[c, s], zr.at[c, s], nxt)

        def fcopy_a(s):
            return remote(pbuf.at[c, s, own], pbuf.at[c, s, own], fs.at[c, s], fr.at[c, s], prv)

        def fcopy_b(s):
            return remote(pbuf.at[c, s], pbuf.at[c, s], fs.at[c, s], fr.at[c, s], prv)

        def gcopy(s):
            return remote(pbuf.at[c, s, own], ybuf.at[c, s, pl.ds(64, 64)], gs.at[c, s], gr.at[c, s], mate)

        def first(i, s, is_a):
            g = 2 * i + c
            expert, part = g // 12, g % 12
            a = g - 192
            in_moe = g < 192
            l_moe = jnp.where(part < 4, expert, 12 + part)
            r_moe = jnp.where(part < 4, part, 4 + expert)
            l_att = jnp.where(a < 16, 24 + a % 8, 32 + (a - 16) // 4)
            r_att = jnp.where(a < 16, 20 + a // 8, 22 + (a - 16) % 4)
            li = jnp.where(in_moe, l_moe, l_att)
            ri = jnp.where(in_moe, r_moe, r_att)
            @pl.when(i < N_CLASS - 1)
            def _():
                pbuf[c, s] = dot_f(lhs[jnp.minimum(li, 33)], rhs[jnp.minimum(ri, 25)])

            @pl.when(i == N_CLASS - 1)
            def _():
                pbuf[c, s] = norms[...]

            @pl.when(is_a)
            def _():
                ycopy_a(s).start()

        def second(i, s, is_a):
            @pl.when(is_a)
            def _():
                ycopy_a(s).wait_recv()

                @pl.when(p > 0)
                def _():
                    zcopy_a(s).wait_recv()
                    zbuf[c, s, half] = zbuf[c, s, half] + (pbuf[c, s, own] + ybuf[c, s, half])

                @pl.when(p == 0)
                def _():
                    zbuf[c, s, half] = pbuf[c, s, own] + ybuf[c, s, half]

                @pl.when(p < last)
                def _():
                    zcopy_a(s).start()

                @pl.when(p == last)
                def _():
                    pbuf[c, s, own] = zbuf[c, s, half]
                    fcopy_a(s).start()
                    gcopy(s).start()

            @pl.when(jnp.logical_not(is_a))
            def _():
                @pl.when(p > 0)
                def _():
                    zcopy_b(s).wait_recv()
                    zbuf[c, s] = zbuf[c, s] + pbuf[c, s]

                @pl.when(p == 0)
                def _():
                    zbuf[c, s] = pbuf[c, s]

                @pl.when(p < last)
                def _():
                    zcopy_b(s).start()

                @pl.when(p == last)
                def _():
                    ycopy_b(s).start()

        def third(i, s, is_a):
            @pl.when(jnp.logical_not(is_a) & (p == last))
            def _():
                ycopy_b(s).wait_recv()
                pbuf[c, s] = zbuf[c, s] + ybuf[c, s]
                fcopy_b(s).start()

        def fourth(i, s, is_a):
            @pl.when(p < last)
            def _():
                @pl.when(is_a)
                def _():
                    fcopy_a(s).wait_recv()

                    @pl.when(p > 0)
                    def _():
                        fcopy_a(s).start()

                    gcopy(s).start()

                @pl.when(jnp.logical_not(is_a))
                def _():
                    fcopy_b(s).wait_recv()

                    @pl.when(p > 0)
                    def _():
                        fcopy_b(s).start()

        def store(s, dst0, dst1):
            pltpu.make_async_copy(pbuf.at[c, s, :, pl.ds(0, 128)], dst0, os0.at[c, s]).start()
            pltpu.make_async_copy(pbuf.at[c, s, :, pl.ds(128, 128)], dst1, os1.at[c, s]).start()

        def fifth(i, s, is_a):
            @pl.when(is_a)
            def _():
                gcopy(s).wait_recv()
                ycopy_a(s).wait_send()
                pbuf[c, s, oth] = ybuf[c, s, pl.ds(64, 64)]

            g = 2 * i + c
            expert, part = g // 12, g % 12
            a = g - 192

            @pl.when((g < 192) & (part < 4))
            def _():
                col = pl.multiple_of(part * 256, 128)
                col1 = pl.multiple_of(part * 256 + 128, 128)
                store(s, o_down.at[expert, :, pl.ds(col, 128)], o_down.at[expert, :, pl.ds(col1, 128)])

            @pl.when((g < 192) & (part >= 4))
            def _():
                rows = pl.ds(pl.multiple_of((part - 4) * 128, 128), 128)
                store(s, o_gate.at[expert, rows], o_up.at[expert, rows])

            @pl.when((g >= 192) & (a < 8))
            def _():
                rows = pl.ds(pl.multiple_of(a * 128, 128), 128)
                store(s, o_q.at[rows, pl.ds(0, 128)], o_q.at[rows, pl.ds(128, 128)])

            @pl.when((a >= 8) & (a < 16))
            def _():
                rows = pl.ds(pl.multiple_of((a - 8) * 128, 128), 128)
                store(s, o_k.at[rows], o_v.at[rows])

            @pl.when(i == N_CLASS - 1)
            def _():
                store(s, o_norm.at[c, :, pl.ds(0, 128)], o_norm.at[c, :, pl.ds(128, 128)])

            @pl.when((a >= 16) & (a < 24))
            def _():
                b = a - 16
                rows = pl.ds(pl.multiple_of((b // 4) * 128, 128), 128)
                col = pl.multiple_of((b % 4) * 256, 128)
                col1 = pl.multiple_of((b % 4) * 256 + 128, 128)
                store(s, o_out.at[rows, pl.ds(col, 128)], o_out.at[rows, pl.ds(col1, 128)])

        def sixth(i, s, is_a):
            pltpu.make_async_copy(pbuf.at[c, s, :, pl.ds(0, 128)], o_k.at[pl.ds(0, 128)], os0.at[c, s]).wait()
            pltpu.make_async_copy(pbuf.at[c, s, :, pl.ds(0, 128)], o_k.at[pl.ds(0, 128)], os1.at[c, s]).wait()

            @pl.when(is_a)
            def _():
                gcopy(s).wait_send()

                @pl.when(p < last)
                def _():
                    zcopy_a(s).wait_send()

                @pl.when(p > 0)
                def _():
                    fcopy_a(s).wait_send()

            @pl.when(jnp.logical_not(is_a))
            def _():
                @pl.when(p < last)
                def _():
                    zcopy_b(s).wait_send()

                @pl.when(p == last)
                def _():
                    ycopy_b(s).wait_send()

                @pl.when(p > 0)
                def _():
                    fcopy_b(s).wait_send()

        t2 = hop * (1 + p)
        t3 = hop * (2 + last)
        t4 = t3 + hop * (last - p)
        t5 = t4 + hop
        t6 = t5 + hop
        return [(0, first, at), (t2, second, at), (t3, third, at), (t4, fourth, at), (t5, fifth, at), (t6, sixth, at)]

    def body(t, carry):
        both = [stage(0, t), stage(1, t)]
        for k in (1, 2, 3, 4, 5, 0):
            if k == 0:
                work(t)
            for st in both:
                delay, fn, at = st[k]
                at(delay, fn)
        return carry

    total = N_CLASS + hop * (2 * last + 4) + 1
    lax.fori_loop(0, total, body, 0)


def run_layer(mesh, *operands):
    groups = mesh.shape["dp"]
    nz = 4 if groups % 8 == 0 else groups // 2
    last = nz - 1
    hop = HOP
    ring = hop * (2 * last + 4) + 2
    ring += ring % 2
    f32, bf16 = jnp.float32, jnp.bfloat16

    def out(shape, kind=f32):
        return jax.ShapeDtypeStruct(shape, kind)

    outs = [
        out((16, 1024, 128)), out((16, 1024, 128)), out((16, 128, 1024)),
        out((1024, 256)), out((1024, 128)), out((1024, 128)), out((256, 1024)), out((2, 128, 256)),
        out((1024, 1024), bf16), out((1024, 1024), bf16), out((1024, 128)),
        out((1024, 1024)), out((1024, 1024)),
    ]
    anywhere = pl.BlockSpec(memory_space=pl.ANY)
    dma = pltpu.SemaphoreType.DMA
    reg = pltpu.SemaphoreType.REGULAR
    vmem = pltpu.VMEM
    res = pl.pallas_call(
        functools.partial(layer_kernel, nz, hop, ring),
        out_shape=outs,
        in_specs=[pl.BlockSpec(memory_space=pltpu.SMEM)] + [anywhere] * (len(operands) - 1),
        out_specs=[anywhere] * len(outs),
        scratch_shapes=[
            vmem((34, 128, 1024), bf16), vmem((26, 1024, 256), bf16),
            vmem((2, ring, 128, 256), f32), vmem((2, ring, 128, 256), f32), vmem((2, ring, 128, 256), f32),
            vmem((1024, 1152), f32), vmem((512, 1152), f32), vmem((512, 1152), f32),
            vmem((1024, 1024), bf16), vmem((2, 1024, 256), bf16), vmem((4, 128, 1024), bf16),
            vmem((4, 1024, 128), bf16), vmem((1024, 128), bf16), vmem((1024, 128), bf16), vmem((128, 1024), bf16),
            vmem((8, 1024), f32), vmem((64, 1024), f32), vmem((64, 1024), f32),
            vmem((4, 1024, 128), bf16), vmem((1024, 128), f32), vmem((1024, 128), f32),
            vmem((1024, 128), f32), vmem((8, 1024), f32), vmem((128, 256), f32),
            dma((17,)), dma((2, 3)), dma((11,)),
        ]
        + [dma((2, ring))] * 10
        + [dma((4,))] * 6
        + [dma((3,))] * 6
        + [reg((3,))] * 3,
        compiler_params=pltpu.CompilerParams(
            collective_id=0, has_side_effects=True, vmem_limit_bytes=62 * 2**20
        ),
    )(*operands)
    sums, rest = tuple(res[:8]), res[8:11]
    if groups > 2 * nz:
        same = [
            [2 * nz * block + place for block in range(groups // (2 * nz))] for place in range(2 * nz)
        ]
        sums = lax.psum(sums, "dp", axis_index_groups=same)
    return sums, rest


def per_device(
    mesh,
    tokens,
    lengths,
    chosen,
    gate_values,
    cotangent,
    norm_attn,
    w_query,
    w_key,
    w_value,
    w_out,
    norm_moe,
    w_gate,
    w_up,
    w_down,
):
    seq_count = lengths.shape[0]
    tok_rows = tokens.shape[0]
    seq_len = tok_rows // seq_count
    width = tokens.shape[1]
    heads_here = w_query.shape[1] // HEAD_DIM
    kv_here = w_key.shape[1] // HEAD_DIM
    scaling = 1.0 / math.sqrt(HEAD_DIM)
    valid = (jnp.arange(seq_len, dtype=jnp.int32)[None, :] < lengths[:, None]).reshape(-1)
    cosine, sine = rope_tables(seq_len, HEAD_DIM)
    w_out_all = lax.all_gather(w_out.astype(jnp.float32), "tensor", axis=0, tiled=True)
    x_in = tokens.astype(jnp.float32)
    h_attn = rms_norm(x_in, norm_attn).astype(jnp.bfloat16)
    q_lin = dot_f(h_attn, w_query).reshape(seq_count, seq_len, heads_here, HEAD_DIM)
    k_lin = dot_f(h_attn, w_key).reshape(seq_count, seq_len, kv_here, HEAD_DIM)
    v_att = (
        dot_f(h_attn, w_value).astype(jnp.bfloat16).reshape(seq_count, seq_len, kv_here, HEAD_DIM)
    )
    q_rot = rotate(q_lin, cosine, sine).astype(jnp.bfloat16)
    k_rot = rotate(k_lin, cosine, sine).astype(jnp.bfloat16)
    attended, lse_all = attend_forward(q_rot, k_rot, v_att, lengths, scaling)
    attn_cat = attended.reshape(tok_rows, heads_here * HEAD_DIM).astype(jnp.bfloat16)
    weights, onehot_f = route_weights(valid, chosen, gate_values)
    d_out = jnp.where(valid[:, None], cotangent, 0)
    q_heads = q_rot.reshape(tok_rows, heads_here, HEAD_DIM).transpose(1, 0, 2)
    q_pad = jnp.concatenate(
        [jnp.pad(q_heads[:2], ((0, 0), (0, 0), (0, 64))), jnp.pad(q_heads[2:], ((0, 0), (0, 0), (64, 0)))]
    )
    wo_heads = w_out.reshape(heads_here, HEAD_DIM, width)
    wo_pad = jnp.concatenate(
        [jnp.pad(wo_heads[:2], ((0, 0), (0, 64), (0, 0))), jnp.pad(wo_heads[2:], ((0, 0), (64, 0), (0, 0)))]
    )
    k_flat = k_rot.reshape(tok_rows, -1)
    lse_rows = lse_all[0].reshape(-1, heads_here, min(512, seq_len)).transpose(1, 0, 2).reshape(heads_here, tok_rows)
    sums, (result, grad_tokens, dots) = run_layer(
        mesh,
        lengths,
        attn_cat.astype(jnp.float32),
        w_out_all,
        tokens,
        d_out,
        jnp.pad(weights, ((0, 0), (0, 128 - EXPERTS))),
        jnp.pad(jnp.stack([norm_moe, norm_attn]), ((0, 6), (0, 0))),
        w_gate,
        w_up,
        w_down,
        q_pad,
        k_flat,
        v_att.reshape(tok_rows, -1),
        k_flat.T,
        jnp.pad(lse_rows, ((0, 8 - heads_here), (0, 0))),
        cosine.T,
        sine.T,
        wo_pad,
        w_query,
        jnp.concatenate([w_key, w_value], axis=1),
    )
    grad_gate, grad_up, grad_down, grad_query, grad_key, grad_value, grad_out, norm_rows = sums
    d_gates = jnp.sum(onehot_f * dots[:, None, :EXPERTS], axis=-1)
    return (
        result,
        grad_tokens,
        d_gates,
        norm_rows[0, 4:8].reshape(-1),
        grad_query,
        grad_key,
        grad_value,
        grad_out,
        norm_rows[0, 0:4].reshape(-1),
        grad_gate,
        grad_up,
        grad_down,
    )


def solution(mesh):
    placed = (
        P("dp", None),
        P("dp"),
        P("dp", None),
        P("dp", None),
        P("dp", None),
        P(),
        P(None, "tensor"),
        P(None, "tensor"),
        P(None, "tensor"),
        P("tensor", None),
        P(),
        P(None, None, "tensor"),
        P(None, None, "tensor"),
        P(None, "tensor", None),
    )
    return jax.shard_map(
        functools.partial(per_device, mesh),
        mesh=mesh,
        in_specs=placed,
        out_specs=(
            P("dp", None),
            P("dp", None),
            P("dp", None),
            P(),
            P(None, "tensor"),
            P(None, "tensor"),
            P(None, "tensor"),
            P("tensor", None),
            P(),
            P(None, None, "tensor"),
            P(None, None, "tensor"),
            P(None, "tensor", None),
        ),
        check_vma=False,
    )
```

```python
import functools
import math

import jax
import jax.numpy as jnp
import numpy as np
from jax import lax
from jax.experimental import pallas as pl
from jax.experimental.pallas import tpu as pltpu
from jax.sharding import PartitionSpec as P

MESH = pl.DeviceIdType.MESH

HEAD_DIM = 64
TOP_K = 8
EXPERTS = 16


EPSILON = 1e-05
THETA = 10000.0
NEGATIVE = -1e30


def dot_f(left, right):
    return jnp.dot(left, right, preferred_element_type=jnp.float32)


def rope_tables(positions, width):
    half_w = width // 2
    freqs = THETA ** (-np.arange(half_w, dtype=np.float64) * 2.0 / width)
    angles = np.concatenate([freqs, freqs])[:, None] * np.arange(positions, dtype=np.float64)[None, :]
    return (np.cos(angles).astype(np.float32), np.sin(angles).astype(np.float32))


LANES = 128
ROWS = 256
N_CLASS = 109
HOP = 2
T_SUM1 = 16
T_MID1 = 33
T_ATT = 37
T_TURN = 53
T_PROJ = 57
T_SUM2 = 61
T_TOK = 78
T_MOE = 82
T_SUM3 = 90
T_RES = 107


def dot_nt(left, right):
    return lax.dot_general(
        left, right, (((1,), (1,)), ((), ())), preferred_element_type=jnp.float32
    )


def dot_tn(left, right):
    return lax.dot_general(
        left, right, (((0,), (0,)), ((), ())), preferred_element_type=jnp.float32
    )


def layer_kernel(
    nz, hop, ring,
    length, x_in, d_out, chosen, gates, gain_attn, gain_moe, w_gate, w_up, w_down,
    cos_in, sin_in, w_out, w_query, w_key, w_value,
    o_gate, o_up, o_down, o_q, o_k, o_v, o_out, o_norm, o_result, o_tokens, o_dots, s_resid, s_dres,
    lhs, rhs, pbuf, zbuf, ybuf, acc, buf, hbuf, wgu, wdb, q2, k2, v2, kt2, vt2, lse, cos_t, sin_t,
    da2, dk_acc, dv_acc, slot_w, gain, norms, picks, pick_w,
    ld, wsem, iosem, ys, yr, zs, zr, fs, fr, gs, gr, os0, os1,
    cs_c, cr_c, cs_x, cr_x, cs_f, cr_f, ws, wr, s1s, s1r, s2s, s2r, s3s, s3r, ready1, ready2, ready3,
):
    f32, bf16 = jnp.float32, jnp.bfloat16
    dp = lax.axis_index("dp")
    tensor = lax.axis_index("tensor")
    base = dp - dp % (2 * nz)
    z, y = (dp % (2 * nz)) // 2, dp % 2
    last = nz - 1
    mate = base + z * 2 + (1 - y)
    up_id = base + jnp.minimum(z + 1, last) * 2 + y
    dn_id = base + jnp.maximum(z - 1, 0) * 2 + y
    core = tensor % 2
    core_mate = tensor - core + (1 - core)
    x_mate = (tensor + 2) % 4

    def local(src, dst, sem):
        return pltpu.make_async_copy(src, dst, sem)

    def remote(src, dst, ssem, rsem, dev, axis="dp"):
        return pltpu.make_async_remote_copy(
            src_ref=src, dst_ref=dst, send_sem=ssem, recv_sem=rsem,
            device_id={axis: dev}, device_id_type=MESH,
        )

    def block(b, size=ROWS):
        return pl.ds(pl.multiple_of(b * size, size), size)

    bar = pltpu.get_barrier_semaphore()
    for axis, dev in (("dp", mate), ("tensor", core_mate), ("tensor", x_mate)):
        pl.semaphore_signal(bar, inc=1, device_id={axis: dev}, device_id_type=MESH)

    @pl.when(z < last)
    def _():
        pl.semaphore_signal(bar, inc=1, device_id={"dp": up_id}, device_id_type=MESH)

    @pl.when(z > 0)
    def _():
        pl.semaphore_signal(bar, inc=1, device_id={"dp": dn_id}, device_id_type=MESH)

    wide = pl.ds(0, 1024)
    share = block(tensor)
    token_load = [
        local(x_in, hbuf, ld.at[0]),
        local(gain_attn, gain.at[pl.ds(1, 1)], ld.at[1]),
        local(gain_moe, gain.at[pl.ds(0, 1)], ld.at[2]),
        local(cos_in, cos_t, ld.at[3]),
        local(sin_in, sin_t, ld.at[4]),
    ]
    proj_load = [
        local(w_query, wgu.at[0], ld.at[5]),
        local(w_key, wgu.at[1, :, pl.ds(0, LANES)], ld.at[6]),
        local(w_value, wgu.at[1, :, pl.ds(LANES, LANES)], ld.at[7]),
    ]
    out_load = [local(w_out.at[:, block(c)], rhs.at[22 + c, share], ld.at[8 + c]) for c in range(4)]
    late_load = [local(d_out.at[:, block(c)], rhs.at[c], ld.at[12 + c]) for c in range(4)] + [
        local(chosen, picks, ld.at[16]),
        local(gates, pick_w, ld.at[17]),
    ]

    def expert_load(e, s):
        return [
            local(w_gate.at[e], wgu.at[s, :, pl.ds(0, LANES)], wsem.at[s, 0]),
            local(w_up.at[e], wgu.at[s, :, pl.ds(LANES, LANES)], wsem.at[s, 1]),
            local(w_down.at[e], wdb.at[s], wsem.at[s, 2]),
        ]

    def start(copies):
        for copy in copies:
            copy.start()

    def wait(copies):
        for copy in copies:
            copy.wait()

    start(out_load + token_load + proj_load + late_load)
    pl.semaphore_wait(bar, 3 + (z < last).astype(jnp.int32) + (z > 0).astype(jnp.int32))

    part_w = buf.at[share, wide]
    w_x = remote(part_w, part_w, ws.at[0], wr.at[0], x_mate, "tensor")
    w_c = remote(part_w, part_w, ws.at[1], wr.at[1], core_mate, "tensor")
    part_f = buf.at[block(x_mate), wide]
    w_f = remote(part_f, part_f, ws.at[2], wr.at[2], core_mate, "tensor")
    wait(out_load)
    for c in range(4):
        buf[share, 256 * c : 256 * c + 256] = rhs[22 + c, share, :].astype(f32)
    w_x.start()
    w_c.start()

    def gather_x(b):
        return remote(
            acc.at[block(b), share], acc.at[block(b), share], cs_x.at[b], cr_x.at[b], x_mate, "tensor"
        )

    def gather_c(b):
        return remote(
            acc.at[block(b), share], acc.at[block(b), share], cs_c.at[b], cr_c.at[b], core_mate, "tensor"
        )

    def gather_f(b):
        part = acc.at[block(b), block(x_mate)]
        return remote(part, part, cs_f.at[b], cr_f.at[b], core_mate, "tensor")

    def rotate_t(values, cols):
        turned = jnp.concatenate([-values[32:], values[:32]], axis=0)
        return values * cos_t[:, cols] + turned * sin_t[:, cols]

    def head_rows(b, carry):
        rows = block(b)
        vals = [hbuf[rows, 256 * col : 256 * col + 256].astype(f32) for col in range(4)]
        square = sum(jnp.sum(v * v, axis=1, keepdims=True) for v in vals)
        scale_r = lax.rsqrt(square * (1.0 / 1024.0) + EPSILON)
        query, key_value = 0.0, 0.0
        for col in range(4):
            normed = vals[col] * scale_r * gain[1:2, 256 * col : 256 * col + 256]
            for half_c in range(2):
                lhs[24 + 2 * col + half_c, :, rows] = normed[:, 128 * half_c : 128 * half_c + 128].T.astype(bf16)
            normed = normed.astype(bf16)
            query = query + dot_f(normed, wgu[0, 256 * col : 256 * col + 256, :])
            key_value = key_value + dot_f(normed, wgu[1, 256 * col : 256 * col + 256, :])
        query = query.T
        nothing = jnp.zeros((64, ROWS), f32)
        for h in range(4):
            turned = rotate_t(query[64 * h : 64 * h + 64], rows)
            both = [turned, nothing] if h < 2 else [nothing, turned]
            q2[h, rows, :] = jnp.concatenate(both, axis=0).T.astype(bf16)
        key = key_value[:, :LANES].T
        key = jnp.concatenate([rotate_t(key[:64], rows), rotate_t(key[64:], rows)], axis=0)
        kt2[:, rows] = key.astype(bf16)
        k2[rows, :] = key.T.astype(bf16)
        value = key_value[:, LANES:]
        v2[rows, :] = value.astype(bf16)
        vt2[:, rows] = value.T.astype(bf16)
        return carry

    scaling = 1.0 / math.sqrt(HEAD_DIM)

    def masked_scores(h, qb):
        keys = ROWS * (qb + 1)
        rows = pl.ds(ROWS * qb, ROWS)
        scores = dot_nt(k2[0:keys, :], q2[h, rows, :]) * scaling
        k_pos = lax.broadcasted_iota(jnp.int32, (keys, ROWS), 0)
        q_pos = lax.broadcasted_iota(jnp.int32, (keys, ROWS), 1) + ROWS * qb
        allowed = (k_pos <= q_pos) & (k_pos < length[0])
        return jnp.where(allowed, scores, NEGATIVE)

    def attend(qb):
        keys = ROWS * (qb + 1)
        rows = pl.ds(ROWS * qb, ROWS)

        def one_head(h, carry):
            scores = masked_scores(h, qb)
            top_s = jnp.max(scores, axis=0, keepdims=True)
            expo = jnp.exp(scores - top_s)
            total = jnp.sum(expo, axis=0, keepdims=True)
            probs = (expo / total).astype(bf16)
            lse[pl.ds(h, 1), rows] = top_s + jnp.log(total)
            v_head = vt2[pl.ds(pl.multiple_of((h // 2) * 64, 64), 64), 0:keys]
            lhs[32 + h // 2, pl.ds(pl.multiple_of((h % 2) * 64, 64), 64), rows] = dot_f(v_head, probs).astype(bf16)
            return carry

        lax.fori_loop(0, 4, one_head, 0)
        for half_c in range(2):
            own_c = pl.ds(pl.multiple_of(tensor * 256 + half_c * 128, 128), 128)
            acc[rows, own_c] = lhs[32 + half_c, :, rows].astype(f32).T
        gather_x(qb).start()
        gather_c(qb).start()

    wait(token_load + proj_load)
    lax.fori_loop(0, 4, head_rows, 0)
    start(expert_load(0, 0))
    for qb in range(4):
        attend(qb)

    wait(late_load)

    def route_hits(b, carry):
        rows = block(b)
        lane = lax.broadcasted_iota(jnp.int32, (ROWS, LANES), 1)
        pos = lax.broadcasted_iota(jnp.int32, (ROWS, LANES), 0) + b * ROWS
        pos_wide = lax.broadcasted_iota(jnp.int32, (ROWS, 256), 0) + b * ROWS
        hits = jnp.zeros((ROWS, LANES), f32)
        weight = jnp.zeros((ROWS, LANES), f32)
        for k in range(TOP_K):
            same = picks[rows, k : k + 1] == lane
            hits = jnp.where(same, 1.0, hits)
            weight = jnp.where(same, pick_w[rows, k : k + 1], weight)
        live = pos < length[0]
        da2[0, rows, :] = jnp.where(live, hits, 0.0).astype(bf16)
        slot_w[rows, :] = jnp.where(live, weight, 0.0)
        for c in range(4):
            rhs[c, rows, :] = jnp.where(pos_wide < length[0], rhs[c, rows, :].astype(f32), 0.0).astype(bf16)
        return carry

    lax.fori_loop(0, 4, route_hits, 0)
    limit = ((5 * TOP_K * length[0] + 4 * EXPERTS - 1) // (4 * EXPERTS)).astype(f32)

    def route_kept(b, carry):
        rows = block(b)
        row = lax.broadcasted_iota(jnp.int32, (ROWS, 1024), 0) + b * ROWS
        earlier = jnp.where(lax.broadcasted_iota(jnp.int32, (ROWS, 1024), 1) < row, 1.0, 0.0).astype(bf16)
        places = dot_f(earlier, da2[0])
        slot_w[rows, :] = jnp.where(places < limit, slot_w[rows, :], 0.0)
        return carry

    lax.fori_loop(0, 4, route_kept, 0)

    w_x.wait_recv()
    w_f.start()
    w_c.wait_recv()
    w_f.wait_recv()

    def cast_out(b, carry):
        for c in range(4):
            rhs[22 + c, block(b, 64), :] = buf[block(b, 64), 256 * c : 256 * c + 256].astype(bf16)
        return carry

    lax.fori_loop(0, 16, cast_out, 0)

    def forward_rows(b, carry):
        rows = block(b)
        for k in range(4):
            part = acc[rows, 256 * k : 256 * k + 256].astype(bf16)
            if k == 0:
                sums = [
                    hbuf[rows, 256 * col : 256 * col + 256].astype(f32) + dot_f(part, rhs[22 + col, 0:256, :])
                    for col in range(4)
                ]
            else:
                sums = [
                    sums[col] + dot_f(part, rhs[22 + col, 256 * k : 256 * k + 256, :]) for col in range(4)
                ]
        square = sum(jnp.sum(v * v, axis=1, keepdims=True) for v in sums)
        scale_r = lax.rsqrt(square * (1.0 / 1024.0) + EPSILON)
        for col in range(4):
            acc[rows, 256 * col : 256 * col + 256] = sums[col]
            normed = sums[col] * scale_r * gain[0:1, 256 * col : 256 * col + 256]
            hbuf[rows, 256 * col : 256 * col + 256] = normed.astype(bf16)
            for half_c in range(2):
                lhs[16 + 2 * col + half_c, :, rows] = normed[:, 128 * half_c : 128 * half_c + 128].T.astype(bf16)
        return carry

    for b in range(4):
        gather_x(b).wait_recv()
        gather_f(b).start()
    for b in range(4):
        gather_c(b).wait_recv()
        gather_f(b).wait_recv()
        gather_f(b).wait_send()
        gather_x(b).wait_send()
        gather_c(b).wait_send()
        forward_rows(b, 0)
    w_x.wait_send()
    w_c.wait_send()
    w_f.wait_send()
    keep = local(acc.at[:, wide], s_resid, iosem.at[0])
    keep.start()
    keep.wait()

    def clear(b, carry):
        acc[block(b, 64), :] = jnp.zeros((64, 1152), f32)
        return carry

    lax.fori_loop(0, 16, clear, 0)
    dk_acc[...] = jnp.zeros_like(dk_acc)
    dv_acc[...] = jnp.zeros_like(dv_acc)
    norms[...] = jnp.zeros_like(norms)

    def expert(e):
        s = e % 2
        for copy in expert_load(e, s):
            copy.wait()

        @pl.when(e + 1 < EXPERTS)
        def _():
            for copy in expert_load(e + 1, 1 - s):
                copy.start()

        def rows_of(b, carry):
            rows = block(b)
            both = dot_f(hbuf[rows, :], wgu[s])
            gate, up = both[:, :LANES], both[:, LANES:]
            d_raw = dot_nt(rhs[0, rows, :], wdb[s, :, 0:256])
            for col in range(1, 4):
                d_raw = d_raw + dot_nt(rhs[col, rows, :], wdb[s, :, 256 * col : 256 * col + 256])
            lane = lax.broadcasted_iota(jnp.int32, (ROWS, LANES), 1)
            weight = jnp.sum(jnp.where(lane == e, slot_w[rows, :], 0.0), axis=1, keepdims=True)
            sigma = 1.0 / (1.0 + jnp.exp(-gate))
            silu = gate * sigma
            hidden = silu * up
            lhs[e, :, rows] = (hidden * weight).T.astype(bf16)
            inner = jnp.sum(hidden * d_raw, axis=1, keepdims=True)
            inner = jnp.where(weight > 0.0, inner, 0.0)
            acc[rows, 1024:1152] = jnp.where(lane == e, inner, acc[rows, 1024:1152])
            d_hidden = d_raw * weight
            d_gate = (d_hidden * up * sigma * (1.0 + gate * (1.0 - sigma))).astype(bf16)
            d_up = (d_hidden * silu).astype(bf16)
            rhs[4 + e, rows, 0:LANES] = d_gate
            rhs[4 + e, rows, LANES:] = d_up
            acc[rows, 0:1024] += dot_nt(rhs[4 + e, rows, :], wgu[s])
            return carry

        lax.fori_loop(0, 4, rows_of, 0)

    mine = pl.ds(pl.multiple_of(core * 512, 512), 512)
    other = pl.ds(pl.multiple_of((1 - core) * 512, 512), 512)

    def span(k):
        return pl.ds(0, 1152 if k == 0 else 1024)

    def sum_a(k):
        return remote(acc.at[other, span(k)], buf.at[pl.ds(0, 512), span(k)], s1s.at[k], s1r.at[k], core_mate, "tensor")

    def sum_b(k):
        return remote(acc.at[mine, span(k)], buf.at[pl.ds(512, 512), span(k)], s2s.at[k], s2r.at[k], x_mate, "tensor")

    def sum_c(k):
        part = acc.at[mine, span(k)]
        return remote(part, part, s3s.at[k], s3r.at[k], core_mate, "tensor")

    def add_in(k, at_row):
        def step(b, carry):
            rows = pl.ds(pl.multiple_of(core * 512 + b * 64, 64), 64)
            acc[rows, span(k)] += buf[pl.ds(pl.multiple_of(at_row + b * 64, 64), 64), span(k)]
            return carry

        lax.fori_loop(0, 8, step, 0)

    def sum_first(k):
        pl.semaphore_signal(ready1.at[k], inc=1, device_id={"tensor": core_mate}, device_id_type=MESH)
        pl.semaphore_signal(ready2.at[k], inc=1, device_id={"tensor": x_mate}, device_id_type=MESH)
        pl.semaphore_wait(ready1.at[k], 1)
        sum_a(k).start()

    def sum_second(k):
        sum_a(k).wait_recv()
        add_in(k, 0)
        sum_a(k).wait_send()
        pl.semaphore_signal(ready3.at[k], inc=1, device_id={"tensor": core_mate}, device_id_type=MESH)
        pl.semaphore_wait(ready2.at[k], 1)
        sum_b(k).start()

    def sum_third(k):
        sum_b(k).wait_recv()
        sum_b(k).wait_send()
        add_in(k, 512)
        pl.semaphore_wait(ready3.at[k], 1)
        sum_c(k).start()

    def sum_last(k):
        sum_c(k).wait_recv()
        sum_c(k).wait_send()

    def norm_back(values, scale_r, grads, which):
        inner = sum(
            jnp.sum(v * scale_r * (g * gain[which : which + 1, 256 * c : 256 * c + 256]), axis=1, keepdims=True)
            for c, (v, g) in enumerate(zip(values, grads))
        ) * (1.0 / 1024.0)
        outs = []
        for c, (v, g) in enumerate(zip(values, grads)):
            normed = v * scale_r
            row = 4 * which + c
            norms[row : row + 1, :] += jnp.sum(g * normed, axis=0, keepdims=True)
            outs.append(scale_r * (g * gain[which : which + 1, 256 * c : 256 * c + 256] - normed * inner))
        return outs

    def middle_rows(b):
        rows = block(b)

        values = [buf[rows, 256 * c : 256 * c + 256] for c in range(4)]
        grads = [acc[rows, 256 * c : 256 * c + 256] for c in range(4)]
        square = sum(jnp.sum(v * v, axis=1, keepdims=True) for v in values)
        scale_r = lax.rsqrt(square * (1.0 / 1024.0) + EPSILON)
        back = norm_back(values, scale_r, grads, 0)
        for c in range(4):
            total = rhs[c, rows, :].astype(f32) + back[c]
            acc[rows, 256 * c : 256 * c + 256] = total
            rhs[22 + c, rows, :] = total.astype(bf16)
        for h in range(4):
            d_head = dot_nt(rhs[22, rows, :], wdb[h, :, 0:256])
            for c in range(1, 4):
                d_head = d_head + dot_nt(rhs[22 + c, rows, :], wdb[h, :, 256 * c : 256 * c + 256])
            da2[h, rows, :] = d_head.astype(bf16)

    def turn_back(grad, cols):
        sine = grad * sin_t[:, cols]
        return grad * cos_t[:, cols] + jnp.concatenate([sine[32:], -sine[:32]], axis=0)

    def attend_back(h, qb):
        keys = ROWS * (qb + 1)
        rows = pl.ds(ROWS * qb, ROWS)
        q_rows = q2[h, rows, :]
        d_rows = da2[h, rows, :]
        exact = jnp.exp(masked_scores(h, qb) - lse[pl.ds(h, 1), rows])
        d_probs = dot_nt(v2[0:keys, :], d_rows)
        inner = jnp.sum(exact * d_probs, axis=0, keepdims=True)
        d_scores = (exact * (d_probs - inner)).astype(bf16)
        dk_acc[0:keys, :] += dot_f(d_scores, q_rows)
        dv_acc[0:keys, :] += dot_f(exact.astype(bf16), d_rows)
        k_head = kt2[pl.ds(pl.multiple_of((h // 2) * 64, 64), 64), 0:keys]
        d_q = dot_f(k_head, d_scores) * scaling
        buf[pl.ds(pl.multiple_of(h * 64, 64), 64), rows] = turn_back(d_q, rows)

    def turn_rows(b):
        rows = block(b)
        rhs[20, rows, :] = buf[0:256, rows].T.astype(bf16)
        d_k = (dk_acc[rows, :] * scaling).T
        d_k = jnp.concatenate([turn_back(d_k[:64], rows), turn_back(d_k[64:], rows)], axis=0)
        rhs[21, rows, 0:LANES] = d_k.T.astype(bf16)
        rhs[21, rows, LANES:] = dv_acc[rows, :].astype(bf16)

    def project_rows(b):
        rows = block(b)
        acc[rows, 0:1024] = dot_nt(rhs[20, rows, :], wgu[0]) + dot_nt(rhs[21, rows, :], wgu[1])

    def token_rows(b):
        rows = block(b)

        values = [hbuf[rows, 256 * c : 256 * c + 256].astype(f32) for c in range(4)]
        grads = [acc[rows, 256 * c : 256 * c + 256] for c in range(4)]
        square = sum(jnp.sum(v * v, axis=1, keepdims=True) for v in values)
        scale_r = lax.rsqrt(square * (1.0 / 1024.0) + EPSILON)
        back = norm_back(values, scale_r, grads, 1)
        for c in range(4):
            cols = slice(256 * c, 256 * c + 256)
            hbuf[rows, cols] = (buf[rows, cols] + back[c]).astype(bf16)

    def pair_load(pair, s):
        return local(w_down.at[pl.ds(2 * pair, 2)], wdb.at[pl.ds(2 * s, 2)], wsem.at[s, 2])

    def moe_pair(pair):
        s = pair % 2
        pair_load(pair, s).wait()

        @pl.when(pair + 1 < EXPERTS // 2)
        def _():
            pair_load(pair + 1, 1 - s).start()

        def rows_of(b, carry):
            rows = block(b)
            hidden = lhs[pl.ds(2 * pair, 2), :, rows].reshape(256, ROWS)
            down = wdb[pl.ds(2 * s, 2)].reshape(256, 1024)
            part = dot_tn(hidden, down)

            @pl.when(pair == 0)
            def _():
                acc[rows, 0:1024] = part

            @pl.when(pair > 0)
            def _():
                acc[rows, 0:1024] += part

            return carry

        lax.fori_loop(0, 4, rows_of, 0)

    def result_rows(b):
        rows = block(b)

        pos = lax.broadcasted_iota(jnp.int32, (ROWS, 1024), 0) + b * ROWS
        total = buf[rows, wide] + acc[rows, 0:1024]
        hbuf[rows, :] = jnp.where(pos < length[0], total, 0.0).astype(bf16)

    def halves_in(src):
        return [local(src, buf.at[:, wide], iosem.at[1])]

    tokens_in = [local(x_in, hbuf, iosem.at[3])]
    wo_load = [
        local(w_out.at[pl.ds(64 * h, 64)], wdb.at[h, pl.ds(64 * (h // 2), 64)], ld.at[8 + h]) for h in range(4)
    ]
    dots_out = [local(acc.at[:, pl.ds(1024, LANES)], o_dots, iosem.at[7])]
    dres_out = [local(acc.at[:, wide], s_dres, iosem.at[8])]
    tokens_out = [local(hbuf, o_tokens, iosem.at[9])]
    result_out = [local(hbuf, o_result, iosem.at[10])]

    def clear_wo():
        for h in range(4):
            wdb[h, 64 - 64 * (h // 2) : 128 - 64 * (h // 2), :] = jnp.zeros((64, 1024), bf16)

    def do_all(*steps):
        for step in steps:
            step()

    once = {
        T_SUM1: lambda: do_all(lambda: sum_first(0), clear_wo, lambda: start(tokens_in + wo_load + proj_load)),
        T_SUM1 + 2: lambda: do_all(lambda: sum_second(0), lambda: wait(tokens_in)),
        T_MID1 - 3: lambda: sum_third(0),
        T_MID1 - 1: lambda: do_all(
            lambda: sum_last(0), lambda: start(halves_in(s_resid) + dots_out), lambda: wait(wo_load)
        ),
        T_ATT: lambda: do_all(lambda: wait(dots_out), lambda: start(dres_out)),
        T_PROJ - 1: lambda: do_all(lambda: wait(dres_out), lambda: wait(proj_load)),
        T_SUM2: lambda: sum_first(1),
        T_SUM2 + 2: lambda: sum_second(1),
        T_TOK - 3: lambda: sum_third(1),
        T_TOK - 1: lambda: do_all(
            lambda: sum_last(1), lambda: start(halves_in(s_dres)), lambda: start([pair_load(0, 0)])
        ),
        T_MOE: lambda: start(tokens_out),
        T_SUM3: lambda: do_all(lambda: wait(tokens_out), lambda: sum_first(2)),
        T_SUM3 + 2: lambda: sum_second(2),
        T_RES - 3: lambda: sum_third(2),
        T_RES - 1: lambda: do_all(lambda: sum_last(2), lambda: start(halves_in(s_resid))),
        T_RES + 4: lambda: start(result_out),
        T_RES + 8: lambda: wait(result_out),
    }
    halves_wait = {T_MID1: s_resid, T_TOK: s_dres, T_RES: s_resid}

    def work(t):
        for when_t, fn in sorted(once.items()):
            pl.when(t == when_t)(fn)
        for when_t, src in halves_wait.items():
            pl.when(t == when_t)(lambda src=src: wait(halves_in(src)))
        for begin, count, fn in (
            (0, EXPERTS, expert),
            (T_MID1, 4, middle_rows),
            (T_TURN, 4, turn_rows),
            (T_PROJ, 4, project_rows),
            (T_TOK, 4, token_rows),
            (T_MOE, EXPERTS // 2, moe_pair),
            (T_RES, 4, result_rows),
        ):
            pl.when((t >= begin) & (t < begin + count))(lambda fn=fn, begin=begin: fn(t - begin))
        for qb in range(4):
            u = t - T_ATT
            pl.when((u >= 0) & (u < 16) & (u % 4 == qb))(lambda qb=qb, u=u: attend_back(u // 4, qb))

    own = pl.ds(pl.multiple_of(y * 64, 64), 64)
    oth = pl.ds(pl.multiple_of((1 - y) * 64, 64), 64)
    half = pl.ds(0, 64)

    def stage(c, t):
        p = z if c == 0 else last - z
        nxt, prv = (up_id, dn_id) if c == 0 else (dn_id, up_id)
        def at(delay, body):
            i = t - delay

            @pl.when((i >= 0) & (i < N_CLASS))
            def _():
                body(i, i % ring, i % 2 == 0)

        def ycopy_a(s):
            return remote(pbuf.at[c, s, oth], ybuf.at[c, s, half], ys.at[c, s], yr.at[c, s], mate)

        def ycopy_b(s):
            return remote(zbuf.at[c, s], ybuf.at[c, s], ys.at[c, s], yr.at[c, s], mate)

        def zcopy_a(s):
            return remote(zbuf.at[c, s, half], zbuf.at[c, s, half], zs.at[c, s], zr.at[c, s], nxt)

        def zcopy_b(s):
            return remote(zbuf.at[c, s], zbuf.at[c, s], zs.at[c, s], zr.at[c, s], nxt)

        def fcopy_a(s):
            return remote(pbuf.at[c, s, own], pbuf.at[c, s, own], fs.at[c, s], fr.at[c, s], prv)

        def fcopy_b(s):
            return remote(pbuf.at[c, s], pbuf.at[c, s], fs.at[c, s], fr.at[c, s], prv)

        def gcopy(s):
            return remote(pbuf.at[c, s, own], ybuf.at[c, s, pl.ds(64, 64)], gs.at[c, s], gr.at[c, s], mate)

        def first(i, s, is_a):
            g = 2 * i + c
            expert, part = g // 12, g % 12
            a = g - 192
            in_moe = g < 192
            l_moe = jnp.where(part < 4, expert, 12 + part)
            r_moe = jnp.where(part < 4, part, 4 + expert)
            l_att = jnp.where(a < 16, 24 + a % 8, 32 + (a - 16) // 4)
            r_att = jnp.where(a < 16, 20 + a // 8, 22 + (a - 16) % 4)
            li = jnp.where(in_moe, l_moe, l_att)
            ri = jnp.where(in_moe, r_moe, r_att)
            @pl.when(i < N_CLASS - 1)
            def _():
                pbuf[c, s] = dot_f(lhs[jnp.minimum(li, 33)], rhs[jnp.minimum(ri, 25)])

            @pl.when(i == N_CLASS - 1)
            def _():
                pbuf[c, s] = norms[...]

            @pl.when(is_a)
            def _():
                ycopy_a(s).start()

        def second(i, s, is_a):
            @pl.when(is_a)
            def _():
                ycopy_a(s).wait_recv()

                @pl.when(p > 0)
                def _():
                    zcopy_a(s).wait_recv()
                    zbuf[c, s, half] = zbuf[c, s, half] + (pbuf[c, s, own] + ybuf[c, s, half])

                @pl.when(p == 0)
                def _():
                    zbuf[c, s, half] = pbuf[c, s, own] + ybuf[c, s, half]

                @pl.when(p < last)
                def _():
                    zcopy_a(s).start()

                @pl.when(p == last)
                def _():
                    pbuf[c, s, own] = zbuf[c, s, half]
                    fcopy_a(s).start()
                    gcopy(s).start()

            @pl.when(jnp.logical_not(is_a))
            def _():
                @pl.when(p > 0)
                def _():
                    zcopy_b(s).wait_recv()
                    zbuf[c, s] = zbuf[c, s] + pbuf[c, s]

                @pl.when(p == 0)
                def _():
                    zbuf[c, s] = pbuf[c, s]

                @pl.when(p < last)
                def _():
                    zcopy_b(s).start()

                @pl.when(p == last)
                def _():
                    ycopy_b(s).start()

        def third(i, s, is_a):
            @pl.when(jnp.logical_not(is_a) & (p == last))
            def _():
                ycopy_b(s).wait_recv()
                pbuf[c, s] = zbuf[c, s] + ybuf[c, s]
                fcopy_b(s).start()

        def fourth(i, s, is_a):
            @pl.when(p < last)
            def _():
                @pl.when(is_a)
                def _():
                    fcopy_a(s).wait_recv()

                    @pl.when(p > 0)
                    def _():
                        fcopy_a(s).start()

                    gcopy(s).start()

                @pl.when(jnp.logical_not(is_a))
                def _():
                    fcopy_b(s).wait_recv()

                    @pl.when(p > 0)
                    def _():
                        fcopy_b(s).start()

        def store(s, dst0, dst1):
            pltpu.make_async_copy(pbuf.at[c, s, :, pl.ds(0, 128)], dst0, os0.at[c, s]).start()
            pltpu.make_async_copy(pbuf.at[c, s, :, pl.ds(128, 128)], dst1, os1.at[c, s]).start()

        def fifth(i, s, is_a):
            @pl.when(is_a)
            def _():
                gcopy(s).wait_recv()
                ycopy_a(s).wait_send()
                pbuf[c, s, oth] = ybuf[c, s, pl.ds(64, 64)]

            g = 2 * i + c
            expert, part = g // 12, g % 12
            a = g - 192

            @pl.when((g < 192) & (part < 4))
            def _():
                col = pl.multiple_of(part * 256, 128)
                col1 = pl.multiple_of(part * 256 + 128, 128)
                store(s, o_down.at[expert, :, pl.ds(col, 128)], o_down.at[expert, :, pl.ds(col1, 128)])

            @pl.when((g < 192) & (part >= 4))
            def _():
                rows = pl.ds(pl.multiple_of((part - 4) * 128, 128), 128)
                store(s, o_gate.at[expert, rows], o_up.at[expert, rows])

            @pl.when((g >= 192) & (a < 8))
            def _():
                rows = pl.ds(pl.multiple_of(a * 128, 128), 128)
                store(s, o_q.at[rows, pl.ds(0, 128)], o_q.at[rows, pl.ds(128, 128)])

            @pl.when((a >= 8) & (a < 16))
            def _():
                rows = pl.ds(pl.multiple_of((a - 8) * 128, 128), 128)
                store(s, o_k.at[rows], o_v.at[rows])

            @pl.when(i == N_CLASS - 1)
            def _():
                store(s, o_norm.at[c, :, pl.ds(0, 128)], o_norm.at[c, :, pl.ds(128, 128)])

            @pl.when((a >= 16) & (a < 24))
            def _():
                b = a - 16
                rows = pl.ds(pl.multiple_of((b // 4) * 128, 128), 128)
                col = pl.multiple_of((b % 4) * 256, 128)
                col1 = pl.multiple_of((b % 4) * 256 + 128, 128)
                store(s, o_out.at[rows, pl.ds(col, 128)], o_out.at[rows, pl.ds(col1, 128)])

        def sixth(i, s, is_a):
            pltpu.make_async_copy(pbuf.at[c, s, :, pl.ds(0, 128)], o_k.at[pl.ds(0, 128)], os0.at[c, s]).wait()
            pltpu.make_async_copy(pbuf.at[c, s, :, pl.ds(0, 128)], o_k.at[pl.ds(0, 128)], os1.at[c, s]).wait()

            @pl.when(is_a)
            def _():
                gcopy(s).wait_send()

                @pl.when(p < last)
                def _():
                    zcopy_a(s).wait_send()

                @pl.when(p > 0)
                def _():
                    fcopy_a(s).wait_send()

            @pl.when(jnp.logical_not(is_a))
            def _():
                @pl.when(p < last)
                def _():
                    zcopy_b(s).wait_send()

                @pl.when(p == last)
                def _():
                    ycopy_b(s).wait_send()

                @pl.when(p > 0)
                def _():
                    fcopy_b(s).wait_send()

        t2 = hop * (1 + p)
        t3 = hop * (2 + last)
        t4 = t3 + hop * (last - p)
        t5 = t4 + hop
        t6 = t5 + hop
        return [(0, first, at), (t2, second, at), (t3, third, at), (t4, fourth, at), (t5, fifth, at), (t6, sixth, at)]

    def body(t, carry):
        both = [stage(0, t), stage(1, t)]
        for k in (1, 2, 3, 4, 5, 0):
            if k == 0:
                work(t)
            for st in both:
                delay, fn, at = st[k]
                at(delay, fn)
        return carry

    total = N_CLASS + hop * (2 * last + 4) + 1
    lax.fori_loop(0, total, body, 0)


def run_layer(mesh, *operands):
    groups = mesh.shape["dp"]
    nz = 4 if groups % 8 == 0 else groups // 2
    last = nz - 1
    hop = HOP
    ring = hop * (2 * last + 4) + 2
    ring += ring % 2
    f32, bf16 = jnp.float32, jnp.bfloat16

    def out(shape, kind=f32):
        return jax.ShapeDtypeStruct(shape, kind)

    outs = [
        out((16, 1024, 128)), out((16, 1024, 128)), out((16, 128, 1024)),
        out((1024, 256)), out((1024, 128)), out((1024, 128)), out((256, 1024)), out((2, 128, 256)),
        out((1024, 1024), bf16), out((1024, 1024), bf16), out((1024, 128)),
        out((1024, 1024)), out((1024, 1024)),
    ]
    anywhere = pl.BlockSpec(memory_space=pl.ANY)
    dma = pltpu.SemaphoreType.DMA
    reg = pltpu.SemaphoreType.REGULAR
    vmem = pltpu.VMEM
    res = pl.pallas_call(
        functools.partial(layer_kernel, nz, hop, ring),
        out_shape=outs,
        in_specs=[pl.BlockSpec(memory_space=pltpu.SMEM)] + [anywhere] * (len(operands) - 1),
        out_specs=[anywhere] * len(outs),
        scratch_shapes=[
            vmem((34, 128, 1024), bf16), vmem((26, 1024, 256), bf16),
            vmem((2, ring, 128, 256), f32), vmem((2, ring, 128, 256), f32), vmem((2, ring, 128, 256), f32),
            vmem((1024, 1152), f32), vmem((1024, 1152), f32),
            vmem((1024, 1024), bf16), vmem((2, 1024, 256), bf16), vmem((4, 128, 1024), bf16),
            vmem((4, 1024, 128), bf16), vmem((1024, 128), bf16), vmem((1024, 128), bf16),
            vmem((128, 1024), bf16), vmem((128, 1024), bf16),
            vmem((8, 1024), f32), vmem((64, 1024), f32), vmem((64, 1024), f32),
            vmem((4, 1024, 128), bf16), vmem((1024, 128), f32), vmem((1024, 128), f32),
            vmem((1024, 128), f32), vmem((8, 1024), f32), vmem((128, 256), f32),
            vmem((1024, 8), jnp.int32), vmem((1024, 8), f32),
            dma((18,)), dma((2, 3)), dma((11,)),
        ]
        + [dma((2, ring))] * 10
        + [dma((4,))] * 6
        + [dma((3,))] * 2
        + [dma((3,))] * 6
        + [reg((3,))] * 3,
        compiler_params=pltpu.CompilerParams(
            collective_id=0, has_side_effects=True, vmem_limit_bytes=62 * 2**20
        ),
    )(*operands)
    sums, rest = tuple(res[:8]), res[8:11]
    if groups > 2 * nz:
        same = [
            [2 * nz * block + place for block in range(groups // (2 * nz))] for place in range(2 * nz)
        ]
        sums = lax.psum(sums, "dp", axis_index_groups=same)
    return sums, rest


def per_device(
    mesh,
    tokens,
    lengths,
    chosen,
    gate_values,
    cotangent,
    norm_attn,
    w_query,
    w_key,
    w_value,
    w_out,
    norm_moe,
    w_gate,
    w_up,
    w_down,
):
    seq_len = tokens.shape[0] // lengths.shape[0]
    cosine, sine = rope_tables(seq_len, HEAD_DIM)
    sums, (result, grad_tokens, dots) = run_layer(
        mesh,
        lengths,
        tokens,
        cotangent,
        chosen,
        gate_values,
        norm_attn[None, :],
        norm_moe[None, :],
        w_gate,
        w_up,
        w_down,
        cosine,
        sine,
        w_out,
        w_query,
        w_key,
        w_value,
    )
    grad_gate, grad_up, grad_down, grad_query, grad_key, grad_value, grad_out, norm_rows = sums
    picked = chosen[:, :, None] == jnp.arange(EXPERTS, dtype=jnp.int32)[None, None, :]
    d_gates = jnp.sum(jnp.where(picked, dots[:, None, :EXPERTS], 0.0), axis=-1)
    return (
        result,
        grad_tokens,
        d_gates,
        norm_rows[0, 4:8].reshape(-1),
        grad_query,
        grad_key,
        grad_value,
        grad_out,
        norm_rows[0, 0:4].reshape(-1),
        grad_gate,
        grad_up,
        grad_down,
    )


def solution(mesh):
    placed = (
        P("dp", None),
        P("dp"),
        P("dp", None),
        P("dp", None),
        P("dp", None),
        P(),
        P(None, "tensor"),
        P(None, "tensor"),
        P(None, "tensor"),
        P("tensor", None),
        P(),
        P(None, None, "tensor"),
        P(None, None, "tensor"),
        P(None, "tensor", None),
    )
    return jax.shard_map(
        functools.partial(per_device, mesh),
        mesh=mesh,
        in_specs=placed,
        out_specs=(
            P("dp", None),
            P("dp", None),
            P("dp", None),
            P(),
            P(None, "tensor"),
            P(None, "tensor"),
            P(None, "tensor"),
            P("tensor", None),
            P(),
            P(None, None, "tensor"),
            P(None, None, "tensor"),
            P(None, "tensor", None),
        ),
        check_vma=False,
    )
```

```python
import functools
import math

import jax
import jax.numpy as jnp
import numpy as np
from jax import lax
from jax.experimental import pallas as pl
from jax.experimental.pallas import tpu as pltpu
from jax.sharding import PartitionSpec as P

MESH = pl.DeviceIdType.MESH

HEAD_DIM = 64
TOP_K = 8
EXPERTS = 16


EPSILON = 1e-05
THETA = 10000.0
NEGATIVE = -1e30


def dot_f(left, right):
    return jnp.dot(left, right, preferred_element_type=jnp.float32)


def rope_tables(positions, width):
    half_w = width // 2
    freqs = THETA ** (-np.arange(half_w, dtype=np.float64) * 2.0 / width)
    angles = np.concatenate([freqs, freqs])[:, None] * np.arange(positions, dtype=np.float64)[None, :]
    return (np.cos(angles).astype(np.float32), np.sin(angles).astype(np.float32))


LANES = 128
ROWS = 256
N_CLASS = 109
HOP = 2
SPARE = 5
T_SUM1 = 16
T_MID1 = 33
T_ATT = 37
T_TURN = 53
T_PROJ = 57
T_SUM2 = 61
T_TOK = 78
T_MOE = 82
T_SUM3 = 90
T_RES = 107


def dot_nt(left, right):
    return lax.dot_general(
        left, right, (((1,), (1,)), ((), ())), preferred_element_type=jnp.float32
    )


def dot_tn(left, right):
    return lax.dot_general(
        left, right, (((0,), (0,)), ((), ())), preferred_element_type=jnp.float32
    )


def layer_kernel(
    nz, hop, ring,
    length, x_in, d_out, chosen, gates, gain_attn, gain_moe, w_gate, w_up, w_down,
    cos_in, sin_in, w_out, w_query, w_key, w_value,
    o_gate, o_up, o_down, o_q, o_k, o_v, o_out, o_norm, o_result, o_tokens, o_dots, s_resid, s_dres,
    lhs, rhs, pbuf, zbuf, ybuf, xbuf, acc, buf, hbuf, wgu, wdb, q2, k2, v2, kt2, vt2, lse, cos_t, sin_t,
    da2, dk_acc, dv_acc, slot_w, gain, norms, picks, pick_w,
    ld, wsem, iosem, ys, yr, zs, zr, fs, fr, gs, gr, os0, os1, xr,
    cs_c, cr_c, cs_x, cr_x, cs_f, cr_f, ws, wr, s1s, s1r, s2s, s2r, s3s, s3r, ready1, ready2, ready3,
):
    f32, bf16 = jnp.float32, jnp.bfloat16
    dp = lax.axis_index("dp")
    tensor = lax.axis_index("tensor")
    base = dp - dp % (2 * nz)
    z, y = (dp % (2 * nz)) // 2, dp % 2
    last = nz - 1
    mate = base + z * 2 + (1 - y)
    up_id = base + jnp.minimum(z + 1, last) * 2 + y
    dn_id = base + jnp.maximum(z - 1, 0) * 2 + y
    core = tensor % 2
    core_mate = tensor - core + (1 - core)
    x_mate = (tensor + 2) % 4

    def local(src, dst, sem):
        return pltpu.make_async_copy(src, dst, sem)

    def remote(src, dst, ssem, rsem, dev, axis="dp"):
        return pltpu.make_async_remote_copy(
            src_ref=src, dst_ref=dst, send_sem=ssem, recv_sem=rsem,
            device_id={axis: dev}, device_id_type=MESH,
        )

    def block(b, size=ROWS):
        return pl.ds(pl.multiple_of(b * size, size), size)

    bar = pltpu.get_barrier_semaphore()
    for axis, dev in (("dp", mate), ("tensor", core_mate), ("tensor", x_mate)):
        pl.semaphore_signal(bar, inc=1, device_id={axis: dev}, device_id_type=MESH)

    @pl.when(z < last)
    def _():
        pl.semaphore_signal(bar, inc=1, device_id={"dp": up_id}, device_id_type=MESH)

    @pl.when(z > 0)
    def _():
        pl.semaphore_signal(bar, inc=1, device_id={"dp": dn_id}, device_id_type=MESH)

    wide = pl.ds(0, 1024)
    share = block(tensor)
    token_load = [
        local(x_in, hbuf, ld.at[0]),
        local(gain_attn, gain.at[pl.ds(1, 1)], ld.at[1]),
        local(gain_moe, gain.at[pl.ds(0, 1)], ld.at[2]),
        local(cos_in, cos_t, ld.at[3]),
        local(sin_in, sin_t, ld.at[4]),
    ]
    proj_load = [
        local(w_query, wgu.at[0], ld.at[5]),
        local(w_key, wgu.at[1, :, pl.ds(0, LANES)], ld.at[6]),
        local(w_value, wgu.at[1, :, pl.ds(LANES, LANES)], ld.at[7]),
    ]
    out_load = [local(w_out.at[:, block(c)], rhs.at[22 + c, share], ld.at[8 + c]) for c in range(4)]
    late_load = [local(d_out.at[:, block(c)], rhs.at[c], ld.at[12 + c]) for c in range(4)] + [
        local(chosen, picks, ld.at[16]),
        local(gates, pick_w, ld.at[17]),
    ]

    def expert_load(e, s):
        return [
            local(w_gate.at[e], wgu.at[s, :, pl.ds(0, LANES)], wsem.at[s, 0]),
            local(w_up.at[e], wgu.at[s, :, pl.ds(LANES, LANES)], wsem.at[s, 1]),
            local(w_down.at[e], wdb.at[s], wsem.at[s, 2]),
        ]

    def start(copies):
        for copy in copies:
            copy.start()

    def wait(copies):
        for copy in copies:
            copy.wait()

    start(out_load + token_load + proj_load + late_load)
    pl.semaphore_wait(bar, 3 + (z < last).astype(jnp.int32) + (z > 0).astype(jnp.int32))

    part_w = buf.at[share, wide]
    w_x = remote(part_w, part_w, ws.at[0], wr.at[0], x_mate, "tensor")
    w_c = remote(part_w, part_w, ws.at[1], wr.at[1], core_mate, "tensor")
    part_f = buf.at[block(x_mate), wide]
    w_f = remote(part_f, part_f, ws.at[2], wr.at[2], core_mate, "tensor")
    wait(out_load)
    for c in range(4):
        buf[share, 256 * c : 256 * c + 256] = rhs[22 + c, share, :].astype(f32)
    w_x.start()
    w_c.start()

    def gather_x(b):
        return remote(
            acc.at[block(b), share], acc.at[block(b), share], cs_x.at[b], cr_x.at[b], x_mate, "tensor"
        )

    def gather_c(b):
        return remote(
            acc.at[block(b), share], acc.at[block(b), share], cs_c.at[b], cr_c.at[b], core_mate, "tensor"
        )

    def gather_f(b):
        part = acc.at[block(b), block(x_mate)]
        return remote(part, part, cs_f.at[b], cr_f.at[b], core_mate, "tensor")

    def rotate_t(values, cols):
        turned = jnp.concatenate([-values[32:], values[:32]], axis=0)
        return values * cos_t[:, cols] + turned * sin_t[:, cols]

    def head_rows(b, carry):
        rows = block(b)
        vals = [hbuf[rows, 256 * col : 256 * col + 256].astype(f32) for col in range(4)]
        square = sum(jnp.sum(v * v, axis=1, keepdims=True) for v in vals)
        scale_r = lax.rsqrt(square * (1.0 / 1024.0) + EPSILON)
        query, key_value = 0.0, 0.0
        for col in range(4):
            normed = vals[col] * scale_r * gain[1:2, 256 * col : 256 * col + 256]
            for half_c in range(2):
                lhs[24 + 2 * col + half_c, :, rows] = normed[:, 128 * half_c : 128 * half_c + 128].T.astype(bf16)
            normed = normed.astype(bf16)
            query = query + dot_f(normed, wgu[0, 256 * col : 256 * col + 256, :])
            key_value = key_value + dot_f(normed, wgu[1, 256 * col : 256 * col + 256, :])
        query = query.T
        nothing = jnp.zeros((64, ROWS), f32)
        for h in range(4):
            turned = rotate_t(query[64 * h : 64 * h + 64], rows)
            both = [turned, nothing] if h < 2 else [nothing, turned]
            q2[h, rows, :] = jnp.concatenate(both, axis=0).T.astype(bf16)
        key = key_value[:, :LANES].T
        key = jnp.concatenate([rotate_t(key[:64], rows), rotate_t(key[64:], rows)], axis=0)
        kt2[:, rows] = key.astype(bf16)
        k2[rows, :] = key.T.astype(bf16)
        value = key_value[:, LANES:]
        v2[rows, :] = value.astype(bf16)
        vt2[:, rows] = value.T.astype(bf16)
        return carry

    scaling = 1.0 / math.sqrt(HEAD_DIM)

    def masked_scores(h, qb):
        keys = ROWS * (qb + 1)
        rows = pl.ds(ROWS * qb, ROWS)
        scores = dot_nt(k2[0:keys, :], q2[h, rows, :]) * scaling
        k_pos = lax.broadcasted_iota(jnp.int32, (keys, ROWS), 0)
        q_pos = lax.broadcasted_iota(jnp.int32, (keys, ROWS), 1) + ROWS * qb
        allowed = (k_pos <= q_pos) & (k_pos < length[0])
        return jnp.where(allowed, scores, NEGATIVE)

    def attend(qb):
        keys = ROWS * (qb + 1)
        rows = pl.ds(ROWS * qb, ROWS)

        def one_head(h, carry):
            scores = masked_scores(h, qb)
            top_s = jnp.max(scores, axis=0, keepdims=True)
            expo = jnp.exp(scores - top_s)
            total = jnp.sum(expo, axis=0, keepdims=True)
            probs = (expo / total).astype(bf16)
            lse[pl.ds(h, 1), rows] = top_s + jnp.log(total)
            v_head = vt2[pl.ds(pl.multiple_of((h // 2) * 64, 64), 64), 0:keys]
            lhs[32 + h // 2, pl.ds(pl.multiple_of((h % 2) * 64, 64), 64), rows] = dot_f(v_head, probs).astype(bf16)
            return carry

        lax.fori_loop(0, 4, one_head, 0)
        for half_c in range(2):
            own_c = pl.ds(pl.multiple_of(tensor * 256 + half_c * 128, 128), 128)
            acc[rows, own_c] = lhs[32 + half_c, :, rows].astype(f32).T
        gather_x(qb).start()
        gather_c(qb).start()

    wait(token_load + proj_load)
    lax.fori_loop(0, 4, head_rows, 0)
    start(expert_load(0, 0))
    for qb in range(4):
        attend(qb)

    wait(late_load)

    expert_id = lax.broadcasted_iota(jnp.int32, (EXPERTS, 1024), 0)
    alive = lax.broadcasted_iota(jnp.int32, (EXPERTS, 1024), 1) < length[0]
    hits = jnp.zeros((EXPERTS, 1024), f32)
    weight = jnp.zeros((EXPERTS, 1024), f32)
    for k in range(TOP_K):
        same = (picks[k : k + 1, :] == expert_id) & alive
        hits = jnp.where(same, 1.0, hits)
        weight = jnp.where(same, pick_w[k : k + 1, :], weight)
    hits = hits.astype(bf16)
    limit = ((5 * TOP_K * length[0] + 4 * EXPERTS - 1) // (4 * EXPERTS)).astype(f32)
    for b in range(4):
        rows = pl.ds(ROWS * b, ROWS)
        token = lax.broadcasted_iota(jnp.int32, (1024, ROWS), 1) + ROWS * b
        earlier = jnp.where(lax.broadcasted_iota(jnp.int32, (1024, ROWS), 0) < token, 1.0, 0.0).astype(bf16)
        places = dot_f(hits, earlier)
        kept = jnp.where(places < limit, weight[:, ROWS * b : ROWS * b + ROWS], 0.0)
        slot_w[rows, :] = jnp.concatenate([kept, jnp.zeros((LANES - EXPERTS, ROWS), f32)], axis=0).T

    def mask_rows(b, carry):
        rows = block(b)
        pos = lax.broadcasted_iota(jnp.int32, (ROWS, 256), 0) + b * ROWS
        for c in range(4):
            rhs[c, rows, :] = jnp.where(pos < length[0], rhs[c, rows, :].astype(f32), 0.0).astype(bf16)
        return carry

    lax.fori_loop(0, 4, mask_rows, 0)

    w_x.wait_recv()
    w_f.start()
    w_c.wait_recv()
    w_f.wait_recv()

    def cast_out(b, carry):
        for c in range(4):
            rhs[22 + c, block(b, 64), :] = buf[block(b, 64), 256 * c : 256 * c + 256].astype(bf16)
        return carry

    lax.fori_loop(0, 16, cast_out, 0)

    def forward_rows(b, carry):
        rows = block(b)
        for k in range(4):
            part = acc[rows, 256 * k : 256 * k + 256].astype(bf16)
            if k == 0:
                sums = [
                    hbuf[rows, 256 * col : 256 * col + 256].astype(f32) + dot_f(part, rhs[22 + col, 0:256, :])
                    for col in range(4)
                ]
            else:
                sums = [
                    sums[col] + dot_f(part, rhs[22 + col, 256 * k : 256 * k + 256, :]) for col in range(4)
                ]
        square = sum(jnp.sum(v * v, axis=1, keepdims=True) for v in sums)
        scale_r = lax.rsqrt(square * (1.0 / 1024.0) + EPSILON)
        for col in range(4):
            acc[rows, 256 * col : 256 * col + 256] = sums[col]
            normed = sums[col] * scale_r * gain[0:1, 256 * col : 256 * col + 256]
            hbuf[rows, 256 * col : 256 * col + 256] = normed.astype(bf16)
            for half_c in range(2):
                lhs[16 + 2 * col + half_c, :, rows] = normed[:, 128 * half_c : 128 * half_c + 128].T.astype(bf16)
        return carry

    for b in range(4):
        gather_x(b).wait_recv()
        gather_f(b).start()
    for b in range(4):
        gather_c(b).wait_recv()
        gather_f(b).wait_recv()
        gather_f(b).wait_send()
        gather_x(b).wait_send()
        gather_c(b).wait_send()
        forward_rows(b, 0)
    w_x.wait_send()
    w_c.wait_send()
    w_f.wait_send()
    keep = local(acc.at[:, wide], s_resid, iosem.at[0])
    keep.start()
    keep.wait()

    def clear(b, carry):
        acc[block(b, 64), :] = jnp.zeros((64, 1152), f32)
        return carry

    lax.fori_loop(0, 16, clear, 0)
    dk_acc[...] = jnp.zeros_like(dk_acc)
    dv_acc[...] = jnp.zeros_like(dv_acc)
    norms[...] = jnp.zeros_like(norms)

    def expert(e):
        s = e % 2
        for copy in expert_load(e, s):
            copy.wait()

        @pl.when(e + 1 < EXPERTS)
        def _():
            for copy in expert_load(e + 1, 1 - s):
                copy.start()

        def rows_of(b, carry):
            rows = block(b)
            both = dot_f(hbuf[rows, :], wgu[s])
            gate, up = both[:, :LANES], both[:, LANES:]
            d_raw = dot_nt(rhs[0, rows, :], wdb[s, :, 0:256])
            for col in range(1, 4):
                d_raw = d_raw + dot_nt(rhs[col, rows, :], wdb[s, :, 256 * col : 256 * col + 256])
            lane = lax.broadcasted_iota(jnp.int32, (ROWS, LANES), 1)
            weight = jnp.sum(jnp.where(lane == e, slot_w[rows, :], 0.0), axis=1, keepdims=True)
            sigma = 1.0 / (1.0 + jnp.exp(-gate))
            silu = gate * sigma
            hidden = silu * up
            lhs[e, :, rows] = (hidden * weight).T.astype(bf16)
            inner = jnp.sum(hidden * d_raw, axis=1, keepdims=True)
            inner = jnp.where(weight > 0.0, inner, 0.0)
            acc[rows, 1024:1152] = jnp.where(lane == e, inner, acc[rows, 1024:1152])
            d_hidden = d_raw * weight
            d_gate = (d_hidden * up * sigma * (1.0 + gate * (1.0 - sigma))).astype(bf16)
            d_up = (d_hidden * silu).astype(bf16)
            rhs[4 + e, rows, 0:LANES] = d_gate
            rhs[4 + e, rows, LANES:] = d_up
            acc[rows, 0:1024] += dot_nt(rhs[4 + e, rows, :], wgu[s])
            return carry

        lax.fori_loop(0, 4, rows_of, 0)

    mine = pl.ds(pl.multiple_of(core * 512, 512), 512)
    other = pl.ds(pl.multiple_of((1 - core) * 512, 512), 512)

    def span(k):
        return pl.ds(0, 1152 if k == 0 else 1024)

    def sum_a(k):
        return remote(acc.at[other, span(k)], buf.at[pl.ds(0, 512), span(k)], s1s.at[k], s1r.at[k], core_mate, "tensor")

    def sum_b(k):
        return remote(acc.at[mine, span(k)], buf.at[pl.ds(512, 512), span(k)], s2s.at[k], s2r.at[k], x_mate, "tensor")

    def sum_c(k):
        part = acc.at[mine, span(k)]
        return remote(part, part, s3s.at[k], s3r.at[k], core_mate, "tensor")

    def add_in(k, at_row):
        def step(b, carry):
            rows = pl.ds(pl.multiple_of(core * 512 + b * 64, 64), 64)
            acc[rows, span(k)] += buf[pl.ds(pl.multiple_of(at_row + b * 64, 64), 64), span(k)]
            return carry

        lax.fori_loop(0, 8, step, 0)

    def sum_first(k):
        pl.semaphore_signal(ready1.at[k], inc=1, device_id={"tensor": core_mate}, device_id_type=MESH)
        pl.semaphore_signal(ready2.at[k], inc=1, device_id={"tensor": x_mate}, device_id_type=MESH)
        pl.semaphore_wait(ready1.at[k], 1)
        sum_a(k).start()

    def sum_second(k):
        sum_a(k).wait_recv()
        add_in(k, 0)
        sum_a(k).wait_send()
        pl.semaphore_signal(ready3.at[k], inc=1, device_id={"tensor": core_mate}, device_id_type=MESH)
        pl.semaphore_wait(ready2.at[k], 1)
        sum_b(k).start()

    def sum_third(k):
        sum_b(k).wait_recv()
        sum_b(k).wait_send()
        add_in(k, 512)
        pl.semaphore_wait(ready3.at[k], 1)
        sum_c(k).start()

    def sum_last(k):
        sum_c(k).wait_recv()
        sum_c(k).wait_send()

    def norm_back(values, scale_r, grads, which):
        inner = sum(
            jnp.sum(v * scale_r * (g * gain[which : which + 1, 256 * c : 256 * c + 256]), axis=1, keepdims=True)
            for c, (v, g) in enumerate(zip(values, grads))
        ) * (1.0 / 1024.0)
        outs = []
        for c, (v, g) in enumerate(zip(values, grads)):
            normed = v * scale_r
            row = 4 * which + c
            norms[row : row + 1, :] += jnp.sum(g * normed, axis=0, keepdims=True)
            outs.append(scale_r * (g * gain[which : which + 1, 256 * c : 256 * c + 256] - normed * inner))
        return outs

    def middle_rows(b):
        rows = block(b)

        values = [buf[rows, 256 * c : 256 * c + 256] for c in range(4)]
        grads = [acc[rows, 256 * c : 256 * c + 256] for c in range(4)]
        square = sum(jnp.sum(v * v, axis=1, keepdims=True) for v in values)
        scale_r = lax.rsqrt(square * (1.0 / 1024.0) + EPSILON)
        back = norm_back(values, scale_r, grads, 0)
        for c in range(4):
            total = rhs[c, rows, :].astype(f32) + back[c]
            acc[rows, 256 * c : 256 * c + 256] = total
            rhs[22 + c, rows, :] = total.astype(bf16)
        for h in range(4):
            d_head = dot_nt(rhs[22, rows, :], wdb[h, :, 0:256])
            for c in range(1, 4):
                d_head = d_head + dot_nt(rhs[22 + c, rows, :], wdb[h, :, 256 * c : 256 * c + 256])
            da2[h, rows, :] = d_head.astype(bf16)

    def turn_back(grad, cols):
        sine = grad * sin_t[:, cols]
        return grad * cos_t[:, cols] + jnp.concatenate([sine[32:], -sine[:32]], axis=0)

    def attend_back(h, qb):
        keys = ROWS * (qb + 1)
        rows = pl.ds(ROWS * qb, ROWS)
        q_rows = q2[h, rows, :]
        d_rows = da2[h, rows, :]
        exact = jnp.exp(masked_scores(h, qb) - lse[pl.ds(h, 1), rows])
        d_probs = dot_nt(v2[0:keys, :], d_rows)
        inner = jnp.sum(exact * d_probs, axis=0, keepdims=True)
        d_scores = (exact * (d_probs - inner)).astype(bf16)
        dk_acc[0:keys, :] += dot_f(d_scores, q_rows)
        dv_acc[0:keys, :] += dot_f(exact.astype(bf16), d_rows)
        k_head = kt2[pl.ds(pl.multiple_of((h // 2) * 64, 64), 64), 0:keys]
        d_q = dot_f(k_head, d_scores) * scaling
        buf[pl.ds(pl.multiple_of(h * 64, 64), 64), rows] = turn_back(d_q, rows)

    def turn_rows(b):
        rows = block(b)
        rhs[20, rows, :] = buf[0:256, rows].T.astype(bf16)
        d_k = (dk_acc[rows, :] * scaling).T
        d_k = jnp.concatenate([turn_back(d_k[:64], rows), turn_back(d_k[64:], rows)], axis=0)
        rhs[21, rows, 0:LANES] = d_k.T.astype(bf16)
        rhs[21, rows, LANES:] = dv_acc[rows, :].astype(bf16)

    def project_rows(b):
        rows = block(b)
        acc[rows, 0:1024] = dot_nt(rhs[20, rows, :], wgu[0]) + dot_nt(rhs[21, rows, :], wgu[1])

    def token_rows(b):
        rows = block(b)

        values = [hbuf[rows, 256 * c : 256 * c + 256].astype(f32) for c in range(4)]
        grads = [acc[rows, 256 * c : 256 * c + 256] for c in range(4)]
        square = sum(jnp.sum(v * v, axis=1, keepdims=True) for v in values)
        scale_r = lax.rsqrt(square * (1.0 / 1024.0) + EPSILON)
        back = norm_back(values, scale_r, grads, 1)
        for c in range(4):
            cols = slice(256 * c, 256 * c + 256)
            hbuf[rows, cols] = (buf[rows, cols] + back[c]).astype(bf16)

    def pair_load(pair, s):
        return local(w_down.at[pl.ds(2 * pair, 2)], wdb.at[pl.ds(2 * s, 2)], wsem.at[s, 2])

    def moe_pair(pair):
        s = pair % 2
        pair_load(pair, s).wait()

        @pl.when(pair + 1 < EXPERTS // 2)
        def _():
            pair_load(pair + 1, 1 - s).start()

        def rows_of(b, carry):
            rows = block(b)
            hidden = lhs[pl.ds(2 * pair, 2), :, rows].reshape(256, ROWS)
            down = wdb[pl.ds(2 * s, 2)].reshape(256, 1024)
            part = dot_tn(hidden, down)

            @pl.when(pair == 0)
            def _():
                acc[rows, 0:1024] = part

            @pl.when(pair > 0)
            def _():
                acc[rows, 0:1024] += part

            return carry

        lax.fori_loop(0, 4, rows_of, 0)

    def result_rows(b):
        rows = block(b)

        pos = lax.broadcasted_iota(jnp.int32, (ROWS, 1024), 0) + b * ROWS
        total = buf[rows, wide] + acc[rows, 0:1024]
        hbuf[rows, :] = jnp.where(pos < length[0], total, 0.0).astype(bf16)

    def halves_in(src):
        return [local(src, buf.at[:, wide], iosem.at[1])]

    tokens_in = [local(x_in, hbuf, iosem.at[3])]
    wo_load = [
        local(w_out.at[pl.ds(64 * h, 64)], wdb.at[h, pl.ds(64 * (h // 2), 64)], ld.at[8 + h]) for h in range(4)
    ]
    dots_out = [local(acc.at[:, pl.ds(1024, LANES)], o_dots, iosem.at[7])]
    dres_out = [local(acc.at[:, wide], s_dres, iosem.at[8])]
    tokens_out = [local(hbuf, o_tokens, iosem.at[9])]
    result_out = [local(hbuf, o_result, iosem.at[10])]

    def clear_wo():
        for h in range(4):
            wdb[h, 64 - 64 * (h // 2) : 128 - 64 * (h // 2), :] = jnp.zeros((64, 1024), bf16)

    def do_all(*steps):
        for step in steps:
            step()

    once = {
        T_SUM1: lambda: do_all(lambda: sum_first(0), clear_wo, lambda: start(tokens_in + wo_load + proj_load)),
        T_SUM1 + 2: lambda: do_all(lambda: sum_second(0), lambda: wait(tokens_in)),
        T_MID1 - 3: lambda: sum_third(0),
        T_MID1 - 1: lambda: do_all(
            lambda: sum_last(0), lambda: start(halves_in(s_resid) + dots_out), lambda: wait(wo_load)
        ),
        T_ATT: lambda: do_all(lambda: wait(dots_out), lambda: start(dres_out)),
        T_PROJ - 1: lambda: do_all(lambda: wait(dres_out), lambda: wait(proj_load)),
        T_SUM2: lambda: sum_first(1),
        T_SUM2 + 2: lambda: sum_second(1),
        T_TOK - 3: lambda: sum_third(1),
        T_TOK - 1: lambda: do_all(
            lambda: sum_last(1), lambda: start(halves_in(s_dres)), lambda: start([pair_load(0, 0)])
        ),
        T_MOE: lambda: start(tokens_out),
        T_SUM3: lambda: do_all(lambda: wait(tokens_out), lambda: sum_first(2)),
        T_SUM3 + 2: lambda: sum_second(2),
        T_RES - 3: lambda: sum_third(2),
        T_RES - 1: lambda: do_all(lambda: sum_last(2), lambda: start(halves_in(s_resid))),
        T_RES + 4: lambda: start(result_out),
        T_RES + 8: lambda: wait(result_out),
    }
    halves_wait = {T_MID1: s_resid, T_TOK: s_dres, T_RES: s_resid}

    def work(t):
        for when_t, fn in sorted(once.items()):
            pl.when(t == when_t)(fn)
        for when_t, src in halves_wait.items():
            pl.when(t == when_t)(lambda src=src: wait(halves_in(src)))
        for begin, count, fn in (
            (0, EXPERTS, expert),
            (T_MID1, 4, middle_rows),
            (T_TURN, 4, turn_rows),
            (T_PROJ, 4, project_rows),
            (T_TOK, 4, token_rows),
            (T_MOE, EXPERTS // 2, moe_pair),
            (T_RES, 4, result_rows),
        ):
            pl.when((t >= begin) & (t < begin + count))(lambda fn=fn, begin=begin: fn(t - begin))
        for qb in range(4):
            u = t - T_ATT
            pl.when((u >= 0) & (u < 16) & (u % 4 == qb))(lambda qb=qb, u=u: attend_back(u // 4, qb))

    own = pl.ds(pl.multiple_of(y * 64, 64), 64)
    oth = pl.ds(pl.multiple_of((1 - y) * 64, 64), 64)
    half = pl.ds(0, 64)

    def stage(c, t):
        p = z if c == 0 else last - z
        nxt, prv = (up_id, dn_id) if c == 0 else (dn_id, up_id)
        def at(delay, body):
            i = t - delay

            @pl.when((i >= 0) & (i < N_CLASS))
            def _():
                body(i, i % ring, i % 5)

        def ycopy_a(s):
            return remote(pbuf.at[c, s, oth], ybuf.at[c, s, half], ys.at[c, s], yr.at[c, s], mate)

        def ycopy_b(s):
            return remote(zbuf.at[c, s], ybuf.at[c, s], ys.at[c, s], yr.at[c, s], mate)

        def ycopy_c(s, k):
            return remote(zbuf.at[c, s], xbuf.at[c, k], ys.at[c, s], xr.at[c, k], mate)

        def leaf_copy(s):
            return remote(pbuf.at[c, s], ybuf.at[c, s], ys.at[c, s], yr.at[c, s], prv)

        def fcopy_c(s):
            return remote(pbuf.at[c, s], zbuf.at[c, s], gs.at[c, s], fr.at[c, s], nxt)

        def zcopy_a(s):
            return remote(zbuf.at[c, s, half], zbuf.at[c, s, half], zs.at[c, s], zr.at[c, s], nxt)

        def zcopy_b(s):
            return remote(zbuf.at[c, s], zbuf.at[c, s], zs.at[c, s], zr.at[c, s], nxt)

        def fcopy_a(s):
            return remote(pbuf.at[c, s, own], pbuf.at[c, s, own], fs.at[c, s], fr.at[c, s], prv)

        def fcopy_b(s):
            return remote(pbuf.at[c, s], pbuf.at[c, s], fs.at[c, s], fr.at[c, s], prv)

        def gcopy(s):
            return remote(pbuf.at[c, s, own], ybuf.at[c, s, pl.ds(64, 64)], gs.at[c, s], gr.at[c, s], mate)

        def first(i, s, kind):
            g = 2 * i + c
            expert, part = g // 12, g % 12
            a = g - 192
            in_moe = g < 192
            l_moe = jnp.where(part < 4, expert, 12 + part)
            r_moe = jnp.where(part < 4, part, 4 + expert)
            l_att = jnp.where(a < 16, 24 + a % 8, 32 + (a - 16) // 4)
            r_att = jnp.where(a < 16, 20 + a // 8, 22 + (a - 16) % 4)
            li = jnp.where(in_moe, l_moe, l_att)
            ri = jnp.where(in_moe, r_moe, r_att)
            @pl.when(i < N_CLASS - 1)
            def _():
                pbuf[c, s] = dot_f(lhs[jnp.minimum(li, 33)], rhs[jnp.minimum(ri, 25)])

            @pl.when(i == N_CLASS - 1)
            def _():
                pbuf[c, s] = norms[...]

            @pl.when(kind % 2 == 0)
            def _():
                ycopy_a(s).start()

            @pl.when((kind == 3) & (p == last))
            def _():
                leaf_copy(s).start()

        def second(i, s, kind):
            @pl.when(kind % 2 == 0)
            def _():
                ycopy_a(s).wait_recv()

                @pl.when(p > 0)
                def _():
                    zcopy_a(s).wait_recv()
                    zbuf[c, s, half] = zbuf[c, s, half] + (pbuf[c, s, own] + ybuf[c, s, half])

                @pl.when(p == 0)
                def _():
                    zbuf[c, s, half] = pbuf[c, s, own] + ybuf[c, s, half]

                @pl.when(p < last)
                def _():
                    zcopy_a(s).start()

                @pl.when(p == last)
                def _():
                    pbuf[c, s, own] = zbuf[c, s, half]
                    fcopy_a(s).start()
                    gcopy(s).start()

            @pl.when((kind % 2 == 1) & ((kind == 1) | (p < last)))
            def _():
                @pl.when(p > 0)
                def _():
                    zcopy_b(s).wait_recv()
                    zbuf[c, s] = zbuf[c, s] + pbuf[c, s]

                @pl.when(p == 0)
                def _():
                    zbuf[c, s] = pbuf[c, s]

                @pl.when((p < last - 1) | ((kind == 1) & (p < last)))
                def _():
                    zcopy_b(s).start()

                @pl.when((kind == 1) & (p == last))
                def _():
                    ycopy_b(s).start()

                @pl.when((kind == 3) & (p == last - 1))
                def _():
                    leaf_copy(s).wait_recv()
                    zbuf[c, s] = zbuf[c, s] + ybuf[c, s]
                    ycopy_c(s, (i // 5) % SPARE).start()

        def third(i, s, kind):
            @pl.when((kind == 1) & (p == last))
            def _():
                ycopy_b(s).wait_recv()
                pbuf[c, s] = zbuf[c, s] + ybuf[c, s]
                fcopy_b(s).start()

            @pl.when((kind == 3) & (p == last - 1))
            def _():
                k = (i // 5) % SPARE
                ycopy_c(s, k).wait_recv()
                pbuf[c, s] = zbuf[c, s] + xbuf[c, k]
                fcopy_c(s).start()

                @pl.when(p > 0)
                def _():
                    fcopy_b(s).start()

        def fourth(i, s, kind):
            @pl.when(p < last)
            def _():
                @pl.when(kind % 2 == 0)
                def _():
                    fcopy_a(s).wait_recv()

                    @pl.when(p > 0)
                    def _():
                        fcopy_a(s).start()

                    gcopy(s).start()

                @pl.when((kind == 1) | ((kind == 3) & (p < last - 1)))
                def _():
                    fcopy_b(s).wait_recv()

                    @pl.when(p > 0)
                    def _():
                        fcopy_b(s).start()

        def store(s, dst0, dst1):
            pltpu.make_async_copy(pbuf.at[c, s, :, pl.ds(0, 128)], dst0, os0.at[c, s]).start()
            pltpu.make_async_copy(pbuf.at[c, s, :, pl.ds(128, 128)], dst1, os1.at[c, s]).start()

        def fifth(i, s, kind):
            @pl.when(kind % 2 == 0)
            def _():
                gcopy(s).wait_recv()
                ycopy_a(s).wait_send()
                pbuf[c, s, oth] = ybuf[c, s, pl.ds(64, 64)]

            @pl.when((kind == 3) & (p == last))
            def _():
                fcopy_c(s).wait_recv()
                leaf_copy(s).wait_send()
                pbuf[c, s] = zbuf[c, s]

            g = 2 * i + c
            expert, part = g // 12, g % 12
            a = g - 192

            @pl.when((g < 192) & (part < 4))
            def _():
                col = pl.multiple_of(part * 256, 128)
                col1 = pl.multiple_of(part * 256 + 128, 128)
                store(s, o_down.at[expert, :, pl.ds(col, 128)], o_down.at[expert, :, pl.ds(col1, 128)])

            @pl.when((g < 192) & (part >= 4))
            def _():
                rows = pl.ds(pl.multiple_of((part - 4) * 128, 128), 128)
                store(s, o_gate.at[expert, rows], o_up.at[expert, rows])

            @pl.when((g >= 192) & (a < 8))
            def _():
                rows = pl.ds(pl.multiple_of(a * 128, 128), 128)
                store(s, o_q.at[rows, pl.ds(0, 128)], o_q.at[rows, pl.ds(128, 128)])

            @pl.when((a >= 8) & (a < 16))
            def _():
                rows = pl.ds(pl.multiple_of((a - 8) * 128, 128), 128)
                store(s, o_k.at[rows], o_v.at[rows])

            @pl.when(i == N_CLASS - 1)
            def _():
                store(s, o_norm.at[c, :, pl.ds(0, 128)], o_norm.at[c, :, pl.ds(128, 128)])

            @pl.when((a >= 16) & (a < 24))
            def _():
                b = a - 16
                rows = pl.ds(pl.multiple_of((b // 4) * 128, 128), 128)
                col = pl.multiple_of((b % 4) * 256, 128)
                col1 = pl.multiple_of((b % 4) * 256 + 128, 128)
                store(s, o_out.at[rows, pl.ds(col, 128)], o_out.at[rows, pl.ds(col1, 128)])

        def sixth(i, s, kind):
            pltpu.make_async_copy(pbuf.at[c, s, :, pl.ds(0, 128)], o_k.at[pl.ds(0, 128)], os0.at[c, s]).wait()
            pltpu.make_async_copy(pbuf.at[c, s, :, pl.ds(0, 128)], o_k.at[pl.ds(0, 128)], os1.at[c, s]).wait()

            @pl.when(kind % 2 == 0)
            def _():
                gcopy(s).wait_send()

                @pl.when(p < last)
                def _():
                    zcopy_a(s).wait_send()

                @pl.when(p > 0)
                def _():
                    fcopy_a(s).wait_send()

            @pl.when((kind == 1) | ((kind == 3) & (p < last)))
            def _():
                @pl.when((p < last - 1) | ((kind == 1) & (p < last)))
                def _():
                    zcopy_b(s).wait_send()

                @pl.when((kind == 1) & (p == last))
                def _():
                    ycopy_b(s).wait_send()

                @pl.when((kind == 3) & (p == last - 1))
                def _():
                    ycopy_c(s, 0).wait_send()
                    fcopy_c(s).wait_send()

                @pl.when(p > 0)
                def _():
                    fcopy_b(s).wait_send()

        t2 = hop * (1 + p)
        t3 = hop * (2 + last)
        t4 = t3 + hop * (last - p)
        t5 = t4 + hop
        t6 = t5 + hop
        return [(0, first, at), (t2, second, at), (t3, third, at), (t4, fourth, at), (t5, fifth, at), (t6, sixth, at)]

    def body(t, carry):
        both = [stage(0, t), stage(1, t)]
        for k in (1, 2, 3, 4, 5, 0):
            if k == 0:
                work(t)
            for st in both:
                delay, fn, at = st[k]
                at(delay, fn)
        return carry

    total = N_CLASS + hop * (2 * last + 4) + 1
    lax.fori_loop(0, total, body, 0)


def run_layer(mesh, *operands):
    groups = mesh.shape["dp"]
    nz = 4 if groups % 8 == 0 else groups // 2
    last = nz - 1
    hop = HOP
    ring = hop * (2 * last + 4) + 2
    ring += -ring % 5
    f32, bf16 = jnp.float32, jnp.bfloat16

    def out(shape, kind=f32):
        return jax.ShapeDtypeStruct(shape, kind)

    outs = [
        out((16, 1024, 128)), out((16, 1024, 128)), out((16, 128, 1024)),
        out((1024, 256)), out((1024, 128)), out((1024, 128)), out((256, 1024)), out((2, 128, 256)),
        out((1024, 1024), bf16), out((1024, 1024), bf16), out((1024, 128)),
        out((1024, 1024)), out((1024, 1024)),
    ]
    anywhere = pl.BlockSpec(memory_space=pl.ANY)
    dma = pltpu.SemaphoreType.DMA
    reg = pltpu.SemaphoreType.REGULAR
    vmem = pltpu.VMEM
    res = pl.pallas_call(
        functools.partial(layer_kernel, nz, hop, ring),
        out_shape=outs,
        in_specs=[pl.BlockSpec(memory_space=pltpu.SMEM)] + [anywhere] * (len(operands) - 1),
        out_specs=[anywhere] * len(outs),
        scratch_shapes=[
            vmem((34, 128, 1024), bf16), vmem((26, 1024, 256), bf16),
            vmem((2, ring, 128, 256), f32), vmem((2, ring, 128, 256), f32), vmem((2, ring, 128, 256), f32),
            vmem((2, SPARE, 128, 256), f32), vmem((1024, 1152), f32), vmem((1024, 1152), f32),
            vmem((1024, 1024), bf16), vmem((2, 1024, 256), bf16), vmem((4, 128, 1024), bf16),
            vmem((4, 1024, 128), bf16), vmem((1024, 128), bf16), vmem((1024, 128), bf16),
            vmem((128, 1024), bf16), vmem((128, 1024), bf16),
            vmem((8, 1024), f32), vmem((64, 1024), f32), vmem((64, 1024), f32),
            vmem((4, 1024, 128), bf16), vmem((1024, 128), f32), vmem((1024, 128), f32),
            vmem((1024, 128), f32), vmem((8, 1024), f32), vmem((128, 256), f32),
            vmem((8, 1024), jnp.int32), vmem((8, 1024), f32),
            dma((18,)), dma((2, 3)), dma((11,)),
        ]
        + [dma((2, ring))] * 10
        + [dma((2, SPARE))]
        + [dma((4,))] * 6
        + [dma((3,))] * 2
        + [dma((3,))] * 6
        + [reg((3,))] * 3,
        compiler_params=pltpu.CompilerParams(
            collective_id=0, has_side_effects=True, vmem_limit_bytes=63 * 2**20
        ),
    )(*operands)
    sums, rest = tuple(res[:8]), res[8:11]
    if groups > 2 * nz:
        same = [
            [2 * nz * block + place for block in range(groups // (2 * nz))] for place in range(2 * nz)
        ]
        sums = lax.psum(sums, "dp", axis_index_groups=same)
    return sums, rest


def per_device(
    mesh,
    tokens,
    lengths,
    chosen,
    gate_values,
    cotangent,
    norm_attn,
    w_query,
    w_key,
    w_value,
    w_out,
    norm_moe,
    w_gate,
    w_up,
    w_down,
):
    seq_len = tokens.shape[0] // lengths.shape[0]
    cosine, sine = rope_tables(seq_len, HEAD_DIM)
    sums, (result, grad_tokens, dots) = run_layer(
        mesh,
        lengths,
        tokens,
        cotangent,
        chosen.T,
        gate_values.T,
        norm_attn[None, :],
        norm_moe[None, :],
        w_gate,
        w_up,
        w_down,
        cosine,
        sine,
        w_out,
        w_query,
        w_key,
        w_value,
    )
    grad_gate, grad_up, grad_down, grad_query, grad_key, grad_value, grad_out, norm_rows = sums
    picked = chosen[:, :, None] == jnp.arange(EXPERTS, dtype=jnp.int32)[None, None, :]
    d_gates = jnp.sum(jnp.where(picked, dots[:, None, :EXPERTS], 0.0), axis=-1)
    return (
        result,
        grad_tokens,
        d_gates,
        norm_rows[0, 4:8].reshape(-1),
        grad_query,
        grad_key,
        grad_value,
        grad_out,
        norm_rows[0, 0:4].reshape(-1),
        grad_gate,
        grad_up,
        grad_down,
    )


def solution(mesh):
    placed = (
        P("dp", None),
        P("dp"),
        P("dp", None),
        P("dp", None),
        P("dp", None),
        P(),
        P(None, "tensor"),
        P(None, "tensor"),
        P(None, "tensor"),
        P("tensor", None),
        P(),
        P(None, None, "tensor"),
        P(None, None, "tensor"),
        P(None, "tensor", None),
    )
    return jax.shard_map(
        functools.partial(per_device, mesh),
        mesh=mesh,
        in_specs=placed,
        out_specs=(
            P("dp", None),
            P("dp", None),
            P("dp", None),
            P(),
            P(None, "tensor"),
            P(None, "tensor"),
            P(None, "tensor"),
            P("tensor", None),
            P(),
            P(None, None, "tensor"),
            P(None, None, "tensor"),
            P(None, "tensor", None),
        ),
        check_vma=False,
    )
```

```python
import functools
import math

import jax
import jax.numpy as jnp
import numpy as np
from jax import lax
from jax.experimental import pallas as pl
from jax.experimental.pallas import tpu as pltpu
from jax.sharding import PartitionSpec as P

MESH = pl.DeviceIdType.MESH

HEAD_DIM = 64
TOP_K = 8
EXPERTS = 16


EPSILON = 1e-05
THETA = 10000.0
NEGATIVE = -1e30


def dot_f(left, right):
    return jnp.dot(left, right, preferred_element_type=jnp.float32)


def rope_tables(positions, width):
    half_w = width // 2
    freqs = THETA ** (-np.arange(half_w, dtype=np.float64) * 2.0 / width)
    angles = freqs[:, None] * np.arange(positions, dtype=np.float64)[None, :]
    return (np.cos(angles).astype(np.float32), np.sin(angles).astype(np.float32))


LANES = 128
ROWS = 256
N_CLASS = 108
HOP = 2
SPARE = 3
T_SUM1 = 30
T_MID1 = 47
T_ATT = 51
T_TURN = 59
T_PROJ = 63
T_SUM2 = 67
T_TOK = 84
T_MOE = 88
T_SUM3 = 96
T_RES = 113


def dot_nt(left, right):
    return lax.dot_general(
        left, right, (((1,), (1,)), ((), ())), preferred_element_type=jnp.float32
    )


def dot_tn(left, right):
    return lax.dot_general(
        left, right, (((0,), (0,)), ((), ())), preferred_element_type=jnp.float32
    )


def layer_kernel(
    nz, hop, ring,
    length, x_in, d_out, chosen, gates, gain_attn, gain_moe, w_gate, w_up, w_down,
    cos_in, sin_in, w_out, w_query, w_key, w_value,
    o_gate, o_up, o_down, o_q, o_k, o_v, o_out, o_norm0, o_norm1, o_result, o_tokens, o_dots, s_resid, s_dres,
    lhs, rhs, pbuf, zbuf, ybuf, xbuf, acc, buf, hbuf, wgu, wdb, q2, k2, v2, kt2, vt2, lse, cos_t, sin_t,
    da2, dk_acc, dv_acc, slot_w, gain, norms, picks, pick_w, norm_in, d_pick,
    ld, wsem, iosem, ys, yr, zs, zr, fs, fr, gs, gr, os0, os1, xr,
    cs_c, cr_c, cs_x, cr_x, cs_f, cr_f, ws, wr, s1s, s1r, s2s, s2r, s3s, s3r, ready1, ready2, ready3, ns, nr,
):
    f32, bf16 = jnp.float32, jnp.bfloat16
    dp = lax.axis_index("dp")
    tensor = lax.axis_index("tensor")
    base = dp - dp % (2 * nz)
    z, y = (dp % (2 * nz)) // 2, dp % 2
    last = nz - 1
    mate = base + z * 2 + (1 - y)
    up_id = base + jnp.minimum(z + 1, last) * 2 + y
    dn_id = base + jnp.maximum(z - 1, 0) * 2 + y
    far = base + ((z + 2) % nz) * 2 + y
    core = tensor % 2
    core_mate = tensor - core + (1 - core)
    x_mate = (tensor + 2) % 4

    def local(src, dst, sem):
        return pltpu.make_async_copy(src, dst, sem)

    def remote(src, dst, ssem, rsem, dev, axis="dp"):
        return pltpu.make_async_remote_copy(
            src_ref=src, dst_ref=dst, send_sem=ssem, recv_sem=rsem,
            device_id={axis: dev}, device_id_type=MESH,
        )

    def block(b, size=ROWS):
        return pl.ds(pl.multiple_of(b * size, size), size)

    bar = pltpu.get_barrier_semaphore()
    for axis, dev in (("dp", mate), ("dp", far), ("tensor", core_mate), ("tensor", x_mate)):
        pl.semaphore_signal(bar, inc=1, device_id={axis: dev}, device_id_type=MESH)

    @pl.when(z < last)
    def _():
        pl.semaphore_signal(bar, inc=1, device_id={"dp": up_id}, device_id_type=MESH)

    @pl.when(z > 0)
    def _():
        pl.semaphore_signal(bar, inc=1, device_id={"dp": dn_id}, device_id_type=MESH)

    wide = pl.ds(0, 1024)
    share = block(tensor)
    token_load = [
        local(x_in, hbuf, ld.at[0]),
        local(gain_attn, gain.at[pl.ds(1, 1)], ld.at[1]),
        local(gain_moe, gain.at[pl.ds(0, 1)], ld.at[2]),
        local(cos_in, cos_t, ld.at[3]),
        local(sin_in, sin_t, ld.at[4]),
    ]
    proj_load = [
        local(w_query, wgu.at[0], ld.at[5]),
        local(w_key, wgu.at[1, :, pl.ds(0, LANES)], ld.at[6]),
        local(w_value, wgu.at[1, :, pl.ds(LANES, LANES)], ld.at[7]),
    ]
    out_load = [local(w_out.at[:, block(c)], rhs.at[22 + c, share], ld.at[8 + c]) for c in range(4)]
    late_load = [local(d_out.at[:, block(c)], rhs.at[c], ld.at[12 + c]) for c in range(4)] + [
        local(chosen, picks, ld.at[16]),
        local(gates, pick_w, ld.at[17]),
    ]

    def expert_load(e, s):
        return [
            local(w_gate.at[e], wgu.at[s, :, pl.ds(0, LANES)], wsem.at[s, 0]),
            local(w_up.at[e], wgu.at[s, :, pl.ds(LANES, LANES)], wsem.at[s, 1]),
            local(w_down.at[e], wdb.at[s], wsem.at[s, 2]),
        ]

    def start(copies):
        for copy in copies:
            copy.start()

    def wait(copies):
        for copy in copies:
            copy.wait()

    start(out_load + token_load + proj_load + late_load)
    pl.semaphore_wait(bar, 4 + (z < last).astype(jnp.int32) + (z > 0).astype(jnp.int32))

    part_w = buf.at[share, wide]
    quarter = 2 * (z % 2) + y
    part_q = buf.at[pl.ds(pl.multiple_of(tensor * 256 + quarter * 64, 64), 64), wide]
    part_y = buf.at[pl.ds(pl.multiple_of(x_mate * 256 + quarter * 64, 64), 64), wide]
    part_z = buf.at[pl.ds(pl.multiple_of(x_mate * 256 + (z % 2) * 128, 128), 128), wide]
    pair = base + (z + 1 - 2 * (z % 2)) * 2 + y
    w_x = remote(part_q, part_q, ws.at[0], wr.at[0], x_mate, "tensor")
    w_y = remote(part_y, part_y, ws.at[3], wr.at[3], mate)
    w_z = remote(part_z, part_z, ws.at[4], wr.at[4], pair)
    w_c = remote(part_w, part_w, ws.at[1], wr.at[1], core_mate, "tensor")
    part_f = buf.at[block(x_mate), wide]
    w_f = remote(part_f, part_f, ws.at[2], wr.at[2], core_mate, "tensor")
    wait(out_load)
    for c in range(4):
        buf[share, 256 * c : 256 * c + 256] = rhs[22 + c, share, :].astype(f32)
    w_x.start()
    w_c.start()

    def gather_x(b):
        return remote(
            acc.at[block(b), share], acc.at[block(b), share], cs_x.at[b], cr_x.at[b], x_mate, "tensor"
        )

    def gather_c(b):
        return remote(
            acc.at[block(b), share], acc.at[block(b), share], cs_c.at[b], cr_c.at[b], core_mate, "tensor"
        )

    def gather_f(b):
        part = acc.at[block(b), block(x_mate)]
        return remote(part, part, cs_f.at[b], cr_f.at[b], core_mate, "tensor")

    def rotate_t(values, cols):
        one, two = values[:32], values[32:]
        cosine, sine = cos_t[:, cols], sin_t[:, cols]
        return jnp.concatenate([one * cosine - two * sine, two * cosine + one * sine], axis=0)

    def head_rows(b, carry):
        rows = block(b)
        vals = [hbuf[rows, 256 * col : 256 * col + 256].astype(f32) for col in range(4)]
        square = sum(jnp.sum(v * v, axis=1, keepdims=True) for v in vals)
        scale_r = lax.rsqrt(square * (1.0 / 1024.0) + EPSILON)
        query, key_value = 0.0, 0.0
        for col in range(4):
            normed = vals[col] * scale_r * gain[1:2, 256 * col : 256 * col + 256]
            for half_c in range(2):
                lhs[24 + 2 * col + half_c, :, rows] = normed[:, 128 * half_c : 128 * half_c + 128].T.astype(bf16)
            normed = normed.astype(bf16)
            query = query + dot_f(normed, wgu[0, 256 * col : 256 * col + 256, :])
            key_value = key_value + dot_f(normed, wgu[1, 256 * col : 256 * col + 256, :])
        query = query.T
        nothing = jnp.zeros((64, ROWS), f32)
        for h in range(4):
            turned = rotate_t(query[64 * h : 64 * h + 64], rows)
            both = [turned, nothing] if h < 2 else [nothing, turned]
            q2[h, rows, :] = jnp.concatenate(both, axis=0).T.astype(bf16)
        key = key_value[:, :LANES].T
        key = jnp.concatenate([rotate_t(key[:64], rows), rotate_t(key[64:], rows)], axis=0)
        kt2[:, rows] = key.astype(bf16)
        k2[rows, :] = key.T.astype(bf16)
        value = key_value[:, LANES:]
        v2[rows, :] = value.astype(bf16)
        vt2[:, rows] = value.T.astype(bf16)
        return carry

    scaling = 1.0 / math.sqrt(HEAD_DIM)

    def masked_scores(h, qb):
        keys = ROWS * (qb + 1)
        rows = pl.ds(ROWS * qb, ROWS)
        scores = dot_nt(k2[0:keys, :], q2[h, rows, :]) * scaling
        k_pos = lax.broadcasted_iota(jnp.int32, (keys, ROWS), 0)
        q_pos = lax.broadcasted_iota(jnp.int32, (keys, ROWS), 1) + ROWS * qb
        allowed = (k_pos <= q_pos) & (k_pos < length[0])
        return jnp.where(allowed, scores, NEGATIVE)

    def attend(qb):
        keys = ROWS * (qb + 1)
        rows = pl.ds(ROWS * qb, ROWS)

        def one_head(h, carry):
            scores = masked_scores(h, qb)
            top_s = jnp.max(scores, axis=0, keepdims=True)
            expo = jnp.exp(scores - top_s)
            total = jnp.sum(expo, axis=0, keepdims=True)
            probs = (expo / total).astype(bf16)
            lse[pl.ds(h, 1), rows] = top_s + jnp.log(total)
            v_head = vt2[pl.ds(pl.multiple_of((h // 2) * 64, 64), 64), 0:keys]
            lhs[32 + h // 2, pl.ds(pl.multiple_of((h % 2) * 64, 64), 64), rows] = dot_f(v_head, probs).astype(bf16)
            return carry

        lax.fori_loop(0, 4, one_head, 0)
        for half_c in range(2):
            own_c = pl.ds(pl.multiple_of(tensor * 256 + half_c * 128, 128), 128)
            acc[rows, own_c] = lhs[32 + half_c, :, rows].astype(f32).T
        gather_x(qb).start()
        gather_c(qb).start()

    wait(token_load + proj_load)
    head_rows(0, 0)
    attend(0)
    head_rows(1, 0)
    w_x.wait_recv()
    w_y.start()
    attend(1)
    head_rows(2, 0)
    w_y.wait_recv()
    w_z.start()
    attend(2)
    head_rows(3, 0)
    start(expert_load(0, 0))
    attend(3)
    dk_acc[...] = jnp.zeros_like(dk_acc)
    dv_acc[...] = jnp.zeros_like(dv_acc)
    norms[...] = jnp.zeros_like(norms)

    wait(late_load)

    expert_id = lax.broadcasted_iota(jnp.int32, (EXPERTS, 1024), 0)
    alive = lax.broadcasted_iota(jnp.int32, (EXPERTS, 1024), 1) < length[0]
    hits = jnp.zeros((EXPERTS, 1024), f32)
    weight = jnp.zeros((EXPERTS, 1024), f32)
    for k in range(TOP_K):
        same = (picks[k : k + 1, :] == expert_id) & alive
        hits = jnp.where(same, 1.0, hits)
        weight = jnp.where(same, pick_w[k : k + 1, :], weight)
    hits = hits.astype(bf16)
    limit = ((5 * TOP_K * length[0] + 4 * EXPERTS - 1) // (4 * EXPERTS)).astype(f32)
    for b in range(4):
        rows = pl.ds(ROWS * b, ROWS)
        token = lax.broadcasted_iota(jnp.int32, (1024, ROWS), 1) + ROWS * b
        earlier = jnp.where(lax.broadcasted_iota(jnp.int32, (1024, ROWS), 0) < token, 1.0, 0.0).astype(bf16)
        places = dot_f(hits, earlier)
        kept = jnp.where(places < limit, weight[:, ROWS * b : ROWS * b + ROWS], 0.0)
        slot_w[rows, :] = jnp.concatenate([kept, jnp.zeros((LANES - EXPERTS, ROWS), f32)], axis=0).T

    def mask_rows(b, carry):
        rows = block(b)
        pos = lax.broadcasted_iota(jnp.int32, (ROWS, 256), 0) + b * ROWS
        for c in range(4):
            rhs[c, rows, :] = jnp.where(pos < length[0], rhs[c, rows, :].astype(f32), 0.0).astype(bf16)
        return carry

    lax.fori_loop(0, 4, mask_rows, 0)

    w_z.wait_recv()
    w_f.start()
    w_c.wait_recv()
    w_f.wait_recv()

    def cast_out(b, carry):
        for c in range(4):
            rhs[22 + c, block(b, 64), :] = buf[block(b, 64), 256 * c : 256 * c + 256].astype(bf16)
        return carry

    lax.fori_loop(0, 16, cast_out, 0)

    def forward_rows(b, carry):
        rows = block(b)
        for k in range(4):
            part = acc[rows, 256 * k : 256 * k + 256].astype(bf16)
            if k == 0:
                sums = [
                    hbuf[rows, 256 * col : 256 * col + 256].astype(f32) + dot_f(part, rhs[22 + col, 0:256, :])
                    for col in range(4)
                ]
            else:
                sums = [
                    sums[col] + dot_f(part, rhs[22 + col, 256 * k : 256 * k + 256, :]) for col in range(4)
                ]
        square = sum(jnp.sum(v * v, axis=1, keepdims=True) for v in sums)
        scale_r = lax.rsqrt(square * (1.0 / 1024.0) + EPSILON)
        for col in range(4):
            buf[rows, 256 * col : 256 * col + 256] = sums[col]
            normed = sums[col] * scale_r * gain[0:1, 256 * col : 256 * col + 256]
            hbuf[rows, 256 * col : 256 * col + 256] = normed.astype(bf16)
            for half_c in range(2):
                lhs[16 + 2 * col + half_c, :, rows] = normed[:, 128 * half_c : 128 * half_c + 128].T.astype(bf16)
        return carry

    def expert(e, begin, count, first=False):
        s = e % 2

        if not first:

            @pl.when(begin == 0)
            def _():
                wait(expert_load(e, s))

                @pl.when(e + 1 < EXPERTS)
                def _():
                    start(expert_load(e + 1, 1 - s))

        def rows_of(b, carry):
            rows = block(b)
            both = dot_f(hbuf[rows, :], wgu[s])
            gate, up = both[:, :LANES], both[:, LANES:]
            d_raw = dot_nt(rhs[0, rows, :], wdb[s, :, 0:256])
            for col in range(1, 4):
                d_raw = d_raw + dot_nt(rhs[col, rows, :], wdb[s, :, 256 * col : 256 * col + 256])
            lane = lax.broadcasted_iota(jnp.int32, (ROWS, LANES), 1)
            weight = jnp.sum(jnp.where(lane == e, slot_w[rows, :], 0.0), axis=1, keepdims=True)
            sigma = 1.0 / (1.0 + jnp.exp(-gate))
            silu = gate * sigma
            hidden = silu * up
            lhs[e, :, rows] = (hidden * weight).T.astype(bf16)
            inner = jnp.sum(hidden * d_raw, axis=1, keepdims=True)
            inner = jnp.where(weight > 0.0, inner, 0.0)
            acc[rows, 1024:1152] = jnp.where(lane == e, inner, 0.0 if first else acc[rows, 1024:1152])
            d_hidden = d_raw * weight
            d_gate = (d_hidden * up * sigma * (1.0 + gate * (1.0 - sigma))).astype(bf16)
            d_up = (d_hidden * silu).astype(bf16)
            rhs[4 + e, rows, 0:LANES] = d_gate
            rhs[4 + e, rows, LANES:] = d_up
            part = dot_nt(rhs[4 + e, rows, :], wgu[s])
            acc[rows, 0:1024] = part if first else acc[rows, 0:1024] + part
            return carry

        if first:
            rows_of(begin, 0)
        else:
            lax.fori_loop(begin, begin + count, rows_of, 0)

    def forward_step(b, carry):
        @pl.when(b < 4)
        def _():
            gather_x(b).wait_recv()
            gather_f(b).start()

        @pl.when(b > 0)
        def _():
            gather_c(b - 1).wait_recv()
            gather_f(b - 1).wait_recv()
            gather_f(b - 1).wait_send()
            gather_x(b - 1).wait_send()
            gather_c(b - 1).wait_send()
            forward_rows(b - 1, 0)
            expert(0, b - 1, 1, True)

        return carry

    for copy in (w_x, w_c, w_f, w_y, w_z):
        copy.wait_send()
    wait(expert_load(0, 0))
    start(expert_load(1, 1))
    lax.fori_loop(0, 5, forward_step, 0)
    keep = local(buf.at[:, wide], s_resid, iosem.at[0])
    keep.start()

    def half_expert(u):
        expert(u // 2 + 1, (u % 2) * 2, 2)

    mine = pl.ds(pl.multiple_of(core * 512, 512), 512)
    other = pl.ds(pl.multiple_of((1 - core) * 512, 512), 512)

    def span(k):
        return pl.ds(0, 1152 if k == 0 else 1024)

    def sum_a(k):
        return remote(acc.at[other, span(k)], buf.at[pl.ds(0, 512), span(k)], s1s.at[k], s1r.at[k], core_mate, "tensor")

    def sum_b(k):
        return remote(acc.at[mine, span(k)], buf.at[pl.ds(512, 512), span(k)], s2s.at[k], s2r.at[k], x_mate, "tensor")

    def sum_c(k):
        part = acc.at[mine, span(k)]
        return remote(part, part, s3s.at[k], s3r.at[k], core_mate, "tensor")

    def add_in(k, at_row):
        def step(b, carry):
            rows = pl.ds(pl.multiple_of(core * 512 + b * 64, 64), 64)
            acc[rows, span(k)] += buf[pl.ds(pl.multiple_of(at_row + b * 64, 64), 64), span(k)]
            return carry

        lax.fori_loop(0, 8, step, 0)

    def sum_first(k):
        pl.semaphore_signal(ready1.at[k], inc=1, device_id={"tensor": core_mate}, device_id_type=MESH)
        pl.semaphore_signal(ready2.at[k], inc=1, device_id={"tensor": x_mate}, device_id_type=MESH)
        pl.semaphore_wait(ready1.at[k], 1)
        sum_a(k).start()

    def sum_second(k):
        sum_a(k).wait_recv()
        add_in(k, 0)
        sum_a(k).wait_send()
        pl.semaphore_signal(ready3.at[k], inc=1, device_id={"tensor": core_mate}, device_id_type=MESH)
        pl.semaphore_wait(ready2.at[k], 1)
        sum_b(k).start()

    def sum_third(k):
        sum_b(k).wait_recv()
        sum_b(k).wait_send()
        add_in(k, 512)
        pl.semaphore_wait(ready3.at[k], 1)
        sum_c(k).start()

    def sum_last(k):
        sum_c(k).wait_recv()
        sum_c(k).wait_send()

    def norm_sum(step, dev):
        return remote(norms.at[pl.ds(0, 16)], norm_in.at[step], ns.at[step], nr.at[step], dev)

    partners = (mate, pair, far)

    def norm_next(step):
        if step > 0:
            norm_sum(step - 1, partners[step - 1]).wait_recv()
            norm_sum(step - 1, partners[step - 1]).wait_send()
            norms[...] = norms[...] + norm_in[step - 1]
        if step < 3:
            norm_sum(step, partners[step]).start()

    def norm_back(values, scale_r, grads, which):
        inner = sum(
            jnp.sum(v * scale_r * (g * gain[which : which + 1, 256 * c : 256 * c + 256]), axis=1, keepdims=True)
            for c, (v, g) in enumerate(zip(values, grads))
        ) * (1.0 / 1024.0)
        outs = []
        for c, (v, g) in enumerate(zip(values, grads)):
            normed = v * scale_r
            total = jnp.sum(g * normed, axis=0, keepdims=True)
            row = 8 * which + 2 * c
            norms[row : row + 1, :] += total[:, :LANES]
            norms[row + 1 : row + 2, :] += total[:, LANES:]
            outs.append(scale_r * (g * gain[which : which + 1, 256 * c : 256 * c + 256] - normed * inner))
        return outs

    def middle_rows(b):
        rows = block(b)

        values = [buf[rows, 256 * c : 256 * c + 256] for c in range(4)]
        grads = [acc[rows, 256 * c : 256 * c + 256] for c in range(4)]
        square = sum(jnp.sum(v * v, axis=1, keepdims=True) for v in values)
        scale_r = lax.rsqrt(square * (1.0 / 1024.0) + EPSILON)
        back = norm_back(values, scale_r, grads, 0)
        for c in range(4):
            total = rhs[c, rows, :].astype(f32) + back[c]
            acc[rows, 256 * c : 256 * c + 256] = total
            rhs[22 + c, rows, :] = total.astype(bf16)
        for h in range(4):
            d_head = dot_nt(rhs[22, rows, :], wdb[h, :, 0:256])
            for c in range(1, 4):
                d_head = d_head + dot_nt(rhs[22 + c, rows, :], wdb[h, :, 256 * c : 256 * c + 256])
            da2[h, rows, :] = d_head.astype(bf16)

    def turn_back(grad, cols):
        one, two = grad[:32], grad[32:]
        cosine, sine = cos_t[:, cols], sin_t[:, cols]
        return jnp.concatenate([one * cosine + two * sine, two * cosine - one * sine], axis=0)

    def attend_back(h, qb):
        keys = ROWS * (qb + 1)
        rows = pl.ds(ROWS * qb, ROWS)
        q_rows = q2[h, rows, :]
        d_rows = da2[h, rows, :]
        exact = jnp.exp(masked_scores(h, qb) - lse[pl.ds(h, 1), rows])
        d_probs = dot_nt(v2[0:keys, :], d_rows)
        inner = jnp.sum(exact * d_probs, axis=0, keepdims=True)
        d_scores = (exact * (d_probs - inner)).astype(bf16)
        dk_acc[0:keys, :] += dot_f(d_scores, q_rows)
        dv_acc[0:keys, :] += dot_f(exact.astype(bf16), d_rows)
        k_head = kt2[pl.ds(pl.multiple_of((h // 2) * 64, 64), 64), 0:keys]
        d_q = dot_f(k_head, d_scores) * scaling
        buf[pl.ds(pl.multiple_of(h * 64, 64), 64), rows] = turn_back(d_q, rows)

    def turn_rows(b):
        rows = block(b)
        rhs[20, rows, :] = buf[0:256, rows].T.astype(bf16)
        d_k = (dk_acc[rows, :] * scaling).T
        d_k = jnp.concatenate([turn_back(d_k[:64], rows), turn_back(d_k[64:], rows)], axis=0)
        rhs[21, rows, 0:LANES] = d_k.T.astype(bf16)
        rhs[21, rows, LANES:] = dv_acc[rows, :].astype(bf16)

    def project_rows(b):
        rows = block(b)
        acc[rows, 0:1024] = dot_nt(rhs[20, rows, :], wgu[0]) + dot_nt(rhs[21, rows, :], wgu[1])

    def token_rows(b):
        rows = block(b)

        values = [hbuf[rows, 256 * c : 256 * c + 256].astype(f32) for c in range(4)]
        grads = [acc[rows, 256 * c : 256 * c + 256] for c in range(4)]
        square = sum(jnp.sum(v * v, axis=1, keepdims=True) for v in values)
        scale_r = lax.rsqrt(square * (1.0 / 1024.0) + EPSILON)
        back = norm_back(values, scale_r, grads, 1)
        for c in range(4):
            cols = slice(256 * c, 256 * c + 256)
            hbuf[rows, cols] = (buf[rows, cols] + back[c]).astype(bf16)

    def pair_load(pair, s):
        return local(w_down.at[pl.ds(2 * pair, 2)], wdb.at[pl.ds(2 * s, 2)], wsem.at[s, 2])

    def moe_pair(pair):
        s = pair % 2
        pair_load(pair, s).wait()

        @pl.when(pair + 1 < EXPERTS // 2)
        def _():
            pair_load(pair + 1, 1 - s).start()

        def rows_of(b, carry):
            rows = block(b)
            hidden = lhs[pl.ds(2 * pair, 2), :, rows].reshape(256, ROWS)
            down = wdb[pl.ds(2 * s, 2)].reshape(256, 1024)
            part = dot_tn(hidden, down)

            @pl.when(pair == 0)
            def _():
                acc[rows, 0:1024] = part

            @pl.when(pair > 0)
            def _():
                acc[rows, 0:1024] += part

            return carry

        lax.fori_loop(0, 4, rows_of, 0)

    def result_rows(b):
        rows = block(b)

        pos = lax.broadcasted_iota(jnp.int32, (ROWS, 1024), 0) + b * ROWS
        total = buf[rows, wide] + acc[rows, 0:1024]
        hbuf[rows, :] = jnp.where(pos < length[0], total, 0.0).astype(bf16)

    def halves_in(src):
        return [local(src, buf.at[:, wide], iosem.at[1])]

    tokens_in = [local(x_in, hbuf, iosem.at[3])]
    wo_load = [
        local(w_out.at[pl.ds(64 * h, 64)], wdb.at[h, pl.ds(64 * (h // 2), 64)], ld.at[8 + h]) for h in range(4)
    ]
    dots_out = [local(d_pick, o_dots, iosem.at[7])]
    norms_out = [
        local(norms.at[pl.ds(0, 8)], o_norm0, iosem.at[2]),
        local(norms.at[pl.ds(8, 8)], o_norm1, iosem.at[4]),
    ]

    def pick_dots():
        for b in range(4):
            rows = pl.ds(ROWS * b, ROWS)
            dots = acc[rows, 1024:1152].T[:EXPERTS]
            lane_e = lax.broadcasted_iota(jnp.int32, (EXPERTS, ROWS), 0)
            for k in range(TOP_K):
                mine_k = jnp.where(picks[k : k + 1, rows] == lane_e, dots, 0.0)
                d_pick[k : k + 1, rows] = jnp.sum(mine_k, axis=0, keepdims=True)
    dres_out = [local(acc.at[:, wide], s_dres, iosem.at[8])]
    tokens_out = [local(hbuf, o_tokens, iosem.at[9])]
    result_out = [local(hbuf, o_result, iosem.at[10])]

    def clear_wo():
        for h in range(4):
            wdb[h, 64 - 64 * (h // 2) : 128 - 64 * (h // 2), :] = jnp.zeros((64, 1024), bf16)

    def do_all(*steps):
        for step in steps:
            step()

    once = {
        T_SUM1: lambda: do_all(keep.wait, lambda: sum_first(0), clear_wo, lambda: start(tokens_in + wo_load + proj_load)),
        T_SUM1 + 2: lambda: do_all(lambda: sum_second(0), lambda: wait(tokens_in)),
        T_MID1 - 3: lambda: sum_third(0),
        T_MID1 - 1: lambda: do_all(
            lambda: sum_last(0), pick_dots, lambda: start(halves_in(s_resid) + dots_out), lambda: wait(wo_load)
        ),
        T_ATT: lambda: do_all(lambda: wait(dots_out), lambda: start(dres_out)),
        T_PROJ - 1: lambda: do_all(lambda: wait(dres_out), lambda: wait(proj_load)),
        T_SUM2: lambda: sum_first(1),
        T_SUM2 + 2: lambda: sum_second(1),
        T_TOK - 3: lambda: sum_third(1),
        T_TOK - 1: lambda: do_all(
            lambda: sum_last(1), lambda: start(halves_in(s_dres)), lambda: start([pair_load(0, 0)])
        ),
        T_MOE: lambda: do_all(lambda: start(tokens_out), lambda: norm_next(0)),
        T_MOE + 2: lambda: norm_next(1),
        T_MOE + 4: lambda: norm_next(2),
        T_MOE + 6: lambda: do_all(lambda: norm_next(3), lambda: start(norms_out)),
        T_SUM3: lambda: do_all(lambda: wait(tokens_out + norms_out), lambda: sum_first(2)),
        T_SUM3 + 2: lambda: sum_second(2),
        T_RES - 3: lambda: sum_third(2),
        T_RES - 1: lambda: do_all(lambda: sum_last(2), lambda: start(halves_in(s_resid))),
        T_RES + 4: lambda: start(result_out),
        T_RES + 8: lambda: wait(result_out),
    }
    halves_wait = {T_MID1: s_resid, T_TOK: s_dres, T_RES: s_resid}

    def work(t):
        for when_t, fn in sorted(once.items()):
            pl.when(t == when_t)(fn)
        for when_t, src in halves_wait.items():
            pl.when(t == when_t)(lambda src=src: wait(halves_in(src)))
        for begin, count, fn in (
            (0, 2 * EXPERTS - 2, half_expert),
            (T_MID1, 4, middle_rows),
            (T_TURN, 4, turn_rows),
            (T_PROJ, 4, project_rows),
            (T_TOK, 4, token_rows),
            (T_MOE, EXPERTS // 2, moe_pair),
            (T_RES, 4, result_rows),
        ):
            pl.when((t >= begin) & (t < begin + count))(lambda fn=fn, begin=begin: fn(t - begin))
        for pair_b in range(2):
            u = t - T_ATT

            def two(pair_b=pair_b, u=u):
                attend_back(u // 2, pair_b)
                attend_back(u // 2, 3 - pair_b)

            pl.when((u >= 0) & (u < 8) & (u % 2 == pair_b))(two)

    own = pl.ds(pl.multiple_of(y * 64, 64), 64)
    oth = pl.ds(pl.multiple_of((1 - y) * 64, 64), 64)
    half = pl.ds(0, 64)

    def stage(c, t):
        p = z if c == 0 else last - z
        nxt, prv = (up_id, dn_id) if c == 0 else (dn_id, up_id)
        def at(delay, body):
            i = t - delay

            @pl.when((i >= 0) & (i < N_CLASS))
            def _():
                body(i, i % ring, i % 5)

        def ycopy_a(s):
            return remote(pbuf.at[c, s, oth], ybuf.at[c, s, half], ys.at[c, s], yr.at[c, s], mate)

        def ycopy_b(s):
            return remote(zbuf.at[c, s], ybuf.at[c, s], ys.at[c, s], yr.at[c, s], mate)

        def ycopy_c(s, k):
            return remote(zbuf.at[c, s], xbuf.at[c, k], ys.at[c, s], xr.at[c, k], mate)

        def leaf_copy(s):
            return remote(pbuf.at[c, s], ybuf.at[c, s], ys.at[c, s], yr.at[c, s], prv)

        def fcopy_c(s):
            return remote(pbuf.at[c, s], zbuf.at[c, s], gs.at[c, s], fr.at[c, s], nxt)

        def zcopy_a(s):
            return remote(zbuf.at[c, s, half], zbuf.at[c, s, half], zs.at[c, s], zr.at[c, s], nxt)

        def zcopy_b(s):
            return remote(zbuf.at[c, s], zbuf.at[c, s], zs.at[c, s], zr.at[c, s], nxt)

        def fcopy_a(s):
            return remote(pbuf.at[c, s, own], pbuf.at[c, s, own], fs.at[c, s], fr.at[c, s], prv)

        def fcopy_b(s):
            return remote(pbuf.at[c, s], pbuf.at[c, s], fs.at[c, s], fr.at[c, s], prv)

        def gcopy(s):
            return remote(pbuf.at[c, s, own], ybuf.at[c, s, pl.ds(64, 64)], gs.at[c, s], gr.at[c, s], mate)

        def first(i, s, kind):
            g = 2 * i + c
            expert, part = g // 12, g % 12
            a = g - 192
            in_moe = g < 192
            l_moe = jnp.where(part < 4, expert, 12 + part)
            r_moe = jnp.where(part < 4, part, 4 + expert)
            l_att = jnp.where(a < 16, 24 + a % 8, 32 + (a - 16) // 4)
            r_att = jnp.where(a < 16, 20 + a // 8, 22 + (a - 16) % 4)
            li = jnp.where(in_moe, l_moe, l_att)
            ri = jnp.where(in_moe, r_moe, r_att)
            pbuf[c, s] = dot_f(lhs[li], rhs[ri])

            @pl.when(kind % 2 == 0)
            def _():
                ycopy_a(s).start()

            @pl.when((kind == 3) & (p == last))
            def _():
                leaf_copy(s).start()

        def second(i, s, kind):
            @pl.when(kind % 2 == 0)
            def _():
                ycopy_a(s).wait_recv()

                @pl.when(p > 0)
                def _():
                    zcopy_a(s).wait_recv()
                    zbuf[c, s, half] = zbuf[c, s, half] + (pbuf[c, s, own] + ybuf[c, s, half])

                @pl.when(p == 0)
                def _():
                    zbuf[c, s, half] = pbuf[c, s, own] + ybuf[c, s, half]

                @pl.when(p < last)
                def _():
                    zcopy_a(s).start()

                @pl.when(p == last)
                def _():
                    pbuf[c, s, own] = zbuf[c, s, half]
                    fcopy_a(s).start()
                    gcopy(s).start()

            @pl.when((kind % 2 == 1) & ((kind == 1) | (p < last)))
            def _():
                @pl.when(p > 0)
                def _():
                    zcopy_b(s).wait_recv()
                    zbuf[c, s] = zbuf[c, s] + pbuf[c, s]

                @pl.when(p == 0)
                def _():
                    zbuf[c, s] = pbuf[c, s]

                @pl.when((p < last - 1) | ((kind == 1) & (p < last)))
                def _():
                    zcopy_b(s).start()

                @pl.when((kind == 1) & (p == last))
                def _():
                    ycopy_b(s).start()

                @pl.when((kind == 3) & (p == last - 1))
                def _():
                    leaf_copy(s).wait_recv()
                    zbuf[c, s] = zbuf[c, s] + ybuf[c, s]
                    ycopy_c(s, (i // 5) % SPARE).start()

        def third(i, s, kind):
            @pl.when((kind == 1) & (p == last))
            def _():
                ycopy_b(s).wait_recv()
                pbuf[c, s] = zbuf[c, s] + ybuf[c, s]
                fcopy_b(s).start()

            @pl.when((kind == 3) & (p == last - 1))
            def _():
                k = (i // 5) % SPARE
                ycopy_c(s, k).wait_recv()
                pbuf[c, s] = zbuf[c, s] + xbuf[c, k]
                fcopy_c(s).start()

                @pl.when(p > 0)
                def _():
                    fcopy_b(s).start()

        def fourth(i, s, kind):
            @pl.when(p < last)
            def _():
                @pl.when(kind % 2 == 0)
                def _():
                    fcopy_a(s).wait_recv()

                    @pl.when(p > 0)
                    def _():
                        fcopy_a(s).start()

                    gcopy(s).start()

                @pl.when((kind == 1) | ((kind == 3) & (p < last - 1)))
                def _():
                    fcopy_b(s).wait_recv()

                    @pl.when(p > 0)
                    def _():
                        fcopy_b(s).start()

        def store(s, dst0, dst1):
            pltpu.make_async_copy(pbuf.at[c, s, :, pl.ds(0, 128)], dst0, os0.at[c, s]).start()
            pltpu.make_async_copy(pbuf.at[c, s, :, pl.ds(128, 128)], dst1, os1.at[c, s]).start()

        def fifth(i, s, kind):
            @pl.when(kind % 2 == 0)
            def _():
                gcopy(s).wait_recv()
                ycopy_a(s).wait_send()
                pbuf[c, s, oth] = ybuf[c, s, pl.ds(64, 64)]

            @pl.when((kind == 3) & (p == last))
            def _():
                fcopy_c(s).wait_recv()
                leaf_copy(s).wait_send()
                pbuf[c, s] = zbuf[c, s]

            g = 2 * i + c
            expert, part = g // 12, g % 12
            a = g - 192

            @pl.when((g < 192) & (part < 4))
            def _():
                col = pl.multiple_of(part * 256, 128)
                col1 = pl.multiple_of(part * 256 + 128, 128)
                store(s, o_down.at[expert, :, pl.ds(col, 128)], o_down.at[expert, :, pl.ds(col1, 128)])

            @pl.when((g < 192) & (part >= 4))
            def _():
                rows = pl.ds(pl.multiple_of((part - 4) * 128, 128), 128)
                store(s, o_gate.at[expert, rows], o_up.at[expert, rows])

            @pl.when((g >= 192) & (a < 8))
            def _():
                rows = pl.ds(pl.multiple_of(a * 128, 128), 128)
                store(s, o_q.at[rows, pl.ds(0, 128)], o_q.at[rows, pl.ds(128, 128)])

            @pl.when((a >= 8) & (a < 16))
            def _():
                rows = pl.ds(pl.multiple_of((a - 8) * 128, 128), 128)
                store(s, o_k.at[rows], o_v.at[rows])

            @pl.when(a >= 16)
            def _():
                b = a - 16
                rows = pl.ds(pl.multiple_of((b // 4) * 128, 128), 128)
                col = pl.multiple_of((b % 4) * 256, 128)
                col1 = pl.multiple_of((b % 4) * 256 + 128, 128)
                store(s, o_out.at[rows, pl.ds(col, 128)], o_out.at[rows, pl.ds(col1, 128)])

        def sixth(i, s, kind):
            pltpu.make_async_copy(pbuf.at[c, s, :, pl.ds(0, 128)], o_k.at[pl.ds(0, 128)], os0.at[c, s]).wait()
            pltpu.make_async_copy(pbuf.at[c, s, :, pl.ds(0, 128)], o_k.at[pl.ds(0, 128)], os1.at[c, s]).wait()

            @pl.when(kind % 2 == 0)
            def _():
                gcopy(s).wait_send()

                @pl.when(p < last)
                def _():
                    zcopy_a(s).wait_send()

                @pl.when(p > 0)
                def _():
                    fcopy_a(s).wait_send()

            @pl.when((kind == 1) | ((kind == 3) & (p < last)))
            def _():
                @pl.when((p < last - 1) | ((kind == 1) & (p < last)))
                def _():
                    zcopy_b(s).wait_send()

                @pl.when((kind == 1) & (p == last))
                def _():
                    ycopy_b(s).wait_send()

                @pl.when((kind == 3) & (p == last - 1))
                def _():
                    ycopy_c(s, 0).wait_send()
                    fcopy_c(s).wait_send()

                @pl.when(p > 0)
                def _():
                    fcopy_b(s).wait_send()

        t2 = hop * (1 + p)
        t3 = hop * (2 + last)
        t4 = t3 + hop * (last - p)
        t5 = t4 + hop
        t6 = t5 + hop
        return [(0, first, at), (t2, second, at), (t3, third, at), (t4, fourth, at), (t5, fifth, at), (t6, sixth, at)]

    def body(t, carry):
        both = [stage(0, t), stage(1, t)]
        for k in (1, 2, 3, 4, 5, 0):
            if k == 0:
                work(t)
            for st in both:
                delay, fn, at = st[k]
                at(delay, fn)
        return carry

    total = N_CLASS + hop * (2 * last + 4) + 1
    lax.fori_loop(0, total, body, 0)


def run_layer(mesh, *operands):
    groups = mesh.shape["dp"]
    nz = 4 if groups % 8 == 0 else groups // 2
    last = nz - 1
    hop = HOP
    ring = hop * (2 * last + 4) + 2
    ring += -ring % 5
    f32, bf16 = jnp.float32, jnp.bfloat16

    def out(shape, kind=f32):
        return jax.ShapeDtypeStruct(shape, kind)

    outs = [
        out((16, 1024, 128)), out((16, 1024, 128)), out((16, 128, 1024)),
        out((1024, 256)), out((1024, 128)), out((1024, 128)), out((256, 1024)), out((8, 128)), out((8, 128)),
        out((1024, 1024), bf16), out((1024, 1024), bf16), out((8, 1024)),
        out((1024, 1024)), out((1024, 1024)),
    ]
    anywhere = pl.BlockSpec(memory_space=pl.ANY)
    dma = pltpu.SemaphoreType.DMA
    reg = pltpu.SemaphoreType.REGULAR
    vmem = pltpu.VMEM
    res = pl.pallas_call(
        functools.partial(layer_kernel, nz, hop, ring),
        out_shape=outs,
        in_specs=[pl.BlockSpec(memory_space=pltpu.SMEM)] + [anywhere] * (len(operands) - 1),
        out_specs=[anywhere] * len(outs),
        scratch_shapes=[
            vmem((34, 128, 1024), bf16), vmem((26, 1024, 256), bf16),
            vmem((2, ring, 128, 256), f32), vmem((2, ring, 128, 256), f32), vmem((2, ring, 128, 256), f32),
            vmem((2, SPARE, 128, 256), f32), vmem((1024, 1152), f32), vmem((1024, 1152), f32),
            vmem((1024, 1024), bf16), vmem((2, 1024, 256), bf16), vmem((4, 128, 1024), bf16),
            vmem((4, 1024, 128), bf16), vmem((1024, 128), bf16), vmem((1024, 128), bf16),
            vmem((128, 1024), bf16), vmem((128, 1024), bf16),
            vmem((8, 1024), f32), vmem((32, 1024), f32), vmem((32, 1024), f32),
            vmem((4, 1024, 128), bf16), vmem((1024, 128), f32), vmem((1024, 128), f32),
            vmem((1024, 128), f32), vmem((8, 1024), f32), vmem((16, 128), f32),
            vmem((8, 1024), jnp.int32), vmem((8, 1024), f32),
            vmem((3, 16, 128), f32), vmem((8, 1024), f32),
            dma((18,)), dma((2, 3)), dma((11,)),
        ]
        + [dma((2, ring))] * 10
        + [dma((2, SPARE))]
        + [dma((4,))] * 6
        + [dma((5,))] * 2
        + [dma((3,))] * 6
        + [reg((3,))] * 3
        + [dma((3,))] * 2,
        compiler_params=pltpu.CompilerParams(
            collective_id=0, has_side_effects=True, vmem_limit_bytes=63 * 2**20
        ),
    )(*operands)
    sums, rest = tuple(res[:9]), res[9:12]
    if groups > 2 * nz:
        same = [
            [2 * nz * block + place for block in range(groups // (2 * nz))] for place in range(2 * nz)
        ]
        sums = lax.psum(sums, "dp", axis_index_groups=same)
    return sums, rest


def per_device(
    mesh,
    tokens,
    lengths,
    chosen,
    gate_values,
    cotangent,
    norm_attn,
    w_query,
    w_key,
    w_value,
    w_out,
    norm_moe,
    w_gate,
    w_up,
    w_down,
):
    seq_len = tokens.shape[0] // lengths.shape[0]
    cosine, sine = rope_tables(seq_len, HEAD_DIM)
    sums, (result, grad_tokens, dots) = run_layer(
        mesh,
        lengths,
        tokens,
        cotangent,
        chosen.T,
        gate_values.T,
        norm_attn[None, :],
        norm_moe[None, :],
        w_gate,
        w_up,
        w_down,
        cosine,
        sine,
        w_out,
        w_query,
        w_key,
        w_value,
    )
    grad_gate, grad_up, grad_down, grad_query, grad_key, grad_value, grad_out, grad_norm_moe, grad_norm_attn = sums
    return (
        result,
        grad_tokens,
        dots.T,
        grad_norm_attn.reshape(-1),
        grad_query,
        grad_key,
        grad_value,
        grad_out,
        grad_norm_moe.reshape(-1),
        grad_gate,
        grad_up,
        grad_down,
    )


def solution(mesh):
    placed = (
        P("dp", None),
        P("dp"),
        P("dp", None),
        P("dp", None),
        P("dp", None),
        P(),
        P(None, "tensor"),
        P(None, "tensor"),
        P(None, "tensor"),
        P("tensor", None),
        P(),
        P(None, None, "tensor"),
        P(None, None, "tensor"),
        P(None, "tensor", None),
    )
    return jax.shard_map(
        functools.partial(per_device, mesh),
        mesh=mesh,
        in_specs=placed,
        out_specs=(
            P("dp", None),
            P("dp", None),
            P("dp", None),
            P(),
            P(None, "tensor"),
            P(None, "tensor"),
            P(None, "tensor"),
            P("tensor", None),
            P(),
            P(None, None, "tensor"),
            P(None, None, "tensor"),
            P(None, "tensor", None),
        ),
        check_vma=False,
    )
```

```python
import functools
import math

import jax
import jax.numpy as jnp
import numpy as np
from jax import lax
from jax.experimental import pallas as pl
from jax.experimental.pallas import tpu as pltpu
from jax.sharding import PartitionSpec as P

MESH = pl.DeviceIdType.MESH

HEAD_DIM = 64
TOP_K = 8
EXPERTS = 16


EPSILON = 1e-05
THETA = 10000.0
NEGATIVE = -1e30


def dot_f(left, right):
    return jnp.dot(left, right, preferred_element_type=jnp.float32)


def rope_tables(positions, width):
    half_w = width // 2
    freqs = THETA ** (-np.arange(half_w, dtype=np.float64) * 2.0 / width)
    angles = freqs[:, None] * np.arange(positions, dtype=np.float64)[None, :]
    return (np.cos(angles).astype(np.float32), np.sin(angles).astype(np.float32))


LANES = 128
ROWS = 256
CHUNK = 64
N_EXPERT = 96
N_CLASS = 120
HOP = 2
HALF = EXPERTS // 2
T_SUM1 = 30
T_MID1 = 52
T_ATT = 56
T_TURN = 64
T_PROJ = 68
T_SUM2 = 72
T_TOK = 92
T_MOE = 96
T_SUM3 = 104
T_RES = 124


def dot_nt(left, right):
    return lax.dot_general(
        left, right, (((1,), (1,)), ((), ())), preferred_element_type=jnp.float32
    )


def dot_tn(left, right):
    return lax.dot_general(
        left, right, (((0,), (0,)), ((), ())), preferred_element_type=jnp.float32
    )


def layer_kernel(
    nz, hop, ring,
    length, x_in, d_out, chosen, gates, gain_attn, gain_moe, w_gate, w_up, w_down,
    cos_in, sin_in, w_out, w_query, w_key, w_value,
    o_gate, o_up, o_down, o_q, o_k, o_v, o_out, o_norm0, o_norm1, o_result, o_tokens, o_dots, s_resid, s_dres,
    lhs, rhs, pbuf, zbuf, ybuf, acc, buf, hbuf, wgu, wdb, q2, k2, v2, kt2, vt2, lse, cos_t, sin_t,
    da2, dk_acc, dv_acc, slot_w, gain, norms, picks, pick_w, norm_in, d_pick, kept_out, kept_in, slot_m,
    ld, wsem, iosem, ys, yr, zs, zr, fs, fr, gs, gr, os0, os1,
    cs_c, cr_c, cs_x, cr_x, cs_f, cr_f, ws, wr, s1s, s1r, s2s, s2r, s3s, s3r, ready1, ready2, ready3, ns, nr, go,
    hys, hyr, hcs, hcr, hxs, hxr, hfs, hfr, dys, dyr, dcs, dcr, dxs, dxr, dfs, dfr, ks, kr,
):
    f32, bf16 = jnp.float32, jnp.bfloat16
    dp = lax.axis_index("dp")
    tensor = lax.axis_index("tensor")
    base = dp - dp % (2 * nz)
    z, y = (dp % (2 * nz)) // 2, dp % 2
    last = nz - 1
    mate = base + z * 2 + (1 - y)
    up_id = base + jnp.minimum(z + 1, last) * 2 + y
    dn_id = base + jnp.maximum(z - 1, 0) * 2 + y
    far = base + ((z + 2) % nz) * 2 + y
    core = tensor % 2
    core_mate = tensor - core + (1 - core)
    x_mate = (tensor + 2) % 4

    def local(src, dst, sem):
        return pltpu.make_async_copy(src, dst, sem)

    def remote(src, dst, ssem, rsem, dev, axis="dp"):
        return pltpu.make_async_remote_copy(
            src_ref=src, dst_ref=dst, send_sem=ssem, recv_sem=rsem,
            device_id={axis: dev}, device_id_type=MESH,
        )

    def block(b, size=ROWS):
        return pl.ds(pl.multiple_of(b * size, size), size)

    bar = pltpu.get_barrier_semaphore()
    for axis, dev in (("dp", mate), ("dp", far), ("tensor", core_mate), ("tensor", x_mate)):
        pl.semaphore_signal(bar, inc=1, device_id={axis: dev}, device_id_type=MESH)

    @pl.when(z < last)
    def _():
        pl.semaphore_signal(bar, inc=1, device_id={"dp": up_id}, device_id_type=MESH)

    @pl.when(z > 0)
    def _():
        pl.semaphore_signal(bar, inc=1, device_id={"dp": dn_id}, device_id_type=MESH)

    wide = pl.ds(0, 1024)
    share = block(tensor)
    token_load = [
        local(x_in, hbuf, ld.at[0]),
        local(gain_attn, gain.at[pl.ds(1, 1)], ld.at[1]),
        local(gain_moe, gain.at[pl.ds(0, 1)], ld.at[2]),
        local(cos_in, cos_t, ld.at[3]),
        local(sin_in, sin_t, ld.at[4]),
    ]
    proj_load = [
        local(w_query, wgu.at[0], ld.at[5]),
        local(w_key, wgu.at[1, :, pl.ds(0, LANES)], ld.at[6]),
        local(w_value, wgu.at[1, :, pl.ds(LANES, LANES)], ld.at[7]),
    ]
    out_load = [local(w_out.at[:, block(c)], rhs.at[26 + c, share], ld.at[8 + c]) for c in range(4)]
    late_load = [local(d_out.at[:, block(c)], rhs.at[c], ld.at[12 + c]) for c in range(4)] + [
        local(chosen, picks, ld.at[16]),
        local(gates, pick_w, ld.at[17]),
    ]

    def expert_load(e, s):
        return [
            local(w_gate.at[e], wgu.at[s, :, pl.ds(0, LANES)], wsem.at[s, 0]),
            local(w_up.at[e], wgu.at[s, :, pl.ds(LANES, LANES)], wsem.at[s, 1]),
            local(w_down.at[e], wdb.at[s], wsem.at[s, 2]),
        ]

    def start(copies):
        for copy in copies:
            copy.start()

    def wait(copies):
        for copy in copies:
            copy.wait()

    start(out_load + token_load + proj_load + late_load)
    pl.semaphore_wait(bar, 4 + (z < last).astype(jnp.int32) + (z > 0).astype(jnp.int32))

    part_w = buf.at[share, wide]
    quarter = 2 * (z % 2) + y
    part_q = buf.at[pl.ds(pl.multiple_of(tensor * 256 + quarter * 64, 64), 64), wide]
    part_y = buf.at[pl.ds(pl.multiple_of(x_mate * 256 + quarter * 64, 64), 64), wide]
    part_z = buf.at[pl.ds(pl.multiple_of(x_mate * 256 + (z % 2) * 128, 128), 128), wide]
    pair = base + (z + 1 - 2 * (z % 2)) * 2 + y
    w_x = remote(part_q, part_q, ws.at[0], wr.at[0], x_mate, "tensor")
    w_y = remote(part_y, part_y, ws.at[3], wr.at[3], mate)
    w_z = remote(part_z, part_z, ws.at[4], wr.at[4], pair)
    w_c = remote(part_w, part_w, ws.at[1], wr.at[1], core_mate, "tensor")
    part_f = buf.at[block(x_mate), wide]
    w_f = remote(part_f, part_f, ws.at[2], wr.at[2], core_mate, "tensor")
    wait(out_load)
    for c in range(4):
        buf[share, 256 * c : 256 * c + 256] = rhs[26 + c, share, :].astype(f32)
    w_x.start()
    w_c.start()

    def gather_x(b):
        return remote(
            acc.at[block(b), share], acc.at[block(b), share], cs_x.at[b], cr_x.at[b], x_mate, "tensor"
        )

    def gather_c(b):
        return remote(
            acc.at[block(b), share], acc.at[block(b), share], cs_c.at[b], cr_c.at[b], core_mate, "tensor"
        )

    def gather_f(b):
        part = acc.at[block(b), block(x_mate)]
        return remote(part, part, cs_f.at[b], cr_f.at[b], core_mate, "tensor")

    def rotate_t(values, cols):
        one, two = values[:32], values[32:]
        cosine, sine = cos_t[:, cols], sin_t[:, cols]
        return jnp.concatenate([one * cosine - two * sine, two * cosine + one * sine], axis=0)

    def head_rows(b, carry):
        rows = block(b)
        vals = [hbuf[rows, 256 * col : 256 * col + 256].astype(f32) for col in range(4)]
        square = sum(jnp.sum(v * v, axis=1, keepdims=True) for v in vals)
        scale_r = lax.rsqrt(square * (1.0 / 1024.0) + EPSILON)
        query, key_value = 0.0, 0.0
        for col in range(4):
            normed = vals[col] * scale_r * gain[1:2, 256 * col : 256 * col + 256]
            for half_c in range(2):
                lhs[24 + 2 * col + half_c, :, rows] = normed[:, 128 * half_c : 128 * half_c + 128].T.astype(bf16)
            normed = normed.astype(bf16)
            query = query + dot_f(normed, wgu[0, 256 * col : 256 * col + 256, :])
            key_value = key_value + dot_f(normed, wgu[1, 256 * col : 256 * col + 256, :])
        query = query.T
        nothing = jnp.zeros((64, ROWS), f32)
        for h in range(4):
            turned = rotate_t(query[64 * h : 64 * h + 64], rows)
            both = [turned, nothing] if h < 2 else [nothing, turned]
            q2[h, rows, :] = jnp.concatenate(both, axis=0).T.astype(bf16)
        key = key_value[:, :LANES].T
        key = jnp.concatenate([rotate_t(key[:64], rows), rotate_t(key[64:], rows)], axis=0)
        kt2[:, rows] = key.astype(bf16)
        k2[rows, :] = key.T.astype(bf16)
        value = key_value[:, LANES:]
        v2[rows, :] = value.astype(bf16)
        vt2[:, rows] = value.T.astype(bf16)
        return carry

    scaling = 1.0 / math.sqrt(HEAD_DIM)

    def masked_scores(h, qb):
        keys = ROWS * (qb + 1)
        rows = pl.ds(ROWS * qb, ROWS)
        scores = dot_nt(k2[0:keys, :], q2[h, rows, :]) * scaling
        k_pos = lax.broadcasted_iota(jnp.int32, (keys, ROWS), 0)
        q_pos = lax.broadcasted_iota(jnp.int32, (keys, ROWS), 1) + ROWS * qb
        allowed = (k_pos <= q_pos) & (k_pos < length[0])
        return jnp.where(allowed, scores, NEGATIVE)

    def attend(qb):
        keys = ROWS * (qb + 1)
        rows = pl.ds(ROWS * qb, ROWS)

        def one_head(h, carry):
            scores = masked_scores(h, qb)
            top_s = jnp.max(scores, axis=0, keepdims=True)
            expo = jnp.exp(scores - top_s)
            total = jnp.sum(expo, axis=0, keepdims=True)
            probs = (expo / total).astype(bf16)
            lse[pl.ds(h, 1), rows] = top_s + jnp.log(total)
            v_head = vt2[pl.ds(pl.multiple_of((h // 2) * 64, 64), 64), 0:keys]
            lhs[32 + h // 2, pl.ds(pl.multiple_of((h % 2) * 64, 64), 64), rows] = dot_f(v_head, probs).astype(bf16)
            return carry

        lax.fori_loop(0, 4, one_head, 0)
        for half_c in range(2):
            own_c = pl.ds(pl.multiple_of(tensor * 256 + half_c * 128, 128), 128)
            acc[rows, own_c] = lhs[32 + half_c, :, rows].astype(f32).T
        gather_x(qb).start()
        gather_c(qb).start()

    def mask_rows(b, carry):
        rows = block(b)
        pos = lax.broadcasted_iota(jnp.int32, (ROWS, 256), 0) + b * ROWS
        for c in range(4):
            rhs[c, rows, :] = jnp.where(pos < length[0], rhs[c, rows, :].astype(f32), 0.0).astype(bf16)
        return carry

    near_d = [2 * tensor + j for j in range(2)]
    direct_d = [8 + 4 * core + j for j in range(4)]

    def slab(k):
        return pl.ds(pl.multiple_of(4 * k, 4), 4)

    def d_copy(k, sends, recvs, dev, axis, src=None):
        return remote((ybuf if src is None else src).at[slab(k)], ybuf.at[slab(k)], sends.at[k], recvs.at[k], dev, axis)

    def d_y(k):
        return d_copy(k, dys, dyr, mate, "dp", pbuf)

    def d_c(k):
        return d_copy(k, dcs, dcr, core_mate, "tensor")

    def d_x(k):
        return d_copy(k, dxs, dxr, x_mate, "tensor")

    def d_f(k):
        return d_copy(k, dfs, dfr, core_mate, "tensor")

    def stage_d(k):
        rows = block(k, 64)
        for c in range(4):
            pbuf[4 * k + c] = rhs[c, rows, :].astype(f32)
        d_y(k).start()

    def h_piece(b, t):
        return 4 * b + t

    def h_copy(b, t, sends, recvs, dev, axis):
        part = zbuf.at[slab(h_piece(b, t))]
        return remote(part, part, sends.at[b], recvs.at[b], dev, axis)

    def h_stage(b):
        return 2 * x_mate + b if isinstance(b, int) and b < 2 else 2 * jnp.where(b < 2, x_mate, core_mate) + b % 2

    def h_y(b):
        return remote(
            pbuf.at[slab(h_stage(b))], zbuf.at[slab(h_piece(b, tensor))], hys.at[b], hyr.at[b], mate
        )

    def h_c(b):
        return h_copy(b, tensor, hcs, hcr, core_mate, "tensor")

    def h_x(b):
        return h_copy(b, tensor, hxs, hxr, x_mate, "tensor")

    def h_f(b):
        return h_copy(b, x_mate, hfs, hfr, core_mate, "tensor")

    def h_send(b):
        rows = pl.ds(pl.multiple_of(b * 256 + tensor * 64, 64), 64)
        for c in range(4):
            pbuf[4 * h_stage(b) + c] = hbuf[rows, 256 * c : 256 * c + 256].astype(f32)
        h_y(b).start()

    def h_share(b):
        h_y(b).wait_recv()
        h_x(b).start()
        h_c(b).start()

    def h_forward(b):
        h_x(b).wait_recv()
        h_f(b).start()

    def d_share(j):
        k = near_d[j]
        d_y(k).wait_recv()
        d_x(k).start()
        d_c(k).start()

    def d_forward(j):
        k = 2 * x_mate + j
        d_x(k).wait_recv()
        d_f(k).start()

    def d_direct(j):
        k = direct_d[j]
        d_y(k).wait_recv()
        d_c(k).start()

    wait(token_load + proj_load)
    head_rows(0, 0)
    attend(0)
    head_rows(1, 0)
    w_x.wait_recv()
    w_y.start()
    attend(1)
    head_rows(2, 0)
    w_y.wait_recv()
    w_z.start()
    wait(late_load)
    lax.fori_loop(0, 4, mask_rows, 0)
    for j in range(2):
        stage_d(near_d[j])
    for j in range(2):
        stage_d(direct_d[j])
    attend(2)
    head_rows(3, 0)
    start(expert_load(8 * y, 0))
    attend(3)
    dk_acc[...] = jnp.zeros_like(dk_acc)
    dv_acc[...] = jnp.zeros_like(dv_acc)
    norms[...] = jnp.zeros_like(norms)


    expert_id = lax.broadcasted_iota(jnp.int32, (EXPERTS, 1024), 0)
    alive = lax.broadcasted_iota(jnp.int32, (EXPERTS, 1024), 1) < length[0]
    hits = jnp.zeros((EXPERTS, 1024), f32)
    weight = jnp.zeros((EXPERTS, 1024), f32)
    for k in range(TOP_K):
        same = (picks[k : k + 1, :] == expert_id) & alive
        hits = jnp.where(same, 1.0, hits)
        weight = jnp.where(same, pick_w[k : k + 1, :], weight)
    hits = hits.astype(bf16)
    limit = ((5 * TOP_K * length[0] + 4 * EXPERTS - 1) // (4 * EXPERTS)).astype(f32)
    for b in range(4):
        rows = pl.ds(ROWS * b, ROWS)
        token = lax.broadcasted_iota(jnp.int32, (1024, ROWS), 1) + ROWS * b
        earlier = jnp.where(lax.broadcasted_iota(jnp.int32, (1024, ROWS), 0) < token, 1.0, 0.0).astype(bf16)
        places = dot_f(hits, earlier)
        kept = jnp.where(places < limit, weight[:, ROWS * b : ROWS * b + ROWS], 0.0)
        kept_out[:, rows] = kept
        slot_w[rows, :] = jnp.concatenate([kept, jnp.zeros((LANES - EXPERTS, ROWS), f32)], axis=0).T

    kept_copy = remote(kept_out, kept_in, ks.at[0], kr.at[0], mate)
    kept_copy.start()

    w_z.wait_recv()
    w_f.start()
    w_c.wait_recv()
    w_f.wait_recv()

    def cast_out(b, carry):
        for c in range(4):
            rhs[26 + c, block(b, 64), :] = buf[block(b, 64), 256 * c : 256 * c + 256].astype(bf16)
        return carry

    lax.fori_loop(0, 16, cast_out, 0)

    def forward_rows(b, carry):
        rows = block(b)
        for k in range(4):
            part = acc[rows, 256 * k : 256 * k + 256].astype(bf16)
            if k == 0:
                sums = [
                    hbuf[rows, 256 * col : 256 * col + 256].astype(f32) + dot_f(part, rhs[26 + col, 0:256, :])
                    for col in range(4)
                ]
            else:
                sums = [
                    sums[col] + dot_f(part, rhs[26 + col, 256 * k : 256 * k + 256, :]) for col in range(4)
                ]
        square = sum(jnp.sum(v * v, axis=1, keepdims=True) for v in sums)
        scale_r = lax.rsqrt(square * (1.0 / 1024.0) + EPSILON)
        for col in range(4):
            buf[rows, 256 * col : 256 * col + 256] = sums[col]
            normed = sums[col] * scale_r * gain[0:1, 256 * col : 256 * col + 256]
            hbuf[rows, 256 * col : 256 * col + 256] = normed.astype(bf16)
            for half_c in range(2):
                lhs[16 + 2 * col + half_c, :, rows] = normed[:, 128 * half_c : 128 * half_c + 128].T.astype(bf16)
        return carry

    def expert_of(k):
        return jnp.where(k < 16, 8 * y + k % 8, 8 * (1 - y) + k % 8)

    def next_weights(k):
        wait(expert_load(expert_of(k), k % 2))

        @pl.when(k < 23)
        def _():
            start(expert_load(expert_of(k + 1), (k + 1) % 2))

    def unit(k, b, kind):
        rows = block(b)
        s = k % 2
        e = expert_of(k)
        el = k % 8
        if kind == "mate":
            both = dot_f(rhs[26, rows, :], wgu[s, 0:256, :])
            for c in range(1, 4):
                both = both + dot_f(rhs[26 + c, rows, :], wgu[s, 256 * c : 256 * c + 256, :])
        else:
            both = dot_f(hbuf[rows, :], wgu[s])
        d_base = 12 if kind == "mate" else 0
        gate, up = both[:, :LANES], both[:, LANES:]
        d_raw = dot_nt(rhs[d_base, rows, :], wdb[s, :, 0:256])
        for c in range(1, 4):
            d_raw = d_raw + dot_nt(rhs[d_base + c, rows, :], wdb[s, :, 256 * c : 256 * c + 256])
        lane = lax.broadcasted_iota(jnp.int32, (ROWS, LANES), 1)
        weights = slot_m if kind == "mate" else slot_w
        weight = jnp.sum(jnp.where(lane == e, weights[rows, :], 0.0), axis=1, keepdims=True)
        sigma = 1.0 / (1.0 + jnp.exp(-gate))
        silu = gate * sigma
        hidden = silu * up
        hidden_t = (hidden * weight).T.astype(bf16)
        d_hidden = d_raw * weight
        d_gate = (d_hidden * up * sigma * (1.0 + gate * (1.0 - sigma))).astype(bf16)
        d_up = (d_hidden * silu).astype(bf16)
        if kind == "mate":
            lhs[42 + el, :, rows] = hidden_t
            rhs[16 + el, rows, 0:LANES] = d_gate
            rhs[16 + el, rows, LANES:] = d_up
            return
        lhs[e, :, rows] = hidden_t
        inner = jnp.sum(hidden * d_raw, axis=1, keepdims=True)
        inner = jnp.where(weight > 0.0, inner, 0.0)
        is_first = kind == "first"
        acc[rows, 1024:1152] = jnp.where(lane == e, inner, 0.0 if is_first else acc[rows, 1024:1152])
        if kind == "other":
            part = dot_nt(jnp.concatenate([d_gate, d_up], axis=1), wgu[s])
        else:
            rhs[4 + el, rows, 0:LANES] = d_gate
            rhs[4 + el, rows, LANES:] = d_up
            part = dot_nt(rhs[4 + el, rows, :], wgu[s])
        acc[rows, 0:1024] = part if is_first else acc[rows, 0:1024] + part

    def units(k, begin, count, kind):
        def step(b, carry):
            unit(k, b, kind)
            return carry

        lax.fori_loop(begin, begin + count, step, 0)

    def forward_step(b, carry):
        @pl.when(b < 4)
        def _():
            gather_x(b).wait_recv()
            gather_f(b).start()

        @pl.when(b > 0)
        def _():
            gather_c(b - 1).wait_recv()
            gather_f(b - 1).wait_recv()
            gather_f(b - 1).wait_send()
            gather_x(b - 1).wait_send()
            gather_c(b - 1).wait_send()
            forward_rows(b - 1, 0)
            h_send(b - 1)
            unit(0, b - 1, "first")

        @pl.when(b == 4)
        def _():
            d_share(0)
            d_share(1)
            stage_d(direct_d[2])
            stage_d(direct_d[3])

        return carry

    for copy in (w_x, w_c, w_f, w_y, w_z):
        copy.wait_send()
    next_weights(0)
    lax.fori_loop(0, 5, forward_step, 0)
    keep = local(buf.at[:, wide], s_resid, iosem.at[0])
    keep.start()

    chores = {
        5: [(h_share, 0)],
        8: [(d_direct, 0), (d_direct, 1)],
        11: [(h_share, 1)],
        13: [(h_forward, 0), (d_forward, 0)],
        16: [(h_share, 2), (d_forward, 1)],
        20: [(h_forward, 1)],
        23: [(h_share, 3)],
        26: [(h_forward, 2)],
        29: [(d_direct, 2)],
        31: [(h_forward, 3), (d_direct, 3)],
    }

    def own_unit(u, carry):
        k = u // 4

        @pl.when(u % 4 == 0)
        def _():
            next_weights(k)

        unit(k, u % 4, "own")
        for when_u, jobs in chores.items():

            @pl.when(u == when_u)
            def _(jobs=jobs):
                for job, arg in jobs:
                    job(arg)

        return carry

    lax.fori_loop(4, 32, own_unit, 0)

    kept_copy.wait_recv()
    for b in range(4):
        rows = pl.ds(ROWS * b, ROWS)
        slot_m[rows, :] = jnp.concatenate(
            [kept_in[:, rows], jnp.zeros((LANES - EXPERTS, ROWS), f32)], axis=0
        ).T
    other_core = tensor - core + (1 - core)
    for j in range(2):
        d_c(2 * other_core + j).wait_recv()
        d_f(2 * (3 - tensor) + j).wait_recv()
    for j in range(4):
        d_c(8 + 4 * (1 - core) + j).wait_recv()
    for b in range(4):
        h_c(b).wait_recv()
        h_f(b).wait_recv()

    def take_d(k, carry):
        for c in range(4):
            rhs[12 + c, block(k, 64), :] = ybuf[4 * k + c].astype(bf16)
        return carry

    def take_h(b, carry):
        rows = block(b)
        for c in range(4):
            whole = jnp.concatenate([zbuf[4 * (4 * b + t) + c] for t in range(4)], axis=0)
            rhs[26 + c, rows, :] = whole.astype(bf16)
            for half_c in range(2):
                lhs[34 + 2 * c + half_c, :, rows] = whole[:, 128 * half_c : 128 * half_c + 128].T.astype(bf16)
        return carry

    lax.fori_loop(0, 16, take_d, 0)
    lax.fori_loop(0, 4, take_h, 0)
    next_weights(8)
    units(8, 0, 4, "mate")
    kept_copy.wait_send()
    for j in range(2):
        d_y(near_d[j]).wait_send()
        d_x(near_d[j]).wait_send()
        d_c(near_d[j]).wait_send()
        d_f(2 * x_mate + j).wait_send()
    for j in range(4):
        d_y(direct_d[j]).wait_send()
        d_c(direct_d[j]).wait_send()
    for b in range(4):
        h_y(b).wait_send()
        h_x(b).wait_send()
        h_c(b).wait_send()
        h_f(b).wait_send()

    pl.semaphore_signal(go, inc=1, device_id={"dp": mate}, device_id_type=MESH)

    @pl.when(z < last)
    def _():
        pl.semaphore_signal(go, inc=1, device_id={"dp": up_id}, device_id_type=MESH)

    @pl.when(z > 0)
    def _():
        pl.semaphore_signal(go, inc=1, device_id={"dp": dn_id}, device_id_type=MESH)

    pl.semaphore_wait(go, 1 + (z < last).astype(jnp.int32) + (z > 0).astype(jnp.int32))

    def half_pass(u):
        k = 9 + u // 2
        begin = (u % 2) * 2

        @pl.when(begin == 0)
        def _():
            next_weights(k)

        @pl.when(k < 16)
        def _():
            units(k, begin, 2, "mate")

        @pl.when(k >= 16)
        def _():
            units(k, begin, 2, "other")

    mine = pl.ds(pl.multiple_of(core * 512, 512), 512)
    other = pl.ds(pl.multiple_of((1 - core) * 512, 512), 512)

    def span(k):
        return pl.ds(0, 1152 if k == 0 else 1024)

    def sum_a(k):
        return remote(acc.at[other, span(k)], buf.at[pl.ds(0, 512), span(k)], s1s.at[k], s1r.at[k], core_mate, "tensor")

    def sum_b(k):
        return remote(acc.at[mine, span(k)], buf.at[pl.ds(512, 512), span(k)], s2s.at[k], s2r.at[k], x_mate, "tensor")

    def sum_c(k):
        part = acc.at[mine, span(k)]
        return remote(part, part, s3s.at[k], s3r.at[k], core_mate, "tensor")

    def add_in(k, at_row):
        def step(b, carry):
            rows = pl.ds(pl.multiple_of(core * 512 + b * 64, 64), 64)
            acc[rows, span(k)] += buf[pl.ds(pl.multiple_of(at_row + b * 64, 64), 64), span(k)]
            return carry

        lax.fori_loop(0, 8, step, 0)

    def sum_first(k):
        pl.semaphore_signal(ready1.at[k], inc=1, device_id={"tensor": core_mate}, device_id_type=MESH)
        pl.semaphore_signal(ready2.at[k], inc=1, device_id={"tensor": x_mate}, device_id_type=MESH)
        pl.semaphore_wait(ready1.at[k], 1)
        sum_a(k).start()

    def sum_second(k):
        sum_a(k).wait_recv()
        add_in(k, 0)
        sum_a(k).wait_send()
        pl.semaphore_signal(ready3.at[k], inc=1, device_id={"tensor": core_mate}, device_id_type=MESH)
        pl.semaphore_wait(ready2.at[k], 1)
        sum_b(k).start()

    def sum_third(k):
        sum_b(k).wait_recv()
        sum_b(k).wait_send()
        add_in(k, 512)
        pl.semaphore_wait(ready3.at[k], 1)
        sum_c(k).start()

    def sum_last(k):
        sum_c(k).wait_recv()
        sum_c(k).wait_send()

    def norm_sum(step, dev):
        return remote(norms.at[pl.ds(0, 16)], norm_in.at[step], ns.at[step], nr.at[step], dev)

    partners = (mate, pair, far)

    def norm_next(step):
        if step > 0:
            norm_sum(step - 1, partners[step - 1]).wait_recv()
            norm_sum(step - 1, partners[step - 1]).wait_send()
            norms[...] = norms[...] + norm_in[step - 1]
        if step < 3:
            norm_sum(step, partners[step]).start()

    def norm_back(values, scale_r, grads, which):
        inner = sum(
            jnp.sum(v * scale_r * (g * gain[which : which + 1, 256 * c : 256 * c + 256]), axis=1, keepdims=True)
            for c, (v, g) in enumerate(zip(values, grads))
        ) * (1.0 / 1024.0)
        outs = []
        for c, (v, g) in enumerate(zip(values, grads)):
            normed = v * scale_r
            total = jnp.sum(g * normed, axis=0, keepdims=True)
            row = 8 * which + 2 * c
            norms[row : row + 1, :] += total[:, :LANES]
            norms[row + 1 : row + 2, :] += total[:, LANES:]
            outs.append(scale_r * (g * gain[which : which + 1, 256 * c : 256 * c + 256] - normed * inner))
        return outs

    def middle_rows(b):
        rows = block(b)

        values = [buf[rows, 256 * c : 256 * c + 256] for c in range(4)]
        grads = [acc[rows, 256 * c : 256 * c + 256] for c in range(4)]
        square = sum(jnp.sum(v * v, axis=1, keepdims=True) for v in values)
        scale_r = lax.rsqrt(square * (1.0 / 1024.0) + EPSILON)
        back = norm_back(values, scale_r, grads, 0)
        for c in range(4):
            total = rhs[c, rows, :].astype(f32) + back[c]
            acc[rows, 256 * c : 256 * c + 256] = total
            rhs[26 + c, rows, :] = total.astype(bf16)
        for h in range(4):
            d_head = dot_nt(rhs[26, rows, :], wdb[h, :, 0:256])
            for c in range(1, 4):
                d_head = d_head + dot_nt(rhs[26 + c, rows, :], wdb[h, :, 256 * c : 256 * c + 256])
            da2[h, rows, :] = d_head.astype(bf16)

    def turn_back(grad, cols):
        one, two = grad[:32], grad[32:]
        cosine, sine = cos_t[:, cols], sin_t[:, cols]
        return jnp.concatenate([one * cosine + two * sine, two * cosine - one * sine], axis=0)

    def attend_back(h, qb):
        keys = ROWS * (qb + 1)
        rows = pl.ds(ROWS * qb, ROWS)
        q_rows = q2[h, rows, :]
        d_rows = da2[h, rows, :]
        exact = jnp.exp(masked_scores(h, qb) - lse[pl.ds(h, 1), rows])
        d_probs = dot_nt(v2[0:keys, :], d_rows)
        inner = jnp.sum(exact * d_probs, axis=0, keepdims=True)
        d_scores = (exact * (d_probs - inner)).astype(bf16)
        dk_acc[0:keys, :] += dot_f(d_scores, q_rows)
        dv_acc[0:keys, :] += dot_f(exact.astype(bf16), d_rows)
        k_head = kt2[pl.ds(pl.multiple_of((h // 2) * 64, 64), 64), 0:keys]
        d_q = dot_f(k_head, d_scores) * scaling
        buf[pl.ds(pl.multiple_of(h * 64, 64), 64), rows] = turn_back(d_q, rows)

    def turn_rows(b):
        rows = block(b)
        rhs[24, rows, :] = buf[0:256, rows].T.astype(bf16)
        d_k = (dk_acc[rows, :] * scaling).T
        d_k = jnp.concatenate([turn_back(d_k[:64], rows), turn_back(d_k[64:], rows)], axis=0)
        rhs[25, rows, 0:LANES] = d_k.T.astype(bf16)
        rhs[25, rows, LANES:] = dv_acc[rows, :].astype(bf16)

    def project_rows(b):
        rows = block(b)
        acc[rows, 0:1024] = dot_nt(rhs[24, rows, :], wgu[0]) + dot_nt(rhs[25, rows, :], wgu[1])

    def token_rows(b):
        rows = block(b)

        values = [hbuf[rows, 256 * c : 256 * c + 256].astype(f32) for c in range(4)]
        grads = [acc[rows, 256 * c : 256 * c + 256] for c in range(4)]
        square = sum(jnp.sum(v * v, axis=1, keepdims=True) for v in values)
        scale_r = lax.rsqrt(square * (1.0 / 1024.0) + EPSILON)
        back = norm_back(values, scale_r, grads, 1)
        for c in range(4):
            cols = slice(256 * c, 256 * c + 256)
            hbuf[rows, cols] = (buf[rows, cols] + back[c]).astype(bf16)

    def pair_load(pair, s):
        return local(w_down.at[pl.ds(2 * pair, 2)], wdb.at[pl.ds(2 * s, 2)], wsem.at[s, 2])

    def moe_pair(pair):
        s = pair % 2
        pair_load(pair, s).wait()

        @pl.when(pair + 1 < EXPERTS // 2)
        def _():
            pair_load(pair + 1, 1 - s).start()

        def rows_of(b, carry):
            rows = block(b)
            hidden = lhs[pl.ds(2 * pair, 2), :, rows].reshape(256, ROWS)
            down = wdb[pl.ds(2 * s, 2)].reshape(256, 1024)
            part = dot_tn(hidden, down)

            @pl.when(pair == 0)
            def _():
                acc[rows, 0:1024] = part

            @pl.when(pair > 0)
            def _():
                acc[rows, 0:1024] += part

            return carry

        lax.fori_loop(0, 4, rows_of, 0)

    def result_rows(b):
        rows = block(b)

        pos = lax.broadcasted_iota(jnp.int32, (ROWS, 1024), 0) + b * ROWS
        total = buf[rows, wide] + acc[rows, 0:1024]
        hbuf[rows, :] = jnp.where(pos < length[0], total, 0.0).astype(bf16)

    def halves_in(src):
        return [local(src, buf.at[:, wide], iosem.at[1])]

    tokens_in = [local(x_in, hbuf, iosem.at[3])]
    wo_load = [
        local(w_out.at[pl.ds(64 * h, 64)], wdb.at[h, pl.ds(64 * (h // 2), 64)], ld.at[8 + h]) for h in range(4)
    ]
    dots_out = [local(d_pick, o_dots, iosem.at[7])]
    norms_out = [
        local(norms.at[pl.ds(0, 8)], o_norm0, iosem.at[2]),
        local(norms.at[pl.ds(8, 8)], o_norm1, iosem.at[4]),
    ]

    def pick_dots():
        for b in range(4):
            rows = pl.ds(ROWS * b, ROWS)
            dots = acc[rows, 1024:1152].T[:EXPERTS]
            lane_e = lax.broadcasted_iota(jnp.int32, (EXPERTS, ROWS), 0)
            for k in range(TOP_K):
                mine_k = jnp.where(picks[k : k + 1, rows] == lane_e, dots, 0.0)
                d_pick[k : k + 1, rows] = jnp.sum(mine_k, axis=0, keepdims=True)
    dres_out = [local(acc.at[:, wide], s_dres, iosem.at[8])]
    tokens_out = [local(hbuf, o_tokens, iosem.at[9])]
    result_out = [local(hbuf, o_result, iosem.at[10])]

    def clear_wo():
        for h in range(4):
            wdb[h, 64 - 64 * (h // 2) : 128 - 64 * (h // 2), :] = jnp.zeros((64, 1024), bf16)

    def do_all(*steps):
        for step in steps:
            step()

    once = {
        T_SUM1: lambda: do_all(keep.wait, lambda: sum_first(0), clear_wo, lambda: start(tokens_in + wo_load + proj_load)),
        T_SUM1 + 2: lambda: do_all(lambda: sum_second(0), lambda: wait(tokens_in)),
        T_MID1 - 3: lambda: sum_third(0),
        T_MID1 - 1: lambda: do_all(
            lambda: sum_last(0), pick_dots, lambda: start(halves_in(s_resid) + dots_out), lambda: wait(wo_load)
        ),
        T_ATT: lambda: do_all(lambda: wait(dots_out), lambda: start(dres_out)),
        T_PROJ - 1: lambda: do_all(lambda: wait(dres_out), lambda: wait(proj_load)),
        T_SUM2: lambda: sum_first(1),
        T_SUM2 + 2: lambda: sum_second(1),
        T_TOK - 3: lambda: sum_third(1),
        T_TOK - 1: lambda: do_all(
            lambda: sum_last(1), lambda: start(halves_in(s_dres)), lambda: start([pair_load(0, 0)])
        ),
        T_MOE: lambda: do_all(lambda: start(tokens_out), lambda: norm_next(0)),
        T_MOE + 2: lambda: norm_next(1),
        T_MOE + 4: lambda: norm_next(2),
        T_MOE + 6: lambda: do_all(lambda: norm_next(3), lambda: start(norms_out)),
        T_SUM3: lambda: do_all(lambda: wait(tokens_out + norms_out), lambda: sum_first(2)),
        T_SUM3 + 2: lambda: sum_second(2),
        T_RES - 3: lambda: sum_third(2),
        T_RES - 1: lambda: do_all(lambda: sum_last(2), lambda: start(halves_in(s_resid))),
        T_RES + 4: lambda: start(result_out),
        T_RES + 8: lambda: wait(result_out),
    }
    halves_wait = {T_MID1: s_resid, T_TOK: s_dres, T_RES: s_resid}

    def work(t):
        for when_t, fn in sorted(once.items()):
            pl.when(t == when_t)(fn)
        for when_t, src in halves_wait.items():
            pl.when(t == when_t)(lambda src=src: wait(halves_in(src)))
        for begin, count, fn in (
            (0, 30, half_pass),
            (T_MID1, 4, middle_rows),
            (T_TURN, 4, turn_rows),
            (T_PROJ, 4, project_rows),
            (T_TOK, 4, token_rows),
            (T_MOE, EXPERTS // 2, moe_pair),
            (T_RES, 4, result_rows),
        ):
            pl.when((t >= begin) & (t < begin + count))(lambda fn=fn, begin=begin: fn(t - begin))
        for pair_b in range(2):
            u = t - T_ATT

            def two(pair_b=pair_b, u=u):
                attend_back(u // 2, pair_b)
                attend_back(u // 2, 3 - pair_b)

            pl.when((u >= 0) & (u < 8) & (u % 2 == pair_b))(two)

    own = pl.ds(pl.multiple_of(y * 32, 32), 32)
    oth = pl.ds(pl.multiple_of((1 - y) * 32, 32), 32)
    half = pl.ds(0, 32)
    upper = pl.ds(32, 32)

    def stage(c, t):
        p = z if c == 0 else last - z
        nxt, prv = (up_id, dn_id) if c == 0 else (dn_id, up_id)
        def at(delay, body):
            i = t - delay

            @pl.when((i >= 0) & (i < N_CLASS))
            def _():
                s = c * ring + i % ring
                body(i, s, i < N_EXPERT, (i >= N_EXPERT) & (i % 2 == 0), (i >= N_EXPERT) & (i % 2 == 1))

        def ycopy_a(s):
            return remote(pbuf.at[s, oth], ybuf.at[s, half], ys.at[s], yr.at[s], mate)

        def ycopy_b(s):
            return remote(zbuf.at[s], ybuf.at[s], ys.at[s], yr.at[s], mate)

        def zcopy_a(s):
            return remote(zbuf.at[s, half], zbuf.at[s, half], zs.at[s], zr.at[s], nxt)

        def zcopy(s):
            return remote(zbuf.at[s], zbuf.at[s], zs.at[s], zr.at[s], nxt)

        def fcopy_a(s):
            return remote(pbuf.at[s, own], pbuf.at[s, own], fs.at[s], fr.at[s], prv)

        def fcopy(s):
            return remote(pbuf.at[s], pbuf.at[s], fs.at[s], fr.at[s], prv)

        def gcopy_a(s):
            return remote(pbuf.at[s, own], ybuf.at[s, upper], gs.at[s], gr.at[s], mate)

        def gcopy(s):
            return remote(pbuf.at[s], ybuf.at[s], gs.at[s], gr.at[s], mate)

        def first(i, s, is_e, is_a, is_b):
            m = i // 2
            g = 2 * m + c

            @pl.when((i % 2 == 0) & is_e)
            def _():
                el, part = g // 12, g % 12
                down = part < 4
                l_one = jnp.where(down, 8 * y + el, 12 + part)
                r_one = jnp.where(down, part, 4 + el)
                l_two = jnp.where(down, 42 + el, 30 + part)
                r_two = jnp.where(down, 12 + part, 16 + el)
                total = dot_f(lhs[l_one], rhs[r_one]) + dot_f(lhs[l_two], rhs[r_two])
                pbuf[s] = total[:CHUNK]
                pbuf[s + 1] = total[CHUNK:]

            @pl.when((i % 2 == 0) & jnp.logical_not(is_e))
            def _():
                a = g - N_EXPERT
                l_one = jnp.where(a < 8, 32 + a // 4, 24 + a % 8)
                r_one = jnp.where(a < 8, 26 + a % 4, 23 + a // 8)
                total = dot_f(lhs[l_one], rhs[r_one])
                pbuf[s] = total[:CHUNK]
                pbuf[s + 1] = total[CHUNK:]

            @pl.when(is_a)
            def _():
                ycopy_a(s).start()

        def second(i, s, is_e, is_a, is_b):
            @pl.when(is_a)
            def _():
                ycopy_a(s).wait_recv()

                @pl.when(p > 0)
                def _():
                    zcopy_a(s).wait_recv()
                    zbuf[s, half] = zbuf[s, half] + (pbuf[s, own] + ybuf[s, half])

                @pl.when(p == 0)
                def _():
                    zbuf[s, half] = pbuf[s, own] + ybuf[s, half]

                @pl.when(p < last)
                def _():
                    zcopy_a(s).start()

                @pl.when(p == last)
                def _():
                    pbuf[s, own] = zbuf[s, half]
                    fcopy_a(s).start()
                    gcopy_a(s).start()

            @pl.when(jnp.logical_not(is_a))
            def _():
                @pl.when(p > 0)
                def _():
                    zcopy(s).wait_recv()
                    zbuf[s] = zbuf[s] + pbuf[s]

                @pl.when(p == 0)
                def _():
                    zbuf[s] = pbuf[s]

                @pl.when(p < last)
                def _():
                    zcopy(s).start()

                @pl.when((p == last) & is_e)
                def _():
                    pbuf[s] = zbuf[s]
                    fcopy(s).start()
                    gcopy(s).start()

                @pl.when((p == last) & is_b)
                def _():
                    ycopy_b(s).start()

        def third(i, s, is_e, is_a, is_b):
            @pl.when(is_b & (p == last))
            def _():
                ycopy_b(s).wait_recv()
                pbuf[s] = zbuf[s] + ybuf[s]
                fcopy(s).start()

        def fourth(i, s, is_e, is_a, is_b):
            @pl.when(p < last)
            def _():
                @pl.when(is_a)
                def _():
                    fcopy_a(s).wait_recv()

                    @pl.when(p > 0)
                    def _():
                        fcopy_a(s).start()

                    gcopy_a(s).start()

                @pl.when(jnp.logical_not(is_a))
                def _():
                    fcopy(s).wait_recv()

                    @pl.when(p > 0)
                    def _():
                        fcopy(s).start()

                    @pl.when(is_e)
                    def _():
                        gcopy(s).start()

        def store(buf_s, sem, dst0, dst1):
            local(buf_s.at[:, pl.ds(0, LANES)], dst0, sem).start()
            local(buf_s.at[:, pl.ds(LANES, LANES)], dst1, sem).start()

        def fifth(i, s, is_e, is_a, is_b):
            @pl.when(is_a)
            def _():
                gcopy_a(s).wait_recv()
                ycopy_a(s).wait_send()
                pbuf[s, oth] = ybuf[s, upper]

            @pl.when(is_e)
            def _():
                gcopy(s).wait_recv()

            g = 2 * (i // 2) + c
            el, part = g // 12, g % 12
            a = g - N_EXPERT
            low = CHUNK * (i % 2)

            def at_rows(start_row):
                return pl.ds(pl.multiple_of(start_row + low, CHUNK), CHUNK)

            def both_rows(write):
                write(pbuf.at[s], os0.at[s], 8 * y + el)
                write(ybuf.at[s], os1.at[s], 8 * (1 - y) + el)

            @pl.when(is_e & (part < 4))
            def _():
                col = pl.ds(pl.multiple_of(part * 256, LANES), LANES)
                col1 = pl.ds(pl.multiple_of(part * 256 + LANES, LANES), LANES)
                both_rows(
                    lambda src, sem, e: store(
                        src, sem, o_down.at[e, at_rows(0), col], o_down.at[e, at_rows(0), col1]
                    )
                )

            @pl.when(is_e & (part >= 4))
            def _():
                rows = at_rows((part - 4) * 128)
                both_rows(lambda src, sem, e: store(src, sem, o_gate.at[e, rows], o_up.at[e, rows]))

            @pl.when(jnp.logical_not(is_e) & (a < 8))
            def _():
                rows = at_rows((a // 4) * 128)
                col = pl.ds(pl.multiple_of((a % 4) * 256, LANES), LANES)
                col1 = pl.ds(pl.multiple_of((a % 4) * 256 + LANES, LANES), LANES)
                store(pbuf.at[s], os0.at[s], o_out.at[rows, col], o_out.at[rows, col1])

            @pl.when(jnp.logical_not(is_e) & (a >= 8) & (a < 16))
            def _():
                rows = at_rows((a - 8) * 128)
                store(pbuf.at[s], os0.at[s], o_q.at[rows, pl.ds(0, LANES)], o_q.at[rows, pl.ds(LANES, LANES)])

            @pl.when(jnp.logical_not(is_e) & (a >= 16))
            def _():
                rows = at_rows((a - 16) * 128)
                store(pbuf.at[s], os0.at[s], o_k.at[rows], o_v.at[rows])

        def sixth(i, s, is_e, is_a, is_b):
            local(pbuf.at[s], o_q.at[pl.ds(0, CHUNK)], os0.at[s]).wait()

            @pl.when(is_e)
            def _():
                local(ybuf.at[s], o_q.at[pl.ds(0, CHUNK)], os1.at[s]).wait()
                gcopy(s).wait_send()

            @pl.when(is_a)
            def _():
                gcopy_a(s).wait_send()

                @pl.when(p < last)
                def _():
                    zcopy_a(s).wait_send()

                @pl.when(p > 0)
                def _():
                    fcopy_a(s).wait_send()

            @pl.when(jnp.logical_not(is_a))
            def _():
                @pl.when(p < last)
                def _():
                    zcopy(s).wait_send()

                @pl.when((p == last) & is_b)
                def _():
                    ycopy_b(s).wait_send()

                @pl.when(p > 0)
                def _():
                    fcopy(s).wait_send()

        t2 = hop * (1 + p)
        t3 = hop * (2 + last)
        t4 = t3 + hop * (last - p)
        t5 = t4 + hop
        t6 = t5 + hop
        return [(0, first, at), (t2, second, at), (t3, third, at), (t4, fourth, at), (t5, fifth, at), (t6, sixth, at)]

    def body(t, carry):
        both = [stage(0, t), stage(1, t)]
        for k in (1, 2, 3, 4, 5, 0):
            if k == 0:
                work(t)
            for st in both:
                delay, fn, at = st[k]
                at(delay, fn)
        return carry

    total = N_CLASS + hop * (2 * last + 4) + 1
    lax.fori_loop(0, total, body, 0)


def run_layer(mesh, *operands):
    groups = mesh.shape["dp"]
    nz = 4 if groups % 8 == 0 else groups // 2
    last = nz - 1
    hop = HOP
    ring = hop * (2 * last + 4) + 2
    ring = max(32, ring + ring % 2)
    f32, bf16 = jnp.float32, jnp.bfloat16

    def out(shape, kind=f32):
        return jax.ShapeDtypeStruct(shape, kind)

    outs = [
        out((16, 1024, 128)), out((16, 1024, 128)), out((16, 128, 1024)),
        out((1024, 256)), out((1024, 128)), out((1024, 128)), out((256, 1024)), out((8, 128)), out((8, 128)),
        out((1024, 1024), bf16), out((1024, 1024), bf16), out((8, 1024)),
        out((1024, 1024)), out((1024, 1024)),
    ]
    anywhere = pl.BlockSpec(memory_space=pl.ANY)
    dma = pltpu.SemaphoreType.DMA
    reg = pltpu.SemaphoreType.REGULAR
    vmem = pltpu.VMEM
    res = pl.pallas_call(
        functools.partial(layer_kernel, nz, hop, ring),
        out_shape=outs,
        in_specs=[pl.BlockSpec(memory_space=pltpu.SMEM)] + [anywhere] * (len(operands) - 1),
        out_specs=[anywhere] * len(outs),
        scratch_shapes=[
            vmem((50, 128, 1024), bf16), vmem((30, 1024, 256), bf16),
            vmem((2 * ring, CHUNK, 256), f32), vmem((2 * ring, CHUNK, 256), f32), vmem((2 * ring, CHUNK, 256), f32),
            vmem((1024, 1152), f32), vmem((1024, 1152), f32),
            vmem((1024, 1024), bf16), vmem((2, 1024, 256), bf16), vmem((4, 128, 1024), bf16),
            vmem((4, 1024, 128), bf16), vmem((1024, 128), bf16), vmem((1024, 128), bf16),
            vmem((128, 1024), bf16), vmem((128, 1024), bf16),
            vmem((8, 1024), f32), vmem((32, 1024), f32), vmem((32, 1024), f32),
            vmem((4, 1024, 128), bf16), vmem((1024, 128), f32), vmem((1024, 128), f32),
            vmem((1024, 128), f32), vmem((8, 1024), f32), vmem((16, 128), f32),
            vmem((8, 1024), jnp.int32), vmem((8, 1024), f32),
            vmem((3, 16, 128), f32), vmem((8, 1024), f32),
            vmem((EXPERTS, 1024), f32), vmem((EXPERTS, 1024), f32), vmem((1024, 128), f32),
            dma((18,)), dma((2, 3)), dma((11,)),
        ]
        + [dma((2 * ring,))] * 10
        + [dma((4,))] * 6
        + [dma((5,))] * 2
        + [dma((3,))] * 6
        + [reg((3,))] * 3
        + [dma((3,))] * 2
        + [reg]
        + [dma((4,))] * 8
        + [dma((16,))] * 8
        + [dma((1,))] * 2,
        compiler_params=pltpu.CompilerParams(
            collective_id=0, has_side_effects=True, vmem_limit_bytes=63 * 2**20
        ),
    )(*operands)
    sums, rest = tuple(res[:9]), res[9:12]
    if groups > 2 * nz:
        same = [
            [2 * nz * block + place for block in range(groups // (2 * nz))] for place in range(2 * nz)
        ]
        sums = lax.psum(sums, "dp", axis_index_groups=same)
    return sums, rest


def per_device(
    mesh,
    tokens,
    lengths,
    chosen,
    gate_values,
    cotangent,
    norm_attn,
    w_query,
    w_key,
    w_value,
    w_out,
    norm_moe,
    w_gate,
    w_up,
    w_down,
):
    seq_len = tokens.shape[0] // lengths.shape[0]
    cosine, sine = rope_tables(seq_len, HEAD_DIM)
    sums, (result, grad_tokens, dots) = run_layer(
        mesh,
        lengths,
        tokens,
        cotangent,
        chosen.T,
        gate_values.T,
        norm_attn[None, :],
        norm_moe[None, :],
        w_gate,
        w_up,
        w_down,
        cosine,
        sine,
        w_out,
        w_query,
        w_key,
        w_value,
    )
    grad_gate, grad_up, grad_down, grad_query, grad_key, grad_value, grad_out, grad_norm_moe, grad_norm_attn = sums
    return (
        result,
        grad_tokens,
        dots.T,
        grad_norm_attn.reshape(-1),
        grad_query,
        grad_key,
        grad_value,
        grad_out,
        grad_norm_moe.reshape(-1),
        grad_gate,
        grad_up,
        grad_down,
    )


def solution(mesh):
    placed = (
        P("dp", None),
        P("dp"),
        P("dp", None),
        P("dp", None),
        P("dp", None),
        P(),
        P(None, "tensor"),
        P(None, "tensor"),
        P(None, "tensor"),
        P("tensor", None),
        P(),
        P(None, None, "tensor"),
        P(None, None, "tensor"),
        P(None, "tensor", None),
    )
    return jax.shard_map(
        functools.partial(per_device, mesh),
        mesh=mesh,
        in_specs=placed,
        out_specs=(
            P("dp", None),
            P("dp", None),
            P("dp", None),
            P(),
            P(None, "tensor"),
            P(None, "tensor"),
            P(None, "tensor"),
            P("tensor", None),
            P(),
            P(None, None, "tensor"),
            P(None, None, "tensor"),
            P(None, "tensor", None),
        ),
        check_vma=False,
    )
```

```python
import functools
import math

import jax
import jax.numpy as jnp
import numpy as np
from jax import lax
from jax.experimental import pallas as pl
from jax.experimental.pallas import tpu as pltpu
from jax.sharding import PartitionSpec as P

MESH = pl.DeviceIdType.MESH

HEAD_DIM = 64
TOP_K = 8
EXPERTS = 16


EPSILON = 1e-05
THETA = 10000.0
NEGATIVE = -1e30


def dot_f(left, right):
    return jnp.dot(left, right, preferred_element_type=jnp.float32)


def rope_tables(positions, width):
    half_w = width // 2
    freqs = THETA ** (-np.arange(half_w, dtype=np.float64) * 2.0 / width)
    angles = freqs[:, None] * np.arange(positions, dtype=np.float64)[None, :]
    return (np.cos(angles).astype(np.float32), np.sin(angles).astype(np.float32))


LANES = 128
ROWS = 256
CHUNK = 64
N_EXPERT = 96
N_CLASS = 120
HOP = 2
HALF = EXPERTS // 2
T_SUM1 = 30
T_MID1 = 56
T_ATT = 60
T_TURN = 68
T_PROJ = 70
T_SUM2 = 72
T_TOK = 96
T_MOE = 98
T_SUM3 = 102
T_RES = 126


def dot_nt(left, right):
    return lax.dot_general(
        left, right, (((1,), (1,)), ((), ())), preferred_element_type=jnp.float32
    )


def dot_tn(left, right):
    return lax.dot_general(
        left, right, (((0,), (0,)), ((), ())), preferred_element_type=jnp.float32
    )


def layer_kernel(
    nz, hop, ring,
    length, x_in, d_out, chosen, gates, gain_attn, gain_moe, w_gate, w_up, w_down,
    cos_in, sin_in, w_out, w_query, w_key, w_value,
    o_gate, o_up, o_down, o_q, o_k, o_v, o_out, o_norm0, o_norm1, o_result, o_tokens, o_dots, s_resid, s_dres,
    lhs, rhs, pbuf, zbuf, ybuf, acc, buf, hbuf, wgu, wdb, q2, k2, v2, kt2, vt2, lse, cos_t, sin_t,
    da2, dk_acc, dv_acc, slot_w, gain, norms, picks, pick_w, norm_in, d_pick, kept_out, kept_in, slot_m,
    ld, wsem, iosem, ys, yr, zs, zr, fs, fr, gs, gr, os0, os1,
    cs_c, cr_c, cs_x, cr_x, cs_f, cr_f, ws, wr, s1s, s1r, s2s, s2r, s3s, s3r, ready1, ready2, ready3, ns, nr, go,
    hys, hyr, hcs, hcr, hxs, hxr, hfs, hfr, dys, dyr, dcs, dcr, dxs, dxr, dfs, dfr, ks, kr,
):
    f32, bf16 = jnp.float32, jnp.bfloat16
    dp = lax.axis_index("dp")
    tensor = lax.axis_index("tensor")
    base = dp - dp % (2 * nz)
    z, y = (dp % (2 * nz)) // 2, dp % 2
    last = nz - 1
    mate = base + z * 2 + (1 - y)
    up_id = base + jnp.minimum(z + 1, last) * 2 + y
    dn_id = base + jnp.maximum(z - 1, 0) * 2 + y
    far = base + ((z + 2) % nz) * 2 + y
    core = tensor % 2
    core_mate = tensor - core + (1 - core)
    x_mate = (tensor + 2) % 4

    def local(src, dst, sem):
        return pltpu.make_async_copy(src, dst, sem)

    def remote(src, dst, ssem, rsem, dev, axis="dp"):
        return pltpu.make_async_remote_copy(
            src_ref=src, dst_ref=dst, send_sem=ssem, recv_sem=rsem,
            device_id={axis: dev}, device_id_type=MESH,
        )

    def block(b, size=ROWS):
        return pl.ds(pl.multiple_of(b * size, size), size)

    bar = pltpu.get_barrier_semaphore()
    for axis, dev in (("dp", mate), ("dp", far), ("tensor", core_mate), ("tensor", x_mate)):
        pl.semaphore_signal(bar, inc=1, device_id={axis: dev}, device_id_type=MESH)

    @pl.when(z < last)
    def _():
        pl.semaphore_signal(bar, inc=1, device_id={"dp": up_id}, device_id_type=MESH)

    @pl.when(z > 0)
    def _():
        pl.semaphore_signal(bar, inc=1, device_id={"dp": dn_id}, device_id_type=MESH)

    wide = pl.ds(0, 1024)
    share = block(tensor)
    token_load = [
        local(x_in, hbuf, ld.at[0]),
        local(gain_attn, gain.at[pl.ds(1, 1)], ld.at[1]),
        local(gain_moe, gain.at[pl.ds(0, 1)], ld.at[2]),
        local(cos_in, cos_t, ld.at[3]),
        local(sin_in, sin_t, ld.at[4]),
    ]
    proj_load = [
        local(w_query, wgu.at[0], ld.at[5]),
        local(w_key, wgu.at[1, :, pl.ds(0, LANES)], ld.at[6]),
        local(w_value, wgu.at[1, :, pl.ds(LANES, LANES)], ld.at[7]),
    ]
    out_load = [local(w_out.at[:, block(c)], rhs.at[26 + c, share], ld.at[8 + c]) for c in range(4)]
    late_load = [local(d_out.at[:, block(c)], rhs.at[c], ld.at[12 + c]) for c in range(4)] + [
        local(chosen, picks, ld.at[16]),
        local(gates, pick_w, ld.at[17]),
    ]

    def expert_load(e, s):
        return [
            local(w_gate.at[e], wgu.at[s, :, pl.ds(0, LANES)], wsem.at[s, 0]),
            local(w_up.at[e], wgu.at[s, :, pl.ds(LANES, LANES)], wsem.at[s, 1]),
            local(w_down.at[e], wdb.at[s], wsem.at[s, 2]),
        ]

    def start(copies):
        for copy in copies:
            copy.start()

    def wait(copies):
        for copy in copies:
            copy.wait()

    start(out_load + token_load + proj_load + late_load)
    pl.semaphore_wait(bar, 4 + (z < last).astype(jnp.int32) + (z > 0).astype(jnp.int32))

    part_w = buf.at[share, wide]
    quarter = 2 * (z % 2) + y
    part_q = buf.at[pl.ds(pl.multiple_of(tensor * 256 + quarter * 64, 64), 64), wide]
    part_y = buf.at[pl.ds(pl.multiple_of(x_mate * 256 + quarter * 64, 64), 64), wide]
    part_z = buf.at[pl.ds(pl.multiple_of(x_mate * 256 + (z % 2) * 128, 128), 128), wide]
    pair = base + (z + 1 - 2 * (z % 2)) * 2 + y
    w_x = remote(part_q, part_q, ws.at[0], wr.at[0], x_mate, "tensor")
    w_y = remote(part_y, part_y, ws.at[3], wr.at[3], mate)
    w_z = remote(part_z, part_z, ws.at[4], wr.at[4], pair)
    w_c = remote(part_w, part_w, ws.at[1], wr.at[1], core_mate, "tensor")
    part_f = buf.at[block(x_mate), wide]
    w_f = remote(part_f, part_f, ws.at[2], wr.at[2], core_mate, "tensor")
    wait(out_load)
    for c in range(4):
        buf[share, 256 * c : 256 * c + 256] = rhs[26 + c, share, :].astype(f32)
    w_x.start()
    w_c.start()

    def gather_x(b):
        return remote(
            acc.at[block(b), share], acc.at[block(b), share], cs_x.at[b], cr_x.at[b], x_mate, "tensor"
        )

    def gather_c(b):
        return remote(
            acc.at[block(b), share], acc.at[block(b), share], cs_c.at[b], cr_c.at[b], core_mate, "tensor"
        )

    def gather_f(b):
        part = acc.at[block(b), block(x_mate)]
        return remote(part, part, cs_f.at[b], cr_f.at[b], core_mate, "tensor")

    def rotate_t(values, cols):
        one, two = values[:32], values[32:]
        cosine, sine = cos_t[:, cols], sin_t[:, cols]
        return jnp.concatenate([one * cosine - two * sine, two * cosine + one * sine], axis=0)

    def head_rows(b, carry):
        rows = block(b)
        vals = [hbuf[rows, 256 * col : 256 * col + 256].astype(f32) for col in range(4)]
        square = sum(jnp.sum(v * v, axis=1, keepdims=True) for v in vals)
        scale_r = lax.rsqrt(square * (1.0 / 1024.0) + EPSILON)
        query, key_value = 0.0, 0.0
        for col in range(4):
            normed = vals[col] * scale_r * gain[1:2, 256 * col : 256 * col + 256]
            for half_c in range(2):
                lhs[24 + 2 * col + half_c, :, rows] = normed[:, 128 * half_c : 128 * half_c + 128].T.astype(bf16)
            normed = normed.astype(bf16)
            query = query + dot_f(normed, wgu[0, 256 * col : 256 * col + 256, :])
            key_value = key_value + dot_f(normed, wgu[1, 256 * col : 256 * col + 256, :])
        query = query.T
        nothing = jnp.zeros((64, ROWS), f32)
        for h in range(4):
            turned = rotate_t(query[64 * h : 64 * h + 64], rows)
            both = [turned, nothing] if h < 2 else [nothing, turned]
            q2[h, rows, :] = jnp.concatenate(both, axis=0).T.astype(bf16)
        key = key_value[:, :LANES].T
        key = jnp.concatenate([rotate_t(key[:64], rows), rotate_t(key[64:], rows)], axis=0)
        kt2[:, rows] = key.astype(bf16)
        k2[rows, :] = key.T.astype(bf16)
        value = key_value[:, LANES:]
        v2[rows, :] = value.astype(bf16)
        vt2[:, rows] = value.T.astype(bf16)
        return carry

    scaling = 1.0 / math.sqrt(HEAD_DIM)

    def masked_scores(h, qb):
        keys = ROWS * (qb + 1)
        rows = pl.ds(ROWS * qb, ROWS)
        scores = dot_nt(k2[0:keys, :], q2[h, rows, :]) * scaling
        k_pos = lax.broadcasted_iota(jnp.int32, (keys, ROWS), 0)
        q_pos = lax.broadcasted_iota(jnp.int32, (keys, ROWS), 1) + ROWS * qb
        allowed = (k_pos <= q_pos) & (k_pos < length[0])
        return jnp.where(allowed, scores, NEGATIVE)

    def attend(qb):
        keys = ROWS * (qb + 1)
        rows = pl.ds(ROWS * qb, ROWS)

        def one_head(h, carry):
            scores = masked_scores(h, qb)
            top_s = jnp.max(scores, axis=0, keepdims=True)
            expo = jnp.exp(scores - top_s)
            total = jnp.sum(expo, axis=0, keepdims=True)
            probs = (expo / total).astype(bf16)
            lse[pl.ds(h, 1), rows] = top_s + jnp.log(total)
            v_head = vt2[pl.ds(pl.multiple_of((h // 2) * 64, 64), 64), 0:keys]
            lhs[32 + h // 2, pl.ds(pl.multiple_of((h % 2) * 64, 64), 64), rows] = dot_f(v_head, probs).astype(bf16)
            return carry

        lax.fori_loop(0, 4, one_head, 0)
        for half_c in range(2):
            own_c = pl.ds(pl.multiple_of(tensor * 256 + half_c * 128, 128), 128)
            acc[rows, own_c] = lhs[32 + half_c, :, rows].astype(f32).T
        gather_x(qb).start()
        gather_c(qb).start()

    def mask_rows(b, carry):
        rows = block(b)
        pos = lax.broadcasted_iota(jnp.int32, (ROWS, 256), 0) + b * ROWS
        for c in range(4):
            rhs[c, rows, :] = jnp.where(pos < length[0], rhs[c, rows, :].astype(f32), 0.0).astype(bf16)
        return carry

    near_d = [2 * tensor + j for j in range(2)]
    direct_d = [8 + 4 * core + j for j in range(4)]

    def slab(k):
        return pl.ds(pl.multiple_of(4 * k, 4), 4)

    def d_copy(k, sends, recvs, dev, axis, src=None):
        return remote((ybuf if src is None else src).at[slab(k)], ybuf.at[slab(k)], sends.at[k], recvs.at[k], dev, axis)

    def d_y(k):
        return d_copy(k, dys, dyr, mate, "dp", pbuf)

    def d_c(k):
        return d_copy(k, dcs, dcr, core_mate, "tensor")

    def d_x(k):
        return d_copy(k, dxs, dxr, x_mate, "tensor")

    def d_f(k):
        return d_copy(k, dfs, dfr, core_mate, "tensor")

    def stage_d(k):
        rows = block(k, 64)
        for c in range(4):
            pbuf[4 * k + c] = rhs[c, rows, :].astype(f32)
        d_y(k).start()

    def h_piece(b, t):
        return 4 * b + t

    def h_copy(b, t, sends, recvs, dev, axis):
        part = zbuf.at[slab(h_piece(b, t))]
        return remote(part, part, sends.at[b], recvs.at[b], dev, axis)

    def h_stage(b):
        return 2 * x_mate + b if isinstance(b, int) and b < 2 else 2 * jnp.where(b < 2, x_mate, core_mate) + b % 2

    def h_y(b):
        return remote(
            pbuf.at[slab(h_stage(b))], zbuf.at[slab(h_piece(b, tensor))], hys.at[b], hyr.at[b], mate
        )

    def h_c(b):
        return h_copy(b, tensor, hcs, hcr, core_mate, "tensor")

    def h_x(b):
        return h_copy(b, tensor, hxs, hxr, x_mate, "tensor")

    def h_f(b):
        return h_copy(b, x_mate, hfs, hfr, core_mate, "tensor")

    def h_send(b):
        rows = pl.ds(pl.multiple_of(b * 256 + tensor * 64, 64), 64)
        for c in range(4):
            pbuf[4 * h_stage(b) + c] = hbuf[rows, 256 * c : 256 * c + 256].astype(f32)
        h_y(b).start()

    def h_share(b):
        h_y(b).wait_recv()
        h_x(b).start()
        h_c(b).start()

    def h_forward(b):
        h_x(b).wait_recv()
        h_f(b).start()

    def d_share(j):
        k = near_d[j]
        d_y(k).wait_recv()
        d_x(k).start()
        d_c(k).start()

    def d_forward(j):
        k = 2 * x_mate + j
        d_x(k).wait_recv()
        d_f(k).start()

    def d_direct(j):
        k = direct_d[j]
        d_y(k).wait_recv()
        d_c(k).start()

    wait(token_load + proj_load)
    head_rows(0, 0)
    attend(0)
    head_rows(1, 0)
    w_x.wait_recv()
    w_y.start()
    attend(1)
    head_rows(2, 0)
    w_y.wait_recv()
    w_z.start()
    wait(late_load)
    lax.fori_loop(0, 4, mask_rows, 0)
    for j in range(2):
        stage_d(near_d[j])
    for j in range(2):
        stage_d(direct_d[j])
    attend(2)
    head_rows(3, 0)
    start(expert_load(8 * y, 0))
    attend(3)
    dk_acc[...] = jnp.zeros_like(dk_acc)
    dv_acc[...] = jnp.zeros_like(dv_acc)
    norms[...] = jnp.zeros_like(norms)


    expert_id = lax.broadcasted_iota(jnp.int32, (EXPERTS, 1024), 0)
    alive = lax.broadcasted_iota(jnp.int32, (EXPERTS, 1024), 1) < length[0]
    hits = jnp.zeros((EXPERTS, 1024), f32)
    weight = jnp.zeros((EXPERTS, 1024), f32)
    for k in range(TOP_K):
        same = (picks[k : k + 1, :] == expert_id) & alive
        hits = jnp.where(same, 1.0, hits)
        weight = jnp.where(same, pick_w[k : k + 1, :], weight)
    hits = hits.astype(bf16)
    limit = ((5 * TOP_K * length[0] + 4 * EXPERTS - 1) // (4 * EXPERTS)).astype(f32)
    for b in range(4):
        rows = pl.ds(ROWS * b, ROWS)
        token = lax.broadcasted_iota(jnp.int32, (1024, ROWS), 1) + ROWS * b
        earlier = jnp.where(lax.broadcasted_iota(jnp.int32, (1024, ROWS), 0) < token, 1.0, 0.0).astype(bf16)
        places = dot_f(hits, earlier)
        kept = jnp.where(places < limit, weight[:, ROWS * b : ROWS * b + ROWS], 0.0)
        kept_out[:, rows] = kept
        slot_w[rows, :] = jnp.concatenate([kept, jnp.zeros((LANES - EXPERTS, ROWS), f32)], axis=0).T

    kept_copy = remote(kept_out, kept_in, ks.at[0], kr.at[0], mate)
    kept_copy.start()

    w_z.wait_recv()
    w_f.start()
    w_c.wait_recv()
    w_f.wait_recv()

    def cast_out(b, carry):
        for c in range(4):
            rhs[26 + c, block(b, 64), :] = buf[block(b, 64), 256 * c : 256 * c + 256].astype(bf16)
        return carry

    lax.fori_loop(0, 16, cast_out, 0)

    def forward_rows(b, carry):
        rows = block(b)
        for k in range(4):
            part = acc[rows, 256 * k : 256 * k + 256].astype(bf16)
            if k == 0:
                sums = [
                    hbuf[rows, 256 * col : 256 * col + 256].astype(f32) + dot_f(part, rhs[26 + col, 0:256, :])
                    for col in range(4)
                ]
            else:
                sums = [
                    sums[col] + dot_f(part, rhs[26 + col, 256 * k : 256 * k + 256, :]) for col in range(4)
                ]
        square = sum(jnp.sum(v * v, axis=1, keepdims=True) for v in sums)
        scale_r = lax.rsqrt(square * (1.0 / 1024.0) + EPSILON)
        for col in range(4):
            buf[rows, 256 * col : 256 * col + 256] = sums[col]
            normed = sums[col] * scale_r * gain[0:1, 256 * col : 256 * col + 256]
            hbuf[rows, 256 * col : 256 * col + 256] = normed.astype(bf16)
            for half_c in range(2):
                lhs[16 + 2 * col + half_c, :, rows] = normed[:, 128 * half_c : 128 * half_c + 128].T.astype(bf16)
        return carry

    def expert_of(k):
        return jnp.where(k < 16, 8 * y + k % 8, 8 * (1 - y) + k % 8)

    def next_weights(k):
        wait(expert_load(expert_of(k), k % 2))

        @pl.when(k < 23)
        def _():
            start(expert_load(expert_of(k + 1), (k + 1) % 2))

    def unit(k, b, kind):
        rows = block(b)
        s = k % 2
        e = expert_of(k)
        el = k % 8
        if kind == "mate":
            both = dot_f(rhs[26, rows, :], wgu[s, 0:256, :])
            for c in range(1, 4):
                both = both + dot_f(rhs[26 + c, rows, :], wgu[s, 256 * c : 256 * c + 256, :])
        else:
            both = dot_f(hbuf[rows, :], wgu[s])
        d_base = 12 if kind == "mate" else 0
        gate, up = both[:, :LANES], both[:, LANES:]
        d_raw = dot_nt(rhs[d_base, rows, :], wdb[s, :, 0:256])
        for c in range(1, 4):
            d_raw = d_raw + dot_nt(rhs[d_base + c, rows, :], wdb[s, :, 256 * c : 256 * c + 256])
        lane = lax.broadcasted_iota(jnp.int32, (ROWS, LANES), 1)
        weights = slot_m if kind == "mate" else slot_w
        weight = jnp.sum(jnp.where(lane == e, weights[rows, :], 0.0), axis=1, keepdims=True)
        sigma = 1.0 / (1.0 + jnp.exp(-gate))
        silu = gate * sigma
        hidden = silu * up
        hidden_t = (hidden * weight).T.astype(bf16)
        d_hidden = d_raw * weight
        d_gate = (d_hidden * up * sigma * (1.0 + gate * (1.0 - sigma))).astype(bf16)
        d_up = (d_hidden * silu).astype(bf16)
        if kind == "mate":
            lhs[42 + el, :, rows] = hidden_t
            rhs[16 + el, rows, 0:LANES] = d_gate
            rhs[16 + el, rows, LANES:] = d_up
            return
        lhs[e, :, rows] = hidden_t
        inner = jnp.sum(hidden * d_raw, axis=1, keepdims=True)
        inner = jnp.where(weight > 0.0, inner, 0.0)
        is_first = kind == "first"
        acc[rows, 1024:1152] = jnp.where(lane == e, inner, 0.0 if is_first else acc[rows, 1024:1152])
        if kind == "other":
            part = dot_nt(jnp.concatenate([d_gate, d_up], axis=1), wgu[s])
        else:
            rhs[4 + el, rows, 0:LANES] = d_gate
            rhs[4 + el, rows, LANES:] = d_up
            part = dot_nt(rhs[4 + el, rows, :], wgu[s])
        acc[rows, 0:1024] = part if is_first else acc[rows, 0:1024] + part

    def units(k, begin, count, kind):
        def step(b, carry):
            unit(k, b, kind)
            return carry

        lax.fori_loop(begin, begin + count, step, 0)

    def forward_step(b, carry):
        @pl.when(b < 4)
        def _():
            gather_x(b).wait_recv()
            gather_f(b).start()

        @pl.when(b > 0)
        def _():
            gather_c(b - 1).wait_recv()
            gather_f(b - 1).wait_recv()
            gather_f(b - 1).wait_send()
            gather_x(b - 1).wait_send()
            gather_c(b - 1).wait_send()
            forward_rows(b - 1, 0)
            h_send(b - 1)
            unit(0, b - 1, "first")

        @pl.when(b == 4)
        def _():
            d_share(0)
            d_share(1)
            stage_d(direct_d[2])
            stage_d(direct_d[3])

        return carry

    for copy in (w_x, w_c, w_f, w_y, w_z):
        copy.wait_send()
    next_weights(0)
    lax.fori_loop(0, 5, forward_step, 0)
    keep = local(buf.at[:, wide], s_resid, iosem.at[0])
    keep.start()

    chores = {
        5: [(h_share, 0)],
        8: [(d_direct, 0), (d_direct, 1)],
        11: [(h_share, 1)],
        13: [(h_forward, 0), (d_forward, 0)],
        16: [(h_share, 2), (d_forward, 1)],
        20: [(h_forward, 1)],
        23: [(h_share, 3)],
        26: [(h_forward, 2)],
        29: [(d_direct, 2)],
        31: [(h_forward, 3), (d_direct, 3)],
    }

    def own_unit(u, carry):
        k = u // 4

        @pl.when(u % 4 == 0)
        def _():
            next_weights(k)

        unit(k, u % 4, "own")
        for when_u, jobs in chores.items():

            @pl.when(u == when_u)
            def _(jobs=jobs):
                for job, arg in jobs:
                    job(arg)

        return carry

    lax.fori_loop(4, 32, own_unit, 0)

    kept_copy.wait_recv()
    for b in range(4):
        rows = pl.ds(ROWS * b, ROWS)
        slot_m[rows, :] = jnp.concatenate(
            [kept_in[:, rows], jnp.zeros((LANES - EXPERTS, ROWS), f32)], axis=0
        ).T
    other_core = tensor - core + (1 - core)
    for j in range(2):
        d_c(2 * other_core + j).wait_recv()
        d_f(2 * (3 - tensor) + j).wait_recv()
    for j in range(4):
        d_c(8 + 4 * (1 - core) + j).wait_recv()
    for b in range(4):
        h_c(b).wait_recv()
        h_f(b).wait_recv()

    def take_d(k, carry):
        for c in range(4):
            rhs[12 + c, block(k, 64), :] = ybuf[4 * k + c].astype(bf16)
        return carry

    def take_h(b, carry):
        rows = block(b)
        for c in range(4):
            whole = jnp.concatenate([zbuf[4 * (4 * b + t) + c] for t in range(4)], axis=0)
            rhs[26 + c, rows, :] = whole.astype(bf16)
            for half_c in range(2):
                lhs[34 + 2 * c + half_c, :, rows] = whole[:, 128 * half_c : 128 * half_c + 128].T.astype(bf16)
        return carry

    lax.fori_loop(0, 16, take_d, 0)
    lax.fori_loop(0, 4, take_h, 0)
    next_weights(8)
    units(8, 0, 4, "mate")
    kept_copy.wait_send()
    for j in range(2):
        d_y(near_d[j]).wait_send()
        d_x(near_d[j]).wait_send()
        d_c(near_d[j]).wait_send()
        d_f(2 * x_mate + j).wait_send()
    for j in range(4):
        d_y(direct_d[j]).wait_send()
        d_c(direct_d[j]).wait_send()
    for b in range(4):
        h_y(b).wait_send()
        h_x(b).wait_send()
        h_c(b).wait_send()
        h_f(b).wait_send()

    pl.semaphore_signal(go, inc=1, device_id={"dp": mate}, device_id_type=MESH)

    @pl.when(z < last)
    def _():
        pl.semaphore_signal(go, inc=1, device_id={"dp": up_id}, device_id_type=MESH)

    @pl.when(z > 0)
    def _():
        pl.semaphore_signal(go, inc=1, device_id={"dp": dn_id}, device_id_type=MESH)

    pl.semaphore_wait(go, 1 + (z < last).astype(jnp.int32) + (z > 0).astype(jnp.int32))

    def half_pass(u):
        k = 9 + u // 2
        begin = (u % 2) * 2

        @pl.when(begin == 0)
        def _():
            next_weights(k)

        @pl.when(k < 16)
        def _():
            units(k, begin, 2, "mate")

        @pl.when(k >= 16)
        def _():
            units(k, begin, 2, "other")

    mine = pl.ds(pl.multiple_of(core * 512, 512), 512)
    other = pl.ds(pl.multiple_of((1 - core) * 512, 512), 512)

    def span(k):
        return pl.ds(0, 1152 if k == 0 else 1024)

    def sum_a(k):
        return remote(acc.at[other, span(k)], buf.at[pl.ds(0, 512), span(k)], s1s.at[k], s1r.at[k], core_mate, "tensor")

    def sum_b(k):
        return remote(acc.at[mine, span(k)], buf.at[pl.ds(512, 512), span(k)], s2s.at[k], s2r.at[k], x_mate, "tensor")

    def sum_c(k):
        part = acc.at[mine, span(k)]
        return remote(part, part, s3s.at[k], s3r.at[k], core_mate, "tensor")

    def add_in(k, at_row):
        def step(b, carry):
            rows = pl.ds(pl.multiple_of(core * 512 + b * 64, 64), 64)
            acc[rows, span(k)] += buf[pl.ds(pl.multiple_of(at_row + b * 64, 64), 64), span(k)]
            return carry

        lax.fori_loop(0, 8, step, 0)

    def sum_first(k):
        pl.semaphore_signal(ready1.at[k], inc=1, device_id={"tensor": core_mate}, device_id_type=MESH)
        pl.semaphore_signal(ready2.at[k], inc=1, device_id={"tensor": x_mate}, device_id_type=MESH)
        pl.semaphore_wait(ready1.at[k], 1)
        sum_a(k).start()

    def sum_second(k):
        sum_a(k).wait_recv()
        add_in(k, 0)
        sum_a(k).wait_send()
        pl.semaphore_signal(ready3.at[k], inc=1, device_id={"tensor": core_mate}, device_id_type=MESH)
        pl.semaphore_wait(ready2.at[k], 1)
        sum_b(k).start()

    def sum_third(k):
        sum_b(k).wait_recv()
        sum_b(k).wait_send()
        add_in(k, 512)
        pl.semaphore_wait(ready3.at[k], 1)
        sum_c(k).start()

    def sum_last(k):
        sum_c(k).wait_recv()
        sum_c(k).wait_send()

    def norm_sum(step, dev):
        return remote(norms.at[pl.ds(0, 16)], norm_in.at[step], ns.at[step], nr.at[step], dev)

    partners = (mate, pair, far)

    def norm_next(step):
        if step > 0:
            norm_sum(step - 1, partners[step - 1]).wait_recv()
            norm_sum(step - 1, partners[step - 1]).wait_send()
            norms[...] = norms[...] + norm_in[step - 1]
        if step < 3:
            norm_sum(step, partners[step]).start()

    def norm_back(values, scale_r, grads, which):
        inner = sum(
            jnp.sum(v * scale_r * (g * gain[which : which + 1, 256 * c : 256 * c + 256]), axis=1, keepdims=True)
            for c, (v, g) in enumerate(zip(values, grads))
        ) * (1.0 / 1024.0)
        outs = []
        for c, (v, g) in enumerate(zip(values, grads)):
            normed = v * scale_r
            total = jnp.sum(g * normed, axis=0, keepdims=True)
            row = 8 * which + 2 * c
            norms[row : row + 1, :] += total[:, :LANES]
            norms[row + 1 : row + 2, :] += total[:, LANES:]
            outs.append(scale_r * (g * gain[which : which + 1, 256 * c : 256 * c + 256] - normed * inner))
        return outs

    def middle_rows(b):
        rows = block(b)

        values = [buf[rows, 256 * c : 256 * c + 256] for c in range(4)]
        grads = [acc[rows, 256 * c : 256 * c + 256] for c in range(4)]
        square = sum(jnp.sum(v * v, axis=1, keepdims=True) for v in values)
        scale_r = lax.rsqrt(square * (1.0 / 1024.0) + EPSILON)
        back = norm_back(values, scale_r, grads, 0)
        for c in range(4):
            total = rhs[c, rows, :].astype(f32) + back[c]
            acc[rows, 256 * c : 256 * c + 256] = total
            rhs[26 + c, rows, :] = total.astype(bf16)
        for h in range(4):
            d_head = dot_nt(rhs[26, rows, :], wdb[h, :, 0:256])
            for c in range(1, 4):
                d_head = d_head + dot_nt(rhs[26 + c, rows, :], wdb[h, :, 256 * c : 256 * c + 256])
            da2[h, rows, :] = d_head.astype(bf16)

    def turn_back(grad, cols):
        one, two = grad[:32], grad[32:]
        cosine, sine = cos_t[:, cols], sin_t[:, cols]
        return jnp.concatenate([one * cosine + two * sine, two * cosine - one * sine], axis=0)

    def attend_back(h, qb):
        keys = ROWS * (qb + 1)
        rows = pl.ds(ROWS * qb, ROWS)
        q_rows = q2[h, rows, :]
        d_rows = da2[h, rows, :]
        exact = jnp.exp(masked_scores(h, qb) - lse[pl.ds(h, 1), rows])
        d_probs = dot_nt(v2[0:keys, :], d_rows)
        inner = jnp.sum(exact * d_probs, axis=0, keepdims=True)
        d_scores = (exact * (d_probs - inner)).astype(bf16)
        dk_acc[0:keys, :] += dot_f(d_scores, q_rows)
        dv_acc[0:keys, :] += dot_f(exact.astype(bf16), d_rows)
        k_head = kt2[pl.ds(pl.multiple_of((h // 2) * 64, 64), 64), 0:keys]
        d_q = dot_f(k_head, d_scores) * scaling
        buf[pl.ds(pl.multiple_of(h * 64, 64), 64), rows] = turn_back(d_q, rows)

    def turn_rows(b):
        rows = block(b)
        rhs[24, rows, :] = buf[0:256, rows].T.astype(bf16)
        d_k = (dk_acc[rows, :] * scaling).T
        d_k = jnp.concatenate([turn_back(d_k[:64], rows), turn_back(d_k[64:], rows)], axis=0)
        rhs[25, rows, 0:LANES] = d_k.T.astype(bf16)
        rhs[25, rows, LANES:] = dv_acc[rows, :].astype(bf16)

    def project_rows(b):
        rows = block(b)
        acc[rows, 0:1024] = dot_nt(rhs[24, rows, :], wgu[0]) + dot_nt(rhs[25, rows, :], wgu[1])

    def token_rows(b):
        rows = block(b)

        values = [hbuf[rows, 256 * c : 256 * c + 256].astype(f32) for c in range(4)]
        grads = [acc[rows, 256 * c : 256 * c + 256] for c in range(4)]
        square = sum(jnp.sum(v * v, axis=1, keepdims=True) for v in values)
        scale_r = lax.rsqrt(square * (1.0 / 1024.0) + EPSILON)
        back = norm_back(values, scale_r, grads, 1)
        for c in range(4):
            cols = slice(256 * c, 256 * c + 256)
            hbuf[rows, cols] = (buf[rows, cols] + back[c]).astype(bf16)

    def pair_load(pair, s):
        return local(w_down.at[pl.ds(2 * pair, 2)], wdb.at[pl.ds(2 * s, 2)], wsem.at[s, 2])

    def moe_pair(pair):
        s = pair % 2
        pair_load(pair, s).wait()

        @pl.when(pair + 1 < EXPERTS // 2)
        def _():
            pair_load(pair + 1, 1 - s).start()

        def rows_of(b, carry):
            rows = block(b)
            hidden = lhs[pl.ds(2 * pair, 2), :, rows].reshape(256, ROWS)
            down = wdb[pl.ds(2 * s, 2)].reshape(256, 1024)
            part = dot_tn(hidden, down)

            @pl.when(pair == 0)
            def _():
                acc[rows, 0:1024] = part

            @pl.when(pair > 0)
            def _():
                acc[rows, 0:1024] += part

            return carry

        lax.fori_loop(0, 4, rows_of, 0)

    def result_rows(b):
        rows = block(b)

        pos = lax.broadcasted_iota(jnp.int32, (ROWS, 1024), 0) + b * ROWS
        total = buf[rows, wide] + acc[rows, 0:1024]
        hbuf[rows, :] = jnp.where(pos < length[0], total, 0.0).astype(bf16)

    def halves_in(src):
        return [local(src, buf.at[:, wide], iosem.at[1])]

    tokens_in = [local(x_in, hbuf, iosem.at[3])]
    wo_load = [
        local(w_out.at[pl.ds(64 * h, 64)], wdb.at[h, pl.ds(64 * (h // 2), 64)], ld.at[8 + h]) for h in range(4)
    ]
    dots_out = [local(d_pick, o_dots, iosem.at[7])]
    norms_out = [
        local(norms.at[pl.ds(0, 8)], o_norm0, iosem.at[2]),
        local(norms.at[pl.ds(8, 8)], o_norm1, iosem.at[4]),
    ]

    def pick_dots():
        for b in range(4):
            rows = pl.ds(ROWS * b, ROWS)
            dots = acc[rows, 1024:1152].T[:EXPERTS]
            lane_e = lax.broadcasted_iota(jnp.int32, (EXPERTS, ROWS), 0)
            for k in range(TOP_K):
                mine_k = jnp.where(picks[k : k + 1, rows] == lane_e, dots, 0.0)
                d_pick[k : k + 1, rows] = jnp.sum(mine_k, axis=0, keepdims=True)
    dres_out = [local(acc.at[:, wide], s_dres, iosem.at[8])]
    tokens_out = [local(hbuf, o_tokens, iosem.at[9])]
    result_out = [local(hbuf, o_result, iosem.at[10])]

    def clear_wo():
        for h in range(4):
            wdb[h, 64 - 64 * (h // 2) : 128 - 64 * (h // 2), :] = jnp.zeros((64, 1024), bf16)

    def do_all(*steps):
        for step in steps:
            step()

    once = {
        T_SUM1: lambda: do_all(keep.wait, lambda: sum_first(0), clear_wo, lambda: start(tokens_in + wo_load + proj_load)),
        T_SUM1 + 2: lambda: do_all(lambda: sum_second(0), lambda: wait(tokens_in)),
        T_MID1 - 3: lambda: sum_third(0),
        T_MID1 - 1: lambda: do_all(
            lambda: sum_last(0), pick_dots, lambda: start(halves_in(s_resid) + dots_out), lambda: wait(wo_load)
        ),
        T_ATT: lambda: do_all(lambda: wait(dots_out), lambda: start(dres_out)),
        T_PROJ - 1: lambda: do_all(lambda: wait(dres_out), lambda: wait(proj_load)),
        T_SUM2: lambda: sum_first(1),
        T_SUM2 + 2: lambda: sum_second(1),
        T_TOK - 3: lambda: sum_third(1),
        T_TOK - 1: lambda: do_all(
            lambda: sum_last(1), lambda: start(halves_in(s_dres)), lambda: start([pair_load(0, 0)])
        ),
        T_MOE: lambda: start(tokens_out),
        T_SUM3 + 5: lambda: norm_next(0),
        T_SUM3 + 7: lambda: norm_next(1),
        T_SUM3 + 9: lambda: norm_next(2),
        T_SUM3 + 11: lambda: do_all(lambda: norm_next(3), lambda: start(norms_out)),
        T_SUM3: lambda: sum_first(2),
        T_SUM3 + 2: lambda: sum_second(2),
        T_RES - 3: lambda: sum_third(2),
        T_RES - 1: lambda: do_all(
            lambda: sum_last(2), lambda: wait(tokens_out + norms_out), lambda: start(halves_in(s_resid))
        ),
        T_RES + 4: lambda: start(result_out),
        T_RES + 8: lambda: wait(result_out),
    }
    halves_wait = {T_MID1: s_resid, T_TOK: s_dres, T_RES: s_resid}

    def work(t):
        for when_t, fn in sorted(once.items()):
            pl.when(t == when_t)(fn)
        for when_t, src in halves_wait.items():
            pl.when(t == when_t)(lambda src=src: wait(halves_in(src)))
        for begin, count, fn in (
            (0, 30, half_pass),
            (T_MID1, 4, middle_rows),
            (T_TURN, 2, lambda u: do_all(lambda: turn_rows(2 * u), lambda: turn_rows(2 * u + 1))),
            (T_PROJ, 2, lambda u: do_all(lambda: project_rows(2 * u), lambda: project_rows(2 * u + 1))),
            (T_TOK, 2, lambda u: do_all(lambda: token_rows(2 * u), lambda: token_rows(2 * u + 1))),
            (T_MOE, EXPERTS // 4, lambda u: do_all(lambda: moe_pair(2 * u), lambda: moe_pair(2 * u + 1))),
            (T_RES, 4, result_rows),
        ):
            pl.when((t >= begin) & (t < begin + count))(lambda fn=fn, begin=begin: fn(t - begin))
        for pair_b in range(2):
            u = t - T_ATT

            def two(pair_b=pair_b, u=u):
                attend_back(u // 2, pair_b)
                attend_back(u // 2, 3 - pair_b)

            pl.when((u >= 0) & (u < 8) & (u % 2 == pair_b))(two)

    own = pl.ds(pl.multiple_of(y * 32, 32), 32)
    oth = pl.ds(pl.multiple_of((1 - y) * 32, 32), 32)
    half = pl.ds(0, 32)
    upper = pl.ds(32, 32)

    def stage(c, t):
        p = z if c == 0 else last - z
        nxt, prv = (up_id, dn_id) if c == 0 else (dn_id, up_id)
        def at(delay, body):
            i = t - delay - c

            @pl.when((i >= 0) & (i < N_CLASS))
            def _():
                s = c * ring + i % ring
                body(i, s, i < N_EXPERT, (i >= N_EXPERT) & (i % 2 == 0), (i >= N_EXPERT) & (i % 2 == 1))

        def ycopy_a(s):
            return remote(pbuf.at[s, oth], ybuf.at[s, half], ys.at[s], yr.at[s], mate)

        def ycopy_b(s):
            return remote(zbuf.at[s], ybuf.at[s], ys.at[s], yr.at[s], mate)

        def zcopy_a(s):
            return remote(zbuf.at[s, half], zbuf.at[s, half], zs.at[s], zr.at[s], nxt)

        def zcopy(s):
            return remote(zbuf.at[s], zbuf.at[s], zs.at[s], zr.at[s], nxt)

        def fcopy_a(s):
            return remote(pbuf.at[s, own], pbuf.at[s, own], fs.at[s], fr.at[s], prv)

        def fcopy(s):
            return remote(pbuf.at[s], pbuf.at[s], fs.at[s], fr.at[s], prv)

        def gcopy_a(s):
            return remote(pbuf.at[s, own], ybuf.at[s, upper], gs.at[s], gr.at[s], mate)

        def gcopy(s):
            return remote(pbuf.at[s], ybuf.at[s], gs.at[s], gr.at[s], mate)

        def first(i, s, is_e, is_a, is_b):
            m = i // 2
            g = 2 * m + c

            @pl.when((i % 2 == 0) & is_e)
            def _():
                el, part = g // 12, g % 12
                down = part < 4
                l_one = jnp.where(down, 8 * y + el, 12 + part)
                r_one = jnp.where(down, part, 4 + el)
                l_two = jnp.where(down, 42 + el, 30 + part)
                r_two = jnp.where(down, 12 + part, 16 + el)
                total = dot_f(lhs[l_one], rhs[r_one]) + dot_f(lhs[l_two], rhs[r_two])
                pbuf[s] = total[:CHUNK]
                pbuf[s + 1] = total[CHUNK:]

            @pl.when((i % 2 == 0) & jnp.logical_not(is_e))
            def _():
                a = g - N_EXPERT
                l_one = jnp.where(a < 8, 32 + a // 4, 24 + a % 8)
                r_one = jnp.where(a < 8, 26 + a % 4, 23 + a // 8)
                total = dot_f(lhs[l_one], rhs[r_one])
                pbuf[s] = total[:CHUNK]
                pbuf[s + 1] = total[CHUNK:]

            @pl.when(is_a)
            def _():
                ycopy_a(s).start()

        def second(i, s, is_e, is_a, is_b):
            @pl.when(is_a)
            def _():
                ycopy_a(s).wait_recv()

                @pl.when(p > 0)
                def _():
                    zcopy_a(s).wait_recv()
                    zbuf[s, half] = zbuf[s, half] + (pbuf[s, own] + ybuf[s, half])

                @pl.when(p == 0)
                def _():
                    zbuf[s, half] = pbuf[s, own] + ybuf[s, half]

                @pl.when(p < last)
                def _():
                    zcopy_a(s).start()

                @pl.when(p == last)
                def _():
                    pbuf[s, own] = zbuf[s, half]
                    fcopy_a(s).start()
                    gcopy_a(s).start()

            @pl.when(jnp.logical_not(is_a))
            def _():
                @pl.when(p > 0)
                def _():
                    zcopy(s).wait_recv()
                    zbuf[s] = zbuf[s] + pbuf[s]

                @pl.when(p == 0)
                def _():
                    zbuf[s] = pbuf[s]

                @pl.when(p < last)
                def _():
                    zcopy(s).start()

                @pl.when((p == last) & is_e)
                def _():
                    pbuf[s] = zbuf[s]
                    fcopy(s).start()
                    gcopy(s).start()

                @pl.when((p == last) & is_b)
                def _():
                    ycopy_b(s).start()

        def third(i, s, is_e, is_a, is_b):
            @pl.when(is_b & (p == last))
            def _():
                ycopy_b(s).wait_recv()
                pbuf[s] = zbuf[s] + ybuf[s]
                fcopy(s).start()

        def fourth(i, s, is_e, is_a, is_b):
            @pl.when(p < last)
            def _():
                @pl.when(is_a)
                def _():
                    fcopy_a(s).wait_recv()

                    @pl.when(p > 0)
                    def _():
                        fcopy_a(s).start()

                    gcopy_a(s).start()

                @pl.when(jnp.logical_not(is_a))
                def _():
                    fcopy(s).wait_recv()

                    @pl.when(p > 0)
                    def _():
                        fcopy(s).start()

                    @pl.when(is_e)
                    def _():
                        gcopy(s).start()

        def store(buf_s, sem, dst0, dst1):
            local(buf_s.at[:, pl.ds(0, LANES)], dst0, sem).start()
            local(buf_s.at[:, pl.ds(LANES, LANES)], dst1, sem).start()

        def fifth(i, s, is_e, is_a, is_b):
            @pl.when(is_a)
            def _():
                gcopy_a(s).wait_recv()
                ycopy_a(s).wait_send()
                pbuf[s, oth] = ybuf[s, upper]

            @pl.when(is_e)
            def _():
                gcopy(s).wait_recv()

            g = 2 * (i // 2) + c
            el, part = g // 12, g % 12
            a = g - N_EXPERT
            low = CHUNK * (i % 2)

            def at_rows(start_row):
                return pl.ds(pl.multiple_of(start_row + low, CHUNK), CHUNK)

            def both_rows(write):
                write(pbuf.at[s], os0.at[s], 8 * y + el)
                write(ybuf.at[s], os1.at[s], 8 * (1 - y) + el)

            @pl.when(is_e & (part < 4))
            def _():
                col = pl.ds(pl.multiple_of(part * 256, LANES), LANES)
                col1 = pl.ds(pl.multiple_of(part * 256 + LANES, LANES), LANES)
                both_rows(
                    lambda src, sem, e: store(
                        src, sem, o_down.at[e, at_rows(0), col], o_down.at[e, at_rows(0), col1]
                    )
                )

            @pl.when(is_e & (part >= 4))
            def _():
                rows = at_rows((part - 4) * 128)
                both_rows(lambda src, sem, e: store(src, sem, o_gate.at[e, rows], o_up.at[e, rows]))

            @pl.when(jnp.logical_not(is_e) & (a < 8))
            def _():
                rows = at_rows((a // 4) * 128)
                col = pl.ds(pl.multiple_of((a % 4) * 256, LANES), LANES)
                col1 = pl.ds(pl.multiple_of((a % 4) * 256 + LANES, LANES), LANES)
                store(pbuf.at[s], os0.at[s], o_out.at[rows, col], o_out.at[rows, col1])

            @pl.when(jnp.logical_not(is_e) & (a >= 8) & (a < 16))
            def _():
                rows = at_rows((a - 8) * 128)
                store(pbuf.at[s], os0.at[s], o_q.at[rows, pl.ds(0, LANES)], o_q.at[rows, pl.ds(LANES, LANES)])

            @pl.when(jnp.logical_not(is_e) & (a >= 16))
            def _():
                rows = at_rows((a - 16) * 128)
                store(pbuf.at[s], os0.at[s], o_k.at[rows], o_v.at[rows])

        def sixth(i, s, is_e, is_a, is_b):
            local(pbuf.at[s], o_q.at[pl.ds(0, CHUNK)], os0.at[s]).wait()

            @pl.when(is_e)
            def _():
                local(ybuf.at[s], o_q.at[pl.ds(0, CHUNK)], os1.at[s]).wait()
                gcopy(s).wait_send()

            @pl.when(is_a)
            def _():
                gcopy_a(s).wait_send()

                @pl.when(p < last)
                def _():
                    zcopy_a(s).wait_send()

                @pl.when(p > 0)
                def _():
                    fcopy_a(s).wait_send()

            @pl.when(jnp.logical_not(is_a))
            def _():
                @pl.when(p < last)
                def _():
                    zcopy(s).wait_send()

                @pl.when((p == last) & is_b)
                def _():
                    ycopy_b(s).wait_send()

                @pl.when(p > 0)
                def _():
                    fcopy(s).wait_send()

        t2 = hop * (1 + p)
        t3 = hop * (2 + last)
        t4 = t3 + hop * (last - p)
        t5 = t4 + hop
        t6 = t5 + hop
        return [(0, first, at), (t2, second, at), (t3, third, at), (t4, fourth, at), (t5, fifth, at), (t6, sixth, at)]

    def body(t, carry):
        both = [stage(0, t), stage(1, t)]
        for k in (1, 2, 3, 4, 5, 0):
            if k == 0:
                work(t)
            for st in both:
                delay, fn, at = st[k]
                at(delay, fn)
        return carry

    total = N_CLASS + hop * (2 * last + 4) + 2
    lax.fori_loop(0, total, body, 0)


def run_layer(mesh, *operands):
    groups = mesh.shape["dp"]
    nz = 4 if groups % 8 == 0 else groups // 2
    last = nz - 1
    hop = HOP
    ring = hop * (2 * last + 4) + 2
    ring = max(32, ring + ring % 2)
    f32, bf16 = jnp.float32, jnp.bfloat16

    def out(shape, kind=f32):
        return jax.ShapeDtypeStruct(shape, kind)

    outs = [
        out((16, 1024, 128)), out((16, 1024, 128)), out((16, 128, 1024)),
        out((1024, 256)), out((1024, 128)), out((1024, 128)), out((256, 1024)), out((8, 128)), out((8, 128)),
        out((1024, 1024), bf16), out((1024, 1024), bf16), out((8, 1024)),
        out((1024, 1024)), out((1024, 1024)),
    ]
    anywhere = pl.BlockSpec(memory_space=pl.ANY)
    dma = pltpu.SemaphoreType.DMA
    reg = pltpu.SemaphoreType.REGULAR
    vmem = pltpu.VMEM
    res = pl.pallas_call(
        functools.partial(layer_kernel, nz, hop, ring),
        out_shape=outs,
        in_specs=[pl.BlockSpec(memory_space=pltpu.SMEM)] + [anywhere] * (len(operands) - 1),
        out_specs=[anywhere] * len(outs),
        scratch_shapes=[
            vmem((50, 128, 1024), bf16), vmem((30, 1024, 256), bf16),
            vmem((2 * ring, CHUNK, 256), f32), vmem((2 * ring, CHUNK, 256), f32), vmem((2 * ring, CHUNK, 256), f32),
            vmem((1024, 1152), f32), vmem((1024, 1152), f32),
            vmem((1024, 1024), bf16), vmem((2, 1024, 256), bf16), vmem((4, 128, 1024), bf16),
            vmem((4, 1024, 128), bf16), vmem((1024, 128), bf16), vmem((1024, 128), bf16),
            vmem((128, 1024), bf16), vmem((128, 1024), bf16),
            vmem((8, 1024), f32), vmem((32, 1024), f32), vmem((32, 1024), f32),
            vmem((4, 1024, 128), bf16), vmem((1024, 128), f32), vmem((1024, 128), f32),
            vmem((1024, 128), f32), vmem((8, 1024), f32), vmem((16, 128), f32),
            vmem((8, 1024), jnp.int32), vmem((8, 1024), f32),
            vmem((3, 16, 128), f32), vmem((8, 1024), f32),
            vmem((EXPERTS, 1024), f32), vmem((EXPERTS, 1024), f32), vmem((1024, 128), f32),
            dma((18,)), dma((2, 3)), dma((11,)),
        ]
        + [dma((2 * ring,))] * 10
        + [dma((4,))] * 6
        + [dma((5,))] * 2
        + [dma((3,))] * 6
        + [reg((3,))] * 3
        + [dma((3,))] * 2
        + [reg]
        + [dma((4,))] * 8
        + [dma((16,))] * 8
        + [dma((1,))] * 2,
        compiler_params=pltpu.CompilerParams(
            collective_id=0, has_side_effects=True, vmem_limit_bytes=63 * 2**20
        ),
    )(*operands)
    sums, rest = tuple(res[:9]), res[9:12]
    if groups > 2 * nz:
        same = [
            [2 * nz * block + place for block in range(groups // (2 * nz))] for place in range(2 * nz)
        ]
        sums = lax.psum(sums, "dp", axis_index_groups=same)
    return sums, rest


def per_device(
    mesh,
    tokens,
    lengths,
    chosen,
    gate_values,
    cotangent,
    norm_attn,
    w_query,
    w_key,
    w_value,
    w_out,
    norm_moe,
    w_gate,
    w_up,
    w_down,
):
    seq_len = tokens.shape[0] // lengths.shape[0]
    cosine, sine = rope_tables(seq_len, HEAD_DIM)
    sums, (result, grad_tokens, dots) = run_layer(
        mesh,
        lengths,
        tokens,
        cotangent,
        chosen.T,
        gate_values.T,
        norm_attn[None, :],
        norm_moe[None, :],
        w_gate,
        w_up,
        w_down,
        cosine,
        sine,
        w_out,
        w_query,
        w_key,
        w_value,
    )
    grad_gate, grad_up, grad_down, grad_query, grad_key, grad_value, grad_out, grad_norm_moe, grad_norm_attn = sums
    return (
        result,
        grad_tokens,
        dots.T,
        grad_norm_attn.reshape(-1),
        grad_query,
        grad_key,
        grad_value,
        grad_out,
        grad_norm_moe.reshape(-1),
        grad_gate,
        grad_up,
        grad_down,
    )


def solution(mesh):
    placed = (
        P("dp", None),
        P("dp"),
        P("dp", None),
        P("dp", None),
        P("dp", None),
        P(),
        P(None, "tensor"),
        P(None, "tensor"),
        P(None, "tensor"),
        P("tensor", None),
        P(),
        P(None, None, "tensor"),
        P(None, None, "tensor"),
        P(None, "tensor", None),
    )
    return jax.shard_map(
        functools.partial(per_device, mesh),
        mesh=mesh,
        in_specs=placed,
        out_specs=(
            P("dp", None),
            P("dp", None),
            P("dp", None),
            P(),
            P(None, "tensor"),
            P(None, "tensor"),
            P(None, "tensor"),
            P("tensor", None),
            P(),
            P(None, None, "tensor"),
            P(None, None, "tensor"),
            P(None, "tensor", None),
        ),
        check_vma=False,
    )
```

```python
import functools
import math

import jax
import jax.numpy as jnp
import numpy as np
from jax import lax
from jax.experimental import pallas as pl
from jax.experimental.pallas import tpu as pltpu
from jax.sharding import PartitionSpec as P

MESH = pl.DeviceIdType.MESH

HEAD_DIM = 64
TOP_K = 8
EXPERTS = 16


EPSILON = 1e-05
THETA = 10000.0
NEGATIVE = -1e30


def dot_f(left, right):
    return jnp.dot(left, right, preferred_element_type=jnp.float32)


def rope_tables(positions, width):
    half_w = width // 2
    freqs = THETA ** (-np.arange(half_w, dtype=np.float64) * 2.0 / width)
    angles = freqs[:, None] * np.arange(positions, dtype=np.float64)[None, :]
    return (np.cos(angles).astype(np.float32), np.sin(angles).astype(np.float32))


LANES = 128
ROWS = 256
CHUNK = 64
N_EXPERT = 96
N_CLASS = 120
HOP = 2
EARLY = 7
T_SUM1 = 32
T_MID1 = 58
T_ATT = 62
T_TURN = 70
T_PROJ = 72
T_SUM2 = 74
T_TOK = 98
T_MOE = 100
T_SUM3 = 104
T_RES = 128


def dot_nt(left, right):
    return lax.dot_general(
        left, right, (((1,), (1,)), ((), ())), preferred_element_type=jnp.float32
    )


def dot_tn(left, right):
    return lax.dot_general(
        left, right, (((0,), (0,)), ((), ())), preferred_element_type=jnp.float32
    )


def layer_kernel(
    nz, hop, ring,
    length, x_in, d_out, chosen, gates, gain_attn, gain_moe, w_gate, w_up, w_down,
    cos_in, sin_in, w_out, w_query, w_key, w_value,
    o_gate, o_up, o_down, o_q, o_k, o_v, o_out, o_norm0, o_norm1, o_result, o_tokens, o_dots, s_resid, s_dres,
    lhs, rhs, pbuf, zbuf, ybuf, acc, buf, hbuf, wgu, wdb, q2, k2, v2, kt2, vt2, lse, cos_t, sin_t,
    da2, dk_acc, dv_acc, slot_w, gain, norms, picks, pick_w, norm_in, d_pick, kept_out, kept_in, slot_m,
    ld, wsem, iosem, ys, yr, zs, zr, fs, fr, gs, gr, os0, os1,
    cs_c, cr_c, cs_x, cr_x, cs_f, cr_f, ws, wr, s1s, s1r, s2s, s2r, s3s, s3r, ready1, ready2, ready3, ns, nr, go,
    hys, hyr, hcs, hcr, hxs, hxr, hfs, hfr, dys, dyr, dcs, dcr, dxs, dxr, dfs, dfr, ks, kr,
):
    f32, bf16 = jnp.float32, jnp.bfloat16
    dp = lax.axis_index("dp")
    tensor = lax.axis_index("tensor")
    base = dp - dp % (2 * nz)
    z, y = (dp % (2 * nz)) // 2, dp % 2
    last = nz - 1
    mate = base + z * 2 + (1 - y)
    up_id = base + jnp.minimum(z + 1, last) * 2 + y
    dn_id = base + jnp.maximum(z - 1, 0) * 2 + y
    far = base + ((z + 2) % nz) * 2 + y
    core = tensor % 2
    core_mate = tensor - core + (1 - core)
    x_mate = (tensor + 2) % 4

    def local(src, dst, sem):
        return pltpu.make_async_copy(src, dst, sem)

    def remote(src, dst, ssem, rsem, dev, axis="dp"):
        return pltpu.make_async_remote_copy(
            src_ref=src, dst_ref=dst, send_sem=ssem, recv_sem=rsem,
            device_id={axis: dev}, device_id_type=MESH,
        )

    def block(b, size=ROWS):
        return pl.ds(pl.multiple_of(b * size, size), size)

    bar = pltpu.get_barrier_semaphore()
    for axis, dev in (("dp", mate), ("dp", far), ("tensor", core_mate), ("tensor", x_mate)):
        pl.semaphore_signal(bar, inc=1, device_id={axis: dev}, device_id_type=MESH)

    @pl.when(z < last)
    def _():
        pl.semaphore_signal(bar, inc=1, device_id={"dp": up_id}, device_id_type=MESH)

    @pl.when(z > 0)
    def _():
        pl.semaphore_signal(bar, inc=1, device_id={"dp": dn_id}, device_id_type=MESH)

    wide = pl.ds(0, 1024)
    share = block(tensor)
    token_load = [
        local(x_in, hbuf, ld.at[0]),
        local(gain_attn, gain.at[pl.ds(1, 1)], ld.at[1]),
        local(gain_moe, gain.at[pl.ds(0, 1)], ld.at[2]),
        local(cos_in, cos_t, ld.at[3]),
        local(sin_in, sin_t, ld.at[4]),
    ]
    proj_load = [
        local(w_query, wgu.at[0], ld.at[5]),
        local(w_key, wgu.at[1, :, pl.ds(0, LANES)], ld.at[6]),
        local(w_value, wgu.at[1, :, pl.ds(LANES, LANES)], ld.at[7]),
    ]
    out_load = [local(w_out.at[:, block(c)], rhs.at[26 + c, share], ld.at[8 + c]) for c in range(4)]
    late_load = [local(d_out.at[:, block(c)], rhs.at[c], ld.at[12 + c]) for c in range(4)] + [
        local(chosen, picks, ld.at[16]),
        local(gates, pick_w, ld.at[17]),
    ]

    def expert_load(e, s):
        return [
            local(w_gate.at[e], wgu.at[s, :, pl.ds(0, LANES)], wsem.at[s, 0]),
            local(w_up.at[e], wgu.at[s, :, pl.ds(LANES, LANES)], wsem.at[s, 1]),
            local(w_down.at[e], wdb.at[s], wsem.at[s, 2]),
        ]

    def start(copies):
        for copy in copies:
            copy.start()

    def wait(copies):
        for copy in copies:
            copy.wait()

    start(out_load + token_load + proj_load + late_load)
    pl.semaphore_wait(bar, 4 + (z < last).astype(jnp.int32) + (z > 0).astype(jnp.int32))

    part_w = buf.at[share, wide]
    quarter = 2 * (z % 2) + y
    part_q = buf.at[pl.ds(pl.multiple_of(tensor * 256 + quarter * 64, 64), 64), wide]
    part_y = buf.at[pl.ds(pl.multiple_of(x_mate * 256 + quarter * 64, 64), 64), wide]
    part_z = buf.at[pl.ds(pl.multiple_of(x_mate * 256 + (z % 2) * 128, 128), 128), wide]
    pair = base + (z + 1 - 2 * (z % 2)) * 2 + y
    w_x = remote(part_q, part_q, ws.at[0], wr.at[0], x_mate, "tensor")
    w_y = remote(part_y, part_y, ws.at[3], wr.at[3], mate)
    w_z = remote(part_z, part_z, ws.at[4], wr.at[4], pair)
    w_c = remote(part_w, part_w, ws.at[1], wr.at[1], core_mate, "tensor")
    part_f = buf.at[block(x_mate), wide]
    w_f = remote(part_f, part_f, ws.at[2], wr.at[2], core_mate, "tensor")
    wait(out_load)
    for c in range(4):
        buf[share, 256 * c : 256 * c + 256] = rhs[26 + c, share, :].astype(f32)
    w_x.start()
    w_c.start()

    def gather_x(b):
        return remote(
            acc.at[block(b), share], acc.at[block(b), share], cs_x.at[b], cr_x.at[b], x_mate, "tensor"
        )

    def gather_c(b):
        return remote(
            acc.at[block(b), share], acc.at[block(b), share], cs_c.at[b], cr_c.at[b], core_mate, "tensor"
        )

    def gather_f(b):
        part = acc.at[block(b), block(x_mate)]
        return remote(part, part, cs_f.at[b], cr_f.at[b], core_mate, "tensor")

    def rotate_t(values, cols):
        one, two = values[:32], values[32:]
        cosine, sine = cos_t[:, cols], sin_t[:, cols]
        return jnp.concatenate([one * cosine - two * sine, two * cosine + one * sine], axis=0)

    def head_rows(b, carry):
        rows = block(b)
        vals = [hbuf[rows, 256 * col : 256 * col + 256].astype(f32) for col in range(4)]
        square = sum(jnp.sum(v * v, axis=1, keepdims=True) for v in vals)
        scale_r = lax.rsqrt(square * (1.0 / 1024.0) + EPSILON)
        query, key_value = 0.0, 0.0
        for col in range(4):
            normed = vals[col] * scale_r * gain[1:2, 256 * col : 256 * col + 256]
            for half_c in range(2):
                lhs[24 + 2 * col + half_c, :, rows] = normed[:, 128 * half_c : 128 * half_c + 128].T.astype(bf16)
            normed = normed.astype(bf16)
            query = query + dot_f(normed, wgu[0, 256 * col : 256 * col + 256, :])
            key_value = key_value + dot_f(normed, wgu[1, 256 * col : 256 * col + 256, :])
        query = query.T
        nothing = jnp.zeros((64, ROWS), f32)
        for h in range(4):
            turned = rotate_t(query[64 * h : 64 * h + 64], rows)
            both = [turned, nothing] if h < 2 else [nothing, turned]
            q2[h, rows, :] = jnp.concatenate(both, axis=0).T.astype(bf16)
        key = key_value[:, :LANES].T
        key = jnp.concatenate([rotate_t(key[:64], rows), rotate_t(key[64:], rows)], axis=0)
        kt2[:, rows] = key.astype(bf16)
        k2[rows, :] = key.T.astype(bf16)
        value = key_value[:, LANES:]
        v2[rows, :] = value.astype(bf16)
        vt2[:, rows] = value.T.astype(bf16)
        return carry

    scaling = 1.0 / math.sqrt(HEAD_DIM)

    def masked_scores(h, qb):
        keys = ROWS * (qb + 1)
        rows = pl.ds(ROWS * qb, ROWS)
        scores = dot_nt(k2[0:keys, :], q2[h, rows, :]) * scaling
        k_pos = lax.broadcasted_iota(jnp.int32, (keys, ROWS), 0)
        q_pos = lax.broadcasted_iota(jnp.int32, (keys, ROWS), 1) + ROWS * qb
        allowed = (k_pos <= q_pos) & (k_pos < length[0])
        return jnp.where(allowed, scores, NEGATIVE)

    def attend(qb):
        keys = ROWS * (qb + 1)
        rows = pl.ds(ROWS * qb, ROWS)

        def one_head(h, carry):
            scores = masked_scores(h, qb)
            top_s = jnp.max(scores, axis=0, keepdims=True)
            expo = jnp.exp(scores - top_s)
            total = jnp.sum(expo, axis=0, keepdims=True)
            probs = (expo / total).astype(bf16)
            lse[pl.ds(h, 1), rows] = top_s + jnp.log(total)
            v_head = vt2[pl.ds(pl.multiple_of((h // 2) * 64, 64), 64), 0:keys]
            lhs[32 + h // 2, pl.ds(pl.multiple_of((h % 2) * 64, 64), 64), rows] = dot_f(v_head, probs).astype(bf16)
            return carry

        lax.fori_loop(0, 4, one_head, 0)
        for half_c in range(2):
            own_c = pl.ds(pl.multiple_of(tensor * 256 + half_c * 128, 128), 128)
            acc[rows, own_c] = lhs[32 + half_c, :, rows].astype(f32).T
        gather_x(qb).start()
        gather_c(qb).start()

    def mask_rows(b, carry):
        rows = block(b)
        pos = lax.broadcasted_iota(jnp.int32, (ROWS, 256), 0) + b * ROWS
        for c in range(4):
            rhs[c, rows, :] = jnp.where(pos < length[0], rhs[c, rows, :].astype(f32), 0.0).astype(bf16)
        return carry

    near_d = [2 * tensor + j for j in range(2)]
    direct_d = [8 + 2 * core, 9 + 2 * core, 12 + 2 * core, 13 + 2 * core]

    def slab(k):
        return pl.ds(pl.multiple_of(4 * k, 4), 4)

    def d_copy(k, sends, recvs, dev, axis, src=None):
        return remote((ybuf if src is None else src).at[slab(k)], ybuf.at[slab(k)], sends.at[k], recvs.at[k], dev, axis)

    def d_y(k):
        return d_copy(k, dys, dyr, mate, "dp", pbuf)

    def d_c(k):
        return d_copy(k, dcs, dcr, core_mate, "tensor")

    def d_x(k):
        return d_copy(k, dxs, dxr, x_mate, "tensor")

    def d_f(k):
        return d_copy(k, dfs, dfr, core_mate, "tensor")

    def stage_d(k):
        rows = block(k, 64)
        live = lax.broadcasted_iota(jnp.int32, (64, 256), 0) + k * 64 < length[0]
        for c in range(4):
            pbuf[4 * k + c] = jnp.where(live, rhs[c, rows, :].astype(f32), 0.0)
        d_y(k).start()

    def h_piece(b, t):
        return 4 * b + t

    def h_copy(b, t, sends, recvs, dev, axis):
        part = zbuf.at[slab(h_piece(b, t))]
        return remote(part, part, sends.at[b], recvs.at[b], dev, axis)

    def h_stage(b):
        return 2 * x_mate + b if isinstance(b, int) and b < 2 else 2 * jnp.where(b < 2, x_mate, core_mate) + b % 2

    def h_y(b):
        return remote(
            pbuf.at[slab(h_stage(b))], zbuf.at[slab(h_piece(b, tensor))], hys.at[b], hyr.at[b], mate
        )

    def h_c(b):
        return h_copy(b, tensor, hcs, hcr, core_mate, "tensor")

    def h_x(b):
        return h_copy(b, tensor, hxs, hxr, x_mate, "tensor")

    def h_f(b):
        return h_copy(b, x_mate, hfs, hfr, core_mate, "tensor")

    def h_send(b):
        rows = pl.ds(pl.multiple_of(b * 256 + tensor * 64, 64), 64)
        for c in range(4):
            pbuf[4 * h_stage(b) + c] = hbuf[rows, 256 * c : 256 * c + 256].astype(f32)
        h_y(b).start()

    def h_share(b):
        h_y(b).wait_recv()
        h_x(b).start()
        h_c(b).start()

    def h_forward(b):
        h_x(b).wait_recv()
        h_f(b).start()

    def d_share(j):
        k = near_d[j]
        d_y(k).wait_recv()
        d_x(k).start()
        d_c(k).start()

    def d_forward(j):
        k = 2 * x_mate + j
        d_x(k).wait_recv()
        d_f(k).start()

    def d_direct(j):
        k = direct_d[j]
        d_y(k).wait_recv()
        d_c(k).start()

    wait(late_load)
    stage_d(near_d[0])
    wait(token_load + proj_load)
    head_rows(0, 0)
    attend(0)
    head_rows(1, 0)
    w_x.wait_recv()
    w_y.start()
    attend(1)
    head_rows(2, 0)
    attend(2)
    w_y.wait_recv()
    w_z.start()
    stage_d(near_d[1])
    head_rows(3, 0)
    start(expert_load(8 * y, 0))
    attend(3)
    lax.fori_loop(0, 4, mask_rows, 0)
    for j in range(2):
        stage_d(direct_d[j])
    dk_acc[...] = jnp.zeros_like(dk_acc)
    dv_acc[...] = jnp.zeros_like(dv_acc)
    norms[...] = jnp.zeros_like(norms)


    expert_id = lax.broadcasted_iota(jnp.int32, (EXPERTS, 1024), 0)
    alive = lax.broadcasted_iota(jnp.int32, (EXPERTS, 1024), 1) < length[0]
    hits = jnp.zeros((EXPERTS, 1024), f32)
    weight = jnp.zeros((EXPERTS, 1024), f32)
    for k in range(TOP_K):
        same = (picks[k : k + 1, :] == expert_id) & alive
        hits = jnp.where(same, 1.0, hits)
        weight = jnp.where(same, pick_w[k : k + 1, :], weight)
    hits = hits.astype(bf16)
    limit = ((5 * TOP_K * length[0] + 4 * EXPERTS - 1) // (4 * EXPERTS)).astype(f32)
    for b in range(4):
        rows = pl.ds(ROWS * b, ROWS)
        token = lax.broadcasted_iota(jnp.int32, (1024, ROWS), 1) + ROWS * b
        earlier = jnp.where(lax.broadcasted_iota(jnp.int32, (1024, ROWS), 0) < token, 1.0, 0.0).astype(bf16)
        places = dot_f(hits, earlier)
        kept = jnp.where(places < limit, weight[:, ROWS * b : ROWS * b + ROWS], 0.0)
        kept_out[:, rows] = kept
        slot_w[rows, :] = jnp.concatenate([kept, jnp.zeros((LANES - EXPERTS, ROWS), f32)], axis=0).T

    kept_copy = remote(kept_out, kept_in, ks.at[0], kr.at[0], mate)
    kept_copy.start()

    w_z.wait_recv()
    w_f.start()
    w_c.wait_recv()
    w_f.wait_recv()

    def cast_out(b, carry):
        for c in range(4):
            rhs[26 + c, block(b, 64), :] = buf[block(b, 64), 256 * c : 256 * c + 256].astype(bf16)
        return carry

    lax.fori_loop(0, 16, cast_out, 0)

    def forward_rows(b, carry):
        rows = block(b)
        for k in range(4):
            part = acc[rows, 256 * k : 256 * k + 256].astype(bf16)
            if k == 0:
                sums = [
                    hbuf[rows, 256 * col : 256 * col + 256].astype(f32) + dot_f(part, rhs[26 + col, 0:256, :])
                    for col in range(4)
                ]
            else:
                sums = [
                    sums[col] + dot_f(part, rhs[26 + col, 256 * k : 256 * k + 256, :]) for col in range(4)
                ]
        square = sum(jnp.sum(v * v, axis=1, keepdims=True) for v in sums)
        scale_r = lax.rsqrt(square * (1.0 / 1024.0) + EPSILON)
        for col in range(4):
            buf[rows, 256 * col : 256 * col + 256] = sums[col]
            normed = sums[col] * scale_r * gain[0:1, 256 * col : 256 * col + 256]
            hbuf[rows, 256 * col : 256 * col + 256] = normed.astype(bf16)
            for half_c in range(2):
                lhs[16 + 2 * col + half_c, :, rows] = normed[:, 128 * half_c : 128 * half_c + 128].T.astype(bf16)
        return carry

    def place_of(k):
        paired = EARLY + (k - 2 * EARLY) // 2
        return jnp.where(k < EARLY, k, jnp.where(k < 2 * EARLY, k - EARLY, jnp.where(k < 16, paired, k - 16)))

    def is_mate(k):
        return ((k >= EARLY) & (k < 2 * EARLY)) | ((k >= 2 * EARLY) & (k < 16) & ((k - 2 * EARLY) % 2 == 1))

    def expert_of(k):
        return jnp.where(k < 16, 8 * y + place_of(k), 8 * (1 - y) + place_of(k))

    def next_weights(k):
        wait(expert_load(expert_of(k), k % 2))

        @pl.when(k < 23)
        def _():
            start(expert_load(expert_of(k + 1), (k + 1) % 2))

    def unit(k, b, kind, size=ROWS):
        rows = block(b, size)
        s = k % 2
        e = expert_of(k)
        el = place_of(k)
        if kind == "mate":
            both = dot_f(rhs[26, rows, :], wgu[s, 0:256, :])
            for c in range(1, 4):
                both = both + dot_f(rhs[26 + c, rows, :], wgu[s, 256 * c : 256 * c + 256, :])
        else:
            both = dot_f(hbuf[rows, :], wgu[s])
        d_base = 12 if kind == "mate" else 0
        gate, up = both[:, :LANES], both[:, LANES:]
        d_raw = dot_nt(rhs[d_base, rows, :], wdb[s, :, 0:256])
        for c in range(1, 4):
            d_raw = d_raw + dot_nt(rhs[d_base + c, rows, :], wdb[s, :, 256 * c : 256 * c + 256])
        lane = lax.broadcasted_iota(jnp.int32, (size, LANES), 1)
        weights = slot_m if kind == "mate" else slot_w
        weight = jnp.sum(jnp.where(lane == e, weights[rows, :], 0.0), axis=1, keepdims=True)
        sigma = 1.0 / (1.0 + jnp.exp(-gate))
        silu = gate * sigma
        hidden = silu * up
        hidden_t = (hidden * weight).T.astype(bf16)
        d_hidden = d_raw * weight
        d_gate = (d_hidden * up * sigma * (1.0 + gate * (1.0 - sigma))).astype(bf16)
        d_up = (d_hidden * silu).astype(bf16)
        if kind == "mate":
            lhs[42 + el, :, rows] = hidden_t
            rhs[16 + el, rows, 0:LANES] = d_gate
            rhs[16 + el, rows, LANES:] = d_up
            return
        lhs[e, :, rows] = hidden_t
        inner = jnp.sum(hidden * d_raw, axis=1, keepdims=True)
        inner = jnp.where(weight > 0.0, inner, 0.0)
        is_first = kind == "first"
        acc[rows, 1024:1152] = jnp.where(lane == e, inner, 0.0 if is_first else acc[rows, 1024:1152])
        if kind == "other":
            part = dot_nt(jnp.concatenate([d_gate, d_up], axis=1), wgu[s])
        else:
            rhs[4 + el, rows, 0:LANES] = d_gate
            rhs[4 + el, rows, LANES:] = d_up
            part = dot_nt(rhs[4 + el, rows, :], wgu[s])
        acc[rows, 0:1024] = part if is_first else acc[rows, 0:1024] + part

    def forward_step(b, carry):
        @pl.when(b < 4)
        def _():
            gather_x(b).wait_recv()
            gather_f(b).start()

        @pl.when(b == 3)
        def _():
            d_share(0)
            d_share(1)

        @pl.when(b > 0)
        def _():
            gather_c(b - 1).wait_recv()
            gather_f(b - 1).wait_recv()
            gather_f(b - 1).wait_send()
            gather_x(b - 1).wait_send()
            gather_c(b - 1).wait_send()
            forward_rows(b - 1, 0)
            h_send(b - 1)
            unit(0, b - 1, "first")

        @pl.when(b == 4)
        def _():
            stage_d(direct_d[2])
            stage_d(direct_d[3])

        return carry

    for copy in (w_x, w_c, w_f, w_y, w_z):
        copy.wait_send()
    next_weights(0)
    lax.fori_loop(0, 5, forward_step, 0)
    keep = local(buf.at[:, wide], s_resid, iosem.at[0])
    keep.start()

    chores = {
        4: [(d_direct, 0), (d_direct, 1), (h_share, 0)],
        7: [(h_share, 1)],
        9: [(d_forward, 0)],
        11: [(h_share, 2)],
        13: [(d_forward, 1)],
        15: [(h_share, 3)],
        17: [(h_forward, 0)],
        22: [(h_forward, 1)],
        24: [(d_direct, 2)],
        27: [(h_forward, 2)],
    }

    def own_unit(u, carry):
        k = u // 4

        @pl.when(u % 4 == 0)
        def _():
            next_weights(k)

        @pl.when(u % 2 == 0)
        def _():
            unit(k, (u % 4) // 2, "own", 2 * ROWS)

        for when_u, jobs in chores.items():

            @pl.when(u == when_u)
            def _(jobs=jobs):
                for job, arg in jobs:
                    job(arg)

        return carry

    lax.fori_loop(4, 4 * EARLY, own_unit, 0)

    kept_copy.wait_recv()
    for b in range(4):
        rows = pl.ds(ROWS * b, ROWS)
        slot_m[rows, :] = jnp.concatenate(
            [kept_in[:, rows], jnp.zeros((LANES - EXPERTS, ROWS), f32)], axis=0
        ).T

    def take(b):
        rows = pl.ds(ROWS * b, ROWS)
        h_c(b).wait_recv()
        h_f(b).wait_recv()
        for c in range(4):
            whole = jnp.concatenate([ybuf[4 * (4 * b + j) + c] for j in range(4)], axis=0)
            rhs[12 + c, rows, :] = whole.astype(bf16)
            whole = jnp.concatenate([zbuf[4 * (4 * b + j) + c] for j in range(4)], axis=0)
            rhs[26 + c, rows, :] = whole.astype(bf16)
            for half_c in range(2):
                lhs[34 + 2 * c + half_c, :, rows] = whole[:, 128 * half_c : 128 * half_c + 128].T.astype(bf16)
        unit(EARLY, b, "mate")

    next_weights(EARLY)
    for j in range(2):
        d_c(2 * core_mate + j).wait_recv()
        d_f(2 * (3 - tensor) + j).wait_recv()
    take(0)
    take(1)
    for j in range(2):
        d_c(8 + 2 * (1 - core) + j).wait_recv()
    take(2)
    d_direct(3)
    h_forward(3)
    for j in range(2):
        d_c(12 + 2 * (1 - core) + j).wait_recv()
    take(3)
    kept_copy.wait_send()
    for j in range(2):
        d_y(near_d[j]).wait_send()
        d_x(near_d[j]).wait_send()
        d_c(near_d[j]).wait_send()
        d_f(2 * x_mate + j).wait_send()
    for j in range(4):
        d_y(direct_d[j]).wait_send()
        d_c(direct_d[j]).wait_send()
    for b in range(4):
        h_y(b).wait_send()
        h_x(b).wait_send()
        h_c(b).wait_send()
        h_f(b).wait_send()

    pl.semaphore_signal(go, inc=1, device_id={"dp": mate}, device_id_type=MESH)

    @pl.when(z < last)
    def _():
        pl.semaphore_signal(go, inc=1, device_id={"dp": up_id}, device_id_type=MESH)

    @pl.when(z > 0)
    def _():
        pl.semaphore_signal(go, inc=1, device_id={"dp": dn_id}, device_id_type=MESH)

    pl.semaphore_wait(go, 1 + (z < last).astype(jnp.int32) + (z > 0).astype(jnp.int32))

    def half_pass(u):
        k = EARLY + 1 + u // 2

        @pl.when(u % 2 == 0)
        def _():
            next_weights(k)

        @pl.when(is_mate(k))
        def _():
            unit(k, u % 2, "mate", 2 * ROWS)

        @pl.when((k < 16) & jnp.logical_not(is_mate(k)))
        def _():
            unit(k, u % 2, "own", 2 * ROWS)

        @pl.when(k >= 16)
        def _():
            unit(k, u % 2, "other", 2 * ROWS)

    mine = pl.ds(pl.multiple_of(core * 512, 512), 512)
    other = pl.ds(pl.multiple_of((1 - core) * 512, 512), 512)

    def span(k):
        return pl.ds(0, 1152 if k == 0 else 1024)

    def sum_a(k):
        return remote(acc.at[other, span(k)], buf.at[pl.ds(0, 512), span(k)], s1s.at[k], s1r.at[k], core_mate, "tensor")

    def sum_b(k):
        return remote(acc.at[mine, span(k)], buf.at[pl.ds(512, 512), span(k)], s2s.at[k], s2r.at[k], x_mate, "tensor")

    def sum_c(k):
        part = acc.at[mine, span(k)]
        return remote(part, part, s3s.at[k], s3r.at[k], core_mate, "tensor")

    def add_in(k, at_row):
        def step(b, carry):
            rows = pl.ds(pl.multiple_of(core * 512 + b * 64, 64), 64)
            acc[rows, span(k)] += buf[pl.ds(pl.multiple_of(at_row + b * 64, 64), 64), span(k)]
            return carry

        lax.fori_loop(0, 8, step, 0)

    def sum_first(k):
        pl.semaphore_signal(ready1.at[k], inc=1, device_id={"tensor": core_mate}, device_id_type=MESH)
        pl.semaphore_signal(ready2.at[k], inc=1, device_id={"tensor": x_mate}, device_id_type=MESH)
        pl.semaphore_wait(ready1.at[k], 1)
        sum_a(k).start()

    def sum_second(k):
        sum_a(k).wait_recv()
        add_in(k, 0)
        sum_a(k).wait_send()
        pl.semaphore_signal(ready3.at[k], inc=1, device_id={"tensor": core_mate}, device_id_type=MESH)
        pl.semaphore_wait(ready2.at[k], 1)
        sum_b(k).start()

    def sum_third(k):
        sum_b(k).wait_recv()
        sum_b(k).wait_send()
        add_in(k, 512)
        pl.semaphore_wait(ready3.at[k], 1)
        sum_c(k).start()

    def sum_last(k):
        sum_c(k).wait_recv()
        sum_c(k).wait_send()

    def norm_sum(step, dev):
        return remote(norms.at[pl.ds(0, 16)], norm_in.at[step], ns.at[step], nr.at[step], dev)

    partners = (mate, pair, far)

    def norm_next(step):
        if step > 0:
            norm_sum(step - 1, partners[step - 1]).wait_recv()
            norm_sum(step - 1, partners[step - 1]).wait_send()
            norms[...] = norms[...] + norm_in[step - 1]
        if step < 3:
            norm_sum(step, partners[step]).start()

    def norm_back(values, scale_r, grads, which):
        inner = sum(
            jnp.sum(v * scale_r * (g * gain[which : which + 1, 256 * c : 256 * c + 256]), axis=1, keepdims=True)
            for c, (v, g) in enumerate(zip(values, grads))
        ) * (1.0 / 1024.0)
        outs = []
        for c, (v, g) in enumerate(zip(values, grads)):
            normed = v * scale_r
            total = jnp.sum(g * normed, axis=0, keepdims=True)
            row = 8 * which + 2 * c
            norms[row : row + 1, :] += total[:, :LANES]
            norms[row + 1 : row + 2, :] += total[:, LANES:]
            outs.append(scale_r * (g * gain[which : which + 1, 256 * c : 256 * c + 256] - normed * inner))
        return outs

    def middle_rows(b):
        rows = block(b)

        values = [buf[rows, 256 * c : 256 * c + 256] for c in range(4)]
        grads = [acc[rows, 256 * c : 256 * c + 256] for c in range(4)]
        square = sum(jnp.sum(v * v, axis=1, keepdims=True) for v in values)
        scale_r = lax.rsqrt(square * (1.0 / 1024.0) + EPSILON)
        back = norm_back(values, scale_r, grads, 0)
        for c in range(4):
            total = rhs[c, rows, :].astype(f32) + back[c]
            acc[rows, 256 * c : 256 * c + 256] = total
            rhs[26 + c, rows, :] = total.astype(bf16)
        for h in range(4):
            d_head = dot_nt(rhs[26, rows, :], wdb[h, :, 0:256])
            for c in range(1, 4):
                d_head = d_head + dot_nt(rhs[26 + c, rows, :], wdb[h, :, 256 * c : 256 * c + 256])
            da2[h, rows, :] = d_head.astype(bf16)

    def turn_back(grad, cols):
        one, two = grad[:32], grad[32:]
        cosine, sine = cos_t[:, cols], sin_t[:, cols]
        return jnp.concatenate([one * cosine + two * sine, two * cosine - one * sine], axis=0)

    def attend_back(h, qb):
        keys = ROWS * (qb + 1)
        rows = pl.ds(ROWS * qb, ROWS)
        q_rows = q2[h, rows, :]
        d_rows = da2[h, rows, :]
        exact = jnp.exp(masked_scores(h, qb) - lse[pl.ds(h, 1), rows])
        d_probs = dot_nt(v2[0:keys, :], d_rows)
        inner = jnp.sum(exact * d_probs, axis=0, keepdims=True)
        d_scores = (exact * (d_probs - inner)).astype(bf16)
        dk_acc[0:keys, :] += dot_f(d_scores, q_rows)
        dv_acc[0:keys, :] += dot_f(exact.astype(bf16), d_rows)
        k_head = kt2[pl.ds(pl.multiple_of((h // 2) * 64, 64), 64), 0:keys]
        d_q = dot_f(k_head, d_scores) * scaling
        buf[pl.ds(pl.multiple_of(h * 64, 64), 64), rows] = turn_back(d_q, rows)

    def turn_rows(b):
        rows = block(b)
        rhs[24, rows, :] = buf[0:256, rows].T.astype(bf16)
        d_k = (dk_acc[rows, :] * scaling).T
        d_k = jnp.concatenate([turn_back(d_k[:64], rows), turn_back(d_k[64:], rows)], axis=0)
        rhs[25, rows, 0:LANES] = d_k.T.astype(bf16)
        rhs[25, rows, LANES:] = dv_acc[rows, :].astype(bf16)

    def project_rows(b):
        rows = block(b)
        acc[rows, 0:1024] = dot_nt(rhs[24, rows, :], wgu[0]) + dot_nt(rhs[25, rows, :], wgu[1])

    def token_rows(b):
        rows = block(b)

        values = [hbuf[rows, 256 * c : 256 * c + 256].astype(f32) for c in range(4)]
        grads = [acc[rows, 256 * c : 256 * c + 256] for c in range(4)]
        square = sum(jnp.sum(v * v, axis=1, keepdims=True) for v in values)
        scale_r = lax.rsqrt(square * (1.0 / 1024.0) + EPSILON)
        back = norm_back(values, scale_r, grads, 1)
        for c in range(4):
            cols = slice(256 * c, 256 * c + 256)
            hbuf[rows, cols] = (buf[rows, cols] + back[c]).astype(bf16)

    def pair_load(pair, s):
        return local(w_down.at[pl.ds(2 * pair, 2)], wdb.at[pl.ds(2 * s, 2)], wsem.at[s, 2])

    def moe_pair(pair):
        s = pair % 2
        pair_load(pair, s).wait()

        @pl.when(pair + 1 < EXPERTS // 2)
        def _():
            pair_load(pair + 1, 1 - s).start()

        def rows_of(b, carry):
            rows = block(b)
            hidden = lhs[pl.ds(2 * pair, 2), :, rows].reshape(256, ROWS)
            down = wdb[pl.ds(2 * s, 2)].reshape(256, 1024)
            part = dot_tn(hidden, down)

            @pl.when(pair == 0)
            def _():
                acc[rows, 0:1024] = part

            @pl.when(pair > 0)
            def _():
                acc[rows, 0:1024] += part

            return carry

        lax.fori_loop(0, 4, rows_of, 0)

    def result_rows(b):
        rows = block(b)

        pos = lax.broadcasted_iota(jnp.int32, (ROWS, 1024), 0) + b * ROWS
        total = buf[rows, wide] + acc[rows, 0:1024]
        hbuf[rows, :] = jnp.where(pos < length[0], total, 0.0).astype(bf16)

    def halves_in(src):
        return [local(src, buf.at[:, wide], iosem.at[1])]

    tokens_in = [local(x_in, hbuf, iosem.at[3])]
    wo_load = [
        local(w_out.at[pl.ds(64 * h, 64)], wdb.at[h, pl.ds(64 * (h // 2), 64)], ld.at[8 + h]) for h in range(4)
    ]
    dots_out = [local(d_pick, o_dots, iosem.at[7])]
    norms_out = [
        local(norms.at[pl.ds(0, 8)], o_norm0, iosem.at[2]),
        local(norms.at[pl.ds(8, 8)], o_norm1, iosem.at[4]),
    ]

    def pick_dots():
        for b in range(4):
            rows = pl.ds(ROWS * b, ROWS)
            dots = acc[rows, 1024:1152].T[:EXPERTS]
            lane_e = lax.broadcasted_iota(jnp.int32, (EXPERTS, ROWS), 0)
            for k in range(TOP_K):
                mine_k = jnp.where(picks[k : k + 1, rows] == lane_e, dots, 0.0)
                d_pick[k : k + 1, rows] = jnp.sum(mine_k, axis=0, keepdims=True)
    dres_out = [local(acc.at[:, wide], s_dres, iosem.at[8])]
    tokens_out = [local(hbuf, o_tokens, iosem.at[9])]
    result_out = [local(hbuf, o_result, iosem.at[10])]

    def clear_wo():
        for h in range(4):
            wdb[h, 64 - 64 * (h // 2) : 128 - 64 * (h // 2), :] = jnp.zeros((64, 1024), bf16)

    def do_all(*steps):
        for step in steps:
            step()

    once = {
        T_SUM1: lambda: do_all(keep.wait, lambda: sum_first(0), clear_wo, lambda: start(tokens_in + wo_load + proj_load)),
        T_SUM1 + 2: lambda: do_all(lambda: sum_second(0), lambda: wait(tokens_in)),
        T_MID1 - 3: lambda: sum_third(0),
        T_MID1 - 1: lambda: do_all(
            lambda: sum_last(0), pick_dots, lambda: start(halves_in(s_resid) + dots_out), lambda: wait(wo_load)
        ),
        T_ATT: lambda: do_all(lambda: wait(dots_out), lambda: start(dres_out)),
        T_PROJ - 1: lambda: do_all(lambda: wait(dres_out), lambda: wait(proj_load)),
        T_SUM2: lambda: sum_first(1),
        T_SUM2 + 2: lambda: sum_second(1),
        T_TOK - 3: lambda: sum_third(1),
        T_TOK - 1: lambda: do_all(
            lambda: sum_last(1), lambda: start(halves_in(s_dres)), lambda: start([pair_load(0, 0)])
        ),
        T_MOE: lambda: start(tokens_out),
        T_SUM3 + 5: lambda: norm_next(0),
        T_SUM3 + 7: lambda: norm_next(1),
        T_SUM3 + 9: lambda: norm_next(2),
        T_SUM3 + 11: lambda: do_all(lambda: norm_next(3), lambda: start(norms_out)),
        T_SUM3: lambda: sum_first(2),
        T_SUM3 + 2: lambda: sum_second(2),
        T_RES - 3: lambda: sum_third(2),
        T_RES - 1: lambda: do_all(
            lambda: sum_last(2), lambda: wait(tokens_out + norms_out), lambda: start(halves_in(s_resid))
        ),
        T_RES + 4: lambda: start(result_out),
        T_RES + 8: lambda: wait(result_out),
    }
    halves_wait = {T_MID1: s_resid, T_TOK: s_dres, T_RES: s_resid}

    def work(t):
        for when_t, fn in sorted(once.items()):
            pl.when(t == when_t)(fn)
        for when_t, src in halves_wait.items():
            pl.when(t == when_t)(lambda src=src: wait(halves_in(src)))
        for begin, count, fn in (
            (0, 2 * (23 - EARLY), half_pass),
            (T_MID1, 4, middle_rows),
            (T_TURN, 2, lambda u: do_all(lambda: turn_rows(2 * u), lambda: turn_rows(2 * u + 1))),
            (T_PROJ, 2, lambda u: do_all(lambda: project_rows(2 * u), lambda: project_rows(2 * u + 1))),
            (T_TOK, 2, lambda u: do_all(lambda: token_rows(2 * u), lambda: token_rows(2 * u + 1))),
            (T_MOE, EXPERTS // 4, lambda u: do_all(lambda: moe_pair(2 * u), lambda: moe_pair(2 * u + 1))),
            (T_RES, 4, result_rows),
        ):
            pl.when((t >= begin) & (t < begin + count))(lambda fn=fn, begin=begin: fn(t - begin))
        for pair_b in range(2):
            u = t - T_ATT

            def two(pair_b=pair_b, u=u):
                attend_back(u // 2, pair_b)
                attend_back(u // 2, 3 - pair_b)

            pl.when((u >= 0) & (u < 8) & (u % 2 == pair_b))(two)

    own = pl.ds(pl.multiple_of(y * 32, 32), 32)
    oth = pl.ds(pl.multiple_of((1 - y) * 32, 32), 32)
    half = pl.ds(0, 32)
    upper = pl.ds(32, 32)

    def stage(c, t):
        p = z if c == 0 else last - z
        nxt, prv = (up_id, dn_id) if c == 0 else (dn_id, up_id)
        def at(delay, body):
            i = t - delay - c

            @pl.when((i >= 0) & (i < N_CLASS))
            def _():
                s = c * ring + i % ring
                body(i, s, i < N_EXPERT, (i >= N_EXPERT) & (i % 2 == 0), (i >= N_EXPERT) & (i % 2 == 1))

        def ycopy_a(s):
            return remote(pbuf.at[s, oth], ybuf.at[s, half], ys.at[s], yr.at[s], mate)

        def ycopy_b(s):
            return remote(zbuf.at[s], ybuf.at[s], ys.at[s], yr.at[s], mate)

        def zcopy_a(s):
            return remote(zbuf.at[s, half], zbuf.at[s, half], zs.at[s], zr.at[s], nxt)

        def zcopy(s):
            return remote(zbuf.at[s], zbuf.at[s], zs.at[s], zr.at[s], nxt)

        def fcopy_a(s):
            return remote(pbuf.at[s, own], pbuf.at[s, own], fs.at[s], fr.at[s], prv)

        def fcopy(s):
            return remote(pbuf.at[s], pbuf.at[s], fs.at[s], fr.at[s], prv)

        def gcopy_a(s):
            return remote(pbuf.at[s, own], ybuf.at[s, upper], gs.at[s], gr.at[s], mate)

        def gcopy(s):
            return remote(pbuf.at[s], ybuf.at[s], gs.at[s], gr.at[s], mate)

        def first(i, s, is_e, is_a, is_b):
            m = i // 2
            g = 2 * m + c

            @pl.when((i % 2 == 0) & is_e)
            def _():
                el, part = g // 12, g % 12
                down = part < 4
                l_one = jnp.where(down, 8 * y + el, 12 + part)
                r_one = jnp.where(down, part, 4 + el)
                l_two = jnp.where(down, 42 + el, 30 + part)
                r_two = jnp.where(down, 12 + part, 16 + el)
                total = dot_f(lhs[l_one], rhs[r_one]) + dot_f(lhs[l_two], rhs[r_two])
                pbuf[s] = total[:CHUNK]
                pbuf[s + 1] = total[CHUNK:]

            @pl.when((i % 2 == 0) & jnp.logical_not(is_e))
            def _():
                a = g - N_EXPERT
                l_one = jnp.where(a < 8, 32 + a // 4, 24 + a % 8)
                r_one = jnp.where(a < 8, 26 + a % 4, 23 + a // 8)
                total = dot_f(lhs[l_one], rhs[r_one])
                pbuf[s] = total[:CHUNK]
                pbuf[s + 1] = total[CHUNK:]

            @pl.when(is_a)
            def _():
                ycopy_a(s).start()

        def second(i, s, is_e, is_a, is_b):
            @pl.when(is_a)
            def _():
                ycopy_a(s).wait_recv()

                @pl.when(p > 0)
                def _():
                    zcopy_a(s).wait_recv()
                    zbuf[s, half] = zbuf[s, half] + (pbuf[s, own] + ybuf[s, half])

                @pl.when(p == 0)
                def _():
                    zbuf[s, half] = pbuf[s, own] + ybuf[s, half]

                @pl.when(p < last)
                def _():
                    zcopy_a(s).start()

                @pl.when(p == last)
                def _():
                    pbuf[s, own] = zbuf[s, half]
                    fcopy_a(s).start()
                    gcopy_a(s).start()

            @pl.when(jnp.logical_not(is_a))
            def _():
                @pl.when(p > 0)
                def _():
                    zcopy(s).wait_recv()
                    zbuf[s] = zbuf[s] + pbuf[s]

                @pl.when(p == 0)
                def _():
                    zbuf[s] = pbuf[s]

                @pl.when(p < last)
                def _():
                    zcopy(s).start()

                @pl.when((p == last) & is_e)
                def _():
                    pbuf[s] = zbuf[s]
                    fcopy(s).start()
                    gcopy(s).start()

                @pl.when((p == last) & is_b)
                def _():
                    ycopy_b(s).start()

        def third(i, s, is_e, is_a, is_b):
            @pl.when(is_b & (p == last))
            def _():
                ycopy_b(s).wait_recv()
                pbuf[s] = zbuf[s] + ybuf[s]
                fcopy(s).start()

        def fourth(i, s, is_e, is_a, is_b):
            @pl.when(p < last)
            def _():
                @pl.when(is_a)
                def _():
                    fcopy_a(s).wait_recv()

                    @pl.when(p > 0)
                    def _():
                        fcopy_a(s).start()

                    gcopy_a(s).start()

                @pl.when(jnp.logical_not(is_a))
                def _():
                    fcopy(s).wait_recv()

                    @pl.when(p > 0)
                    def _():
                        fcopy(s).start()

                    @pl.when(is_e)
                    def _():
                        gcopy(s).start()

        def store(buf_s, sem, dst0, dst1):
            local(buf_s.at[:, pl.ds(0, LANES)], dst0, sem).start()
            local(buf_s.at[:, pl.ds(LANES, LANES)], dst1, sem).start()

        def fifth(i, s, is_e, is_a, is_b):
            @pl.when(is_a)
            def _():
                gcopy_a(s).wait_recv()
                ycopy_a(s).wait_send()
                pbuf[s, oth] = ybuf[s, upper]

            @pl.when(is_e)
            def _():
                gcopy(s).wait_recv()

            g = 2 * (i // 2) + c
            el, part = g // 12, g % 12
            a = g - N_EXPERT
            low = CHUNK * (i % 2)

            def at_rows(start_row):
                return pl.ds(pl.multiple_of(start_row + low, CHUNK), CHUNK)

            def both_rows(write):
                write(pbuf.at[s], os0.at[s], 8 * y + el)
                write(ybuf.at[s], os1.at[s], 8 * (1 - y) + el)

            @pl.when(is_e & (part < 4))
            def _():
                col = pl.ds(pl.multiple_of(part * 256, LANES), LANES)
                col1 = pl.ds(pl.multiple_of(part * 256 + LANES, LANES), LANES)
                both_rows(
                    lambda src, sem, e: store(
                        src, sem, o_down.at[e, at_rows(0), col], o_down.at[e, at_rows(0), col1]
                    )
                )

            @pl.when(is_e & (part >= 4))
            def _():
                rows = at_rows((part - 4) * 128)
                both_rows(lambda src, sem, e: store(src, sem, o_gate.at[e, rows], o_up.at[e, rows]))

            @pl.when(jnp.logical_not(is_e) & (a < 8))
            def _():
                rows = at_rows((a // 4) * 128)
                col = pl.ds(pl.multiple_of((a % 4) * 256, LANES), LANES)
                col1 = pl.ds(pl.multiple_of((a % 4) * 256 + LANES, LANES), LANES)
                store(pbuf.at[s], os0.at[s], o_out.at[rows, col], o_out.at[rows, col1])

            @pl.when(jnp.logical_not(is_e) & (a >= 8) & (a < 16))
            def _():
                rows = at_rows((a - 8) * 128)
                store(pbuf.at[s], os0.at[s], o_q.at[rows, pl.ds(0, LANES)], o_q.at[rows, pl.ds(LANES, LANES)])

            @pl.when(jnp.logical_not(is_e) & (a >= 16))
            def _():
                rows = at_rows((a - 16) * 128)
                store(pbuf.at[s], os0.at[s], o_k.at[rows], o_v.at[rows])

        def sixth(i, s, is_e, is_a, is_b):
            local(pbuf.at[s], o_q.at[pl.ds(0, CHUNK)], os0.at[s]).wait()

            @pl.when(is_e)
            def _():
                local(ybuf.at[s], o_q.at[pl.ds(0, CHUNK)], os1.at[s]).wait()
                gcopy(s).wait_send()

            @pl.when(is_a)
            def _():
                gcopy_a(s).wait_send()

                @pl.when(p < last)
                def _():
                    zcopy_a(s).wait_send()

                @pl.when(p > 0)
                def _():
                    fcopy_a(s).wait_send()

            @pl.when(jnp.logical_not(is_a))
            def _():
                @pl.when(p < last)
                def _():
                    zcopy(s).wait_send()

                @pl.when((p == last) & is_b)
                def _():
                    ycopy_b(s).wait_send()

                @pl.when(p > 0)
                def _():
                    fcopy(s).wait_send()

        t2 = hop * (1 + p)
        t3 = hop * (2 + last)
        t4 = t3 + hop * (last - p)
        t5 = t4 + hop
        t6 = t5 + hop
        return [(0, first, at), (t2, second, at), (t3, third, at), (t4, fourth, at), (t5, fifth, at), (t6, sixth, at)]

    def body(t, carry):
        both = [stage(0, t), stage(1, t)]
        for k in (1, 2, 3, 4, 5, 0):
            if k == 0:
                work(t)
            for st in both:
                delay, fn, at = st[k]
                at(delay, fn)
        return carry

    total = N_CLASS + hop * (2 * last + 4) + 2
    lax.fori_loop(0, total, body, 0)


def run_layer(mesh, *operands):
    groups = mesh.shape["dp"]
    nz = 4 if groups % 8 == 0 else groups // 2
    last = nz - 1
    hop = HOP
    ring = hop * (2 * last + 4) + 2
    ring = max(32, ring + ring % 2)
    f32, bf16 = jnp.float32, jnp.bfloat16

    def out(shape, kind=f32):
        return jax.ShapeDtypeStruct(shape, kind)

    outs = [
        out((16, 1024, 128)), out((16, 1024, 128)), out((16, 128, 1024)),
        out((1024, 256)), out((1024, 128)), out((1024, 128)), out((256, 1024)), out((8, 128)), out((8, 128)),
        out((1024, 1024), bf16), out((1024, 1024), bf16), out((8, 1024)),
        out((1024, 1024)), out((1024, 1024)),
    ]
    anywhere = pl.BlockSpec(memory_space=pl.ANY)
    dma = pltpu.SemaphoreType.DMA
    reg = pltpu.SemaphoreType.REGULAR
    vmem = pltpu.VMEM
    res = pl.pallas_call(
        functools.partial(layer_kernel, nz, hop, ring),
        out_shape=outs,
        in_specs=[pl.BlockSpec(memory_space=pltpu.SMEM)] + [anywhere] * (len(operands) - 1),
        out_specs=[anywhere] * len(outs),
        scratch_shapes=[
            vmem((50, 128, 1024), bf16), vmem((30, 1024, 256), bf16),
            vmem((2 * ring, CHUNK, 256), f32), vmem((2 * ring, CHUNK, 256), f32), vmem((2 * ring, CHUNK, 256), f32),
            vmem((1024, 1152), f32), vmem((1024, 1152), f32),
            vmem((1024, 1024), bf16), vmem((2, 1024, 256), bf16), vmem((4, 128, 1024), bf16),
            vmem((4, 1024, 128), bf16), vmem((1024, 128), bf16), vmem((1024, 128), bf16),
            vmem((128, 1024), bf16), vmem((128, 1024), bf16),
            vmem((8, 1024), f32), vmem((32, 1024), f32), vmem((32, 1024), f32),
            vmem((4, 1024, 128), bf16), vmem((1024, 128), f32), vmem((1024, 128), f32),
            vmem((1024, 128), f32), vmem((8, 1024), f32), vmem((16, 128), f32),
            vmem((8, 1024), jnp.int32), vmem((8, 1024), f32),
            vmem((3, 16, 128), f32), vmem((8, 1024), f32),
            vmem((EXPERTS, 1024), f32), vmem((EXPERTS, 1024), f32), vmem((1024, 128), f32),
            dma((18,)), dma((2, 3)), dma((11,)),
        ]
        + [dma((2 * ring,))] * 10
        + [dma((4,))] * 6
        + [dma((5,))] * 2
        + [dma((3,))] * 6
        + [reg((3,))] * 3
        + [dma((3,))] * 2
        + [reg]
        + [dma((4,))] * 8
        + [dma((16,))] * 8
        + [dma((1,))] * 2,
        compiler_params=pltpu.CompilerParams(
            collective_id=0, has_side_effects=True, vmem_limit_bytes=63 * 2**20
        ),
    )(*operands)
    sums, rest = tuple(res[:9]), res[9:12]
    if groups > 2 * nz:
        same = [
            [2 * nz * block + place for block in range(groups // (2 * nz))] for place in range(2 * nz)
        ]
        sums = lax.psum(sums, "dp", axis_index_groups=same)
    return sums, rest


def per_device(
    mesh,
    tokens,
    lengths,
    chosen,
    gate_values,
    cotangent,
    norm_attn,
    w_query,
    w_key,
    w_value,
    w_out,
    norm_moe,
    w_gate,
    w_up,
    w_down,
):
    seq_len = tokens.shape[0] // lengths.shape[0]
    cosine, sine = rope_tables(seq_len, HEAD_DIM)
    sums, (result, grad_tokens, dots) = run_layer(
        mesh,
        lengths,
        tokens,
        cotangent,
        chosen.T,
        gate_values.T,
        norm_attn[None, :],
        norm_moe[None, :],
        w_gate,
        w_up,
        w_down,
        cosine,
        sine,
        w_out,
        w_query,
        w_key,
        w_value,
    )
    grad_gate, grad_up, grad_down, grad_query, grad_key, grad_value, grad_out, grad_norm_moe, grad_norm_attn = sums
    return (
        result,
        grad_tokens,
        dots.T,
        grad_norm_attn.reshape(-1),
        grad_query,
        grad_key,
        grad_value,
        grad_out,
        grad_norm_moe.reshape(-1),
        grad_gate,
        grad_up,
        grad_down,
    )


def solution(mesh):
    placed = (
        P("dp", None),
        P("dp"),
        P("dp", None),
        P("dp", None),
        P("dp", None),
        P(),
        P(None, "tensor"),
        P(None, "tensor"),
        P(None, "tensor"),
        P("tensor", None),
        P(),
        P(None, None, "tensor"),
        P(None, None, "tensor"),
        P(None, "tensor", None),
    )
    return jax.shard_map(
        functools.partial(per_device, mesh),
        mesh=mesh,
        in_specs=placed,
        out_specs=(
            P("dp", None),
            P("dp", None),
            P("dp", None),
            P(),
            P(None, "tensor"),
            P(None, "tensor"),
            P(None, "tensor"),
            P("tensor", None),
            P(),
            P(None, None, "tensor"),
            P(None, None, "tensor"),
            P(None, "tensor", None),
        ),
        check_vma=False,
    )
```

```python
import functools
import math

import jax
import jax.numpy as jnp
import numpy as np
from jax import lax
from jax.experimental import pallas as pl
from jax.experimental.pallas import tpu as pltpu
from jax.sharding import PartitionSpec as P

MESH = pl.DeviceIdType.MESH

HEAD_DIM = 64
TOP_K = 8
EXPERTS = 16


EPSILON = 1e-05
THETA = 10000.0
NEGATIVE = -1e30


def dot_f(left, right):
    return jnp.dot(left, right, preferred_element_type=jnp.float32)


def rope_tables(positions, width):
    half_w = width // 2
    freqs = THETA ** (-np.arange(half_w, dtype=np.float64) * 2.0 / width)
    angles = freqs[:, None] * np.arange(positions, dtype=np.float64)[None, :]
    return (np.cos(angles).astype(np.float32), np.sin(angles).astype(np.float32))


LANES = 128
ROWS = 256
CHUNK = 64
N_EXPERT = 96
N_CLASS = 120
HOP = 2
EARLY = 7
T_SUM1 = 32
T_MID1 = 58
T_ATT = 62
T_TURN = 70
T_PROJ = 72
T_SUM2 = 74
T_TOK = 98
T_MOE = 100
T_SUM3 = 104
T_RES = 128


def dot_nt(left, right):
    return lax.dot_general(
        left, right, (((1,), (1,)), ((), ())), preferred_element_type=jnp.float32
    )


def dot_tn(left, right):
    return lax.dot_general(
        left, right, (((0,), (0,)), ((), ())), preferred_element_type=jnp.float32
    )


def layer_kernel(
    nz, hop, ring,
    length, x_in, d_out, chosen, gates, gain_attn, gain_moe, w_gate, w_up, w_down,
    cos_in, sin_in, w_out, w_query, w_key, w_value,
    o_gate, o_up, o_down, o_q, o_k, o_v, o_out, o_norm0, o_norm1, o_result, o_tokens, o_dots, s_resid, s_dres,
    lhs, rhs, pbuf, zbuf, ybuf, acc, buf, hbuf, wgu, wdb, q2, k2, v2, kt2, vt2, lse, cos_t, sin_t,
    da2, dk_acc, dv_acc, slot_w, gain, norms, picks, pick_w, norm_in, d_pick, kept_out, kept_in, slot_m,
    ld, wsem, iosem, ys, yr, zs, zr, fs, fr, gs, gr, os0, os1,
    cs_c, cr_c, cs_x, cr_x, cs_f, cr_f, ws, wr, s1s, s1r, s2s, s2r, s3s, s3r, ready1, ready2, ready3, ns, nr, go,
    hys, hyr, hcs, hcr, hxs, hxr, hfs, hfr, dys, dyr, dcs, dcr, dxs, dxr, dfs, dfr, ks, kr,
):
    f32, bf16 = jnp.float32, jnp.bfloat16
    dp = lax.axis_index("dp")
    tensor = lax.axis_index("tensor")
    base = dp - dp % (2 * nz)
    z, y = (dp % (2 * nz)) // 2, dp % 2
    last = nz - 1
    mate = base + z * 2 + (1 - y)
    up_id = base + jnp.minimum(z + 1, last) * 2 + y
    dn_id = base + jnp.maximum(z - 1, 0) * 2 + y
    far = base + ((z + 2) % nz) * 2 + y
    core = tensor % 2
    core_mate = tensor - core + (1 - core)
    x_mate = (tensor + 2) % 4

    def local(src, dst, sem):
        return pltpu.make_async_copy(src, dst, sem)

    def remote(src, dst, ssem, rsem, dev, axis="dp"):
        return pltpu.make_async_remote_copy(
            src_ref=src, dst_ref=dst, send_sem=ssem, recv_sem=rsem,
            device_id={axis: dev}, device_id_type=MESH,
        )

    def block(b, size=ROWS):
        return pl.ds(pl.multiple_of(b * size, size), size)

    bar = pltpu.get_barrier_semaphore()
    for axis, dev in (("dp", mate), ("dp", far), ("tensor", core_mate), ("tensor", x_mate)):
        pl.semaphore_signal(bar, inc=1, device_id={axis: dev}, device_id_type=MESH)

    @pl.when(z < last)
    def _():
        pl.semaphore_signal(bar, inc=1, device_id={"dp": up_id}, device_id_type=MESH)

    @pl.when(z > 0)
    def _():
        pl.semaphore_signal(bar, inc=1, device_id={"dp": dn_id}, device_id_type=MESH)

    wide = pl.ds(0, 1024)
    share = block(tensor)
    token_load = [
        local(x_in, hbuf, ld.at[0]),
        local(gain_attn, gain.at[pl.ds(1, 1)], ld.at[1]),
        local(gain_moe, gain.at[pl.ds(0, 1)], ld.at[2]),
        local(cos_in, cos_t, ld.at[3]),
        local(sin_in, sin_t, ld.at[4]),
    ]
    proj_load = [
        local(w_query, wgu.at[0], ld.at[5]),
        local(w_key, wgu.at[1, :, pl.ds(0, LANES)], ld.at[6]),
        local(w_value, wgu.at[1, :, pl.ds(LANES, LANES)], ld.at[7]),
    ]
    out_load = [local(w_out.at[:, block(c)], rhs.at[26 + c, share], ld.at[8 + c]) for c in range(4)]
    late_load = [local(d_out.at[:, block(c)], rhs.at[c], ld.at[12 + c]) for c in range(4)] + [
        local(chosen, picks, ld.at[16]),
        local(gates, pick_w, ld.at[17]),
    ]

    def expert_load(e, s):
        return [
            local(w_gate.at[e], wgu.at[s, :, pl.ds(0, LANES)], wsem.at[s, 0]),
            local(w_up.at[e], wgu.at[s, :, pl.ds(LANES, LANES)], wsem.at[s, 1]),
            local(w_down.at[e], wdb.at[s], wsem.at[s, 2]),
        ]

    def start(copies):
        for copy in copies:
            copy.start()

    def wait(copies):
        for copy in copies:
            copy.wait()

    start(out_load + token_load + proj_load + late_load)
    pl.semaphore_wait(bar, 4 + (z < last).astype(jnp.int32) + (z > 0).astype(jnp.int32))

    part_w = buf.at[share, wide]
    quarter = 2 * (z % 2) + y
    part_q = buf.at[pl.ds(pl.multiple_of(tensor * 256 + quarter * 64, 64), 64), wide]
    part_y = buf.at[pl.ds(pl.multiple_of(x_mate * 256 + quarter * 64, 64), 64), wide]
    near_q = 2 * (z % 2) + 1 - y
    part_z = buf.at[pl.ds(pl.multiple_of(x_mate * 256 + near_q * 64, 64), 64), wide]
    pair = base + (z + 1 - 2 * (z % 2)) * 2 + y
    w_x = remote(part_q, part_q, ws.at[0], wr.at[0], x_mate, "tensor")
    w_y = remote(part_y, part_y, ws.at[3], wr.at[3], mate)
    w_z = remote(part_z, part_z, ws.at[4], wr.at[4], pair)
    w_p = remote(part_y, part_y, ws.at[5], wr.at[5], pair)
    w_c = remote(part_w, part_w, ws.at[1], wr.at[1], core_mate, "tensor")
    part_f = buf.at[block(x_mate), wide]
    w_f = remote(part_f, part_f, ws.at[2], wr.at[2], core_mate, "tensor")
    wait(out_load)
    for c in range(4):
        buf[share, 256 * c : 256 * c + 256] = rhs[26 + c, share, :].astype(f32)
    w_x.start()
    w_c.start()

    def gather_x(b):
        return remote(
            acc.at[block(b), share], acc.at[block(b), share], cs_x.at[b], cr_x.at[b], x_mate, "tensor"
        )

    def gather_c(b):
        return remote(
            acc.at[block(b), share], acc.at[block(b), share], cs_c.at[b], cr_c.at[b], core_mate, "tensor"
        )

    def gather_f(b):
        part = acc.at[block(b), block(x_mate)]
        return remote(part, part, cs_f.at[b], cr_f.at[b], core_mate, "tensor")

    def rotate_t(values, cols):
        one, two = values[:32], values[32:]
        cosine, sine = cos_t[:, cols], sin_t[:, cols]
        return jnp.concatenate([one * cosine - two * sine, two * cosine + one * sine], axis=0)

    def head_rows(b, carry):
        rows = block(b)
        vals = [hbuf[rows, 256 * col : 256 * col + 256].astype(f32) for col in range(4)]
        square = sum(jnp.sum(v * v, axis=1, keepdims=True) for v in vals)
        scale_r = lax.rsqrt(square * (1.0 / 1024.0) + EPSILON)
        query, key_value = 0.0, 0.0
        for col in range(4):
            normed = vals[col] * scale_r * gain[1:2, 256 * col : 256 * col + 256]
            for half_c in range(2):
                lhs[24 + 2 * col + half_c, :, rows] = normed[:, 128 * half_c : 128 * half_c + 128].T.astype(bf16)
            normed = normed.astype(bf16)
            query = query + dot_f(normed, wgu[0, 256 * col : 256 * col + 256, :])
            key_value = key_value + dot_f(normed, wgu[1, 256 * col : 256 * col + 256, :])
        query = query.T
        nothing = jnp.zeros((64, ROWS), f32)
        for h in range(4):
            turned = rotate_t(query[64 * h : 64 * h + 64], rows)
            both = [turned, nothing] if h < 2 else [nothing, turned]
            q2[h, rows, :] = jnp.concatenate(both, axis=0).T.astype(bf16)
        key = key_value[:, :LANES].T
        key = jnp.concatenate([rotate_t(key[:64], rows), rotate_t(key[64:], rows)], axis=0)
        kt2[:, rows] = key.astype(bf16)
        k2[rows, :] = key.T.astype(bf16)
        value = key_value[:, LANES:]
        v2[rows, :] = value.astype(bf16)
        vt2[:, rows] = value.T.astype(bf16)
        return carry

    scaling = 1.0 / math.sqrt(HEAD_DIM)

    def masked_scores(h, qb):
        keys = ROWS * (qb + 1)
        rows = pl.ds(ROWS * qb, ROWS)
        scores = dot_nt(k2[0:keys, :], q2[h, rows, :]) * scaling
        k_pos = lax.broadcasted_iota(jnp.int32, (keys, ROWS), 0)
        q_pos = lax.broadcasted_iota(jnp.int32, (keys, ROWS), 1) + ROWS * qb
        allowed = (k_pos <= q_pos) & (k_pos < length[0])
        return jnp.where(allowed, scores, NEGATIVE)

    def attend(qb):
        keys = ROWS * (qb + 1)
        rows = pl.ds(ROWS * qb, ROWS)

        def one_head(h, carry):
            scores = masked_scores(h, qb)
            top_s = jnp.max(scores, axis=0, keepdims=True)
            expo = jnp.exp(scores - top_s)
            total = jnp.sum(expo, axis=0, keepdims=True)
            probs = (expo / total).astype(bf16)
            lse[pl.ds(h, 1), rows] = top_s + jnp.log(total)
            v_head = vt2[pl.ds(pl.multiple_of((h // 2) * 64, 64), 64), 0:keys]
            lhs[32 + h // 2, pl.ds(pl.multiple_of((h % 2) * 64, 64), 64), rows] = dot_f(v_head, probs).astype(bf16)
            return carry

        lax.fori_loop(0, 4, one_head, 0)
        for half_c in range(2):
            own_c = pl.ds(pl.multiple_of(tensor * 256 + half_c * 128, 128), 128)
            acc[rows, own_c] = lhs[32 + half_c, :, rows].astype(f32).T
        gather_x(qb).start()
        gather_c(qb).start()

    def mask_rows(b, carry):
        rows = block(b)
        pos = lax.broadcasted_iota(jnp.int32, (ROWS, 256), 0) + b * ROWS
        for c in range(4):
            rhs[c, rows, :] = jnp.where(pos < length[0], rhs[c, rows, :].astype(f32), 0.0).astype(bf16)
        return carry

    near_d = [2 * tensor + j for j in range(2)]
    direct_d = [8 + 2 * core, 9 + 2 * core, 12 + 2 * core, 13 + 2 * core]

    def slab(k):
        return pl.ds(pl.multiple_of(4 * k, 4), 4)

    def d_copy(k, sends, recvs, dev, axis, src=None):
        return remote((ybuf if src is None else src).at[slab(k)], ybuf.at[slab(k)], sends.at[k], recvs.at[k], dev, axis)

    def d_y(k):
        return d_copy(k, dys, dyr, mate, "dp", pbuf)

    def d_c(k):
        return d_copy(k, dcs, dcr, core_mate, "tensor")

    def d_x(k):
        return d_copy(k, dxs, dxr, x_mate, "tensor")

    def d_f(k):
        return d_copy(k, dfs, dfr, core_mate, "tensor")

    def stage_d(k):
        rows = block(k, 64)
        live = lax.broadcasted_iota(jnp.int32, (64, 256), 0) + k * 64 < length[0]
        for c in range(4):
            pbuf[4 * k + c] = jnp.where(live, rhs[c, rows, :].astype(f32), 0.0)
        d_y(k).start()

    def h_piece(b, t):
        return 4 * b + t

    def h_copy(b, t, sends, recvs, dev, axis):
        part = zbuf.at[slab(h_piece(b, t))]
        return remote(part, part, sends.at[b], recvs.at[b], dev, axis)

    def h_stage(b):
        return 2 * x_mate + b if isinstance(b, int) and b < 2 else 2 * jnp.where(b < 2, x_mate, core_mate) + b % 2

    def h_y(b):
        return remote(
            pbuf.at[slab(h_stage(b))], zbuf.at[slab(h_piece(b, tensor))], hys.at[b], hyr.at[b], mate
        )

    def h_c(b):
        return h_copy(b, tensor, hcs, hcr, core_mate, "tensor")

    def h_x(b):
        return h_copy(b, tensor, hxs, hxr, x_mate, "tensor")

    def h_f(b):
        return h_copy(b, x_mate, hfs, hfr, core_mate, "tensor")

    def h_send(b):
        rows = pl.ds(pl.multiple_of(b * 256 + tensor * 64, 64), 64)
        for c in range(4):
            pbuf[4 * h_stage(b) + c] = hbuf[rows, 256 * c : 256 * c + 256].astype(f32)
        h_y(b).start()

    def h_share(b):
        h_y(b).wait_recv()
        h_x(b).start()
        h_c(b).start()

    def h_forward(b):
        h_x(b).wait_recv()
        h_f(b).start()

    def d_share(j):
        k = near_d[j]
        d_y(k).wait_recv()
        d_x(k).start()
        d_c(k).start()

    def d_forward(j):
        k = 2 * x_mate + j
        d_x(k).wait_recv()
        d_f(k).start()

    def d_direct(j):
        k = direct_d[j]
        d_y(k).wait_recv()
        d_c(k).start()

    wait(late_load)
    stage_d(near_d[0])
    wait(token_load + proj_load)
    head_rows(0, 0)
    attend(0)
    head_rows(1, 0)
    w_x.wait_recv()
    w_y.start()
    w_p.start()
    attend(1)
    head_rows(2, 0)
    attend(2)
    w_y.wait_recv()
    w_z.start()
    stage_d(near_d[1])
    head_rows(3, 0)
    start(expert_load(8 * y, 0))
    attend(3)
    stage_d(direct_d[0])
    lax.fori_loop(0, 4, mask_rows, 0)
    dk_acc[...] = jnp.zeros_like(dk_acc)
    dv_acc[...] = jnp.zeros_like(dv_acc)
    norms[...] = jnp.zeros_like(norms)


    expert_id = lax.broadcasted_iota(jnp.int32, (EXPERTS, 1024), 0)
    alive = lax.broadcasted_iota(jnp.int32, (EXPERTS, 1024), 1) < length[0]
    hits = jnp.zeros((EXPERTS, 1024), f32)
    weight = jnp.zeros((EXPERTS, 1024), f32)
    for k in range(TOP_K):
        same = (picks[k : k + 1, :] == expert_id) & alive
        hits = jnp.where(same, 1.0, hits)
        weight = jnp.where(same, pick_w[k : k + 1, :], weight)
    hits = hits.astype(bf16)
    limit = ((5 * TOP_K * length[0] + 4 * EXPERTS - 1) // (4 * EXPERTS)).astype(f32)
    for b in range(4):
        rows = pl.ds(ROWS * b, ROWS)
        token = lax.broadcasted_iota(jnp.int32, (1024, ROWS), 1) + ROWS * b
        earlier = jnp.where(lax.broadcasted_iota(jnp.int32, (1024, ROWS), 0) < token, 1.0, 0.0).astype(bf16)
        places = dot_f(hits, earlier)
        kept = jnp.where(places < limit, weight[:, ROWS * b : ROWS * b + ROWS], 0.0)
        kept_out[:, rows] = kept
        slot_w[rows, :] = jnp.concatenate([kept, jnp.zeros((LANES - EXPERTS, ROWS), f32)], axis=0).T

    kept_copy = remote(kept_out, kept_in, ks.at[0], kr.at[0], mate)
    kept_copy.start()

    w_z.wait_recv()
    w_p.wait_recv()
    w_f.start()
    w_c.wait_recv()
    w_f.wait_recv()

    def cast_out(b, carry):
        for c in range(4):
            rhs[26 + c, block(b, 64), :] = buf[block(b, 64), 256 * c : 256 * c + 256].astype(bf16)
        return carry

    lax.fori_loop(0, 16, cast_out, 0)

    def forward_rows(b, carry):
        rows = block(b)
        for k in range(4):
            part = acc[rows, 256 * k : 256 * k + 256].astype(bf16)
            if k == 0:
                sums = [
                    hbuf[rows, 256 * col : 256 * col + 256].astype(f32) + dot_f(part, rhs[26 + col, 0:256, :])
                    for col in range(4)
                ]
            else:
                sums = [
                    sums[col] + dot_f(part, rhs[26 + col, 256 * k : 256 * k + 256, :]) for col in range(4)
                ]
        square = sum(jnp.sum(v * v, axis=1, keepdims=True) for v in sums)
        scale_r = lax.rsqrt(square * (1.0 / 1024.0) + EPSILON)
        for col in range(4):
            buf[rows, 256 * col : 256 * col + 256] = sums[col]
            normed = sums[col] * scale_r * gain[0:1, 256 * col : 256 * col + 256]
            hbuf[rows, 256 * col : 256 * col + 256] = normed.astype(bf16)
            for half_c in range(2):
                lhs[16 + 2 * col + half_c, :, rows] = normed[:, 128 * half_c : 128 * half_c + 128].T.astype(bf16)
        return carry

    def place_of(k):
        paired = EARLY + (k - 2 * EARLY) // 2
        return jnp.where(k < EARLY, k, jnp.where(k < 2 * EARLY, k - EARLY, jnp.where(k < 16, paired, k - 16)))

    def is_mate(k):
        return ((k >= EARLY) & (k < 2 * EARLY)) | ((k >= 2 * EARLY) & (k < 16) & ((k - 2 * EARLY) % 2 == 1))

    def expert_of(k):
        return jnp.where(k < 16, 8 * y + place_of(k), 8 * (1 - y) + place_of(k))

    def next_weights(k):
        wait(expert_load(expert_of(k), k % 2))

        @pl.when(k < 23)
        def _():
            start(expert_load(expert_of(k + 1), (k + 1) % 2))

    def unit(k, b, kind, size=ROWS):
        rows = block(b, size)
        s = k % 2
        e = expert_of(k)
        el = place_of(k)
        if kind == "mate":
            both = dot_f(rhs[26, rows, :], wgu[s, 0:256, :])
            for c in range(1, 4):
                both = both + dot_f(rhs[26 + c, rows, :], wgu[s, 256 * c : 256 * c + 256, :])
        else:
            both = dot_f(hbuf[rows, :], wgu[s])
        d_base = 12 if kind == "mate" else 0
        gate, up = both[:, :LANES], both[:, LANES:]
        d_raw = dot_nt(rhs[d_base, rows, :], wdb[s, :, 0:256])
        for c in range(1, 4):
            d_raw = d_raw + dot_nt(rhs[d_base + c, rows, :], wdb[s, :, 256 * c : 256 * c + 256])
        lane = lax.broadcasted_iota(jnp.int32, (size, LANES), 1)
        weights = slot_m if kind == "mate" else slot_w
        weight = jnp.sum(jnp.where(lane == e, weights[rows, :], 0.0), axis=1, keepdims=True)
        sigma = 1.0 / (1.0 + jnp.exp(-gate))
        silu = gate * sigma
        hidden = silu * up
        hidden_t = (hidden * weight).T.astype(bf16)
        d_hidden = d_raw * weight
        d_gate = (d_hidden * up * sigma * (1.0 + gate * (1.0 - sigma))).astype(bf16)
        d_up = (d_hidden * silu).astype(bf16)
        if kind == "mate":
            lhs[42 + el, :, rows] = hidden_t
            rhs[16 + el, rows, 0:LANES] = d_gate
            rhs[16 + el, rows, LANES:] = d_up
            return
        lhs[e, :, rows] = hidden_t
        inner = jnp.sum(hidden * d_raw, axis=1, keepdims=True)
        inner = jnp.where(weight > 0.0, inner, 0.0)
        is_first = kind == "first"
        acc[rows, 1024:1152] = jnp.where(lane == e, inner, 0.0 if is_first else acc[rows, 1024:1152])
        if kind == "other":
            part = dot_nt(jnp.concatenate([d_gate, d_up], axis=1), wgu[s])
        else:
            rhs[4 + el, rows, 0:LANES] = d_gate
            rhs[4 + el, rows, LANES:] = d_up
            part = dot_nt(rhs[4 + el, rows, :], wgu[s])
        acc[rows, 0:1024] = part if is_first else acc[rows, 0:1024] + part

    def forward_step(b, carry):
        @pl.when(b < 4)
        def _():
            gather_x(b).wait_recv()
            gather_f(b).start()

        @pl.when(b == 3)
        def _():
            d_share(0)
            d_share(1)

        @pl.when(b > 0)
        def _():
            gather_c(b - 1).wait_recv()
            gather_f(b - 1).wait_recv()
            gather_f(b - 1).wait_send()
            gather_x(b - 1).wait_send()
            gather_c(b - 1).wait_send()
            forward_rows(b - 1, 0)
            h_send(b - 1)
            unit(0, b - 1, "first")

        @pl.when(b == 4)
        def _():
            stage_d(direct_d[1])

        return carry

    for copy in (w_x, w_c, w_f, w_y, w_z, w_p):
        copy.wait_send()
    next_weights(0)
    lax.fori_loop(0, 5, forward_step, 0)
    keep = local(buf.at[:, wide], s_resid, iosem.at[0])
    keep.start()

    def d_late(j):
        stage_d(direct_d[j])

    chores = {
        4: [(h_share, 0), (h_share, 1)],
        8: [(d_forward, 0)],
        10: [(h_share, 2), (d_late, 2), (d_late, 3)],
        14: [(h_share, 3)],
        16: [(d_direct, 0), (h_forward, 0)],
        18: [(d_forward, 1), (d_direct, 1)],
        22: [(h_forward, 1)],
        27: [(h_forward, 2)],
    }

    def own_unit(u, carry):
        k = u // 4

        @pl.when(u % 4 == 0)
        def _():
            next_weights(k)

        @pl.when(u % 2 == 0)
        def _():
            unit(k, (u % 4) // 2, "own", 2 * ROWS)

        for when_u, jobs in chores.items():

            @pl.when(u == when_u)
            def _(jobs=jobs):
                for job, arg in jobs:
                    job(arg)

        return carry

    lax.fori_loop(4, 4 * EARLY, own_unit, 0)

    kept_copy.wait_recv()
    for b in range(4):
        rows = pl.ds(ROWS * b, ROWS)
        slot_m[rows, :] = jnp.concatenate(
            [kept_in[:, rows], jnp.zeros((LANES - EXPERTS, ROWS), f32)], axis=0
        ).T

    def take(b):
        rows = pl.ds(ROWS * b, ROWS)
        h_c(b).wait_recv()
        h_f(b).wait_recv()
        for c in range(4):
            whole = jnp.concatenate([ybuf[4 * (4 * b + j) + c] for j in range(4)], axis=0)
            rhs[12 + c, rows, :] = whole.astype(bf16)
            whole = jnp.concatenate([zbuf[4 * (4 * b + j) + c] for j in range(4)], axis=0)
            rhs[26 + c, rows, :] = whole.astype(bf16)
            for half_c in range(2):
                lhs[34 + 2 * c + half_c, :, rows] = whole[:, 128 * half_c : 128 * half_c + 128].T.astype(bf16)
        unit(EARLY, b, "mate")

    next_weights(EARLY)
    for j in range(2):
        d_c(2 * core_mate + j).wait_recv()
        d_f(2 * (3 - tensor) + j).wait_recv()
    take(0)
    take(1)
    for j in range(2):
        d_c(8 + 2 * (1 - core) + j).wait_recv()
    take(2)
    d_direct(2)
    d_direct(3)
    h_forward(3)
    for j in range(2):
        d_c(12 + 2 * (1 - core) + j).wait_recv()
    take(3)
    kept_copy.wait_send()
    for j in range(2):
        d_y(near_d[j]).wait_send()
        d_x(near_d[j]).wait_send()
        d_c(near_d[j]).wait_send()
        d_f(2 * x_mate + j).wait_send()
    for j in range(4):
        d_y(direct_d[j]).wait_send()
        d_c(direct_d[j]).wait_send()
    for b in range(4):
        h_y(b).wait_send()
        h_x(b).wait_send()
        h_c(b).wait_send()
        h_f(b).wait_send()

    pl.semaphore_signal(go, inc=1, device_id={"dp": mate}, device_id_type=MESH)

    @pl.when(z < last)
    def _():
        pl.semaphore_signal(go, inc=1, device_id={"dp": up_id}, device_id_type=MESH)

    @pl.when(z > 0)
    def _():
        pl.semaphore_signal(go, inc=1, device_id={"dp": dn_id}, device_id_type=MESH)

    def half_pass(u):
        k = EARLY + 1 + u // 2

        @pl.when(u % 2 == 0)
        def _():
            next_weights(k)

        @pl.when(is_mate(k))
        def _():
            unit(k, u % 2, "mate", 2 * ROWS)

        @pl.when((k < 16) & jnp.logical_not(is_mate(k)))
        def _():
            unit(k, u % 2, "own", 2 * ROWS)

        @pl.when(k >= 16)
        def _():
            unit(k, u % 2, "other", 2 * ROWS)

    mine = pl.ds(pl.multiple_of(core * 512, 512), 512)
    other = pl.ds(pl.multiple_of((1 - core) * 512, 512), 512)

    def span(k):
        return pl.ds(0, 1152 if k == 0 else 1024)

    def sum_a(k):
        return remote(acc.at[other, span(k)], buf.at[pl.ds(0, 512), span(k)], s1s.at[k], s1r.at[k], core_mate, "tensor")

    def sum_b(k):
        return remote(acc.at[mine, span(k)], buf.at[pl.ds(512, 512), span(k)], s2s.at[k], s2r.at[k], x_mate, "tensor")

    def sum_c(k):
        part = acc.at[mine, span(k)]
        return remote(part, part, s3s.at[k], s3r.at[k], core_mate, "tensor")

    def add_in(k, at_row):
        def step(b, carry):
            rows = pl.ds(pl.multiple_of(core * 512 + b * 64, 64), 64)
            acc[rows, span(k)] += buf[pl.ds(pl.multiple_of(at_row + b * 64, 64), 64), span(k)]
            return carry

        lax.fori_loop(0, 8, step, 0)

    def sum_first(k):
        pl.semaphore_signal(ready1.at[k], inc=1, device_id={"tensor": core_mate}, device_id_type=MESH)
        pl.semaphore_signal(ready2.at[k], inc=1, device_id={"tensor": x_mate}, device_id_type=MESH)
        pl.semaphore_wait(ready1.at[k], 1)
        sum_a(k).start()

    def sum_second(k):
        sum_a(k).wait_recv()
        add_in(k, 0)
        sum_a(k).wait_send()
        pl.semaphore_signal(ready3.at[k], inc=1, device_id={"tensor": core_mate}, device_id_type=MESH)
        pl.semaphore_wait(ready2.at[k], 1)
        sum_b(k).start()

    def sum_third(k):
        sum_b(k).wait_recv()
        sum_b(k).wait_send()
        add_in(k, 512)
        pl.semaphore_wait(ready3.at[k], 1)
        sum_c(k).start()

    def sum_last(k):
        sum_c(k).wait_recv()
        sum_c(k).wait_send()

    def norm_sum(step, dev):
        return remote(norms.at[pl.ds(0, 16)], norm_in.at[step], ns.at[step], nr.at[step], dev)

    partners = (mate, pair, far)

    def norm_next(step):
        if step > 0:
            norm_sum(step - 1, partners[step - 1]).wait_recv()
            norm_sum(step - 1, partners[step - 1]).wait_send()
            norms[...] = norms[...] + norm_in[step - 1]
        if step < 3:
            norm_sum(step, partners[step]).start()

    def norm_back(values, scale_r, grads, which):
        inner = sum(
            jnp.sum(v * scale_r * (g * gain[which : which + 1, 256 * c : 256 * c + 256]), axis=1, keepdims=True)
            for c, (v, g) in enumerate(zip(values, grads))
        ) * (1.0 / 1024.0)
        outs = []
        for c, (v, g) in enumerate(zip(values, grads)):
            normed = v * scale_r
            total = jnp.sum(g * normed, axis=0, keepdims=True)
            row = 8 * which + 2 * c
            norms[row : row + 1, :] += total[:, :LANES]
            norms[row + 1 : row + 2, :] += total[:, LANES:]
            outs.append(scale_r * (g * gain[which : which + 1, 256 * c : 256 * c + 256] - normed * inner))
        return outs

    def middle_rows(b):
        rows = block(b)

        values = [buf[rows, 256 * c : 256 * c + 256] for c in range(4)]
        grads = [acc[rows, 256 * c : 256 * c + 256] for c in range(4)]
        square = sum(jnp.sum(v * v, axis=1, keepdims=True) for v in values)
        scale_r = lax.rsqrt(square * (1.0 / 1024.0) + EPSILON)
        back = norm_back(values, scale_r, grads, 0)
        for c in range(4):
            total = rhs[c, rows, :].astype(f32) + back[c]
            acc[rows, 256 * c : 256 * c + 256] = total
            rhs[26 + c, rows, :] = total.astype(bf16)
        for h in range(4):
            d_head = dot_nt(rhs[26, rows, :], wdb[h, :, 0:256])
            for c in range(1, 4):
                d_head = d_head + dot_nt(rhs[26 + c, rows, :], wdb[h, :, 256 * c : 256 * c + 256])
            da2[h, rows, :] = d_head.astype(bf16)

    def turn_back(grad, cols):
        one, two = grad[:32], grad[32:]
        cosine, sine = cos_t[:, cols], sin_t[:, cols]
        return jnp.concatenate([one * cosine + two * sine, two * cosine - one * sine], axis=0)

    def attend_back(h, qb):
        keys = ROWS * (qb + 1)
        rows = pl.ds(ROWS * qb, ROWS)
        q_rows = q2[h, rows, :]
        d_rows = da2[h, rows, :]
        exact = jnp.exp(masked_scores(h, qb) - lse[pl.ds(h, 1), rows])
        d_probs = dot_nt(v2[0:keys, :], d_rows)
        inner = jnp.sum(exact * d_probs, axis=0, keepdims=True)
        d_scores = (exact * (d_probs - inner)).astype(bf16)
        dk_acc[0:keys, :] += dot_f(d_scores, q_rows)
        dv_acc[0:keys, :] += dot_f(exact.astype(bf16), d_rows)
        k_head = kt2[pl.ds(pl.multiple_of((h // 2) * 64, 64), 64), 0:keys]
        d_q = dot_f(k_head, d_scores) * scaling
        buf[pl.ds(pl.multiple_of(h * 64, 64), 64), rows] = turn_back(d_q, rows)

    def turn_rows(b):
        rows = block(b)
        rhs[24, rows, :] = buf[0:256, rows].T.astype(bf16)
        d_k = (dk_acc[rows, :] * scaling).T
        d_k = jnp.concatenate([turn_back(d_k[:64], rows), turn_back(d_k[64:], rows)], axis=0)
        rhs[25, rows, 0:LANES] = d_k.T.astype(bf16)
        rhs[25, rows, LANES:] = dv_acc[rows, :].astype(bf16)

    def project_rows(b):
        rows = block(b)
        acc[rows, 0:1024] = dot_nt(rhs[24, rows, :], wgu[0]) + dot_nt(rhs[25, rows, :], wgu[1])

    def token_rows(b):
        rows = block(b)

        values = [hbuf[rows, 256 * c : 256 * c + 256].astype(f32) for c in range(4)]
        grads = [acc[rows, 256 * c : 256 * c + 256] for c in range(4)]
        square = sum(jnp.sum(v * v, axis=1, keepdims=True) for v in values)
        scale_r = lax.rsqrt(square * (1.0 / 1024.0) + EPSILON)
        back = norm_back(values, scale_r, grads, 1)
        for c in range(4):
            cols = slice(256 * c, 256 * c + 256)
            hbuf[rows, cols] = (buf[rows, cols] + back[c]).astype(bf16)

    def pair_load(pair, s):
        return local(w_down.at[pl.ds(2 * pair, 2)], wdb.at[pl.ds(2 * s, 2)], wsem.at[s, 2])

    def moe_pair(pair):
        s = pair % 2
        pair_load(pair, s).wait()

        @pl.when(pair + 1 < EXPERTS // 2)
        def _():
            pair_load(pair + 1, 1 - s).start()

        def rows_of(b, carry):
            rows = block(b)
            hidden = lhs[pl.ds(2 * pair, 2), :, rows].reshape(256, ROWS)
            down = wdb[pl.ds(2 * s, 2)].reshape(256, 1024)
            part = dot_tn(hidden, down)

            @pl.when(pair == 0)
            def _():
                acc[rows, 0:1024] = part

            @pl.when(pair > 0)
            def _():
                acc[rows, 0:1024] += part

            return carry

        lax.fori_loop(0, 4, rows_of, 0)

    def result_rows(b):
        rows = block(b)

        pos = lax.broadcasted_iota(jnp.int32, (ROWS, 1024), 0) + b * ROWS
        total = buf[rows, wide] + acc[rows, 0:1024]
        hbuf[rows, :] = jnp.where(pos < length[0], total, 0.0).astype(bf16)

    def halves_in(src):
        return [local(src, buf.at[:, wide], iosem.at[1])]

    tokens_in = [local(x_in, hbuf, iosem.at[3])]
    wo_load = [
        local(w_out.at[pl.ds(64 * h, 64)], wdb.at[h, pl.ds(64 * (h // 2), 64)], ld.at[8 + h]) for h in range(4)
    ]
    dots_out = [local(d_pick, o_dots, iosem.at[7])]
    norms_out = [
        local(norms.at[pl.ds(0, 8)], o_norm0, iosem.at[2]),
        local(norms.at[pl.ds(8, 8)], o_norm1, iosem.at[4]),
    ]

    def pick_dots():
        for b in range(4):
            rows = pl.ds(ROWS * b, ROWS)
            dots = acc[rows, 1024:1152].T[:EXPERTS]
            lane_e = lax.broadcasted_iota(jnp.int32, (EXPERTS, ROWS), 0)
            for k in range(TOP_K):
                mine_k = jnp.where(picks[k : k + 1, rows] == lane_e, dots, 0.0)
                d_pick[k : k + 1, rows] = jnp.sum(mine_k, axis=0, keepdims=True)
    dres_out = [local(acc.at[:, wide], s_dres, iosem.at[8])]
    tokens_out = [local(hbuf, o_tokens, iosem.at[9])]
    result_out = [local(hbuf, o_result, iosem.at[10])]

    def clear_wo():
        for h in range(4):
            wdb[h, 64 - 64 * (h // 2) : 128 - 64 * (h // 2), :] = jnp.zeros((64, 1024), bf16)

    def do_all(*steps):
        for step in steps:
            step()

    once = {
        T_SUM1: lambda: do_all(keep.wait, lambda: sum_first(0), clear_wo, lambda: start(tokens_in + wo_load + proj_load)),
        T_SUM1 + 2: lambda: do_all(lambda: sum_second(0), lambda: wait(tokens_in)),
        T_MID1 - 3: lambda: sum_third(0),
        T_MID1 - 1: lambda: do_all(
            lambda: sum_last(0), pick_dots, lambda: start(halves_in(s_resid) + dots_out), lambda: wait(wo_load)
        ),
        T_ATT: lambda: do_all(lambda: wait(dots_out), lambda: start(dres_out)),
        T_PROJ - 1: lambda: do_all(lambda: wait(dres_out), lambda: wait(proj_load)),
        T_SUM2: lambda: sum_first(1),
        T_SUM2 + 2: lambda: sum_second(1),
        T_TOK - 3: lambda: sum_third(1),
        T_TOK - 1: lambda: do_all(
            lambda: sum_last(1), lambda: start(halves_in(s_dres)), lambda: start([pair_load(0, 0)])
        ),
        T_MOE: lambda: start(tokens_out),
        T_SUM3 + 5: lambda: norm_next(0),
        T_SUM3 + 7: lambda: norm_next(1),
        T_SUM3 + 9: lambda: norm_next(2),
        T_SUM3 + 11: lambda: do_all(lambda: norm_next(3), lambda: start(norms_out)),
        T_SUM3: lambda: sum_first(2),
        T_SUM3 + 2: lambda: sum_second(2),
        T_RES - 3: lambda: sum_third(2),
        T_RES - 1: lambda: do_all(
            lambda: sum_last(2), lambda: wait(tokens_out + norms_out), lambda: start(halves_in(s_resid))
        ),
        T_RES + 4: lambda: start(result_out),
        T_RES + 8: lambda: wait(result_out),
    }
    halves_wait = {T_MID1: s_resid, T_TOK: s_dres, T_RES: s_resid}

    def work(t):
        for when_t, fn in sorted(once.items()):
            pl.when(t == when_t)(fn)
        for when_t, src in halves_wait.items():
            pl.when(t == when_t)(lambda src=src: wait(halves_in(src)))
        for begin, count, fn in (
            (0, 2 * (23 - EARLY), half_pass),
            (T_MID1, 4, middle_rows),
            (T_TURN, 2, lambda u: do_all(lambda: turn_rows(2 * u), lambda: turn_rows(2 * u + 1))),
            (T_PROJ, 2, lambda u: do_all(lambda: project_rows(2 * u), lambda: project_rows(2 * u + 1))),
            (T_TOK, 2, lambda u: do_all(lambda: token_rows(2 * u), lambda: token_rows(2 * u + 1))),
            (T_MOE, EXPERTS // 4, lambda u: do_all(lambda: moe_pair(2 * u), lambda: moe_pair(2 * u + 1))),
            (T_RES, 4, result_rows),
        ):
            pl.when((t >= begin) & (t < begin + count))(lambda fn=fn, begin=begin: fn(t - begin))
        for pair_b in range(2):
            u = t - T_ATT

            def two(pair_b=pair_b, u=u):
                attend_back(u // 2, pair_b)
                attend_back(u // 2, 3 - pair_b)

            pl.when((u >= 0) & (u < 8) & (u % 2 == pair_b))(two)

    own = pl.ds(pl.multiple_of(y * 32, 32), 32)
    oth = pl.ds(pl.multiple_of((1 - y) * 32, 32), 32)
    half = pl.ds(0, 32)
    upper = pl.ds(32, 32)

    def stage(c, t):
        p = z if c == 0 else last - z
        nxt, prv = (up_id, dn_id) if c == 0 else (dn_id, up_id)
        def at(delay, body):
            i = t - delay - c

            @pl.when((i >= 0) & (i < N_CLASS))
            def _():
                s = c * ring + i % ring
                body(i, s, i < N_EXPERT, (i >= N_EXPERT) & (i % 2 == 0), (i >= N_EXPERT) & (i % 2 == 1))

        def ycopy_a(s):
            return remote(pbuf.at[s, oth], ybuf.at[s, half], ys.at[s], yr.at[s], mate)

        def ycopy_b(s):
            return remote(zbuf.at[s], ybuf.at[s], ys.at[s], yr.at[s], mate)

        def zcopy_a(s):
            return remote(zbuf.at[s, half], zbuf.at[s, half], zs.at[s], zr.at[s], nxt)

        def zcopy(s):
            return remote(zbuf.at[s], zbuf.at[s], zs.at[s], zr.at[s], nxt)

        def fcopy_a(s):
            return remote(pbuf.at[s, own], pbuf.at[s, own], fs.at[s], fr.at[s], prv)

        def fcopy(s):
            return remote(pbuf.at[s], pbuf.at[s], fs.at[s], fr.at[s], prv)

        def gcopy_a(s):
            return remote(pbuf.at[s, own], ybuf.at[s, upper], gs.at[s], gr.at[s], mate)

        def gcopy(s):
            return remote(pbuf.at[s], ybuf.at[s], gs.at[s], gr.at[s], mate)

        def first(i, s, is_e, is_a, is_b):
            m = i // 2
            g = 2 * m + c

            @pl.when((i % 2 == 0) & is_e)
            def _():
                el, part = g // 12, g % 12
                down = part < 4
                l_one = jnp.where(down, 8 * y + el, 12 + part)
                r_one = jnp.where(down, part, 4 + el)
                l_two = jnp.where(down, 42 + el, 30 + part)
                r_two = jnp.where(down, 12 + part, 16 + el)
                total = dot_f(lhs[l_one], rhs[r_one]) + dot_f(lhs[l_two], rhs[r_two])
                pbuf[s] = total[:CHUNK]
                pbuf[s + 1] = total[CHUNK:]

            @pl.when((i % 2 == 0) & jnp.logical_not(is_e))
            def _():
                a = g - N_EXPERT
                l_one = jnp.where(a < 8, 32 + a // 4, 24 + a % 8)
                r_one = jnp.where(a < 8, 26 + a % 4, 23 + a // 8)
                total = dot_f(lhs[l_one], rhs[r_one])
                pbuf[s] = total[:CHUNK]
                pbuf[s + 1] = total[CHUNK:]

            @pl.when(is_a)
            def _():
                ycopy_a(s).start()

        def second(i, s, is_e, is_a, is_b):
            @pl.when(is_a)
            def _():
                ycopy_a(s).wait_recv()

                @pl.when(p > 0)
                def _():
                    zcopy_a(s).wait_recv()
                    zbuf[s, half] = zbuf[s, half] + (pbuf[s, own] + ybuf[s, half])

                @pl.when(p == 0)
                def _():
                    zbuf[s, half] = pbuf[s, own] + ybuf[s, half]

                @pl.when(p < last)
                def _():
                    zcopy_a(s).start()

                @pl.when(p == last)
                def _():
                    pbuf[s, own] = zbuf[s, half]
                    fcopy_a(s).start()
                    gcopy_a(s).start()

            @pl.when(jnp.logical_not(is_a))
            def _():
                @pl.when(p > 0)
                def _():
                    zcopy(s).wait_recv()
                    zbuf[s] = zbuf[s] + pbuf[s]

                @pl.when(p == 0)
                def _():
                    zbuf[s] = pbuf[s]

                @pl.when(p < last)
                def _():
                    zcopy(s).start()

                @pl.when((p == last) & is_e)
                def _():
                    pbuf[s] = zbuf[s]
                    fcopy(s).start()
                    gcopy(s).start()

                @pl.when((p == last) & is_b)
                def _():
                    ycopy_b(s).start()

        def third(i, s, is_e, is_a, is_b):
            @pl.when(is_b & (p == last))
            def _():
                ycopy_b(s).wait_recv()
                pbuf[s] = zbuf[s] + ybuf[s]
                fcopy(s).start()

        def fourth(i, s, is_e, is_a, is_b):
            @pl.when(p < last)
            def _():
                @pl.when(is_a)
                def _():
                    fcopy_a(s).wait_recv()

                    @pl.when(p > 0)
                    def _():
                        fcopy_a(s).start()

                    gcopy_a(s).start()

                @pl.when(jnp.logical_not(is_a))
                def _():
                    fcopy(s).wait_recv()

                    @pl.when(p > 0)
                    def _():
                        fcopy(s).start()

                    @pl.when(is_e)
                    def _():
                        gcopy(s).start()

        def store(buf_s, sem, dst0, dst1):
            local(buf_s.at[:, pl.ds(0, LANES)], dst0, sem).start()
            local(buf_s.at[:, pl.ds(LANES, LANES)], dst1, sem).start()

        def fifth(i, s, is_e, is_a, is_b):
            @pl.when(is_a)
            def _():
                gcopy_a(s).wait_recv()
                ycopy_a(s).wait_send()
                pbuf[s, oth] = ybuf[s, upper]

            @pl.when(is_e)
            def _():
                gcopy(s).wait_recv()

            g = 2 * (i // 2) + c
            el, part = g // 12, g % 12
            a = g - N_EXPERT
            low = CHUNK * (i % 2)

            def at_rows(start_row):
                return pl.ds(pl.multiple_of(start_row + low, CHUNK), CHUNK)

            def both_rows(write):
                write(pbuf.at[s], os0.at[s], 8 * y + el)
                write(ybuf.at[s], os1.at[s], 8 * (1 - y) + el)

            @pl.when(is_e & (part < 4))
            def _():
                col = pl.ds(pl.multiple_of(part * 256, LANES), LANES)
                col1 = pl.ds(pl.multiple_of(part * 256 + LANES, LANES), LANES)
                both_rows(
                    lambda src, sem, e: store(
                        src, sem, o_down.at[e, at_rows(0), col], o_down.at[e, at_rows(0), col1]
                    )
                )

            @pl.when(is_e & (part >= 4))
            def _():
                rows = at_rows((part - 4) * 128)
                both_rows(lambda src, sem, e: store(src, sem, o_gate.at[e, rows], o_up.at[e, rows]))

            @pl.when(jnp.logical_not(is_e) & (a < 8))
            def _():
                rows = at_rows((a // 4) * 128)
                col = pl.ds(pl.multiple_of((a % 4) * 256, LANES), LANES)
                col1 = pl.ds(pl.multiple_of((a % 4) * 256 + LANES, LANES), LANES)
                store(pbuf.at[s], os0.at[s], o_out.at[rows, col], o_out.at[rows, col1])

            @pl.when(jnp.logical_not(is_e) & (a >= 8) & (a < 16))
            def _():
                rows = at_rows((a - 8) * 128)
                store(pbuf.at[s], os0.at[s], o_q.at[rows, pl.ds(0, LANES)], o_q.at[rows, pl.ds(LANES, LANES)])

            @pl.when(jnp.logical_not(is_e) & (a >= 16))
            def _():
                rows = at_rows((a - 16) * 128)
                store(pbuf.at[s], os0.at[s], o_k.at[rows], o_v.at[rows])

        def sixth(i, s, is_e, is_a, is_b):
            local(pbuf.at[s], o_q.at[pl.ds(0, CHUNK)], os0.at[s]).wait()

            @pl.when(is_e)
            def _():
                local(ybuf.at[s], o_q.at[pl.ds(0, CHUNK)], os1.at[s]).wait()
                gcopy(s).wait_send()

            @pl.when(is_a)
            def _():
                gcopy_a(s).wait_send()

                @pl.when(p < last)
                def _():
                    zcopy_a(s).wait_send()

                @pl.when(p > 0)
                def _():
                    fcopy_a(s).wait_send()

            @pl.when(jnp.logical_not(is_a))
            def _():
                @pl.when(p < last)
                def _():
                    zcopy(s).wait_send()

                @pl.when((p == last) & is_b)
                def _():
                    ycopy_b(s).wait_send()

                @pl.when(p > 0)
                def _():
                    fcopy(s).wait_send()

        t2 = hop * (1 + p)
        t3 = hop * (2 + last)
        t4 = t3 + hop * (last - p)
        t5 = t4 + hop
        t6 = t5 + hop
        return [(0, first, at), (t2, second, at), (t3, third, at), (t4, fourth, at), (t5, fifth, at), (t6, sixth, at)]

    def body(t, carry):
        @pl.when(t == 1)
        def _():
            pl.semaphore_wait(go, 1 + (z < last).astype(jnp.int32) + (z > 0).astype(jnp.int32))

        both = [stage(0, t), stage(1, t)]
        for k in (1, 2, 3, 4, 5, 0):
            if k == 0:
                work(t)
            for st in both:
                delay, fn, at = st[k]
                at(delay, fn)
        return carry

    total = N_CLASS + hop * (2 * last + 4) + 2
    lax.fori_loop(0, total, body, 0)


def run_layer(mesh, *operands):
    groups = mesh.shape["dp"]
    nz = 4 if groups % 8 == 0 else groups // 2
    last = nz - 1
    hop = HOP
    ring = hop * (2 * last + 4) + 2
    ring = max(32, ring + ring % 2)
    f32, bf16 = jnp.float32, jnp.bfloat16

    def out(shape, kind=f32):
        return jax.ShapeDtypeStruct(shape, kind)

    outs = [
        out((16, 1024, 128)), out((16, 1024, 128)), out((16, 128, 1024)),
        out((1024, 256)), out((1024, 128)), out((1024, 128)), out((256, 1024)), out((8, 128)), out((8, 128)),
        out((1024, 1024), bf16), out((1024, 1024), bf16), out((8, 1024)),
        out((1024, 1024)), out((1024, 1024)),
    ]
    anywhere = pl.BlockSpec(memory_space=pl.ANY)
    dma = pltpu.SemaphoreType.DMA
    reg = pltpu.SemaphoreType.REGULAR
    vmem = pltpu.VMEM
    res = pl.pallas_call(
        functools.partial(layer_kernel, nz, hop, ring),
        out_shape=outs,
        in_specs=[pl.BlockSpec(memory_space=pltpu.SMEM)] + [anywhere] * (len(operands) - 1),
        out_specs=[anywhere] * len(outs),
        scratch_shapes=[
            vmem((50, 128, 1024), bf16), vmem((30, 1024, 256), bf16),
            vmem((2 * ring, CHUNK, 256), f32), vmem((2 * ring, CHUNK, 256), f32), vmem((2 * ring, CHUNK, 256), f32),
            vmem((1024, 1152), f32), vmem((1024, 1152), f32),
            vmem((1024, 1024), bf16), vmem((2, 1024, 256), bf16), vmem((4, 128, 1024), bf16),
            vmem((4, 1024, 128), bf16), vmem((1024, 128), bf16), vmem((1024, 128), bf16),
            vmem((128, 1024), bf16), vmem((128, 1024), bf16),
            vmem((8, 1024), f32), vmem((32, 1024), f32), vmem((32, 1024), f32),
            vmem((4, 1024, 128), bf16), vmem((1024, 128), f32), vmem((1024, 128), f32),
            vmem((1024, 128), f32), vmem((8, 1024), f32), vmem((16, 128), f32),
            vmem((8, 1024), jnp.int32), vmem((8, 1024), f32),
            vmem((3, 16, 128), f32), vmem((8, 1024), f32),
            vmem((EXPERTS, 1024), f32), vmem((EXPERTS, 1024), f32), vmem((1024, 128), f32),
            dma((18,)), dma((2, 3)), dma((11,)),
        ]
        + [dma((2 * ring,))] * 10
        + [dma((4,))] * 6
        + [dma((6,))] * 2
        + [dma((3,))] * 6
        + [reg((3,))] * 3
        + [dma((3,))] * 2
        + [reg]
        + [dma((4,))] * 8
        + [dma((16,))] * 8
        + [dma((1,))] * 2,
        compiler_params=pltpu.CompilerParams(
            collective_id=0, has_side_effects=True, vmem_limit_bytes=63 * 2**20
        ),
    )(*operands)
    sums, rest = tuple(res[:9]), res[9:12]
    if groups > 2 * nz:
        same = [
            [2 * nz * block + place for block in range(groups // (2 * nz))] for place in range(2 * nz)
        ]
        sums = lax.psum(sums, "dp", axis_index_groups=same)
    return sums, rest


def per_device(
    mesh,
    tokens,
    lengths,
    chosen,
    gate_values,
    cotangent,
    norm_attn,
    w_query,
    w_key,
    w_value,
    w_out,
    norm_moe,
    w_gate,
    w_up,
    w_down,
):
    seq_len = tokens.shape[0] // lengths.shape[0]
    cosine, sine = rope_tables(seq_len, HEAD_DIM)
    sums, (result, grad_tokens, dots) = run_layer(
        mesh,
        lengths,
        tokens,
        cotangent,
        chosen.T,
        gate_values.T,
        norm_attn[None, :],
        norm_moe[None, :],
        w_gate,
        w_up,
        w_down,
        cosine,
        sine,
        w_out,
        w_query,
        w_key,
        w_value,
    )
    grad_gate, grad_up, grad_down, grad_query, grad_key, grad_value, grad_out, grad_norm_moe, grad_norm_attn = sums
    return (
        result,
        grad_tokens,
        dots.T,
        grad_norm_attn.reshape(-1),
        grad_query,
        grad_key,
        grad_value,
        grad_out,
        grad_norm_moe.reshape(-1),
        grad_gate,
        grad_up,
        grad_down,
    )


def solution(mesh):
    placed = (
        P("dp", None),
        P("dp"),
        P("dp", None),
        P("dp", None),
        P("dp", None),
        P(),
        P(None, "tensor"),
        P(None, "tensor"),
        P(None, "tensor"),
        P("tensor", None),
        P(),
        P(None, None, "tensor"),
        P(None, None, "tensor"),
        P(None, "tensor", None),
    )
    return jax.shard_map(
        functools.partial(per_device, mesh),
        mesh=mesh,
        in_specs=placed,
        out_specs=(
            P("dp", None),
            P("dp", None),
            P("dp", None),
            P(),
            P(None, "tensor"),
            P(None, "tensor"),
            P(None, "tensor"),
            P("tensor", None),
            P(),
            P(None, None, "tensor"),
            P(None, None, "tensor"),
            P(None, "tensor", None),
        ),
        check_vma=False,
    )
```

```python
import functools
import math

import jax
import jax.numpy as jnp
import numpy as np
from jax import lax
from jax.experimental import pallas as pl
from jax.experimental.pallas import tpu as pltpu
from jax.sharding import PartitionSpec as P

MESH = pl.DeviceIdType.MESH

HEAD_DIM = 64
TOP_K = 8
EXPERTS = 16


EPSILON = 1e-05
THETA = 10000.0
NEGATIVE = -1e30


def dot_f(left, right):
    return jnp.dot(left, right, preferred_element_type=jnp.float32)


def rope_tables(positions, width):
    half_w = width // 2
    freqs = THETA ** (-np.arange(half_w, dtype=np.float64) * 2.0 / width)
    angles = freqs[:, None] * np.arange(positions, dtype=np.float64)[None, :]
    return (np.cos(angles).astype(np.float32), np.sin(angles).astype(np.float32))


LANES = 128
ROWS = 256
CHUNK = 64
N_EXPERT = 96
N_CLASS = 120
HOP = 2
EARLY = 7
T_SUM1 = 32
T_MID1 = 58
T_ATT = 62
T_TURN = 70
T_PROJ = 72
T_SUM2 = 74
T_TOK = 98
T_MOE = 100
T_SUM3 = 104
T_RES = 128


def dot_nt(left, right):
    return lax.dot_general(
        left, right, (((1,), (1,)), ((), ())), preferred_element_type=jnp.float32
    )


def dot_tn(left, right):
    return lax.dot_general(
        left, right, (((0,), (0,)), ((), ())), preferred_element_type=jnp.float32
    )


def layer_kernel(
    nz, hop, ring,
    length, x_in, d_out, chosen, gates, gain_attn, gain_moe, w_gate, w_up, w_down,
    cos_in, sin_in, w_out, w_query, w_key, w_value,
    o_gate, o_up, o_down, o_q, o_k, o_v, o_out, o_norm0, o_norm1, o_result, o_tokens, o_dots, s_resid, s_dres,
    lhs, rhs, pbuf, zbuf, ybuf, acc, buf, hbuf, wgu, wdb, q2, k2, v2, kt2, vt2, lse, cos_t, sin_t,
    da2, dk_acc, dv_acc, slot_w, gain, norms, picks, pick_w, norm_in, d_pick, kept_out, kept_in, slot_m,
    ld, wsem, iosem, ys, yr, zs, zr, fs, fr, gs, gr, os0, os1,
    cs_c, cr_c, cs_x, cr_x, cs_f, cr_f, ws, wr, s1s, s1r, s2s, s2r, s3s, s3r, ready1, ready2, ready3, ns, nr, go,
    hys, hyr, hcs, hcr, hxs, hxr, hfs, hfr, dys, dyr, dcs, dcr, dxs, dxr, dfs, dfr, ks, kr,
):
    f32, bf16 = jnp.float32, jnp.bfloat16
    dp = lax.axis_index("dp")
    tensor = lax.axis_index("tensor")
    base = dp - dp % (2 * nz)
    z, y = (dp % (2 * nz)) // 2, dp % 2
    last = nz - 1
    mate = base + z * 2 + (1 - y)
    up_id = base + jnp.minimum(z + 1, last) * 2 + y
    dn_id = base + jnp.maximum(z - 1, 0) * 2 + y
    far = base + ((z + 2) % nz) * 2 + y
    core = tensor % 2
    core_mate = tensor - core + (1 - core)
    x_mate = (tensor + 2) % 4

    def local(src, dst, sem):
        return pltpu.make_async_copy(src, dst, sem)

    def remote(src, dst, ssem, rsem, dev, axis="dp"):
        return pltpu.make_async_remote_copy(
            src_ref=src, dst_ref=dst, send_sem=ssem, recv_sem=rsem,
            device_id={axis: dev}, device_id_type=MESH,
        )

    def block(b, size=ROWS):
        return pl.ds(pl.multiple_of(b * size, size), size)

    bar = pltpu.get_barrier_semaphore()
    for axis, dev in (("dp", mate), ("dp", far), ("tensor", core_mate), ("tensor", x_mate)):
        pl.semaphore_signal(bar, inc=1, device_id={axis: dev}, device_id_type=MESH)

    @pl.when(z < last)
    def _():
        pl.semaphore_signal(bar, inc=1, device_id={"dp": up_id}, device_id_type=MESH)

    @pl.when(z > 0)
    def _():
        pl.semaphore_signal(bar, inc=1, device_id={"dp": dn_id}, device_id_type=MESH)

    wide = pl.ds(0, 1024)
    share = block(tensor)
    token_load = [
        local(x_in, hbuf, ld.at[0]),
        local(gain_attn, gain.at[pl.ds(1, 1)], ld.at[1]),
        local(gain_moe, gain.at[pl.ds(0, 1)], ld.at[2]),
        local(cos_in, cos_t, ld.at[3]),
        local(sin_in, sin_t, ld.at[4]),
    ]
    proj_load = [
        local(w_query, wgu.at[0], ld.at[5]),
        local(w_key, wgu.at[1, :, pl.ds(0, LANES)], ld.at[6]),
        local(w_value, wgu.at[1, :, pl.ds(LANES, LANES)], ld.at[7]),
    ]
    out_load = [local(w_out.at[:, block(c)], rhs.at[26 + c, share], ld.at[8 + c]) for c in range(4)]
    late_load = [local(d_out.at[:, block(c)], rhs.at[c], ld.at[12 + c]) for c in range(4)] + [
        local(chosen, picks, ld.at[16]),
        local(gates, pick_w, ld.at[17]),
    ]

    def expert_load(e, s):
        return [
            local(w_gate.at[e], wgu.at[s, :, pl.ds(0, LANES)], wsem.at[s, 0]),
            local(w_up.at[e], wgu.at[s, :, pl.ds(LANES, LANES)], wsem.at[s, 1]),
            local(w_down.at[e], wdb.at[s], wsem.at[s, 2]),
        ]

    def start(copies):
        for copy in copies:
            copy.start()

    def wait(copies):
        for copy in copies:
            copy.wait()

    start(out_load + token_load + proj_load + late_load)
    pl.semaphore_wait(bar, 4 + (z < last).astype(jnp.int32) + (z > 0).astype(jnp.int32))

    part_w = buf.at[share, wide]
    quarter = 2 * (z % 2) + y
    part_q = buf.at[pl.ds(pl.multiple_of(tensor * 256 + quarter * 64, 64), 64), wide]
    part_y = buf.at[pl.ds(pl.multiple_of(x_mate * 256 + quarter * 64, 64), 64), wide]
    near_q = 2 * (z % 2) + 1 - y
    part_z = buf.at[pl.ds(pl.multiple_of(x_mate * 256 + near_q * 64, 64), 64), wide]
    pair = base + (z + 1 - 2 * (z % 2)) * 2 + y
    w_x = remote(part_q, part_q, ws.at[0], wr.at[0], x_mate, "tensor")
    w_y = remote(part_y, part_y, ws.at[3], wr.at[3], mate)
    w_z = remote(part_z, part_z, ws.at[4], wr.at[4], pair)
    w_p = remote(part_y, part_y, ws.at[5], wr.at[5], pair)
    w_c = remote(part_w, part_w, ws.at[1], wr.at[1], core_mate, "tensor")
    part_f = buf.at[block(x_mate), wide]
    w_f = remote(part_f, part_f, ws.at[2], wr.at[2], core_mate, "tensor")
    wait(out_load)
    for c in range(4):
        buf[share, 256 * c : 256 * c + 256] = rhs[26 + c, share, :].astype(f32)
    w_x.start()
    w_c.start()

    def gather_x(b):
        return remote(
            acc.at[block(b), share], acc.at[block(b), share], cs_x.at[b], cr_x.at[b], x_mate, "tensor"
        )

    def gather_c(b):
        return remote(
            acc.at[block(b), share], acc.at[block(b), share], cs_c.at[b], cr_c.at[b], core_mate, "tensor"
        )

    def gather_f(b):
        part = acc.at[block(b), block(x_mate)]
        return remote(part, part, cs_f.at[b], cr_f.at[b], core_mate, "tensor")

    def rotate_t(values, cols):
        one, two = values[:32], values[32:]
        cosine, sine = cos_t[:, cols], sin_t[:, cols]
        return jnp.concatenate([one * cosine - two * sine, two * cosine + one * sine], axis=0)

    def head_rows(b, carry):
        rows = block(b)
        vals = [hbuf[rows, 256 * col : 256 * col + 256].astype(f32) for col in range(4)]
        square = sum(jnp.sum(v * v, axis=1, keepdims=True) for v in vals)
        scale_r = lax.rsqrt(square * (1.0 / 1024.0) + EPSILON)
        query, key_value = 0.0, 0.0
        for col in range(4):
            normed = vals[col] * scale_r * gain[1:2, 256 * col : 256 * col + 256]
            normed = normed.astype(bf16)
            for half_c in range(2):
                lhs[24 + 2 * col + half_c, :, rows] = normed[:, 128 * half_c : 128 * half_c + 128].T
            query = query + dot_f(normed, wgu[0, 256 * col : 256 * col + 256, :])
            key_value = key_value + dot_f(normed, wgu[1, 256 * col : 256 * col + 256, :])
        query = query.T
        nothing = jnp.zeros((64, ROWS), f32)
        for h in range(4):
            turned = rotate_t(query[64 * h : 64 * h + 64], rows)
            both = [turned, nothing] if h < 2 else [nothing, turned]
            q2[h, rows, :] = jnp.concatenate(both, axis=0).T.astype(bf16)
        key = key_value[:, :LANES].T
        key = jnp.concatenate([rotate_t(key[:64], rows), rotate_t(key[64:], rows)], axis=0)
        kt2[:, rows] = key.astype(bf16)
        k2[rows, :] = key.T.astype(bf16)
        value = key_value[:, LANES:]
        v2[rows, :] = value.astype(bf16)
        vt2[:, rows] = value.T.astype(bf16)
        return carry

    scaling = 1.0 / math.sqrt(HEAD_DIM)

    def masked_scores(h, qb):
        keys = ROWS * (qb + 1)
        rows = pl.ds(ROWS * qb, ROWS)
        scores = dot_nt(k2[0:keys, :], q2[h, rows, :]) * scaling
        k_pos = lax.broadcasted_iota(jnp.int32, (keys, ROWS), 0)
        q_pos = lax.broadcasted_iota(jnp.int32, (keys, ROWS), 1) + ROWS * qb
        allowed = (k_pos <= q_pos) & (k_pos < length[0])
        return jnp.where(allowed, scores, NEGATIVE)

    def attend(qb):
        keys = ROWS * (qb + 1)
        rows = pl.ds(ROWS * qb, ROWS)

        def one_head(h, carry):
            scores = masked_scores(h, qb)
            top_s = jnp.max(scores, axis=0, keepdims=True)
            expo = jnp.exp(scores - top_s)
            total = jnp.sum(expo, axis=0, keepdims=True)
            probs = (expo / total).astype(bf16)
            lse[pl.ds(h, 1), rows] = top_s + jnp.log(total)
            v_head = vt2[pl.ds(pl.multiple_of((h // 2) * 64, 64), 64), 0:keys]
            lhs[32 + h // 2, pl.ds(pl.multiple_of((h % 2) * 64, 64), 64), rows] = dot_f(v_head, probs).astype(bf16)
            return carry

        lax.fori_loop(0, 4, one_head, 0)
        for half_c in range(2):
            own_c = pl.ds(pl.multiple_of(tensor * 256 + half_c * 128, 128), 128)
            acc[rows, own_c] = lhs[32 + half_c, :, rows].astype(f32).T
        gather_x(qb).start()
        gather_c(qb).start()

    def mask_rows(b, carry):
        rows = block(b)
        pos = lax.broadcasted_iota(jnp.int32, (ROWS, 256), 0) + b * ROWS
        for c in range(4):
            rhs[c, rows, :] = jnp.where(pos < length[0], rhs[c, rows, :].astype(f32), 0.0).astype(bf16)
        return carry

    near_d = [2 * tensor + j for j in range(2)]
    direct_d = [8 + 2 * core, 9 + 2 * core, 12 + 2 * core, 13 + 2 * core]

    def slab(k):
        return pl.ds(pl.multiple_of(4 * k, 4), 4)

    def d_copy(k, sends, recvs, dev, axis, src=None):
        return remote((ybuf if src is None else src).at[slab(k)], ybuf.at[slab(k)], sends.at[k], recvs.at[k], dev, axis)

    def d_y(k):
        return d_copy(k, dys, dyr, mate, "dp", pbuf)

    def d_c(k):
        return d_copy(k, dcs, dcr, core_mate, "tensor")

    def d_x(k):
        return d_copy(k, dxs, dxr, x_mate, "tensor")

    def d_f(k):
        return d_copy(k, dfs, dfr, core_mate, "tensor")

    def stage_d(k):
        rows = block(k, 64)
        live = lax.broadcasted_iota(jnp.int32, (64, 256), 0) + k * 64 < length[0]
        for c in range(4):
            pbuf[4 * k + c] = jnp.where(live, rhs[c, rows, :].astype(f32), 0.0)
        d_y(k).start()

    def h_piece(b, t):
        return 4 * b + t

    def h_copy(b, t, sends, recvs, dev, axis):
        part = zbuf.at[slab(h_piece(b, t))]
        return remote(part, part, sends.at[b], recvs.at[b], dev, axis)

    def h_stage(b):
        return 2 * x_mate + b if isinstance(b, int) and b < 2 else 2 * jnp.where(b < 2, x_mate, core_mate) + b % 2

    def h_y(b):
        return remote(
            pbuf.at[slab(h_stage(b))], zbuf.at[slab(h_piece(b, tensor))], hys.at[b], hyr.at[b], mate
        )

    def h_c(b):
        return h_copy(b, tensor, hcs, hcr, core_mate, "tensor")

    def h_x(b):
        return h_copy(b, tensor, hxs, hxr, x_mate, "tensor")

    def h_f(b):
        return h_copy(b, x_mate, hfs, hfr, core_mate, "tensor")

    def h_send(b):
        rows = pl.ds(pl.multiple_of(b * 256 + tensor * 64, 64), 64)
        for c in range(4):
            pbuf[4 * h_stage(b) + c] = hbuf[rows, 256 * c : 256 * c + 256].astype(f32)
        h_y(b).start()

    def h_share(b):
        h_y(b).wait_recv()
        h_x(b).start()
        h_c(b).start()

    def h_forward(b):
        h_x(b).wait_recv()
        h_f(b).start()

    def d_share(j):
        k = near_d[j]
        d_y(k).wait_recv()
        d_x(k).start()
        d_c(k).start()

    def d_forward(j):
        k = 2 * x_mate + j
        d_x(k).wait_recv()
        d_f(k).start()

    def d_direct(j):
        k = direct_d[j]
        d_y(k).wait_recv()
        d_c(k).start()

    wait(late_load)
    stage_d(near_d[0])
    wait(token_load + proj_load)
    head_rows(0, 0)
    attend(0)
    head_rows(1, 0)
    w_x.wait_recv()
    w_y.start()
    w_p.start()
    attend(1)
    head_rows(2, 0)
    attend(2)
    w_y.wait_recv()
    w_z.start()
    stage_d(near_d[1])
    head_rows(3, 0)
    start(expert_load(8 * y, 0))
    attend(3)
    stage_d(direct_d[0])
    lax.fori_loop(0, 4, mask_rows, 0)
    dk_acc[...] = jnp.zeros_like(dk_acc)
    dv_acc[...] = jnp.zeros_like(dv_acc)
    norms[...] = jnp.zeros_like(norms)


    expert_id = lax.broadcasted_iota(jnp.int32, (EXPERTS, 1024), 0)
    alive = lax.broadcasted_iota(jnp.int32, (EXPERTS, 1024), 1) < length[0]
    hits = jnp.zeros((EXPERTS, 1024), f32)
    weight = jnp.zeros((EXPERTS, 1024), f32)
    for k in range(TOP_K):
        same = (picks[k : k + 1, :] == expert_id) & alive
        hits = jnp.where(same, 1.0, hits)
        weight = jnp.where(same, pick_w[k : k + 1, :], weight)
    hits = hits.astype(bf16)
    limit = ((5 * TOP_K * length[0] + 4 * EXPERTS - 1) // (4 * EXPERTS)).astype(f32)
    for b in range(4):
        rows = pl.ds(ROWS * b, ROWS)
        token = lax.broadcasted_iota(jnp.int32, (1024, ROWS), 1) + ROWS * b
        earlier = jnp.where(lax.broadcasted_iota(jnp.int32, (1024, ROWS), 0) < token, 1.0, 0.0).astype(bf16)
        places = dot_f(hits, earlier)
        kept = jnp.where(places < limit, weight[:, ROWS * b : ROWS * b + ROWS], 0.0)
        kept_out[:, rows] = kept
        slot_w[rows, :] = jnp.concatenate([kept, jnp.zeros((LANES - EXPERTS, ROWS), f32)], axis=0).T

    kept_copy = remote(kept_out, kept_in, ks.at[0], kr.at[0], mate)
    kept_copy.start()

    w_z.wait_recv()
    w_p.wait_recv()
    w_f.start()
    w_c.wait_recv()
    w_f.wait_recv()

    def cast_out(b, carry):
        for c in range(4):
            rhs[26 + c, block(b, 64), :] = buf[block(b, 64), 256 * c : 256 * c + 256].astype(bf16)
        return carry

    lax.fori_loop(0, 16, cast_out, 0)

    def forward_rows(b, carry):
        rows = block(b)
        for k in range(4):
            part = acc[rows, 256 * k : 256 * k + 256].astype(bf16)
            if k == 0:
                sums = [
                    hbuf[rows, 256 * col : 256 * col + 256].astype(f32) + dot_f(part, rhs[26 + col, 0:256, :])
                    for col in range(4)
                ]
            else:
                sums = [
                    sums[col] + dot_f(part, rhs[26 + col, 256 * k : 256 * k + 256, :]) for col in range(4)
                ]
        square = sum(jnp.sum(v * v, axis=1, keepdims=True) for v in sums)
        scale_r = lax.rsqrt(square * (1.0 / 1024.0) + EPSILON)
        for col in range(4):
            buf[rows, 256 * col : 256 * col + 256] = sums[col]
            normed = sums[col] * scale_r * gain[0:1, 256 * col : 256 * col + 256]
            normed = normed.astype(bf16)
            hbuf[rows, 256 * col : 256 * col + 256] = normed
            for half_c in range(2):
                lhs[16 + 2 * col + half_c, :, rows] = normed[:, 128 * half_c : 128 * half_c + 128].T
        return carry

    def place_of(k):
        paired = EARLY + (k - 2 * EARLY) // 2
        return jnp.where(k < EARLY, k, jnp.where(k < 2 * EARLY, k - EARLY, jnp.where(k < 16, paired, k - 16)))

    def is_mate(k):
        return ((k >= EARLY) & (k < 2 * EARLY)) | ((k >= 2 * EARLY) & (k < 16) & ((k - 2 * EARLY) % 2 == 1))

    def expert_of(k):
        return jnp.where(k < 16, 8 * y + place_of(k), 8 * (1 - y) + place_of(k))

    def next_weights(k):
        wait(expert_load(expert_of(k), k % 2))

        @pl.when(k < 23)
        def _():
            start(expert_load(expert_of(k + 1), (k + 1) % 2))

    def unit(k, b, kind, size=ROWS):
        rows = block(b, size)
        s = k % 2
        e = expert_of(k)
        el = place_of(k)
        if kind == "mate":
            both = dot_f(rhs[26, rows, :], wgu[s, 0:256, :])
            for c in range(1, 4):
                both = both + dot_f(rhs[26 + c, rows, :], wgu[s, 256 * c : 256 * c + 256, :])
        else:
            both = dot_f(hbuf[rows, :], wgu[s])
        d_base = 12 if kind == "mate" else 0
        gate, up = both[:, :LANES], both[:, LANES:]
        d_raw = dot_nt(rhs[d_base, rows, :], wdb[s, :, 0:256])
        for c in range(1, 4):
            d_raw = d_raw + dot_nt(rhs[d_base + c, rows, :], wdb[s, :, 256 * c : 256 * c + 256])
        lane = lax.broadcasted_iota(jnp.int32, (size, LANES), 1)
        weights = slot_m if kind == "mate" else slot_w
        weight = jnp.sum(jnp.where(lane == e, weights[rows, :], 0.0), axis=1, keepdims=True)
        sigma = 1.0 / (1.0 + jnp.exp(-gate))
        silu = gate * sigma
        hidden = silu * up
        hidden_t = (hidden * weight).astype(bf16).T
        d_hidden = d_raw * weight
        d_gate = (d_hidden * up * sigma * (1.0 + gate * (1.0 - sigma))).astype(bf16)
        d_up = (d_hidden * silu).astype(bf16)
        if kind == "mate":
            lhs[42 + el, :, rows] = hidden_t
            rhs[16 + el, rows, 0:LANES] = d_gate
            rhs[16 + el, rows, LANES:] = d_up
            return
        lhs[e, :, rows] = hidden_t
        inner = jnp.sum(hidden * d_raw, axis=1, keepdims=True)
        inner = jnp.where(weight > 0.0, inner, 0.0)
        is_first = kind == "first"
        acc[rows, 1024:1152] = jnp.where(lane == e, inner, 0.0 if is_first else acc[rows, 1024:1152])
        if kind == "other":
            part = dot_nt(jnp.concatenate([d_gate, d_up], axis=1), wgu[s])
        else:
            rhs[4 + el, rows, 0:LANES] = d_gate
            rhs[4 + el, rows, LANES:] = d_up
            part = dot_nt(rhs[4 + el, rows, :], wgu[s])
        acc[rows, 0:1024] = part if is_first else acc[rows, 0:1024] + part

    def forward_step(b, carry):
        @pl.when(b < 4)
        def _():
            gather_x(b).wait_recv()
            gather_f(b).start()

        @pl.when(b == 3)
        def _():
            d_share(0)
            d_share(1)

        @pl.when(b > 0)
        def _():
            gather_c(b - 1).wait_recv()
            gather_f(b - 1).wait_recv()
            gather_f(b - 1).wait_send()
            gather_x(b - 1).wait_send()
            gather_c(b - 1).wait_send()
            forward_rows(b - 1, 0)
            h_send(b - 1)
            unit(0, b - 1, "first")

        @pl.when(b == 4)
        def _():
            stage_d(direct_d[1])

        return carry

    for copy in (w_x, w_c, w_f, w_y, w_z, w_p):
        copy.wait_send()
    next_weights(0)
    lax.fori_loop(0, 5, forward_step, 0)
    keep = local(buf.at[:, wide], s_resid, iosem.at[0])
    keep.start()

    def d_late(j):
        stage_d(direct_d[j])

    chores = {
        4: [(h_share, 0), (h_share, 1), (d_late, 2), (d_late, 3)],
        8: [(d_forward, 0)],
        10: [(h_share, 2)],
        14: [(h_share, 3)],
        16: [(d_direct, 0), (h_forward, 0)],
        18: [(d_forward, 1), (d_direct, 1)],
        22: [(h_forward, 1)],
        27: [(h_forward, 2)],
    }

    def own_unit(u, carry):
        k = u // 4

        @pl.when(u % 4 == 0)
        def _():
            next_weights(k)

        @pl.when(u % 2 == 0)
        def _():
            unit(k, (u % 4) // 2, "own", 2 * ROWS)

        for when_u, jobs in chores.items():

            @pl.when(u == when_u)
            def _(jobs=jobs):
                for job, arg in jobs:
                    job(arg)

        return carry

    lax.fori_loop(4, 4 * EARLY, own_unit, 0)

    kept_copy.wait_recv()
    for b in range(4):
        rows = pl.ds(ROWS * b, ROWS)
        slot_m[rows, :] = jnp.concatenate(
            [kept_in[:, rows], jnp.zeros((LANES - EXPERTS, ROWS), f32)], axis=0
        ).T

    def take(b):
        rows = pl.ds(ROWS * b, ROWS)
        h_c(b).wait_recv()
        h_f(b).wait_recv()
        for c in range(4):
            whole = jnp.concatenate([ybuf[4 * (4 * b + j) + c] for j in range(4)], axis=0)
            rhs[12 + c, rows, :] = whole.astype(bf16)
            whole = jnp.concatenate([zbuf[4 * (4 * b + j) + c] for j in range(4)], axis=0)
            whole = whole.astype(bf16)
            rhs[26 + c, rows, :] = whole
            for half_c in range(2):
                lhs[34 + 2 * c + half_c, :, rows] = whole[:, 128 * half_c : 128 * half_c + 128].T
        unit(EARLY, b, "mate")

    next_weights(EARLY)
    for j in range(2):
        d_c(2 * core_mate + j).wait_recv()
        d_f(2 * (3 - tensor) + j).wait_recv()
    take(0)
    take(1)
    for j in range(2):
        d_c(8 + 2 * (1 - core) + j).wait_recv()
    take(2)
    d_direct(2)
    d_direct(3)
    h_forward(3)
    for j in range(2):
        d_c(12 + 2 * (1 - core) + j).wait_recv()
    take(3)
    kept_copy.wait_send()
    for j in range(2):
        d_y(near_d[j]).wait_send()
        d_x(near_d[j]).wait_send()
        d_c(near_d[j]).wait_send()
        d_f(2 * x_mate + j).wait_send()
    for j in range(4):
        d_y(direct_d[j]).wait_send()
        d_c(direct_d[j]).wait_send()
    for b in range(4):
        h_y(b).wait_send()
        h_x(b).wait_send()
        h_c(b).wait_send()
        h_f(b).wait_send()

    pl.semaphore_signal(go, inc=1, device_id={"dp": mate}, device_id_type=MESH)

    @pl.when(z < last)
    def _():
        pl.semaphore_signal(go, inc=1, device_id={"dp": up_id}, device_id_type=MESH)

    @pl.when(z > 0)
    def _():
        pl.semaphore_signal(go, inc=1, device_id={"dp": dn_id}, device_id_type=MESH)

    def half_pass(u):
        k = EARLY + 1 + u // 2

        @pl.when(u % 2 == 0)
        def _():
            next_weights(k)

        @pl.when(is_mate(k))
        def _():
            unit(k, u % 2, "mate", 2 * ROWS)

        @pl.when((k < 16) & jnp.logical_not(is_mate(k)))
        def _():
            unit(k, u % 2, "own", 2 * ROWS)

        @pl.when(k >= 16)
        def _():
            unit(k, u % 2, "other", 2 * ROWS)

    mine = pl.ds(pl.multiple_of(core * 512, 512), 512)
    other = pl.ds(pl.multiple_of((1 - core) * 512, 512), 512)

    def span(k):
        return pl.ds(0, 1152 if k == 0 else 1024)

    def sum_a(k):
        return remote(acc.at[other, span(k)], buf.at[pl.ds(0, 512), span(k)], s1s.at[k], s1r.at[k], core_mate, "tensor")

    def sum_b(k):
        return remote(acc.at[mine, span(k)], buf.at[pl.ds(512, 512), span(k)], s2s.at[k], s2r.at[k], x_mate, "tensor")

    def sum_c(k):
        part = acc.at[mine, span(k)]
        return remote(part, part, s3s.at[k], s3r.at[k], core_mate, "tensor")

    def add_in(k, at_row):
        def step(b, carry):
            rows = pl.ds(pl.multiple_of(core * 512 + b * 64, 64), 64)
            acc[rows, span(k)] += buf[pl.ds(pl.multiple_of(at_row + b * 64, 64), 64), span(k)]
            return carry

        lax.fori_loop(0, 8, step, 0)

    def sum_first(k):
        pl.semaphore_signal(ready1.at[k], inc=1, device_id={"tensor": core_mate}, device_id_type=MESH)
        pl.semaphore_signal(ready2.at[k], inc=1, device_id={"tensor": x_mate}, device_id_type=MESH)
        pl.semaphore_wait(ready1.at[k], 1)
        sum_a(k).start()

    def sum_second(k):
        sum_a(k).wait_recv()
        add_in(k, 0)
        sum_a(k).wait_send()
        pl.semaphore_signal(ready3.at[k], inc=1, device_id={"tensor": core_mate}, device_id_type=MESH)
        pl.semaphore_wait(ready2.at[k], 1)
        sum_b(k).start()

    def sum_third(k):
        sum_b(k).wait_recv()
        sum_b(k).wait_send()
        add_in(k, 512)
        pl.semaphore_wait(ready3.at[k], 1)
        sum_c(k).start()

    def sum_last(k):
        sum_c(k).wait_recv()
        sum_c(k).wait_send()

    def norm_sum(step, dev):
        return remote(norms.at[pl.ds(0, 16)], norm_in.at[step], ns.at[step], nr.at[step], dev)

    partners = (mate, pair, far)

    def norm_next(step):
        if step > 0:
            norm_sum(step - 1, partners[step - 1]).wait_recv()
            norm_sum(step - 1, partners[step - 1]).wait_send()
            norms[...] = norms[...] + norm_in[step - 1]
        if step < 3:
            norm_sum(step, partners[step]).start()

    def norm_back(values, scale_r, grads, which):
        inner = sum(
            jnp.sum(v * scale_r * (g * gain[which : which + 1, 256 * c : 256 * c + 256]), axis=1, keepdims=True)
            for c, (v, g) in enumerate(zip(values, grads))
        ) * (1.0 / 1024.0)
        outs = []
        for c, (v, g) in enumerate(zip(values, grads)):
            normed = v * scale_r
            total = jnp.sum(g * normed, axis=0, keepdims=True)
            row = 8 * which + 2 * c
            norms[row : row + 1, :] += total[:, :LANES]
            norms[row + 1 : row + 2, :] += total[:, LANES:]
            outs.append(scale_r * (g * gain[which : which + 1, 256 * c : 256 * c + 256] - normed * inner))
        return outs

    def middle_rows(b):
        rows = block(b)

        values = [buf[rows, 256 * c : 256 * c + 256] for c in range(4)]
        grads = [acc[rows, 256 * c : 256 * c + 256] for c in range(4)]
        square = sum(jnp.sum(v * v, axis=1, keepdims=True) for v in values)
        scale_r = lax.rsqrt(square * (1.0 / 1024.0) + EPSILON)
        back = norm_back(values, scale_r, grads, 0)
        for c in range(4):
            total = rhs[c, rows, :].astype(f32) + back[c]
            acc[rows, 256 * c : 256 * c + 256] = total
            rhs[26 + c, rows, :] = total.astype(bf16)
        for h in range(4):
            d_head = dot_nt(rhs[26, rows, :], wdb[h, :, 0:256])
            for c in range(1, 4):
                d_head = d_head + dot_nt(rhs[26 + c, rows, :], wdb[h, :, 256 * c : 256 * c + 256])
            da2[h, rows, :] = d_head.astype(bf16)

    def turn_back(grad, cols):
        one, two = grad[:32], grad[32:]
        cosine, sine = cos_t[:, cols], sin_t[:, cols]
        return jnp.concatenate([one * cosine + two * sine, two * cosine - one * sine], axis=0)

    def attend_back(h, qb):
        keys = ROWS * (qb + 1)
        rows = pl.ds(ROWS * qb, ROWS)
        q_rows = q2[h, rows, :]
        d_rows = da2[h, rows, :]
        exact = jnp.exp(masked_scores(h, qb) - lse[pl.ds(h, 1), rows])
        d_probs = dot_nt(v2[0:keys, :], d_rows)
        inner = jnp.sum(exact * d_probs, axis=0, keepdims=True)
        d_scores = (exact * (d_probs - inner)).astype(bf16)
        dk_acc[0:keys, :] += dot_f(d_scores, q_rows)
        dv_acc[0:keys, :] += dot_f(exact.astype(bf16), d_rows)
        k_head = kt2[pl.ds(pl.multiple_of((h // 2) * 64, 64), 64), 0:keys]
        d_q = dot_f(k_head, d_scores) * scaling
        buf[pl.ds(pl.multiple_of(h * 64, 64), 64), rows] = turn_back(d_q, rows)

    def turn_rows(b):
        rows = block(b)
        rhs[24, rows, :] = buf[0:256, rows].T.astype(bf16)
        d_k = (dk_acc[rows, :] * scaling).T
        d_k = jnp.concatenate([turn_back(d_k[:64], rows), turn_back(d_k[64:], rows)], axis=0)
        rhs[25, rows, 0:LANES] = d_k.T.astype(bf16)
        rhs[25, rows, LANES:] = dv_acc[rows, :].astype(bf16)

    def project_rows(b):
        rows = block(b)
        acc[rows, 0:1024] = dot_nt(rhs[24, rows, :], wgu[0]) + dot_nt(rhs[25, rows, :], wgu[1])

    def token_rows(b):
        rows = block(b)

        values = [hbuf[rows, 256 * c : 256 * c + 256].astype(f32) for c in range(4)]
        grads = [acc[rows, 256 * c : 256 * c + 256] for c in range(4)]
        square = sum(jnp.sum(v * v, axis=1, keepdims=True) for v in values)
        scale_r = lax.rsqrt(square * (1.0 / 1024.0) + EPSILON)
        back = norm_back(values, scale_r, grads, 1)
        for c in range(4):
            cols = slice(256 * c, 256 * c + 256)
            hbuf[rows, cols] = (buf[rows, cols] + back[c]).astype(bf16)

    def pair_load(pair, s):
        return local(w_down.at[pl.ds(2 * pair, 2)], wdb.at[pl.ds(2 * s, 2)], wsem.at[s, 2])

    def moe_pair(pair):
        s = pair % 2
        pair_load(pair, s).wait()

        @pl.when(pair + 1 < EXPERTS // 2)
        def _():
            pair_load(pair + 1, 1 - s).start()

        def rows_of(b, carry):
            rows = block(b)
            hidden = lhs[pl.ds(2 * pair, 2), :, rows].reshape(256, ROWS)
            down = wdb[pl.ds(2 * s, 2)].reshape(256, 1024)
            part = dot_tn(hidden, down)

            @pl.when(pair == 0)
            def _():
                acc[rows, 0:1024] = part

            @pl.when(pair > 0)
            def _():
                acc[rows, 0:1024] += part

            return carry

        lax.fori_loop(0, 4, rows_of, 0)

    def result_rows(b):
        rows = block(b)

        pos = lax.broadcasted_iota(jnp.int32, (ROWS, 1024), 0) + b * ROWS
        total = buf[rows, wide] + acc[rows, 0:1024]
        hbuf[rows, :] = jnp.where(pos < length[0], total, 0.0).astype(bf16)

    def halves_in(src):
        return [local(src, buf.at[:, wide], iosem.at[1])]

    tokens_in = [local(x_in, hbuf, iosem.at[3])]
    wo_load = [
        local(w_out.at[pl.ds(64 * h, 64)], wdb.at[h, pl.ds(64 * (h // 2), 64)], ld.at[8 + h]) for h in range(4)
    ]
    dots_out = [local(d_pick, o_dots, iosem.at[7])]
    norms_out = [
        local(norms.at[pl.ds(0, 8)], o_norm0, iosem.at[2]),
        local(norms.at[pl.ds(8, 8)], o_norm1, iosem.at[4]),
    ]

    def pick_dots():
        for b in range(4):
            rows = pl.ds(ROWS * b, ROWS)
            dots = acc[rows, 1024:1152].T[:EXPERTS]
            lane_e = lax.broadcasted_iota(jnp.int32, (EXPERTS, ROWS), 0)
            for k in range(TOP_K):
                mine_k = jnp.where(picks[k : k + 1, rows] == lane_e, dots, 0.0)
                d_pick[k : k + 1, rows] = jnp.sum(mine_k, axis=0, keepdims=True)
    dres_out = [local(acc.at[:, wide], s_dres, iosem.at[8])]
    tokens_out = [local(hbuf, o_tokens, iosem.at[9])]
    result_out = [local(hbuf, o_result, iosem.at[10])]

    def clear_wo():
        for h in range(4):
            wdb[h, 64 - 64 * (h // 2) : 128 - 64 * (h // 2), :] = jnp.zeros((64, 1024), bf16)

    def do_all(*steps):
        for step in steps:
            step()

    once = {
        T_SUM1: lambda: do_all(keep.wait, lambda: sum_first(0), clear_wo, lambda: start(tokens_in + wo_load + proj_load)),
        T_SUM1 + 2: lambda: do_all(lambda: sum_second(0), lambda: wait(tokens_in)),
        T_MID1 - 3: lambda: sum_third(0),
        T_MID1 - 1: lambda: do_all(
            lambda: sum_last(0), pick_dots, lambda: start(halves_in(s_resid) + dots_out), lambda: wait(wo_load)
        ),
        T_ATT: lambda: do_all(lambda: wait(dots_out), lambda: start(dres_out)),
        T_PROJ - 1: lambda: do_all(lambda: wait(dres_out), lambda: wait(proj_load)),
        T_SUM2: lambda: sum_first(1),
        T_SUM2 + 2: lambda: sum_second(1),
        T_TOK - 3: lambda: sum_third(1),
        T_TOK - 1: lambda: do_all(
            lambda: sum_last(1), lambda: start(halves_in(s_dres)), lambda: start([pair_load(0, 0)])
        ),
        T_MOE: lambda: start(tokens_out),
        T_SUM3 + 5: lambda: norm_next(0),
        T_SUM3 + 7: lambda: norm_next(1),
        T_SUM3 + 9: lambda: norm_next(2),
        T_SUM3 + 11: lambda: do_all(lambda: norm_next(3), lambda: start(norms_out)),
        T_SUM3: lambda: sum_first(2),
        T_SUM3 + 2: lambda: sum_second(2),
        T_RES - 3: lambda: sum_third(2),
        T_RES - 1: lambda: do_all(
            lambda: sum_last(2), lambda: wait(tokens_out + norms_out), lambda: start(halves_in(s_resid))
        ),
        T_RES + 4: lambda: start(result_out),
        T_RES + 8: lambda: wait(result_out),
    }
    halves_wait = {T_MID1: s_resid, T_TOK: s_dres, T_RES: s_resid}

    def work(t):
        for when_t, fn in sorted(once.items()):
            pl.when(t == when_t)(fn)
        for when_t, src in halves_wait.items():
            pl.when(t == when_t)(lambda src=src: wait(halves_in(src)))
        for begin, count, fn in (
            (0, 2 * (23 - EARLY), half_pass),
            (T_MID1, 4, middle_rows),
            (T_TURN, 2, lambda u: do_all(lambda: turn_rows(2 * u), lambda: turn_rows(2 * u + 1))),
            (T_PROJ, 2, lambda u: do_all(lambda: project_rows(2 * u), lambda: project_rows(2 * u + 1))),
            (T_TOK, 2, lambda u: do_all(lambda: token_rows(2 * u), lambda: token_rows(2 * u + 1))),
            (T_MOE, EXPERTS // 4, lambda u: do_all(lambda: moe_pair(2 * u), lambda: moe_pair(2 * u + 1))),
            (T_RES, 4, result_rows),
        ):
            pl.when((t >= begin) & (t < begin + count))(lambda fn=fn, begin=begin: fn(t - begin))
        for pair_b in range(2):
            u = t - T_ATT

            def two(pair_b=pair_b, u=u):
                attend_back(u // 2, pair_b)
                attend_back(u // 2, 3 - pair_b)

            pl.when((u >= 0) & (u < 8) & (u % 2 == pair_b))(two)

    own = pl.ds(pl.multiple_of(y * 32, 32), 32)
    oth = pl.ds(pl.multiple_of((1 - y) * 32, 32), 32)
    half = pl.ds(0, 32)
    upper = pl.ds(32, 32)

    def stage(c, t):
        p = z if c == 0 else last - z
        nxt, prv = (up_id, dn_id) if c == 0 else (dn_id, up_id)
        def at(delay, body):
            i = t - delay - c

            @pl.when((i >= 0) & (i < N_CLASS))
            def _():
                s = c * ring + i % ring
                body(i, s, i < N_EXPERT, (i >= N_EXPERT) & (i % 2 == 0), (i >= N_EXPERT) & (i % 2 == 1))

        def ycopy_a(s):
            return remote(pbuf.at[s, oth], ybuf.at[s, half], ys.at[s], yr.at[s], mate)

        def ycopy_b(s):
            return remote(zbuf.at[s], ybuf.at[s], ys.at[s], yr.at[s], mate)

        def zcopy_a(s):
            return remote(zbuf.at[s, half], zbuf.at[s, half], zs.at[s], zr.at[s], nxt)

        def zcopy(s):
            return remote(zbuf.at[s], zbuf.at[s], zs.at[s], zr.at[s], nxt)

        def fcopy_a(s):
            return remote(pbuf.at[s, own], pbuf.at[s, own], fs.at[s], fr.at[s], prv)

        def fcopy(s):
            return remote(pbuf.at[s], pbuf.at[s], fs.at[s], fr.at[s], prv)

        def gcopy_a(s):
            return remote(pbuf.at[s, own], ybuf.at[s, upper], gs.at[s], gr.at[s], mate)

        def gcopy(s):
            return remote(pbuf.at[s], ybuf.at[s], gs.at[s], gr.at[s], mate)

        def first(i, s, is_e, is_a, is_b):
            m = i // 2
            g = 2 * m + c

            @pl.when((i % 2 == 0) & is_e)
            def _():
                el, part = g // 12, g % 12
                down = part < 4
                l_one = jnp.where(down, 8 * y + el, 12 + part)
                r_one = jnp.where(down, part, 4 + el)
                l_two = jnp.where(down, 42 + el, 30 + part)
                r_two = jnp.where(down, 12 + part, 16 + el)
                total = dot_f(lhs[l_one], rhs[r_one]) + dot_f(lhs[l_two], rhs[r_two])
                pbuf[s] = total[:CHUNK]
                pbuf[s + 1] = total[CHUNK:]

            @pl.when((i % 2 == 0) & jnp.logical_not(is_e))
            def _():
                a = g - N_EXPERT
                l_one = jnp.where(a < 8, 32 + a // 4, 24 + a % 8)
                r_one = jnp.where(a < 8, 26 + a % 4, 23 + a // 8)
                total = dot_f(lhs[l_one], rhs[r_one])
                pbuf[s] = total[:CHUNK]
                pbuf[s + 1] = total[CHUNK:]

            @pl.when(is_a)
            def _():
                ycopy_a(s).start()

        def second(i, s, is_e, is_a, is_b):
            @pl.when(is_a)
            def _():
                ycopy_a(s).wait_recv()

                @pl.when(p > 0)
                def _():
                    zcopy_a(s).wait_recv()
                    zbuf[s, half] = zbuf[s, half] + (pbuf[s, own] + ybuf[s, half])

                @pl.when(p == 0)
                def _():
                    zbuf[s, half] = pbuf[s, own] + ybuf[s, half]

                @pl.when(p < last)
                def _():
                    zcopy_a(s).start()

                @pl.when(p == last)
                def _():
                    pbuf[s, own] = zbuf[s, half]
                    fcopy_a(s).start()
                    gcopy_a(s).start()

            @pl.when(jnp.logical_not(is_a))
            def _():
                @pl.when(p > 0)
                def _():
                    zcopy(s).wait_recv()
                    zbuf[s] = zbuf[s] + pbuf[s]

                @pl.when(p == 0)
                def _():
                    zbuf[s] = pbuf[s]

                @pl.when(p < last)
                def _():
                    zcopy(s).start()

                @pl.when((p == last) & is_e)
                def _():
                    pbuf[s] = zbuf[s]
                    fcopy(s).start()
                    gcopy(s).start()

                @pl.when((p == last) & is_b)
                def _():
                    ycopy_b(s).start()

        def third(i, s, is_e, is_a, is_b):
            @pl.when(is_b & (p == last))
            def _():
                ycopy_b(s).wait_recv()
                pbuf[s] = zbuf[s] + ybuf[s]
                fcopy(s).start()

        def fourth(i, s, is_e, is_a, is_b):
            @pl.when(p < last)
            def _():
                @pl.when(is_a)
                def _():
                    fcopy_a(s).wait_recv()

                    @pl.when(p > 0)
                    def _():
                        fcopy_a(s).start()

                    gcopy_a(s).start()

                @pl.when(jnp.logical_not(is_a))
                def _():
                    fcopy(s).wait_recv()

                    @pl.when(p > 0)
                    def _():
                        fcopy(s).start()

                    @pl.when(is_e)
                    def _():
                        gcopy(s).start()

        def store(buf_s, sem, dst0, dst1):
            local(buf_s.at[:, pl.ds(0, LANES)], dst0, sem).start()
            local(buf_s.at[:, pl.ds(LANES, LANES)], dst1, sem).start()

        def fifth(i, s, is_e, is_a, is_b):
            @pl.when(is_a)
            def _():
                gcopy_a(s).wait_recv()
                ycopy_a(s).wait_send()
                pbuf[s, oth] = ybuf[s, upper]

            @pl.when(is_e)
            def _():
                gcopy(s).wait_recv()

            g = 2 * (i // 2) + c
            el, part = g // 12, g % 12
            a = g - N_EXPERT
            low = CHUNK * (i % 2)

            def at_rows(start_row):
                return pl.ds(pl.multiple_of(start_row + low, CHUNK), CHUNK)

            def both_rows(write):
                write(pbuf.at[s], os0.at[s], 8 * y + el)
                write(ybuf.at[s], os1.at[s], 8 * (1 - y) + el)

            @pl.when(is_e & (part < 4))
            def _():
                col = pl.ds(pl.multiple_of(part * 256, LANES), LANES)
                col1 = pl.ds(pl.multiple_of(part * 256 + LANES, LANES), LANES)
                both_rows(
                    lambda src, sem, e: store(
                        src, sem, o_down.at[e, at_rows(0), col], o_down.at[e, at_rows(0), col1]
                    )
                )

            @pl.when(is_e & (part >= 4))
            def _():
                rows = at_rows((part - 4) * 128)
                both_rows(lambda src, sem, e: store(src, sem, o_gate.at[e, rows], o_up.at[e, rows]))

            @pl.when(jnp.logical_not(is_e) & (a < 8))
            def _():
                rows = at_rows((a // 4) * 128)
                col = pl.ds(pl.multiple_of((a % 4) * 256, LANES), LANES)
                col1 = pl.ds(pl.multiple_of((a % 4) * 256 + LANES, LANES), LANES)
                store(pbuf.at[s], os0.at[s], o_out.at[rows, col], o_out.at[rows, col1])

            @pl.when(jnp.logical_not(is_e) & (a >= 8) & (a < 16))
            def _():
                rows = at_rows((a - 8) * 128)
                store(pbuf.at[s], os0.at[s], o_q.at[rows, pl.ds(0, LANES)], o_q.at[rows, pl.ds(LANES, LANES)])

            @pl.when(jnp.logical_not(is_e) & (a >= 16))
            def _():
                rows = at_rows((a - 16) * 128)
                store(pbuf.at[s], os0.at[s], o_k.at[rows], o_v.at[rows])

        def sixth(i, s, is_e, is_a, is_b):
            local(pbuf.at[s], o_q.at[pl.ds(0, CHUNK)], os0.at[s]).wait()

            @pl.when(is_e)
            def _():
                local(ybuf.at[s], o_q.at[pl.ds(0, CHUNK)], os1.at[s]).wait()
                gcopy(s).wait_send()

            @pl.when(is_a)
            def _():
                gcopy_a(s).wait_send()

                @pl.when(p < last)
                def _():
                    zcopy_a(s).wait_send()

                @pl.when(p > 0)
                def _():
                    fcopy_a(s).wait_send()

            @pl.when(jnp.logical_not(is_a))
            def _():
                @pl.when(p < last)
                def _():
                    zcopy(s).wait_send()

                @pl.when((p == last) & is_b)
                def _():
                    ycopy_b(s).wait_send()

                @pl.when(p > 0)
                def _():
                    fcopy(s).wait_send()

        t2 = hop * (1 + p)
        t3 = hop * (2 + last)
        t4 = t3 + hop * (last - p)
        t5 = t4 + hop
        t6 = t5 + hop
        return [(0, first, at), (t2, second, at), (t3, third, at), (t4, fourth, at), (t5, fifth, at), (t6, sixth, at)]

    def body(t, carry):
        @pl.when(t == 1)
        def _():
            pl.semaphore_wait(go, 1 + (z < last).astype(jnp.int32) + (z > 0).astype(jnp.int32))

        both = [stage(0, t), stage(1, t)]
        for k in (1, 2, 3, 4, 5, 0):
            if k == 0:
                work(t)
            for st in both:
                delay, fn, at = st[k]
                at(delay, fn)
        return carry

    total = N_CLASS + hop * (2 * last + 4) + 2
    lax.fori_loop(0, total, body, 0)


def run_layer(mesh, *operands):
    groups = mesh.shape["dp"]
    nz = 4 if groups % 8 == 0 else groups // 2
    last = nz - 1
    hop = HOP
    ring = hop * (2 * last + 4) + 2
    ring = max(32, ring + ring % 2)
    f32, bf16 = jnp.float32, jnp.bfloat16

    def out(shape, kind=f32):
        return jax.ShapeDtypeStruct(shape, kind)

    outs = [
        out((16, 1024, 128)), out((16, 1024, 128)), out((16, 128, 1024)),
        out((1024, 256)), out((1024, 128)), out((1024, 128)), out((256, 1024)), out((8, 128)), out((8, 128)),
        out((1024, 1024), bf16), out((1024, 1024), bf16), out((8, 1024)),
        out((1024, 1024)), out((1024, 1024)),
    ]
    anywhere = pl.BlockSpec(memory_space=pl.ANY)
    dma = pltpu.SemaphoreType.DMA
    reg = pltpu.SemaphoreType.REGULAR
    vmem = pltpu.VMEM
    res = pl.pallas_call(
        functools.partial(layer_kernel, nz, hop, ring),
        out_shape=outs,
        in_specs=[pl.BlockSpec(memory_space=pltpu.SMEM)] + [anywhere] * (len(operands) - 1),
        out_specs=[anywhere] * len(outs),
        scratch_shapes=[
            vmem((50, 128, 1024), bf16), vmem((30, 1024, 256), bf16),
            vmem((2 * ring, CHUNK, 256), f32), vmem((2 * ring, CHUNK, 256), f32), vmem((2 * ring, CHUNK, 256), f32),
            vmem((1024, 1152), f32), vmem((1024, 1152), f32),
            vmem((1024, 1024), bf16), vmem((2, 1024, 256), bf16), vmem((4, 128, 1024), bf16),
            vmem((4, 1024, 128), bf16), vmem((1024, 128), bf16), vmem((1024, 128), bf16),
            vmem((128, 1024), bf16), vmem((128, 1024), bf16),
            vmem((8, 1024), f32), vmem((32, 1024), f32), vmem((32, 1024), f32),
            vmem((4, 1024, 128), bf16), vmem((1024, 128), f32), vmem((1024, 128), f32),
            vmem((1024, 128), f32), vmem((8, 1024), f32), vmem((16, 128), f32),
            vmem((8, 1024), jnp.int32), vmem((8, 1024), f32),
            vmem((3, 16, 128), f32), vmem((8, 1024), f32),
            vmem((EXPERTS, 1024), f32), vmem((EXPERTS, 1024), f32), vmem((1024, 128), f32),
            dma((18,)), dma((2, 3)), dma((11,)),
        ]
        + [dma((2 * ring,))] * 10
        + [dma((4,))] * 6
        + [dma((6,))] * 2
        + [dma((3,))] * 6
        + [reg((3,))] * 3
        + [dma((3,))] * 2
        + [reg]
        + [dma((4,))] * 8
        + [dma((16,))] * 8
        + [dma((1,))] * 2,
        compiler_params=pltpu.CompilerParams(
            collective_id=0, has_side_effects=True, vmem_limit_bytes=63 * 2**20
        ),
    )(*operands)
    sums, rest = tuple(res[:9]), res[9:12]
    if groups > 2 * nz:
        same = [
            [2 * nz * block + place for block in range(groups // (2 * nz))] for place in range(2 * nz)
        ]
        sums = lax.psum(sums, "dp", axis_index_groups=same)
    return sums, rest


def per_device(
    mesh,
    tokens,
    lengths,
    chosen,
    gate_values,
    cotangent,
    norm_attn,
    w_query,
    w_key,
    w_value,
    w_out,
    norm_moe,
    w_gate,
    w_up,
    w_down,
):
    seq_len = tokens.shape[0] // lengths.shape[0]
    cosine, sine = rope_tables(seq_len, HEAD_DIM)
    sums, (result, grad_tokens, dots) = run_layer(
        mesh,
        lengths,
        tokens,
        cotangent,
        chosen.T,
        gate_values.T,
        norm_attn[None, :],
        norm_moe[None, :],
        w_gate,
        w_up,
        w_down,
        cosine,
        sine,
        w_out,
        w_query,
        w_key,
        w_value,
    )
    grad_gate, grad_up, grad_down, grad_query, grad_key, grad_value, grad_out, grad_norm_moe, grad_norm_attn = sums
    return (
        result,
        grad_tokens,
        dots.T,
        grad_norm_attn.reshape(-1),
        grad_query,
        grad_key,
        grad_value,
        grad_out,
        grad_norm_moe.reshape(-1),
        grad_gate,
        grad_up,
        grad_down,
    )


def solution(mesh):
    placed = (
        P("dp", None),
        P("dp"),
        P("dp", None),
        P("dp", None),
        P("dp", None),
        P(),
        P(None, "tensor"),
        P(None, "tensor"),
        P(None, "tensor"),
        P("tensor", None),
        P(),
        P(None, None, "tensor"),
        P(None, None, "tensor"),
        P(None, "tensor", None),
    )
    return jax.shard_map(
        functools.partial(per_device, mesh),
        mesh=mesh,
        in_specs=placed,
        out_specs=(
            P("dp", None),
            P("dp", None),
            P("dp", None),
            P(),
            P(None, "tensor"),
            P(None, "tensor"),
            P(None, "tensor"),
            P("tensor", None),
            P(),
            P(None, None, "tensor"),
            P(None, None, "tensor"),
            P(None, "tensor", None),
        ),
        check_vma=False,
    )
```
